32 devices in a mesh: ctx: 8 (over y, x, core), fsdp: 4 (over z).
Axes of the slice: x: 2, y: 2, z: 4, core: 2. Of those that a mesh axis runs over, the one named last changes fastest.
Arguments:
- tokens: bfloat16 [4096, 960], P(('ctx', 'fsdp')), may hold values from -6 to 6
- pair_order: int32 [32], replicated, may hold values from 0 to 31, each once
- gain_attn: bfloat16 [960], P('fsdp'), may hold values from 0.5 to 1.5
- gain_mlp: bfloat16 [960], P('fsdp'), may hold values from 0.5 to 1.5
- w_query: bfloat16 [960, 960], P('fsdp'), may hold values from -0.3125 to 0.3125
- w_key: bfloat16 [960, 320], P('fsdp'), may hold values from -0.3125 to 0.3125
- w_value: bfloat16 [960, 320], P('fsdp'), may hold values from -0.1875 to 0.1875
- w_out: bfloat16 [960, 960], P('fsdp'), may hold values from -0.75 to 0.75
- w_gate: bfloat16 [960, 2560], P('fsdp'), may hold values from -0.1875 to 0.1875
- w_up: bfloat16 [960, 2560], P('fsdp'), may hold values from -0.1875 to 0.1875
- w_down: bfloat16 [2560, 960], P('fsdp'), may hold values from -0.125 to 0.125
- cotangent: bfloat16 [4096, 960], P(('ctx', 'fsdp')), may hold values from -6 to 6
Outputs:
- layer_out: bfloat16 [4096, 960], P(('ctx', 'fsdp'))
- grad_tokens: float32 [4096, 960], P(('ctx', 'fsdp'))
- grad_gain_attn: float32 [960], P('fsdp')
- grad_gain_mlp: float32 [960], P('fsdp')
- grad_w_query: float32 [960, 960], P('fsdp')
- grad_w_key: float32 [960, 320], P('fsdp')
- grad_w_value: float32 [960, 320], P('fsdp')
- grad_w_out: float32 [960, 960], P('fsdp')
- grad_w_gate: float32 [960, 2560], P('fsdp')
- grad_w_up: float32 [960, 2560], P('fsdp')
- grad_w_down: float32 [2560, 960], P('fsdp')
The draws below stay inside these ranges and needn't reach their ends.
Inputs may be any that keep to these rules, and one draw needn't show every extreme that they name: Slot d holds sequence blocks pair_order[d] and 63 - pair_order[d]; each value appears once.
All inputs are finite; a program needn't handle non-finite values.
Results may differ from the reference program's by a relative error of at most 0.025.
Values may be sent and summed in bfloat16 or wider, within the bound.
No kernel may reach another device: no remote copies, remote signals or barrier semaphores. Data moves between devices by JAX's collectives and lax.ppermute only.
A program may use at most 256 MiB of HBM per device.

```python
import math
import jax
import jax.numpy as jnp
from jax import lax

D = 960
FF = 2560
HEADS = 15
KV_HEADS = 5
HEAD = 64
TOK_DEV = 128
TOKENS = 4096


def steps_of(own_key, extent, cuts, smallest, top_value):
    factor_of, own = 1.0, jax.random.fold_in(own_key, 6)
    for axis_at, blocks in cuts:
        heights = jnp.exp(jax.random.uniform(jax.random.fold_in(own, axis_at), (blocks,), jnp.float32, smallest / len(cuts), top_value / len(cuts)))
        factor_of = factor_of * jnp.repeat(heights, extent[axis_at] // blocks).reshape([-1 if axis == axis_at else 1 for axis in range(len(extent))])
    return factor_of


def scatter_about(stream_key, shape, deviation, limit, cuts=(), held_as=jnp.bfloat16):
    values = jax.random.normal(stream_key, shape, jnp.float32) * deviation
    if len(cuts) > 0:
        values = steps_of(stream_key, shape, cuts, -0.22, 0.18) * values
    return jnp.clip(values, min=-limit, max=limit).astype(held_as)


def setup_inputs(seed: int = 0) -> dict:
    key_of = jax.random.split(jax.random.key(seed), 13)
    tokens = scatter_about(key_of[0], (TOKENS, D), 1.0, 6.0, ((0, 32),))
    pair_order = jax.random.permutation(key_of[1], TOKENS // TOK_DEV).astype(jnp.int32)
    gain_attn = jnp.clip(1.0 + 0.1 * jax.random.normal(key_of[2], (D,), jnp.float32), 0.5, 1.5).astype(jnp.bfloat16)
    gain_mlp = jnp.clip(1.0 + 0.1 * jax.random.normal(key_of[3], (D,), jnp.float32), 0.5, 1.5).astype(jnp.bfloat16)
    w_query = scatter_about(key_of[4], (D, HEADS * HEAD), (D * 2 // 5) ** -0.5, 0.3125, ((0, 4),))
    w_key = scatter_about(key_of[5], (D, KV_HEADS * HEAD), (D * 2 // 5) ** -0.5, 0.3125, ((0, 4),))
    w_value = scatter_about(key_of[6], (D, KV_HEADS * HEAD), D ** -0.5, 0.1875, ((0, 4),))
    w_out = scatter_about(key_of[7], (HEADS * HEAD, D), (HEADS * HEAD // 16) ** -0.5, 0.75, ((0, 4),))
    w_gate = scatter_about(key_of[8], (D, FF), D ** -0.5, 0.1875, ((0, 4),))
    w_up = scatter_about(key_of[9], (D, FF), D ** -0.5, 0.1875, ((0, 4),))
    w_down = scatter_about(key_of[10], (FF, D), FF ** -0.5, 0.125, ((0, 4),))
    cotangent = scatter_about(key_of[11], (TOKENS, D), 1.0, 6.0, ((0, 32),))
    return dict(tokens=tokens, pair_order=pair_order, gain_attn=gain_attn, gain_mlp=gain_mlp, w_query=w_query, w_key=w_key, w_value=w_value, w_out=w_out, w_gate=w_gate, w_up=w_up, w_down=w_down, cotangent=cotangent)


epsilon = 1e-05
base_theta = 100000.0
far_below = -1e+30
HIGH = lax.Precision.HIGHEST

@jax.custom_vjp
def low(v):
    return lax.optimization_barrier(v.astype(jnp.bfloat16)).astype(jnp.float32)

@jax.custom_vjp
def low_back(v):
    return v

def low_keep(v):
    return (low(v), None)

def low_pass(kept, grad):
    return (grad,)

def back_keep(v):
    return (v, None)

def back_low(kept, grad):
    return (low(grad),)
low.defvjp(low_keep, low_pass)
low_back.defvjp(back_keep, back_low)

def positions(pair_order, local_rows):
    devices = pair_order.shape[0]
    half_rows = local_rows // 2
    first_block = pair_order.astype(jnp.int32) * half_rows
    second_block = (2 * devices - 1 - pair_order.astype(jnp.int32)) * half_rows
    offsets = jnp.arange(half_rows, dtype=jnp.int32)
    placed = jnp.concatenate([first_block[:, None] + offsets[None, :], second_block[:, None] + offsets[None, :]], axis=1)
    return placed.reshape(-1)

def rotate(matrix, places, heads, sign):
    width = matrix.shape[1] // heads
    half_width = width // 2
    freqs = base_theta ** (-2.0 * jnp.arange(half_width, dtype=jnp.float32) / width)
    angles = places.astype(jnp.float32)[:, None] * freqs[None, :]
    cosine = jnp.cos(angles)[:, None, :]
    sine = sign * jnp.sin(angles)[:, None, :]
    split = matrix.reshape(matrix.shape[0], heads, width)
    front = split[..., :half_width]
    back = split[..., half_width:]
    turned = jnp.concatenate([front * cosine - back * sine, back * cosine + front * sine], axis=2)
    return turned.reshape(matrix.shape)

def matmul(left, right):
    return jnp.dot(left, right, preferred_element_type=jnp.float32, precision=HIGH)

def normed(matrix, gain):
    scale_rows = lax.rsqrt(lax.optimization_barrier(jnp.mean(matrix * matrix, axis=1, keepdims=True)) + epsilon)
    return matrix * scale_rows * gain[None, :]

def attend(query, key, value, places):
    count = query.shape[0]
    group = HEADS // KV_HEADS
    keys = jnp.repeat(key.reshape(count, KV_HEADS, HEAD), group, axis=1)
    values = jnp.repeat(value.reshape(count, KV_HEADS, HEAD), group, axis=1)
    block_rows = math.gcd(count, 128)
    blocks = count // block_rows
    queries = query.reshape(blocks, block_rows, HEADS, HEAD)
    query_places = places.reshape(blocks, block_rows)

    @jax.checkpoint
    def one_block(inputs):
        block, block_places = inputs
        raw = low_back(jnp.einsum('qhd,khd->hqk', block, keys, precision=HIGH))
        scores = raw * HEAD ** (-0.5)
        allowed = block_places[None, :, None] >= places[None, None, :]
        scores = jnp.where(allowed, scores, far_below)
        probs = low(jax.nn.softmax(scores, axis=-1))
        return jnp.einsum('hqk,khd->qhd', probs, values, precision=HIGH)
    result = lax.map(one_block, (queries, query_places))
    return result.reshape(count, HEADS * HEAD)

def layer(inputs, gain_one, gain_two, mat_query, mat_key, mat_value, mat_out, mat_gate, mat_up, mat_down, places):
    hidden_one = low(normed(inputs, gain_one))
    query = low_back(matmul(hidden_one, mat_query))
    key = low_back(matmul(hidden_one, mat_key))
    value = low(low_back(matmul(hidden_one, mat_value)))
    query_turned = low(rotate(query, places, HEADS, 1.0))
    key_turned = low(rotate(key, places, KV_HEADS, 1.0))
    attended = low(low_back(attend(query_turned, key_turned, value, places)))
    branch = low_back(matmul(attended, mat_out))
    resid = inputs + branch
    hidden_two = low(normed(resid, gain_two))
    gate = low_back(matmul(hidden_two, mat_gate))
    up_part = low_back(matmul(hidden_two, mat_up))
    product = low(jax.nn.silu(gate) * up_part)
    return resid + low_back(matmul(product, mat_down))

def reference(tokens, pair_order, gain_attn, gain_mlp, w_query, w_key, w_value, w_out, w_gate, w_up, w_down, cotangent):
    places = positions(pair_order, TOK_DEV)

    def forward(inputs, gain_one, gain_two, mat_query, mat_key, mat_value, mat_out, mat_gate, mat_up, mat_down):
        return layer(inputs, gain_one, gain_two, mat_query, mat_key, mat_value, mat_out, mat_gate, mat_up, mat_down, places)
    primals = (tokens.astype(jnp.float32), gain_attn.astype(jnp.float32), gain_mlp.astype(jnp.float32), w_query.astype(jnp.float32), w_key.astype(jnp.float32), w_value.astype(jnp.float32), w_out.astype(jnp.float32), w_gate.astype(jnp.float32), w_up.astype(jnp.float32), w_down.astype(jnp.float32))
    result, pullback = jax.vjp(forward, *primals)
    grads = pullback(cotangent.astype(jnp.float32))
    return (result.astype(jnp.bfloat16), grads[0], grads[1], grads[2], grads[3], grads[4], grads[5], grads[6], grads[7], grads[8], grads[9])
```

```python
import functools

import jax
import jax.numpy as jnp
from jax import lax
from jax.experimental import pallas as pl
from jax.experimental.pallas import tpu as pltpu
from jax.sharding import PartitionSpec as P

HEADS = 15
KV_HEADS = 5
HEAD = 64
TP = 8
GROUP = HEADS // KV_HEADS
epsilon = 1e-05
base_theta = 100000.0
far_below = -1e30
f32 = jnp.float32
bf16 = jnp.bfloat16
AXES = ("ctx", "fsdp")


def exchange(array, mask, count):
    return lax.ppermute(array, AXES, [(i, i ^ mask) for i in range(count)])


def nn(left, right):
    return lax.dot_general(left, right, (((1,), (0,)), ((), ())), preferred_element_type=f32)


def tn(left, right):
    return lax.dot_general(left, right, (((0,), (0,)), ((), ())), preferred_element_type=f32)


def nt(left, right):
    return lax.dot_general(left, right, (((1,), (1,)), ((), ())), preferred_element_type=f32)


def query_positions(base_ref, at, width, half_rows):
    lane = lax.broadcasted_iota(jnp.int32, (1, width), 1)
    place = jnp.zeros((1, width), jnp.int32)
    for block in range(width // half_rows):
        start = base_ref[at + block] - block * half_rows
        place = jnp.where(lane >= block * half_rows, start + lane, place)
    return place


def key_positions(base_ref, row, at, count, half_rows, width):
    offset = lax.broadcasted_iota(jnp.int32, (half_rows, width), 0)
    return jnp.concatenate([offset + base_ref[row, at + b] for b in range(count)], axis=0)


def attention_forward(groups, rows, half_rows):
    half = rows // 2
    blocks = half // half_rows
    wide = 256

    def kernel(sel_ref, key_base, query_base, q_ref, kv_ref, out_ref, lse_ref, kvt_ref, pos_ref):
        def turn(at, unused):
            which, group = at // groups, at % groups
            kvt_ref[which, group] = kv_ref[which, group].T
            return unused

        lax.fori_loop(0, 2 * groups, turn, 0)

        def place(at, unused):
            which, group = at // groups, at % groups
            for side in range(2):
                pos_ref[which, group, pl.ds(side * half, half), :] = key_positions(
                    key_base, at, side * blocks, blocks, half_rows, 128
                )
            return unused

        lax.fori_loop(0, 2 * groups, place, 0)
        for head in range(2):
            which = sel_ref[head]
            for q_side in range(2):
                for tile in range(half // wide):
                    lanes = q_side * half + tile * wide
                    places = query_positions(query_base, lanes // half_rows, wide, half_rows)
                    turned = q_ref[pl.ds(head * HEAD, HEAD), pl.ds(lanes, wide)]
                    padded = jnp.concatenate([turned, jnp.zeros_like(turned)], axis=0)

                    def step(k_side, masked, group, carry):
                        highest, mass, accum = carry
                        block = kv_ref[which, group, pl.ds(k_side * half, half), :]
                        scores = nn(block, padded)
                        if masked:
                            at = pos_ref[which, group, pl.ds(k_side * half, half), :]
                            at = jnp.concatenate([at] * (wide // 128), axis=1)
                            scores = jnp.where(at <= places, scores, far_below)
                        top = jnp.maximum(highest, jnp.max(scores, axis=0, keepdims=True))
                        weights = jnp.exp(scores - top)
                        fade = jnp.exp(highest - top)
                        mass = mass * fade + jnp.sum(weights, axis=0, keepdims=True)
                        values = kvt_ref[which, group, pl.ds(HEAD, HEAD), pl.ds(k_side * half, half)]
                        accum = accum * fade + nn(values, weights.astype(bf16))
                        return (top, mass, accum)

                    carry = (
                        jnp.full((1, wide), far_below, f32),
                        jnp.zeros((1, wide), f32),
                        jnp.zeros((HEAD, wide), f32),
                    )
                    carry = lax.fori_loop(
                        0, groups, functools.partial(step, 0, q_side == 0), carry
                    )
                    if q_side == 1:
                        carry = lax.fori_loop(0, groups, functools.partial(step, 1, True), carry)
                    highest, mass, accum = carry
                    out_ref[pl.ds(head * HEAD, HEAD), pl.ds(lanes, wide)] = accum / mass
                    lse_ref[pl.ds(head, 1), pl.ds(lanes, wide)] = highest + jnp.log(mass)

    smem = pl.BlockSpec(memory_space=pltpu.SMEM)
    vmem = pl.BlockSpec(memory_space=pltpu.VMEM)
    return pl.pallas_call(
        kernel,
        out_shape=(
            jax.ShapeDtypeStruct((2 * HEAD, rows), f32),
            jax.ShapeDtypeStruct((2, rows), f32),
        ),
        in_specs=[smem, smem, smem, vmem, vmem],
        out_specs=(vmem, vmem),
        scratch_shapes=[
            pltpu.VMEM((2, groups, 2 * HEAD, rows), bf16),
            pltpu.VMEM((2, groups, rows, 128), jnp.int32),
        ],
        compiler_params=pltpu.CompilerParams(vmem_limit_bytes=48 * 1024 * 1024),
        cost_estimate=pl.CostEstimate(
            flops=6 * rows * rows * groups * HEAD, bytes_accessed=4 * rows * 512, transcendentals=0
        ),
    )


def attention_backward(groups, rows, half_rows):
    half = rows // 2
    blocks = half // half_rows
    wide = 256

    def kernel(
        sel_ref, key_base, query_base, q_ref, kv_ref, g_ref, out_ref, lse_ref, dq_ref, dkv_ref,
        rq_ref, rg_ref, delta_ref, pos_ref,
    ):
        dkv_ref[...] = jnp.zeros_like(dkv_ref)
        dq_ref[...] = jnp.zeros_like(dq_ref)
        for head in range(2):
            own = pl.ds(head * HEAD, HEAD)
            turned = q_ref[own, :].T
            rq_ref[head] = jnp.concatenate([turned, jnp.zeros_like(turned)], axis=1)
            grad = g_ref[own, :]
            turned = grad.T
            rg_ref[head] = jnp.concatenate([jnp.zeros_like(turned), turned], axis=1)
            delta_ref[pl.ds(head, 1), :] = jnp.sum(
                grad.astype(f32) * out_ref[own, :], axis=0, keepdims=True
            )

        def one_group(group, unused):
            for head in range(2):
                which = sel_ref[head]
                own = pl.ds(head * HEAD, HEAD)
                for k_side in range(2):
                    keys_at = pl.ds(k_side * half, half)
                    block = kv_ref[which, group, keys_at, :]
                    turned_keys = block.T[:HEAD]
                    pos_ref[...] = key_positions(
                        key_base, which * groups + group, k_side * blocks, blocks, half_rows, 128
                    )
                    for q_side in range(k_side, 2):
                        for tile in range(half // wide):
                            lanes = pl.ds(q_side * half + tile * wide, wide)
                            turned = q_ref[own, lanes]
                            padded = jnp.concatenate([turned, jnp.zeros_like(turned)], axis=0)
                            scores = nn(block, padded)
                            if q_side == k_side:
                                places = query_positions(
                                    query_base,
                                    (q_side * half + tile * wide) // half_rows,
                                    wide,
                                    half_rows,
                                )
                                at = jnp.concatenate([pos_ref[...]] * (wide // 128), axis=1)
                                scores = jnp.where(at <= places, scores, far_below)
                            probs = jnp.exp(scores - lse_ref[pl.ds(head, 1), lanes])
                            grads = g_ref[own, lanes]
                            padded = jnp.concatenate([jnp.zeros_like(grads), grads], axis=0)
                            grad_probs = nn(block, padded)
                            grad_scores = probs * (grad_probs - delta_ref[pl.ds(head, 1), lanes])
                            probs = probs.astype(bf16)
                            grad_scores = grad_scores.astype(bf16)
                            dkv_ref[which, group, keys_at, :] += nn(
                                grad_scores, rq_ref[head, lanes, :]
                            ) + nn(probs, rg_ref[head, lanes, :])
                            dq_ref[own, lanes] += nn(turned_keys, grad_scores)
            return unused

        lax.fori_loop(0, groups, one_group, 0)

    smem = pl.BlockSpec(memory_space=pltpu.SMEM)
    vmem = pl.BlockSpec(memory_space=pltpu.VMEM)
    return pl.pallas_call(
        kernel,
        out_shape=(
            jax.ShapeDtypeStruct((2 * HEAD, rows), f32),
            jax.ShapeDtypeStruct((2, groups, rows, 2 * HEAD), f32),
        ),
        in_specs=[smem, smem, smem, vmem, vmem, vmem, vmem, vmem],
        out_specs=(vmem, vmem),
        scratch_shapes=[
            pltpu.VMEM((2, rows, 2 * HEAD), bf16),
            pltpu.VMEM((2, rows, 2 * HEAD), bf16),
            pltpu.VMEM((2, rows), f32),
            pltpu.VMEM((half, 128), jnp.int32),
        ],
        compiler_params=pltpu.CompilerParams(vmem_limit_bytes=56 * 1024 * 1024),
        cost_estimate=pl.CostEstimate(
            flops=15 * rows * rows * groups * HEAD, bytes_accessed=4 * rows * 512, transcendentals=0
        ),
    )


def half_swap(matrix):
    rows, width = matrix.shape
    split = matrix.reshape(rows, width // HEAD, 2, HEAD // 2)
    return jnp.flip(split, axis=2).reshape(rows, width)


def body(
    tokens,
    pair_order,
    gain_attn,
    gain_mlp,
    w_query,
    w_key,
    w_value,
    w_out,
    w_gate,
    w_up,
    w_down,
    cotangent,
):
    local_rows, width = tokens.shape
    half_rows = local_rows // 2
    nz = lax.axis_size("fsdp")
    outer = lax.axis_size("ctx") // TP
    count = lax.axis_size(AXES)
    groups = outer * nz
    rows = TP * local_rows
    half = rows // 2
    d_rows = w_query.shape[0]
    me = lax.axis_index(AXES)
    z = lax.axis_index("fsdp")
    tp = lax.axis_index("ctx") % TP
    send = functools.partial(exchange, count=count)
    group_mask = [(g // nz) * TP * nz + g % nz for g in range(groups)]

    def plane_gather(block):
        even = [block] + [send(block, j * nz) for j in range(2, TP, 2)]
        odd = [send(e, nz) for e in even]
        return [piece for pair in zip(even, odd) for piece in pair]

    def plane_scatter(blocks):
        kept = [
            blocks[j].astype(f32) + send(blocks[j + 1].astype(bf16), nz).astype(f32)
            for j in range(0, TP, 2)
        ]
        total = kept[0]
        for j in range(1, TP // 2):
            total = total + send(kept[j].astype(bf16), 2 * j * nz).astype(f32)
        return total

    def plane_trade(blocks):
        crossed = [send(blocks[j + 1], nz) for j in range(0, TP, 2)]
        result = []
        for j in range(0, TP, 2):
            pair = jnp.stack([blocks[j], crossed[j // 2]])
            if j > 0:
                pair = send(pair, j * nz)
            result += [pair[0], pair[1]]
        return result

    def from_z(block):
        slots = jnp.stack([block] + [send(block, s) for s in range(1, nz)])
        return [lax.dynamic_index_in_dim(slots, z ^ s, 0, keepdims=False) for s in range(nz)]

    def to_z(stacked):
        total = lax.dynamic_index_in_dim(stacked, z, 0, keepdims=False).astype(f32)
        for s in range(1, nz):
            piece = lax.dynamic_index_in_dim(stacked, z ^ s, 0, keepdims=False).astype(bf16)
            total = total + send(piece, s).astype(f32)
        step = 1
        while step < outer:
            total = total + send(total.astype(bf16), step * TP * nz).astype(f32)
            step *= 2
        return total

    def by_device(slots):
        stacked = jnp.stack(slots)
        return [lax.dynamic_index_in_dim(stacked, tp ^ j, 0, keepdims=False) for j in range(TP)]

    def in_halves(slots):
        shaped = jnp.stack(slots).reshape(TP, 2, half_rows, slots[0].shape[1])
        return shaped.transpose(1, 0, 2, 3).reshape(rows, slots[0].shape[1])

    def to_slots(matrix):
        shaped = matrix.reshape(2, TP, half_rows, matrix.shape[1])
        return [shaped[:, j].reshape(local_rows, matrix.shape[1]) for j in range(TP)]

    kv_index = (4 * (tp // 2)) // GROUP + tp % 2
    own_heads = 2 * HEAD
    w_q_own = lax.dynamic_slice_in_dim(
        jnp.pad(w_query, ((0, 0), (0, TP * own_heads - HEADS * HEAD))), tp * own_heads, own_heads, 1
    )
    pad_kv = ((0, 0), (0, HEAD))
    w_k_own = lax.dynamic_slice_in_dim(jnp.pad(w_key, pad_kv), kv_index * HEAD, HEAD, 1)
    w_v_own = lax.dynamic_slice_in_dim(jnp.pad(w_value, pad_kv), kv_index * HEAD, HEAD, 1)
    gains = jnp.zeros((16, 2 * own_heads), bf16)
    gains = gains.at[0, :d_rows].set(gain_attn).at[1, :d_rows].set(gain_mlp)
    first = jnp.concatenate([jnp.concatenate([w_q_own, w_k_own, w_v_own], axis=1), gains], axis=0)
    first = from_z(first)
    w_qkv = jnp.concatenate([f[:d_rows] for f in first], axis=0)
    gain_one = jnp.concatenate([f[d_rows, :d_rows] for f in first]).astype(f32)[None, :]
    gain_two = jnp.concatenate([f[d_rows + 1, :d_rows] for f in first]).astype(f32)[None, :]

    gathered = in_halves(plane_gather(tokens))
    last_block = 2 * count - 1
    slot_of = jnp.array(
        [[m | (j * nz) for j in range(TP)] for m in group_mask], dtype=jnp.int32
    )
    low = pair_order[me ^ slot_of]
    base = jnp.stack([low, last_block - low], axis=1) * half_rows
    query_base = base[0].reshape(2 * TP)
    partner = jnp.array([j ^ 1 for j in range(TP)], dtype=jnp.int32)
    key_base = jnp.stack([base, base[:, :, partner]]).reshape(2 * groups, 2 * TP)
    places = (query_base[:, None] + jnp.arange(half_rows, dtype=jnp.int32)[None, :]).reshape(-1)
    lane = jnp.arange(HEAD) % (HEAD // 2)
    freqs = base_theta ** (-2.0 * lane.astype(f32) / HEAD)
    angles = places.astype(f32)[:, None] * freqs[None, :]
    cosine = jnp.cos(angles)
    sine = jnp.sin(angles) * jnp.where(jnp.arange(HEAD) < HEAD // 2, -1.0, 1.0)[None, :]
    ones = jnp.ones_like(cosine)
    cosine = jnp.concatenate([cosine, cosine, cosine, ones], axis=1)
    sine = jnp.concatenate([sine, sine, sine, 0.0 * ones], axis=1)
    head_of = 2 * tp + jnp.arange(2)
    kv_of = head_of // GROUP
    select = jnp.where(kv_of == kv_index, 0, 1).astype(jnp.int32)

    inputs = gathered.astype(f32)
    inverse_one = lax.rsqrt(jnp.mean(inputs * inputs, axis=1, keepdims=True) + epsilon)
    normal_one = inputs * inverse_one
    hidden_one = (normal_one * gain_one).astype(bf16)
    qkv = nn(hidden_one, w_qkv)
    qkv = qkv * cosine + half_swap(qkv) * sine
    query_turned = (qkv[:, :own_heads].astype(bf16) * jnp.asarray(HEAD**-0.5, bf16)).T
    own_kv = qkv[:, own_heads:].astype(bf16)
    kv_slots = [own_kv] + [send(own_kv, m) for m in group_mask[1:]]
    kv_other = [send(slot, nz) for slot in kv_slots]
    kv_all = jnp.stack([jnp.stack(kv_slots), jnp.stack(kv_other)])

    w_out_own = lax.dynamic_slice_in_dim(
        jnp.pad(w_out, ((0, 0), (0, TP * own_heads - width))), tp * own_heads, own_heads, 1
    )
    w_out_cols = jnp.concatenate(from_z(w_out_own), axis=0)
    w_out_all = jnp.concatenate(by_device(plane_gather(w_out_cols)), axis=1)[:, :width]
    ff_z = w_down.shape[0]
    ff_part = ff_z // TP
    ff_own = ff_part * nz

    def ff_columns(matrix):
        shaped = matrix.reshape(d_rows, nz, ff_z)
        return lax.dynamic_slice_in_dim(shaped, tp * ff_part, ff_part, 2).reshape(d_rows, ff_own)

    w_gu = jnp.concatenate(
        from_z(jnp.concatenate([ff_columns(w_gate), ff_columns(w_up)], axis=1)), axis=0
    )
    w_dn = jnp.concatenate(
        from_z(lax.dynamic_slice_in_dim(w_down, tp * ff_part, ff_part, 0)), axis=0
    )
    cot = in_halves(plane_gather(cotangent))

    attended_turned, log_mass = attention_forward(groups, rows, half_rows)(
        select, key_base, query_base, query_turned, kv_all
    )
    attended_own = attended_turned.T.astype(bf16)

    def reorder(matrix, j):
        shaped = matrix.reshape(2, TP, half_rows, matrix.shape[1])
        picked = jnp.stack([shaped[:, k ^ j] for k in range(TP)], axis=1)
        return picked.reshape(matrix.shape)

    attended_slots = plane_gather(attended_own)
    attended_slots = [reorder(slot, j) for j, slot in enumerate(attended_slots)]
    attended_low = jnp.concatenate(by_device(attended_slots), axis=1)[:, :width]

    resid = inputs + nn(attended_low, w_out_all)
    inverse_two = lax.rsqrt(jnp.mean(resid * resid, axis=1, keepdims=True) + epsilon)
    normal_two = resid * inverse_two
    hidden_two = (normal_two * gain_two).astype(bf16)
    gate_up = nn(hidden_two, w_gu)
    gate, up_part = gate_up[:, :ff_own], gate_up[:, ff_own:]
    sigmoid_gate = jax.nn.sigmoid(gate)
    activated = gate * sigmoid_gate
    product = (activated * up_part).astype(bf16)
    grad_product = nt(cot, w_dn)
    grad_gate = grad_product * up_part * sigmoid_gate * (1.0 + gate * (1.0 - sigmoid_gate))
    grad_up = grad_product * activated
    grad_gu = jnp.concatenate([grad_gate.astype(bf16), grad_up.astype(bf16)], axis=1)
    partial_hidden = nt(grad_gu, w_gu)
    grad_gain_two = jnp.sum(partial_hidden * normal_two, axis=0)
    grad_hidden = plane_scatter(to_slots(partial_hidden))

    def own_rows(matrix):
        return jnp.concatenate([matrix[:half_rows], matrix[half : half + half_rows]], axis=0)

    own_resid, own_normal, own_inverse = (own_rows(m) for m in (resid, normal_two, inverse_two))
    grad_normal = grad_hidden * gain_two
    grad_resid = own_inverse * (
        grad_normal - own_normal * jnp.mean(grad_normal * own_normal, axis=1, keepdims=True)
    ) + cotangent.astype(f32)
    grad_branch = grad_resid.astype(bf16)
    grad_attended = nt(grad_branch, w_out_all).astype(bf16)

    def column_blocks(matrix):
        padded = jnp.pad(matrix, ((0, 0), (0, TP * own_heads - width)))
        return [
            lax.dynamic_slice_in_dim(padded, (tp ^ j) * own_heads, own_heads, 1) for j in range(TP)
        ]

    traded = plane_trade(
        [
            jnp.concatenate([a, b], axis=1)
            for a, b in zip(column_blocks(grad_attended), column_blocks(grad_branch))
        ]
    )
    traded = in_halves(traded)
    grads_turned = traded[:, :own_heads].T
    grad_out_own = tn(attended_low, traded[:, own_heads:])

    grad_query, grad_kv = attention_backward(groups, rows, half_rows)(
        select,
        key_base,
        query_base,
        query_turned,
        kv_all,
        grads_turned,
        attended_turned,
        log_mass,
    )
    grad_kv = grad_kv[0] + send(grad_kv[1].astype(bf16), nz).astype(f32)
    total_kv = grad_kv[0]
    for g in range(1, groups):
        total_kv = total_kv + send(grad_kv[g].astype(bf16), group_mask[g]).astype(f32)
    grad_qkv = jnp.concatenate([grad_query.T * HEAD**-0.5, total_kv], axis=1)
    grad_qkv = (grad_qkv * cosine - half_swap(grad_qkv) * sine).astype(bf16)
    grad_qkv_own = tn(hidden_one, grad_qkv)
    partial_hidden = nt(grad_qkv, w_qkv)
    grad_gain_one = jnp.sum(partial_hidden * normal_one, axis=0)
    grad_hidden = plane_scatter(to_slots(partial_hidden))
    own_normal, own_inverse = own_rows(normal_one), own_rows(inverse_one)
    grad_normal = grad_hidden * gain_one
    grad_tokens = (
        own_inverse
        * (grad_normal - own_normal * jnp.mean(grad_normal * own_normal, axis=1, keepdims=True))
        + grad_resid
    )
    layer_out = (own_resid + plane_scatter(to_slots(nn(product, w_dn)))).astype(bf16)

    def finish(matrix):
        part = to_z(matrix.reshape(nz, matrix.shape[0] // nz, matrix.shape[1])).astype(bf16)
        return by_device(plane_gather(part))

    down_parts = finish(tn(product, cot))
    grad_w_down = jnp.concatenate(down_parts, axis=0).astype(f32)
    gu_parts = jnp.stack(finish(tn(hidden_two, grad_gu)))
    gu_parts = gu_parts.reshape(TP, d_rows, 2, nz, ff_part).transpose(2, 1, 3, 0, 4)
    gu_parts = gu_parts.reshape(2, d_rows, nz * ff_z).astype(f32)
    grad_w_out = jnp.concatenate(finish(grad_out_own), axis=1)[:, :width].astype(f32)
    gain_rows = jnp.stack([grad_gain_one, grad_gain_two]).reshape(2, nz, d_rows).transpose(1, 0, 2)
    gain_rows = jnp.pad(gain_rows, ((0, 0), (0, 14), (0, 2 * own_heads - d_rows)))
    last = jnp.concatenate([grad_qkv_own.reshape(nz, d_rows, 2 * own_heads), gain_rows], axis=1)
    last = finish(last.reshape(nz * (d_rows + 16), 2 * own_heads))
    grad_w_query = jnp.concatenate([p[:d_rows, :own_heads] for p in last], axis=1)[:, :width]
    pieces = [p[:d_rows, own_heads:].astype(f32) for p in last]
    pieces = [pieces[0], pieces[1] + pieces[2], pieces[3] + pieces[4], pieces[5], pieces[6]]
    grad_w_key = jnp.concatenate([p[:, :HEAD] for p in pieces], axis=1)
    grad_w_value = jnp.concatenate([p[:, HEAD:] for p in pieces], axis=1)
    grad_gains = sum(p[d_rows : d_rows + 2, :d_rows].astype(f32) for p in last)
    return (
        layer_out,
        grad_tokens,
        grad_gains[0],
        grad_gains[1],
        grad_w_query.astype(f32),
        grad_w_key,
        grad_w_value,
        grad_w_out,
        gu_parts[0],
        gu_parts[1],
        grad_w_down,
    )


def solution(mesh):
    return jax.shard_map(
        body,
        mesh=mesh,
        in_specs=(
            P(("ctx", "fsdp"), None),
            P(),
            P("fsdp"),
            P("fsdp"),
            P("fsdp", None),
            P("fsdp", None),
            P("fsdp", None),
            P("fsdp", None),
            P("fsdp", None),
            P("fsdp", None),
            P("fsdp", None),
            P(("ctx", "fsdp"), None),
        ),
        out_specs=(
            P(("ctx", "fsdp"), None),
            P(("ctx", "fsdp"), None),
            P("fsdp"),
            P("fsdp"),
            P("fsdp", None),
            P("fsdp", None),
            P("fsdp", None),
            P("fsdp", None),
            P("fsdp", None),
            P("fsdp", None),
            P("fsdp", None),
        ),
        check_vma=False,
    )
```

```python
import functools

import jax
import jax.numpy as jnp
from jax import lax
from jax.experimental import pallas as pl
from jax.experimental.pallas import tpu as pltpu
from jax.sharding import PartitionSpec as P

HEADS = 15
KV_HEADS = 5
HEAD = 64
TP = 8
GROUP = HEADS // KV_HEADS
OWN = 2 * HEAD
epsilon = 1e-05
base_theta = 100000.0
far_below = -1e30
f32 = jnp.float32
bf16 = jnp.bfloat16
i32 = jnp.int32
AXES = ("ctx", "fsdp")
MIB = 1024 * 1024
smem = pl.BlockSpec(memory_space=pltpu.SMEM)
vmem = pl.BlockSpec(memory_space=pltpu.VMEM)


def exchange(array, mask, count):
    return lax.ppermute(array, AXES, [(i, i ^ mask) for i in range(count)])


def nn(left, right):
    return lax.dot_general(left, right, (((1,), (0,)), ((), ())), preferred_element_type=f32)


def tn(left, right):
    return lax.dot_general(left, right, (((0,), (0,)), ((), ())), preferred_element_type=f32)


def nt(left, right):
    return lax.dot_general(left, right, (((1,), (1,)), ((), ())), preferred_element_type=f32)


def shape(dims, dtype):
    return jax.ShapeDtypeStruct(dims, dtype)


def call(kernel, outs, inputs, scalars=1, scratch=(), limit=56, cost=1.0):
    specs = [smem] * scalars + [vmem] * (len(inputs) - scalars)
    return pl.pallas_call(
        kernel,
        out_shape=tuple(outs),
        in_specs=specs,
        out_specs=tuple(vmem for unused in outs),
        scratch_shapes=list(scratch),
        compiler_params=pltpu.CompilerParams(vmem_limit_bytes=limit * MIB),
        cost_estimate=pl.CostEstimate(
            flops=int(cost * 1e9), bytes_accessed=int(cost * 1e6), transcendentals=0
        ),
    )(*inputs)


def one_hot(rows, columns, start):
    row = lax.broadcasted_iota(i32, (rows, columns), 0)
    column = lax.broadcasted_iota(i32, (rows, columns), 1)
    return jnp.where(row == column + start, 1.0, 0.0).astype(bf16)


def query_positions(base_ref, at, width, half_rows):
    lane = lax.broadcasted_iota(i32, (1, width), 1)
    place = jnp.zeros((1, width), i32)
    for block in range(width // half_rows):
        start = base_ref[at + block] - block * half_rows
        place = jnp.where(lane >= block * half_rows, start + lane, place)
    return place


def key_positions(base_ref, row, at, count, half_rows, width):
    offset = lax.broadcasted_iota(i32, (half_rows, width), 0)
    return jnp.concatenate([offset + base_ref[row, at + b] for b in range(count)], axis=0)


def swap_halves(matrix):
    lane = lax.broadcasted_iota(i32, matrix.shape, 1)
    ahead = pltpu.roll(matrix, matrix.shape[1] - HEAD // 2, 1)
    behind = pltpu.roll(matrix, HEAD // 2, 1)
    return jnp.where(lane % HEAD < HEAD // 2, ahead, behind)


def norm_scale(matrix):
    return lax.rsqrt(jnp.mean(matrix * matrix, axis=1, keepdims=True) + epsilon)


def slice_attention_weights(at, w_query, w_key, w_value, w_out, gain_one, gain_two):
    d_rows, width = w_query.shape
    lanes = 2 * OWN + OWN

    def kernel(at_ref, q_ref, k_ref, v_ref, o_ref, g1_ref, g2_ref, out_ref):
        tp = at_ref[0]
        kv = at_ref[2]
        pick = one_hot(width, OWN, tp * OWN)
        pick_kv = one_hot(KV_HEADS * HEAD, HEAD, kv * HEAD)
        out_ref[pl.ds(0, d_rows), pl.ds(0, OWN)] = nn(q_ref[...], pick).astype(bf16)
        key = nn(k_ref[...], pick_kv)
        value = nn(v_ref[...], pick_kv)
        out_ref[pl.ds(0, d_rows), pl.ds(OWN, OWN)] = jnp.concatenate([key, value], 1).astype(bf16)
        out_ref[pl.ds(0, d_rows), pl.ds(2 * OWN, OWN)] = nn(o_ref[...], pick).astype(bf16)
        out_ref[pl.ds(d_rows, 16), :] = jnp.zeros((16, lanes), bf16)
        out_ref[pl.ds(d_rows, 1), pl.ds(0, d_rows)] = g1_ref[...]
        out_ref[pl.ds(d_rows + 1, 1), pl.ds(0, d_rows)] = g2_ref[...]

    return call(
        kernel,
        [shape((d_rows + 16, lanes), bf16)],
        [at, w_query, w_key, w_value, w_out, gain_one[None], gain_two[None]],
        cost=2.0,
    )[0]


def slice_ff_weights(at, w_gate, w_up, w_down, nz):
    d_rows = w_gate.shape[0]
    ff_z, width = w_down.shape
    part = ff_z // TP
    own = part * nz
    third = width // 3

    def kernel(at_ref, g_ref, u_ref, d_ref, out_ref):
        tp = at_ref[0]
        pick = one_hot(ff_z, part, tp * part)
        for ref, start in ((g_ref, 0), (u_ref, own)):
            pieces = [nn(ref[:, pl.ds(s * ff_z, ff_z)], pick) for s in range(nz)]
            out_ref[:, pl.ds(start, own)] = jnp.concatenate(pieces, axis=1).astype(bf16)
        rows = d_ref[pl.ds(pl.multiple_of(tp * part, 16), part), :]
        for p in range(3):
            out_ref[pl.ds(p * part, part), pl.ds(2 * own, third)] = rows[
                :, p * third : (p + 1) * third
            ]

    return call(
        kernel,
        [shape((d_rows, 2 * own + third), bf16)],
        [at, w_gate, w_up, w_down],
        cost=4.0,
    )[0]


def project(at, tokens, packs, cosine, sine):
    local, width = tokens[0].shape
    half_rows = local // 2
    rows = TP * local
    nz = len(packs)
    pack_rows, lanes = packs[0].shape
    d_rows = pack_rows - 16

    def kernel(at_ref, *refs):
        toks, refs = refs[:TP], refs[TP:]
        pack, refs = refs[:nz], refs[nz:]
        cos_ref, sin_ref, x_ref, hid_ref, qt_ref, kv_ref, w_ref, wo_ref, gain_ref, hold = refs
        z = at_ref[1]
        for s in range(nz):
            hold[z ^ s] = pack[s][...]
        for s in range(nz):
            w_ref[pl.ds(s * d_rows, d_rows), :] = hold[s, pl.ds(0, d_rows), pl.ds(0, 2 * OWN)]
            wo_ref[pl.ds(s * d_rows, d_rows), :] = hold[s, pl.ds(0, d_rows), pl.ds(2 * OWN, OWN)]
        gains = [hold[s, pl.ds(d_rows, 16), pl.ds(0, d_rows)].astype(f32) for s in range(nz)]
        gain_ref[...] = jnp.concatenate(gains, axis=1)[:8]
        gain = gain_ref[pl.ds(0, 1), :]
        per = 4
        for tile in range(2 * TP // per):
            side, first = (tile * per) // TP, (tile * per) % TP
            at_rows = pl.ds(tile * per * half_rows, per * half_rows)
            block = jnp.concatenate(
                [toks[first + j][pl.ds(side * half_rows, half_rows), :] for j in range(per)], axis=0
            )
            x_ref[at_rows, :] = block
            inputs = block.astype(f32)
            hidden = (inputs * norm_scale(inputs) * gain).astype(bf16)
            hid_ref[at_rows, :] = hidden
            out = nn(hidden, w_ref[...])
            cos, sin = cos_ref[at_rows, :], sin_ref[at_rows, :]
            query = out[:, :OWN]
            query = query * cos + swap_halves(query) * sin
            qt_ref[:, at_rows] = (query.astype(bf16).astype(f32) * HEAD**-0.5).T.astype(bf16)
            pair = out[:, OWN:]
            turned = pair * cos + swap_halves(pair) * sin
            lane = lax.broadcasted_iota(i32, pair.shape, 1)
            kv_ref[at_rows, :] = jnp.where(lane < HEAD, turned, pair).astype(bf16)

    return call(
        kernel,
        [
            shape((rows, width), bf16),
            shape((rows, width), bf16),
            shape((OWN, rows), bf16),
            shape((rows, OWN), bf16),
            shape((width, 2 * OWN), bf16),
            shape((width, OWN), bf16),
            shape((8, width), f32),
        ],
        [at, *tokens, *packs, cosine, sine],
        scratch=[pltpu.VMEM((nz, pack_rows, lanes), bf16)],
        cost=6.0,
    )


def attention_forward(select, key_base, query_base, turned_query, own_kv, other_kv, half_rows):
    groups = len(own_kv)
    rows = own_kv[0].shape[0]
    half = rows // 2
    blocks = half // half_rows
    wide = 256

    def kernel(sel_ref, key_ref, query_ref, q_ref, *refs):
        own, other = refs[:groups], refs[groups : 2 * groups]
        out_ref, low_ref, lse_ref, kv_ref, kvt_ref, top_ref, mass_ref, place_ref = refs[2 * groups :]
        for head in range(2):
            chosen = sel_ref[head] == 0
            for group in range(groups):

                @pl.when(chosen)
                def take_own():
                    kv_ref[head, group] = own[group][...]
                    kvt_ref[head, group] = own[group][...].T

                @pl.when(jnp.logical_not(chosen))
                def take_other():
                    kv_ref[head, group] = other[group][...]
                    kvt_ref[head, group] = other[group][...].T

        top_ref[...] = jnp.full_like(top_ref, far_below)
        mass_ref[...] = jnp.zeros_like(mass_ref)
        out_ref[...] = jnp.zeros_like(out_ref)

        def one_group(group, unused):
            for head in range(2):
                row = sel_ref[head] * groups + group
                own_rows = pl.ds(head * HEAD, HEAD)
                stat = pl.ds(head, 1)
                for k_side in range(2):
                    place_ref[...] = key_positions(
                        key_ref, row, k_side * blocks, blocks, half_rows, 128
                    )
                    block = kv_ref[head, group, pl.ds(k_side * half, half), :]
                    values = kvt_ref[head, group, pl.ds(HEAD, HEAD), pl.ds(k_side * half, half)]
                    for q_side in range(k_side, 2):
                        for tile in range(half // wide):
                            start = q_side * half + tile * wide
                            lanes = pl.ds(start, wide)
                            turned = q_ref[own_rows, lanes]
                            padded = jnp.concatenate([turned, jnp.zeros_like(turned)], axis=0)
                            scores = nn(block, padded)
                            if q_side == k_side:
                                places = query_positions(
                                    query_ref, start // half_rows, wide, half_rows
                                )
                                at = jnp.concatenate([place_ref[...]] * (wide // 128), axis=1)
                                scores = jnp.where(at <= places, scores, far_below)
                            before = top_ref[stat, lanes]
                            top = jnp.maximum(before, jnp.max(scores, axis=0, keepdims=True))
                            weights = jnp.exp(scores - top)
                            fade = jnp.exp(before - top)
                            top_ref[stat, lanes] = top
                            mass_ref[stat, lanes] = mass_ref[stat, lanes] * fade + jnp.sum(
                                weights, axis=0, keepdims=True
                            )
                            out_ref[own_rows, lanes] = out_ref[own_rows, lanes] * fade + nn(
                                values, weights.astype(bf16)
                            )
            return unused

        lax.fori_loop(0, groups, one_group, 0)
        for head in range(2):
            own_rows = pl.ds(head * HEAD, HEAD)
            mass = mass_ref[pl.ds(head, 1), :]
            out_ref[own_rows, :] = out_ref[own_rows, :] / mass
            lse_ref[pl.ds(head, 1), :] = top_ref[pl.ds(head, 1), :] + jnp.log(mass)
        low_ref[...] = out_ref[...].T.astype(bf16)

    return call(
        kernel,
        [shape((OWN, rows), f32), shape((rows, OWN), bf16), shape((2, rows), f32)],
        [select, key_base, query_base, turned_query, *own_kv, *other_kv],
        scalars=3,
        scratch=[
            pltpu.VMEM((2, groups, rows, OWN), bf16),
            pltpu.VMEM((2, groups, OWN, rows), bf16),
            pltpu.VMEM((2, rows), f32),
            pltpu.VMEM((2, rows), f32),
            pltpu.VMEM((half, 128), i32),
        ],
        cost=16.0,
    )


def attention_backward(
    select, key_base, query_base, turned_query, own_kv, other_kv, traded, attended, log_mass, half_rows
):
    groups = len(own_kv)
    rows = own_kv[0].shape[0]
    half = rows // 2
    blocks = half // half_rows
    wide = 256

    def kernel(sel_ref, key_ref, query_ref, q_ref, *refs):
        own, other = refs[:groups], refs[groups : 2 * groups]
        refs = refs[2 * groups :]
        parts, refs = refs[:TP], refs[TP:]
        att_ref, lse_ref, dq_ref, keep_ref, pass_ref, gb_ref = refs[:6]
        kv_ref, sum_ref, g_ref, rq_ref, rg_ref, delta_ref, pos_ref = refs[6:]
        for group in range(groups):
            kv_ref[0, group] = own[group][...]
            kv_ref[1, group] = other[group][...]
        sum_ref[...] = jnp.zeros_like(sum_ref)
        dq_ref[...] = jnp.zeros_like(dq_ref)
        zeros = jnp.zeros((rows, HEAD), bf16)
        for j in range(0, TP, 2):
            for side in range(2):
                at = pl.ds(side * half + j * half_rows, 2 * half_rows)
                pair = jnp.concatenate(
                    [parts[j + k][pl.ds(side * half_rows, half_rows), :] for k in range(2)], axis=0
                )
                g_ref[:, at] = pair[:, :OWN].T
                gb_ref[at, :] = pair[:, OWN:]
        for head in range(2):
            own_rows = pl.ds(head * HEAD, HEAD)
            rq_ref[head] = jnp.concatenate([q_ref[own_rows, :].T, zeros], axis=1)
            grad = g_ref[own_rows, :]
            rg_ref[head] = jnp.concatenate([zeros, grad.T], axis=1)
            delta_ref[pl.ds(head, 1), :] = jnp.sum(
                grad.astype(f32) * att_ref[own_rows, :], axis=0, keepdims=True
            )

        def one_group(group, unused):
            for head in range(2):
                which = sel_ref[head]
                own_rows = pl.ds(head * HEAD, HEAD)
                for k_side in range(2):
                    keys_at = pl.ds(k_side * half, half)
                    block = kv_ref[which, group, keys_at, :]
                    turned_keys = block.T[:HEAD]
                    pos_ref[...] = key_positions(
                        key_ref, which * groups + group, k_side * blocks, blocks, half_rows, 128
                    )
                    for q_side in range(k_side, 2):
                        for tile in range(half // wide):
                            start = q_side * half + tile * wide
                            lanes = pl.ds(start, wide)
                            turned = q_ref[own_rows, lanes]
                            padded = jnp.concatenate([turned, jnp.zeros_like(turned)], axis=0)
                            scores = nn(block, padded)
                            if q_side == k_side:
                                places = query_positions(
                                    query_ref, start // half_rows, wide, half_rows
                                )
                                at = jnp.concatenate([pos_ref[...]] * (wide // 128), axis=1)
                                scores = jnp.where(at <= places, scores, far_below)
                            probs = jnp.exp(scores - lse_ref[pl.ds(head, 1), lanes])
                            grads = g_ref[own_rows, lanes]
                            padded = jnp.concatenate([jnp.zeros_like(grads), grads], axis=0)
                            grad_probs = nn(block, padded)
                            grad_scores = probs * (grad_probs - delta_ref[pl.ds(head, 1), lanes])
                            probs = probs.astype(bf16)
                            grad_scores = grad_scores.astype(bf16)
                            sum_ref[which, group, keys_at, :] += nn(
                                grad_scores, rq_ref[head, lanes, :]
                            ) + nn(probs, rg_ref[head, lanes, :])
                            dq_ref[own_rows, lanes] += nn(turned_keys, grad_scores)
            return unused

        lax.fori_loop(0, groups, one_group, 0)
        keep_ref[...] = sum_ref[0]
        pass_ref[...] = sum_ref[1].astype(bf16)

    return call(
        kernel,
        [
            shape((OWN, rows), f32),
            shape((groups, rows, OWN), f32),
            shape((groups, rows, OWN), bf16),
            shape((rows, OWN), bf16),
        ],
        [
            select,
            key_base,
            query_base,
            turned_query,
            *own_kv,
            *other_kv,
            *traded,
            attended,
            log_mass,
        ],
        scalars=3,
        scratch=[
            pltpu.VMEM((2, groups, rows, OWN), bf16),
            pltpu.VMEM((2, groups, rows, OWN), f32),
            pltpu.VMEM((OWN, rows), bf16),
            pltpu.VMEM((2, rows, OWN), bf16),
            pltpu.VMEM((2, rows, OWN), bf16),
            pltpu.VMEM((2, rows), f32),
            pltpu.VMEM((half, 128), i32),
        ],
        cost=22.0,
    )


def store_blocks(part, tile, per, half_rows, keep_ref, pass_ref):
    side = (tile * per) // TP
    first = lax.rem(tile * per, TP) // 2
    at = pl.ds(pl.multiple_of(side * half_rows, half_rows), half_rows)
    for j in range(per):
        piece = part[j * half_rows : (j + 1) * half_rows]
        if j % 2 == 0:
            keep_ref[first + j // 2, at, :] = piece
        else:
            pass_ref[first + j // 2, at, :] = piece.astype(bf16)


def feed_forward(at, inputs, attended, w_out, packs, cot, gains):
    rows, width = inputs.shape
    local = rows // TP
    half_rows = local // 2
    half = rows // 2
    nz = len(packs)
    d_rows, lanes = packs[0].shape
    third = width // 3
    ff = (lanes - third) // 2
    part_rows = ff // nz
    per = 4
    tile_rows = per * half_rows

    def kernel(at_ref, x_ref, *refs):
        att, refs = refs[:TP], refs[TP:]
        wout, refs = refs[:TP], refs[TP:]
        pack, refs = refs[:nz], refs[nz:]
        cots, refs = refs[:TP], refs[TP:]
        gain_ref, refs = refs[0], refs[1:]
        att_out, wo_out, resid_out, gk_ref, gp_ref, lk_ref, lp_ref, gain_out, own_ref = refs[:9]
        sends, refs = refs[9 : 9 + nz - 1], refs[9 + nz - 1 :]
        gu_w, dn_w, cot_ref, hid_ref, prod_ref, ggu_ref, acc_gu, acc_dn = refs
        tp = at_ref[0]
        z = at_ref[1]
        for j in range(TP):
            columns = pl.ds(pl.multiple_of((tp ^ j) * OWN, OWN), OWN)
            wo_out[:, columns] = wout[j][...]
            for side in range(2):
                for k in range(TP):
                    att_out[pl.ds(side * half + k * half_rows, half_rows), columns] = att[j][
                        pl.ds(side * half + (k ^ j) * half_rows, half_rows), :
                    ]
                cot_ref[pl.ds(side * half + j * half_rows, half_rows), :] = cots[j][
                    pl.ds(side * half_rows, half_rows), :
                ]
        for s in range(nz):
            block = z ^ s
            gu_w[pl.ds(pl.multiple_of(block * d_rows, 16), d_rows), :] = pack[s][:, pl.ds(0, 2 * ff)]
            for p in range(3):
                dn_w[pl.ds(pl.multiple_of(block * part_rows, 16), part_rows), pl.ds(p * third, third)] = (
                    pack[s][pl.ds(p * part_rows, part_rows), pl.ds(2 * ff, third)]
                )
        gain = gain_ref[pl.ds(1, 1), :]
        gain_out[...] = jnp.zeros_like(gain_out)
        acc_gu[...] = jnp.zeros_like(acc_gu)
        acc_dn[...] = jnp.zeros_like(acc_dn)

        def one_tile(tile, unused):
            at_rows = pl.ds(pl.multiple_of(tile * tile_rows, tile_rows), tile_rows)
            branch = nn(att_out[at_rows, :][:, :width], wo_out[...])[:, :width]
            resid = x_ref[at_rows, :].astype(f32) + branch
            side = (tile * per) // TP

            @pl.when(lax.rem(tile * per, TP) == 0)
            def keep_own():
                resid_out[pl.ds(pl.multiple_of(side * half_rows, half_rows), half_rows), :] = resid[
                    :half_rows
                ]

            normal = resid * norm_scale(resid)
            hidden = (normal * gain).astype(bf16)
            gate_up = nn(hidden, gu_w[...])
            gate, up = gate_up[:, :ff], gate_up[:, ff:]
            sigmoid = 1.0 / (1.0 + jnp.exp(-gate))
            activated = gate * sigmoid
            product = (activated * up).astype(bf16)
            cotangent = cot_ref[at_rows, :]
            grad_product = nt(cotangent, dn_w[...])
            grad_gate = grad_product * up * sigmoid * (1.0 + gate * (1.0 - sigmoid))
            grad_gu = jnp.concatenate([grad_gate, grad_product * activated], axis=1).astype(bf16)
            partial = nt(grad_gu, gu_w[...])
            gain_out[pl.ds(0, 1), :] += jnp.sum(partial * normal, axis=0, keepdims=True)
            store_blocks(partial, tile, per, half_rows, gk_ref, gp_ref)
            store_blocks(nn(product, dn_w[...]), tile, per, half_rows, lk_ref, lp_ref)
            acc_gu[...] += tn(hidden, grad_gu)
            acc_dn[...] += tn(product, cotangent)
            return unused

        lax.fori_loop(0, 2 * TP // per, one_tile, 0)
        for s in range(nz):
            block = z ^ s
            gu = acc_gu[pl.ds(pl.multiple_of(block * d_rows, 8), d_rows), :]
            dn = acc_dn[pl.ds(pl.multiple_of(block * part_rows, 8), part_rows), :]
            target = own_ref if s == 0 else sends[s - 1]
            target[:, pl.ds(0, 2 * ff)] = gu.astype(target.dtype)
            for p in range(3):
                target[pl.ds(p * part_rows, part_rows), pl.ds(2 * ff, third)] = dn[
                    :, p * third : (p + 1) * third
                ].astype(target.dtype)

    keep, passed = shape((TP // 2, local, width), f32), shape((TP // 2, local, width), bf16)
    return call(
        kernel,
        [
            shape((rows, TP * OWN), bf16),
            shape((width, TP * OWN), bf16),
            shape((local, width), f32),
            keep,
            passed,
            keep,
            passed,
            shape((8, width), f32),
            shape((d_rows, lanes), f32),
        ]
        + [shape((d_rows, lanes), bf16)] * (nz - 1),
        [at, inputs, *attended, *w_out, *packs, *cot, gains],
        scratch=[
            pltpu.VMEM((width, 2 * ff), bf16),
            pltpu.VMEM((ff, width), bf16),
            pltpu.VMEM((rows, width), bf16),
            pltpu.VMEM((rows, width), bf16),
            pltpu.VMEM((rows, ff), bf16),
            pltpu.VMEM((rows, 2 * ff), bf16),
            pltpu.VMEM((width, 2 * ff), f32),
            pltpu.VMEM((ff, width), f32),
        ],
        cost=18.0,
    )


def add_crossed(keep, crossed):
    count, local, width = keep.shape

    def kernel(keep_ref, cross_ref, own_ref, *sends):
        own_ref[...] = keep_ref[0] + cross_ref[0].astype(f32)
        for j in range(1, count):
            sends[j - 1][...] = (keep_ref[j] + cross_ref[j].astype(f32)).astype(bf16)

    return call(
        kernel,
        [shape((local, width), f32)] + [shape((local, width), bf16)] * (count - 1),
        [keep, crossed],
        scalars=0,
        cost=1.0,
    )


def branch_gradient(at, sums, resid, cotangent, w_out, gains):
    local, width = resid.shape

    def kernel(at_ref, *refs):
        parts, refs = refs[: len(sums)], refs[len(sums) :]
        resid_ref, cot_ref, wo_ref, gain_ref, grad_ref, keep_ref, pass_ref, ga_ref, gb_ref = refs
        tp = at_ref[0]
        grad_hidden = parts[0][...]
        for part in parts[1:]:
            grad_hidden = grad_hidden + part[...].astype(f32)
        resid = resid_ref[...]
        scale = norm_scale(resid)
        normal = resid * scale
        grad = grad_hidden * gain_ref[pl.ds(1, 1), :]
        grad = scale * (grad - normal * jnp.mean(grad * normal, axis=1, keepdims=True))
        grad = grad + cot_ref[...].astype(f32)
        grad_ref[...] = grad
        low = grad.astype(bf16)
        gb_ref[...] = jnp.zeros_like(gb_ref)
        gb_ref[:, pl.ds(0, width)] = low
        ga_ref[...] = jnp.zeros_like(ga_ref)
        ga_ref[:, pl.ds(0, width)] = nt(low, wo_ref[...][:, :width]).astype(bf16)
        for j in range(TP):
            columns = pl.ds(pl.multiple_of((tp ^ j) * OWN, OWN), OWN)
            target = keep_ref if j % 2 == 0 else pass_ref
            target[j // 2, :, pl.ds(0, OWN)] = ga_ref[:, columns]
            target[j // 2, :, pl.ds(OWN, OWN)] = gb_ref[:, columns]

    blocks = shape((TP // 2, local, 2 * OWN), bf16)
    return call(
        kernel,
        [shape((local, width), f32), blocks, blocks],
        [at, *sums, resid, cotangent, w_out, gains],
        scratch=[pltpu.VMEM((local, TP * OWN), bf16), pltpu.VMEM((local, TP * OWN), bf16)],
        cost=3.0,
    )


def pair_up(keep, crossed):
    count, local, width = keep.shape

    def kernel(keep_ref, cross_ref, *outs):
        for j in range(1, count):
            outs[j - 1][0] = keep_ref[j]
            outs[j - 1][1] = cross_ref[j]

    return call(
        kernel, [shape((2, local, width), bf16)] * (count - 1), [keep, crossed], scalars=0, cost=0.7
    )


def projection_gradient(at, grad_query, grad_kv, inputs, hidden, w_qkv, gains, gain_sums, cosine, sine, nz):
    rows, width = inputs.shape
    local = rows // TP
    half_rows = local // 2
    d_rows = width // nz
    per = 4
    tile_rows = per * half_rows
    pieces = len(grad_kv)

    def kernel(at_ref, dq_ref, *refs):
        kvs, refs = refs[:pieces], refs[pieces:]
        x_ref, hid_ref, w_ref, gain_ref, gain_two_ref, cos_ref, sin_ref = refs[:7]
        keep_ref, pass_ref, own_ref = refs[7:10]
        sends, refs = refs[10 : 10 + nz - 1], refs[10 + nz - 1 :]
        turn_ref, acc_ref, gain_acc, hold = refs
        z = at_ref[1]
        turn_ref[...] = dq_ref[...].T * HEAD**-0.5
        acc_ref[...] = jnp.zeros_like(acc_ref)
        gain_acc[...] = jnp.zeros_like(gain_acc)

        def one_tile(tile, unused):
            at_rows = pl.ds(pl.multiple_of(tile * tile_rows, tile_rows), tile_rows)
            cos, sin = cos_ref[at_rows, :], sin_ref[at_rows, :]
            query = turn_ref[at_rows, :]
            query = query * cos - swap_halves(query) * sin
            pair = kvs[0][at_rows, :].astype(f32)
            for piece in kvs[1:]:
                pair = pair + piece[at_rows, :].astype(f32)
            turned = pair * cos - swap_halves(pair) * sin
            lane = lax.broadcasted_iota(i32, pair.shape, 1)
            pair = jnp.where(lane < HEAD, turned, pair)
            grad = jnp.concatenate([query, pair], axis=1).astype(bf16)
            partial = nt(grad, w_ref[...])
            x = x_ref[at_rows, :].astype(f32)
            gain_acc[pl.ds(0, 1), :] += jnp.sum(partial * (x * norm_scale(x)), axis=0, keepdims=True)
            store_blocks(partial, tile, per, half_rows, keep_ref, pass_ref)
            acc_ref[...] += tn(hid_ref[at_rows, :], grad)
            return unused

        lax.fori_loop(0, 2 * TP // per, one_tile, 0)
        hold[...] = jnp.zeros_like(hold)
        for s in range(nz):
            columns = slice(s * d_rows, (s + 1) * d_rows)
            hold[s, pl.ds(0, 1), pl.ds(0, d_rows)] = gain_acc[pl.ds(0, 1), :][:, columns]
            hold[s, pl.ds(1, 1), pl.ds(0, d_rows)] = gain_two_ref[pl.ds(0, 1), :][:, columns]
        for s in range(nz):
            block = z ^ s
            target = own_ref if s == 0 else sends[s - 1]
            target[pl.ds(0, d_rows), :] = acc_ref[
                pl.ds(pl.multiple_of(block * d_rows, 8), d_rows), :
            ].astype(target.dtype)
            target[pl.ds(d_rows, 16), :] = hold[block].astype(target.dtype)

    return call(
        kernel,
        [
            shape((TP // 2, local, width), f32),
            shape((TP // 2, local, width), bf16),
            shape((d_rows + 16, 2 * OWN), f32),
        ]
        + [shape((d_rows + 16, 2 * OWN), bf16)] * (nz - 1),
        [at, grad_query, *grad_kv, inputs, hidden, w_qkv, gains, gain_sums, cosine, sine],
        scratch=[
            pltpu.VMEM((rows, OWN), f32),
            pltpu.VMEM((width, 2 * OWN), f32),
            pltpu.VMEM((8, width), f32),
            pltpu.VMEM((nz, 16, 2 * OWN), f32),
        ],
        cost=8.0,
    )


def token_gradient(sums, tokens, grad_resid, gains):
    local, width = tokens.shape

    def kernel(*refs):
        parts, refs = refs[: len(sums)], refs[len(sums) :]
        x_ref, grad_ref, gain_ref, out_ref = refs
        grad_hidden = parts[0][...]
        for part in parts[1:]:
            grad_hidden = grad_hidden + part[...].astype(f32)
        x = x_ref[...].astype(f32)
        scale = norm_scale(x)
        normal = x * scale
        grad = grad_hidden * gain_ref[pl.ds(0, 1), :]
        grad = scale * (grad - normal * jnp.mean(grad * normal, axis=1, keepdims=True))
        out_ref[...] = grad + grad_ref[...]

    return call(
        kernel,
        [shape((local, width), f32)],
        [*sums, tokens, grad_resid, gains],
        scalars=0,
        cost=1.0,
    )[0]


def layer_output(sums, resid):
    def kernel(*refs):
        parts, (resid_ref, out_ref) = refs[: len(sums)], refs[len(sums) :]
        total = resid_ref[...]
        for part in parts:
            total = total + part[...].astype(f32)
        out_ref[...] = total.astype(bf16)

    return call(kernel, [shape(resid.shape, bf16)], [*sums, resid], scalars=0, cost=1.0)[0]


def ff_outputs(at, slots, ff_z, nz):
    d_rows, lanes = slots[0].shape
    part = ff_z // TP
    ff = part * nz
    third = lanes - 2 * ff
    width = 3 * third

    def kernel(at_ref, *refs):
        parts, (gate_ref, up_ref, down_ref, hold) = refs[:TP], refs[TP:]
        tp = at_ref[0]
        for j in range(TP):
            hold[tp ^ j] = parts[j][...].astype(f32)
        for s in range(nz):
            for ref, start in ((gate_ref, s * part), (up_ref, ff + s * part)):
                ref[:, pl.ds(s * ff_z, ff_z)] = jnp.concatenate(
                    [hold[c][:, start : start + part] for c in range(TP)], axis=1
                )
        for c in range(TP):
            for p in range(3):
                down_ref[pl.ds(c * part, part), pl.ds(p * third, third)] = hold[
                    c, pl.ds(p * part, part), pl.ds(2 * ff, third)
                ]

    return call(
        kernel,
        [
            shape((d_rows, nz * ff_z), f32),
            shape((d_rows, nz * ff_z), f32),
            shape((ff_z, width), f32),
        ],
        [at, *slots],
        scratch=[pltpu.VMEM((TP, d_rows, lanes), f32)],
        cost=5.0,
    )


def out_outputs(at, slots, width):
    d_rows = slots[0].shape[0]

    def kernel(at_ref, *refs):
        parts, (out_ref, hold) = refs[:TP], refs[TP:]
        tp = at_ref[0]
        for j in range(TP):
            columns = pl.ds(pl.multiple_of((tp ^ j) * OWN, OWN), OWN)
            hold[:, columns] = parts[j][...].astype(f32)
        out_ref[...] = hold[...][:, :width]

    return call(
        kernel,
        [shape((d_rows, width), f32)],
        [at, *slots],
        scratch=[pltpu.VMEM((d_rows, TP * OWN), f32)],
        cost=1.0,
    )[0]


def projection_outputs(at, slots, width):
    d_rows = slots[0].shape[0] - 16

    def kernel(at_ref, *refs):
        parts, (q_ref, k_ref, v_ref, one_ref, two_ref, hold) = refs[:TP], refs[TP:]
        tp = at_ref[0]
        total = jnp.zeros((16, 2 * OWN), f32)
        for j in range(TP):
            hold[tp ^ j] = parts[j][...].astype(f32)
            total = total + parts[j][pl.ds(d_rows, 16), :].astype(f32)
        one_ref[...] = total[0:1, :d_rows]
        two_ref[...] = total[1:2, :d_rows]
        heads = [hold[c][:d_rows, :OWN] for c in range(TP)]
        q_ref[...] = jnp.concatenate(heads, axis=1)[:, :width]
        kv = [hold[c][:d_rows, OWN:] for c in range(TP)]
        kv = [kv[0], kv[1] + kv[2], kv[3] + kv[4], kv[5], kv[6]]
        k_ref[...] = jnp.concatenate([p[:, :HEAD] for p in kv], axis=1)
        v_ref[...] = jnp.concatenate([p[:, HEAD:] for p in kv], axis=1)

    return call(
        kernel,
        [
            shape((d_rows, width), f32),
            shape((d_rows, KV_HEADS * HEAD), f32),
            shape((d_rows, KV_HEADS * HEAD), f32),
            shape((1, d_rows), f32),
            shape((1, d_rows), f32),
        ],
        [at, *slots],
        scratch=[pltpu.VMEM((TP, d_rows + 16, 2 * OWN), f32)],
        cost=2.0,
    )


def body(
    tokens,
    pair_order,
    gain_attn,
    gain_mlp,
    w_query,
    w_key,
    w_value,
    w_out,
    w_gate,
    w_up,
    w_down,
    cotangent,
):
    local_rows, width = tokens.shape
    half_rows = local_rows // 2
    nz = lax.axis_size("fsdp")
    outer = lax.axis_size("ctx") // TP
    count = lax.axis_size(AXES)
    groups = outer * nz
    me = lax.axis_index(AXES)
    z = lax.axis_index("fsdp")
    tp = lax.axis_index("ctx") % TP
    kv_index = (4 * (tp // 2)) // GROUP + tp % 2
    at = jnp.stack([tp, z, kv_index]).astype(i32)
    send = functools.partial(exchange, count=count)
    group_mask = [(g // nz) * TP * nz + g % nz for g in range(groups)]

    def after(value, *others):
        return lax.optimization_barrier((value, *others))[0]

    def plane_gather(block):
        even = [block] + [send(block, j * nz) for j in range(2, TP, 2)]
        odd = [send(e, nz) for e in even]
        return [piece for pair in zip(even, odd) for piece in pair]

    def plane_scatter(keep, passed):
        first, *rest = add_crossed(keep, send(passed, nz))
        return [first] + [send(piece, 2 * (j + 1) * nz) for j, piece in enumerate(rest)]

    def from_z(block):
        return [block] + [send(block, s) for s in range(1, nz)]

    def finish(own, sends):
        total = own
        for s, piece in enumerate(sends):
            total = total + send(piece, s + 1).astype(f32)
        step = 1
        while step < outer:
            total = total + send(total.astype(bf16), step * TP * nz).astype(f32)
            step *= 2
        return plane_gather(total.astype(bf16))

    pack_one = slice_attention_weights(at, w_query, w_key, w_value, w_out, gain_attn, gain_mlp)
    token_slots = plane_gather(tokens)
    pack_one = from_z(pack_one)

    slot_of = jnp.array([[m | (j * nz) for j in range(TP)] for m in group_mask], dtype=i32)
    low = pair_order[me ^ slot_of]
    base = jnp.stack([low, 2 * count - 1 - low], axis=1) * half_rows
    query_base = base[0].reshape(2 * TP)
    partner = jnp.array([j ^ 1 for j in range(TP)], dtype=i32)
    key_base = jnp.stack([base, base[:, :, partner]]).reshape(2 * groups, 2 * TP)
    places = (query_base[:, None] + jnp.arange(half_rows, dtype=i32)[None, :]).reshape(-1)
    lane = jnp.arange(OWN)
    freqs = base_theta ** (-2.0 * (lane % (HEAD // 2)).astype(f32) / HEAD)
    angles = places.astype(f32)[:, None] * freqs[None, :]
    cosine = jnp.cos(angles)
    sine = jnp.sin(angles) * jnp.where(lane % HEAD < HEAD // 2, -1.0, 1.0)[None, :]
    select = jnp.where((2 * tp + jnp.arange(2)) // GROUP == kv_index, 0, 1).astype(i32)

    inputs, hidden_one, turned_query, kv, w_qkv, w_out_own, gains = project(
        at, token_slots, pack_one, cosine, sine
    )
    own_kv = [kv] + [send(kv, m) for m in group_mask[1:]]
    other_kv = [send(slot, nz) for slot in own_kv]
    w_out_slots = plane_gather(w_out_own)
    cot_slots = plane_gather(after(cotangent, kv))
    pack_two = slice_ff_weights(at, w_gate, w_up, w_down, nz)
    pack_two = from_z(after(pack_two, *own_kv))
    attended, attended_own, log_mass = attention_forward(
        select, key_base, query_base, turned_query, own_kv, other_kv, half_rows
    )
    attended_slots = plane_gather(attended_own)

    (
        attended_low,
        w_out_all,
        resid,
        grad_keep,
        grad_pass,
        out_keep,
        out_pass,
        gain_sums,
        ff_own,
        *ff_sends,
    ) = feed_forward(at, inputs, attended_slots, w_out_slots, pack_two, cot_slots, gains)
    sums = plane_scatter(grad_keep, grad_pass)
    grad_resid, trade_keep, trade_pass = branch_gradient(
        at, sums, resid, cotangent, w_out_all, gains
    )
    crossed = send(trade_pass, nz)
    pairs = [
        send(pair, 2 * (j + 1) * nz) for j, pair in enumerate(pair_up(trade_keep, crossed))
    ]
    traded = [trade_keep[0], crossed[0]] + [pair[k] for pair in pairs for k in range(2)]

    grad_query, kv_keep, kv_pass, branch_columns = attention_backward(
        select,
        key_base,
        query_base,
        turned_query,
        own_kv,
        other_kv,
        traded,
        attended,
        log_mass,
        half_rows,
    )
    first, *rest = add_crossed(kv_keep, send(kv_pass, nz))
    grad_kv = [first] + [send(piece, m) for piece, m in zip(rest, group_mask[1:])]
    last_keep, last_pass, last_own, *last_sends = projection_gradient(
        at,
        grad_query,
        grad_kv,
        inputs,
        hidden_one,
        w_qkv,
        gains,
        gain_sums,
        cosine,
        sine,
        nz,
    )
    sums = plane_scatter(last_keep, last_pass)
    grad_tokens = token_gradient(sums, tokens, grad_resid, gains)
    layer_out = layer_output(plane_scatter(out_keep, out_pass), resid)

    grad_gate, grad_up, grad_down = ff_outputs(
        at, finish(ff_own, ff_sends), w_down.shape[0], nz
    )
    grad_out = tn(attended_low[:, :width], branch_columns).reshape(nz, -1, OWN)
    out_blocks = [lax.dynamic_index_in_dim(grad_out, z ^ s, 0, keepdims=False) for s in range(nz)]
    grad_out = out_outputs(
        at, finish(out_blocks[0], [b.astype(bf16) for b in out_blocks[1:]]), width
    )
    grad_w_query, grad_w_key, grad_w_value, gain_one, gain_two = projection_outputs(
        at, finish(last_own, last_sends), width
    )
    return (
        layer_out,
        grad_tokens,
        gain_one.reshape(-1),
        gain_two.reshape(-1),
        grad_w_query,
        grad_w_key,
        grad_w_value,
        grad_out,
        grad_gate,
        grad_up,
        grad_down,
    )


def solution(mesh):
    return jax.shard_map(
        body,
        mesh=mesh,
        in_specs=(
            P(("ctx", "fsdp"), None),
            P(),
            P("fsdp"),
            P("fsdp"),
            P("fsdp", None),
            P("fsdp", None),
            P("fsdp", None),
            P("fsdp", None),
            P("fsdp", None),
            P("fsdp", None),
            P("fsdp", None),
            P(("ctx", "fsdp"), None),
        ),
        out_specs=(
            P(("ctx", "fsdp"), None),
            P(("ctx", "fsdp"), None),
            P("fsdp"),
            P("fsdp"),
            P("fsdp", None),
            P("fsdp", None),
            P("fsdp", None),
            P("fsdp", None),
            P("fsdp", None),
            P("fsdp", None),
            P("fsdp", None),
        ),
        check_vma=False,
    )
```

```python
import functools

import jax
import jax.numpy as jnp
from jax import lax
from jax.experimental import pallas as pl
from jax.experimental.pallas import tpu as pltpu
from jax.sharding import PartitionSpec as P

HEADS = 15
KV_HEADS = 5
HEAD = 64
TP = 8
GROUP = HEADS // KV_HEADS
OWN = 2 * HEAD
epsilon = 1e-05
base_theta = 100000.0
far_below = -1e30
f32 = jnp.float32
bf16 = jnp.bfloat16
i32 = jnp.int32
AXES = ("ctx", "fsdp")
MIB = 1024 * 1024
smem = pl.BlockSpec(memory_space=pltpu.SMEM)
vmem = pl.BlockSpec(memory_space=pltpu.VMEM)


def exchange(array, mask, count):
    return lax.ppermute(array, AXES, [(i, i ^ mask) for i in range(count)])


def nn(left, right):
    return lax.dot_general(left, right, (((1,), (0,)), ((), ())), preferred_element_type=f32)


def tn(left, right):
    return lax.dot_general(left, right, (((0,), (0,)), ((), ())), preferred_element_type=f32)


def nt(left, right):
    return lax.dot_general(left, right, (((1,), (1,)), ((), ())), preferred_element_type=f32)


def shape(dims, dtype):
    return jax.ShapeDtypeStruct(dims, dtype)


def call(kernel, outs, inputs, scalars=1, scratch=(), limit=56, cost=1.0, far=()):
    specs = [smem] * scalars + [vmem] * (len(inputs) - scalars)
    for i in far:
        specs[i] = pl.BlockSpec(memory_space=pl.ANY)
    return pl.pallas_call(
        kernel,
        out_shape=tuple(outs),
        in_specs=specs,
        out_specs=tuple(vmem for unused in outs),
        scratch_shapes=list(scratch),
        compiler_params=pltpu.CompilerParams(vmem_limit_bytes=limit * MIB),
        cost_estimate=pl.CostEstimate(
            flops=int(cost * 1e9), bytes_accessed=int(cost * 1e6), transcendentals=0
        ),
    )(*inputs)


def one_hot(rows, columns, start):
    row = lax.broadcasted_iota(i32, (rows, columns), 0)
    column = lax.broadcasted_iota(i32, (rows, columns), 1)
    return jnp.where(row == column + start, 1.0, 0.0).astype(bf16)


def query_positions(base_ref, at, width, half_rows):
    lane = lax.broadcasted_iota(i32, (1, width), 1)
    place = jnp.zeros((1, width), i32)
    for block in range(width // half_rows):
        start = base_ref[at + block] - block * half_rows
        place = jnp.where(lane >= block * half_rows, start + lane, place)
    return place


def key_positions(base_ref, row, at, count, half_rows, width):
    offset = lax.broadcasted_iota(i32, (half_rows, width), 0)
    return jnp.concatenate([offset + base_ref[row, at + b] for b in range(count)], axis=0)


def swap_halves(matrix):
    lane = lax.broadcasted_iota(i32, matrix.shape, 1)
    ahead = pltpu.roll(matrix, matrix.shape[1] - HEAD // 2, 1)
    behind = pltpu.roll(matrix, HEAD // 2, 1)
    return jnp.where(lane % HEAD < HEAD // 2, ahead, behind)


def norm_scale(matrix):
    return lax.rsqrt(jnp.mean(matrix * matrix, axis=1, keepdims=True) + epsilon)


def slice_attention_weights(at, w_query, w_key, w_value, w_out, gain_one, gain_two):
    d_rows, width = w_query.shape
    lanes = 2 * OWN + OWN
    rest = width - (TP - 1) * OWN

    def kernel(at_ref, q_ref, k_ref, v_ref, o_ref, g_ref, out_ref, cols, heads, whole, sems):
        tp = at_ref[0]
        kv = at_ref[2]
        wides, narrows = (q_ref, o_ref), (k_ref, v_ref)

        @pl.when(tp < TP - 1)
        def most():
            columns = pl.ds(pl.multiple_of(tp * OWN, OWN), OWN)
            copies = [
                pltpu.make_async_copy(ref.at[:, columns], cols.at[i], sems.at[i])
                for i, ref in enumerate(wides)
            ]
            for copy in copies:
                copy.start()
            for copy in copies:
                copy.wait()

        @pl.when(tp == TP - 1)
        def last():
            copies = [
                pltpu.make_async_copy(ref, whole.at[i], sems.at[i]) for i, ref in enumerate(wides)
            ]
            for copy in copies:
                copy.start()
            for copy in copies:
                copy.wait()
            for i in range(2):
                cols[i] = jnp.zeros((d_rows, OWN), bf16)
                cols[i, :, pl.ds(0, rest)] = whole[i, :, pl.ds(width - rest, rest)]

        @pl.when(kv < KV_HEADS)
        def real():
            rows = pl.ds(pl.multiple_of(kv * HEAD, HEAD), HEAD)
            copies = [
                pltpu.make_async_copy(ref.at[rows, :], heads.at[i], sems.at[2 + i])
                for i, ref in enumerate(narrows)
            ]
            for copy in copies:
                copy.start()
            for copy in copies:
                copy.wait()

        @pl.when(kv >= KV_HEADS)
        def none():
            heads[...] = jnp.zeros_like(heads)

        out_ref[pl.ds(0, d_rows), pl.ds(0, OWN)] = cols[0]
        turned = jnp.concatenate([heads[0], heads[1]], axis=0).astype(f32).T
        out_ref[pl.ds(0, d_rows), pl.ds(OWN, OWN)] = turned.astype(bf16)
        out_ref[pl.ds(0, d_rows), pl.ds(2 * OWN, OWN)] = cols[1]
        out_ref[pl.ds(d_rows, 16), :] = jnp.zeros((16, lanes), bf16)
        out_ref[pl.ds(d_rows, 2), pl.ds(0, d_rows)] = g_ref[...]

    return call(
        kernel,
        [shape((d_rows + 16, lanes), bf16)],
        [at, w_query, w_key.T, w_value.T, w_out, jnp.stack([gain_one, gain_two])],
        scratch=[
            pltpu.VMEM((2, d_rows, OWN), bf16),
            pltpu.VMEM((2, HEAD, d_rows), bf16),
            pltpu.VMEM((2, d_rows, width), bf16),
            pltpu.SemaphoreType.DMA((4,)),
        ],
        limit=8,
        cost=2.0,
        far=(1, 2, 3, 4),
    )[0]


def slice_ff_weights(at, w_gate, w_up, w_down, nz):
    d_rows = w_gate.shape[0]
    ff_z, width = w_down.shape
    part = ff_z // TP
    own = part * nz

    def kernel(at_ref, g_ref, u_ref, d_ref, out_ref):
        pick = one_hot(ff_z, part, at_ref[0] * part)
        for ref, start in ((g_ref, 0), (u_ref, own)):
            pieces = [nn(ref[:, pl.ds(s * ff_z, ff_z)], pick) for s in range(nz)]
            out_ref[:, pl.ds(start, own)] = jnp.concatenate(pieces, axis=1).astype(bf16)
        pieces = [nn(d_ref[pl.ds(s * d_rows, d_rows), :], pick) for s in range(nz)]
        out_ref[:, pl.ds(2 * own, own)] = jnp.concatenate(pieces, axis=1).astype(bf16)

    return call(
        kernel,
        [shape((d_rows, 3 * own), bf16)],
        [at, w_gate, w_up, w_down.T],
        limit=16,
        cost=4.0,
    )[0]


def project(at, tokens, packs, cosine, sine, cotangent):
    local, width = tokens[0].shape
    half_rows = local // 2
    rows = TP * local
    nz = len(packs)
    pack_rows, lanes = packs[0].shape
    d_rows = pack_rows - 16

    def kernel(at_ref, *refs):
        toks, refs = refs[:TP], refs[TP:]
        pack, refs = refs[:nz], refs[nz:]
        cos_ref, sin_ref, cot_ref, x_ref, hid_ref, qt_ref, kv_ref, w_ref, cot_out, wo_out, gain_ref, hold = refs
        z = at_ref[1]
        for s in range(nz):
            hold[z ^ s] = pack[s][...]
        for s in range(nz):
            w_ref[pl.ds(s * d_rows, d_rows), :] = hold[s, pl.ds(0, d_rows), pl.ds(0, 2 * OWN)]
        gains = [hold[s, pl.ds(d_rows, 16), pl.ds(0, d_rows)].astype(f32) for s in range(nz)]
        gain_ref[...] = jnp.concatenate(gains, axis=1)[:8]
        gain = gain_ref[pl.ds(0, 1), :]
        cot_out[:, pl.ds(0, width)] = cot_ref[...]
        turned = [
            hold[s, pl.ds(0, d_rows), pl.ds(2 * OWN, OWN)].astype(f32) for s in range(nz)
        ]
        wo_out[:, pl.ds(0, width)] = jnp.concatenate(turned, axis=0).T.astype(bf16)
        per = 4
        for tile in range(2 * TP // per):
            side, first = (tile * per) // TP, (tile * per) % TP
            at_rows = pl.ds(tile * per * half_rows, per * half_rows)
            block = jnp.concatenate(
                [toks[first + j][pl.ds(side * half_rows, half_rows), :] for j in range(per)], axis=0
            )
            x_ref[at_rows, :] = block
            inputs = block.astype(f32)
            hidden = (inputs * norm_scale(inputs) * gain).astype(bf16)
            hid_ref[at_rows, :] = hidden
            out = nn(hidden, w_ref[...])
            cos, sin = cos_ref[at_rows, :], sin_ref[at_rows, :]
            query = out[:, :OWN]
            query = query * cos + swap_halves(query) * sin
            qt_ref[:, at_rows] = (query.astype(bf16).astype(f32) * HEAD**-0.5).T.astype(bf16)
            pair = out[:, OWN:]
            turned = pair * cos + swap_halves(pair) * sin
            lane = lax.broadcasted_iota(i32, pair.shape, 1)
            kv_ref[at_rows, :] = jnp.where(lane < HEAD, turned, pair).astype(bf16)

    return call(
        kernel,
        [
            shape((rows, width), bf16),
            shape((rows, width), bf16),
            shape((OWN, rows), bf16),
            shape((rows, OWN), bf16),
            shape((width, 2 * OWN), bf16),
            shape((local, TP * OWN), bf16),
            shape((OWN, TP * OWN), bf16),
            shape((8, width), f32),
        ],
        [at, *tokens, *packs, cosine, sine, cotangent],
        scratch=[pltpu.VMEM((nz, pack_rows, lanes), bf16)],
        limit=24,
        cost=6.0,
    )


def attention_forward(select, key_base, query_base, turned_query, own_kv, other_kv, half_rows):
    groups = len(own_kv)
    rows = own_kv[0].shape[0]
    half = rows // 2
    blocks = half // half_rows
    wide, deep = 128, 128

    def kernel(sel_ref, key_ref, query_ref, q_ref, *refs):
        own, other = refs[:groups], refs[groups : 2 * groups]
        out_ref, low_ref, lse_ref, kv_ref, kvt_ref, top_ref, mass_ref, place_ref = refs[2 * groups :]
        for head in range(2):
            chosen = sel_ref[head] == 0
            for group in range(groups):

                @pl.when(chosen)
                def take_own():
                    kv_ref[head, group] = own[group][...]
                    kvt_ref[head, group] = own[group][...].T

                @pl.when(jnp.logical_not(chosen))
                def take_other():
                    kv_ref[head, group] = other[group][...]
                    kvt_ref[head, group] = other[group][...].T

        top_ref[...] = jnp.full_like(top_ref, far_below)
        mass_ref[...] = jnp.zeros_like(mass_ref)
        out_ref[...] = jnp.zeros_like(out_ref)

        def one_group(group, unused):
            for head in range(2):
                row = sel_ref[head] * groups + group
                own_rows = pl.ds(head * HEAD, HEAD)
                stat = pl.ds(head, 1)
                place_ref[...] = key_positions(key_ref, row, 0, 2 * blocks, half_rows, 128)
                for k_start in range(0, rows, deep):
                    keys_at = pl.ds(k_start, deep)
                    k_side = k_start // half
                    block = kv_ref[head, group, keys_at, :]
                    values = kvt_ref[head, group, pl.ds(HEAD, HEAD), keys_at]
                    for start in range(k_side * half, rows, wide):
                        lanes = pl.ds(start, wide)
                        turned = q_ref[own_rows, lanes]
                        padded = jnp.concatenate([turned, jnp.zeros_like(turned)], axis=0)
                        scores = nn(block, padded)
                        if start // half == k_side:
                            places = query_positions(
                                query_ref, start // half_rows, wide, half_rows
                            )
                            scores = jnp.where(place_ref[keys_at, :] <= places, scores, far_below)
                        before = top_ref[stat, lanes]
                        top = jnp.maximum(before, jnp.max(scores, axis=0, keepdims=True))
                        weights = jnp.exp(scores - top)
                        fade = jnp.exp(before - top)
                        top_ref[stat, lanes] = top
                        mass_ref[stat, lanes] = mass_ref[stat, lanes] * fade + jnp.sum(
                            weights, axis=0, keepdims=True
                        )
                        out_ref[own_rows, lanes] = out_ref[own_rows, lanes] * fade + nn(
                            values, weights.astype(bf16)
                        )
            return unused

        lax.fori_loop(0, groups, one_group, 0)
        for head in range(2):
            own_rows = pl.ds(head * HEAD, HEAD)
            mass = mass_ref[pl.ds(head, 1), :]
            out_ref[own_rows, :] = out_ref[own_rows, :] / mass
            lse_ref[pl.ds(head, 1), :] = top_ref[pl.ds(head, 1), :] + jnp.log(mass)
        low_ref[...] = out_ref[...].T.astype(bf16)

    return call(
        kernel,
        [shape((OWN, rows), f32), shape((rows, OWN), bf16), shape((2, rows), f32)],
        [select, key_base, query_base, turned_query, *own_kv, *other_kv],
        scalars=3,
        scratch=[
            pltpu.VMEM((2, groups, rows, OWN), bf16),
            pltpu.VMEM((2, groups, OWN, rows), bf16),
            pltpu.VMEM((2, rows), f32),
            pltpu.VMEM((2, rows), f32),
            pltpu.VMEM((rows, 128), i32),
        ],
        limit=24,
        cost=14.0,
    )


def attention_backward(
    select, key_base, query_base, turned_query, own_kv, other_kv, traded, attended, log_mass, half_rows
):
    groups = len(own_kv)
    rows = own_kv[0].shape[0]
    half = rows // 2
    blocks = half // half_rows
    wide, deep = 512, 256

    def kernel(sel_ref, key_ref, query_ref, q_ref, *refs):
        own, other = refs[:groups], refs[groups : 2 * groups]
        refs = refs[2 * groups :]
        local = 2 * half_rows
        parts = [refs[0], refs[1]] + [
            refs[2 + j].at[pl.ds(k * local, local), :] for j in range(TP // 2 - 1) for k in range(2)
        ]
        refs = refs[1 + TP // 2 :]
        att_ref, lse_ref, dq_ref, keep_ref, pass_ref, gb_ref = refs[:6]
        kv_ref, sum_ref, g_ref, rq_ref, rg_ref, delta_ref, pos_ref = refs[6:]
        for group in range(groups):
            kv_ref[0, group] = own[group][...]
            kv_ref[1, group] = other[group][...]
        sum_ref[...] = jnp.zeros_like(sum_ref)
        dq_ref[...] = jnp.zeros_like(dq_ref)
        zeros = jnp.zeros((rows, HEAD), bf16)
        for j in range(0, TP, 2):
            for side in range(2):
                at = pl.ds(side * half + j * half_rows, 2 * half_rows)
                pair = jnp.concatenate(
                    [parts[j + k][pl.ds(side * half_rows, half_rows), :] for k in range(2)], axis=0
                )
                g_ref[:, at] = pair[:, :OWN].T
                gb_ref[at, :] = pair[:, OWN:]
        for head in range(2):
            own_rows = pl.ds(head * HEAD, HEAD)
            rq_ref[head] = jnp.concatenate([q_ref[own_rows, :].T, zeros], axis=1)
            grad = g_ref[own_rows, :]
            rg_ref[head] = jnp.concatenate([zeros, grad.T], axis=1)
            delta_ref[pl.ds(head, 1), :] = jnp.sum(
                grad.astype(f32) * att_ref[own_rows, :], axis=0, keepdims=True
            )

        def one_group(group, unused):
            for head in range(2):
                which = sel_ref[head]
                own_rows = pl.ds(head * HEAD, HEAD)
                stat = pl.ds(head, 1)
                pos_ref[...] = key_positions(
                    key_ref, which * groups + group, 0, 2 * blocks, half_rows, 128
                )
                for k_start in range(0, rows, deep):
                    keys_at = pl.ds(k_start, deep)
                    k_side = k_start // half
                    block = kv_ref[which, group, keys_at, :]
                    turned_keys = block.T[:HEAD]
                    for start in range(k_side * half, rows, wide):
                        lanes = pl.ds(start, wide)
                        turned = q_ref[own_rows, lanes]
                        padded = jnp.concatenate([turned, jnp.zeros_like(turned)], axis=0)
                        scores = nn(block, padded)
                        if start // half == k_side:
                            places = query_positions(
                                query_ref, start // half_rows, wide, half_rows
                            )
                            at = jnp.concatenate([pos_ref[keys_at, :]] * (wide // 128), axis=1)
                            scores = jnp.where(at <= places, scores, far_below)
                        probs = jnp.exp(scores - lse_ref[stat, lanes])
                        grads = g_ref[own_rows, lanes]
                        padded = jnp.concatenate([jnp.zeros_like(grads), grads], axis=0)
                        grad_probs = nn(block, padded)
                        grad_scores = probs * (grad_probs - delta_ref[stat, lanes])
                        probs = probs.astype(bf16)
                        grad_scores = grad_scores.astype(bf16)
                        sum_ref[which, group, keys_at, :] += nn(
                            grad_scores, rq_ref[head, lanes, :]
                        ) + nn(probs, rg_ref[head, lanes, :])
                        dq_ref[own_rows, lanes] += nn(turned_keys, grad_scores)
            return unused

        lax.fori_loop(0, groups, one_group, 0)
        for group in range(groups):
            keep_ref[pl.ds(group * rows, rows), :] = sum_ref[0, group]
            pass_ref[pl.ds(group * rows, rows), :] = sum_ref[1, group].astype(bf16)

    return call(
        kernel,
        [
            shape((OWN, rows), f32),
            shape((groups * rows, OWN), f32),
            shape((groups * rows, OWN), bf16),
            shape((rows, OWN), bf16),
        ],
        [
            select,
            key_base,
            query_base,
            turned_query,
            *own_kv,
            *other_kv,
            *traded,
            attended,
            log_mass,
        ],
        scalars=3,
        scratch=[
            pltpu.VMEM((2, groups, rows, OWN), bf16),
            pltpu.VMEM((2, groups, rows, OWN), f32),
            pltpu.VMEM((OWN, rows), bf16),
            pltpu.VMEM((2, rows, OWN), bf16),
            pltpu.VMEM((2, rows, OWN), bf16),
            pltpu.VMEM((2, rows), f32),
            pltpu.VMEM((rows, 128), i32),
        ],
        limit=40,
        cost=18.0,
    )


def store_blocks(part, tile, per, half_rows, keep_ref, pass_ref):
    side = (tile * per) // TP
    first = lax.rem(tile * per, TP) // 2
    for j in range(per):
        piece = part[j * half_rows : (j + 1) * half_rows]
        row = (2 * (first + j // 2) + side) * half_rows
        at = pl.ds(pl.multiple_of(row, half_rows), half_rows)
        target = keep_ref if j % 2 == 0 else pass_ref
        target[at, pl.ds(0, piece.shape[1])] = piece.astype(target.dtype)


def feed_forward(at, inputs, attended, sides, packs, gains, nz):
    rows, width = inputs.shape
    local = rows // TP
    half_rows = local // 2
    half = rows // 2
    d_rows, lanes = packs[0].shape[0] // 2, packs[0].shape[1]
    ff = lanes // 3
    part_rows = ff // nz
    per = 4
    tile_rows = per * half_rows

    def kernel(at_ref, x_ref, *refs):
        att, refs = refs[:TP], refs[TP:]
        cot_even, wo_even, odd, pack_near, pack_far = refs[:5]
        refs = refs[5:]
        gain_ref, refs = refs[0], refs[1:]
        att_out, wo_out, resid_out, gk_ref, gp_ref, lk_ref, lp_ref, gain_out, own_ref = refs[:9]
        send_ref, refs = refs[9], refs[10:]
        gu_w, dn_w, cot_ref, acc_gu, acc_dn, hold, blocks = refs
        tp = at_ref[0]
        z = at_ref[1]
        for j in range(TP):
            columns = pl.ds(pl.multiple_of((tp ^ j) * OWN, OWN), OWN)
            from_wo, row = (odd, local * TP // 2) if j % 2 else (wo_even, 0)
            row += OWN * (2 * (j // 2 % 2) + j // 4)
            wo_out[columns, :] = from_wo[pl.ds(row, OWN), pl.ds(0, width)]
            from_cot = odd if j % 2 else cot_even
            for side in range(2):
                for k in range(TP):
                    att_out[pl.ds(side * half + k * half_rows, half_rows), columns] = att[j][
                        pl.ds(side * half + (k ^ j) * half_rows, half_rows), :
                    ]
                cot_ref[pl.ds(side * half + j * half_rows, half_rows), :] = from_cot[
                    pl.ds(local * (j // 2) + side * half_rows, half_rows), pl.ds(0, width)
                ]
        for s in range(nz):
            hold[z ^ s] = (pack_far if s % 2 else pack_near)[pl.ds(d_rows * (s // 2), d_rows), :]
        for s in range(nz):
            rows_at = pl.ds(s * d_rows, d_rows)
            gu_w[rows_at, :] = hold[s, :, pl.ds(0, 2 * ff)]
            dn_w[rows_at, :] = jnp.concatenate(
                [
                    hold[b][:, 2 * ff + s * part_rows : 2 * ff + (s + 1) * part_rows]
                    for b in range(nz)
                ],
                axis=1,
            )
        gain = gain_ref[pl.ds(1, 1), :]
        gain_out[...] = jnp.zeros_like(gain_out)
        acc_gu[...] = jnp.zeros_like(acc_gu)
        acc_dn[...] = jnp.zeros_like(acc_dn)

        def one_tile(tile, unused):
            at_rows = pl.ds(pl.multiple_of(tile * tile_rows, tile_rows), tile_rows)
            branch = nt(att_out[at_rows, :][:, :width], wo_out[pl.ds(0, width), :])
            resid = x_ref[at_rows, :].astype(f32) + branch
            side = (tile * per) // TP

            @pl.when(lax.rem(tile * per, TP) == 0)
            def keep_own():
                resid_out[pl.ds(pl.multiple_of(side * half_rows, half_rows), half_rows), :] = resid[
                    :half_rows
                ]

            normal = resid * norm_scale(resid)
            hidden = (normal * gain).astype(bf16)
            gate_up = nn(hidden, gu_w[...])
            gate, up = gate_up[:, :ff], gate_up[:, ff:]
            sigmoid = 1.0 / (1.0 + jnp.exp(-gate))
            activated = gate * sigmoid
            product = (activated * up).astype(bf16)
            cotangent = cot_ref[at_rows, :]
            grad_product = nn(cotangent, dn_w[...])
            grad_gate = grad_product * up * sigmoid * (1.0 + gate * (1.0 - sigmoid))
            grad_gu = jnp.concatenate([grad_gate, grad_product * activated], axis=1).astype(bf16)
            partial = nt(grad_gu, gu_w[...])
            gain_out[pl.ds(0, 1), :] += jnp.sum(partial * normal, axis=0, keepdims=True)
            store_blocks(partial, tile, per, half_rows, gk_ref, gp_ref)
            store_blocks(nt(product, dn_w[...]), tile, per, half_rows, lk_ref, lp_ref)
            acc_gu[...] += tn(hidden, grad_gu)
            acc_dn[...] += tn(cotangent, product)
            return unused

        lax.fori_loop(0, 2 * TP // per, one_tile, 0)
        for b in range(nz):
            blocks[b, :, pl.ds(0, 2 * ff)] = acc_gu[pl.ds(b * d_rows, d_rows), :]
            blocks[b, :, pl.ds(2 * ff, ff)] = jnp.concatenate(
                [
                    acc_dn[pl.ds(s * d_rows, d_rows), :][:, b * part_rows : (b + 1) * part_rows]
                    for s in range(nz)
                ],
                axis=1,
            )
        for s in range(nz):
            target = send_ref if s % 2 else own_ref
            target[pl.ds(d_rows * (s // 2), d_rows), :] = blocks[z ^ s].astype(target.dtype)

    keep = shape((TP // 2 * local, width), f32)
    passed = shape((TP // 2 * local, TP * OWN), bf16)
    return call(
        kernel,
        [
            shape((rows, TP * OWN), bf16),
            shape((TP * OWN, width), bf16),
            shape((local, width), f32),
            keep,
            passed,
            keep,
            passed,
            shape((8, width), f32),
            shape((2 * d_rows, lanes), f32),
            shape((2 * d_rows, lanes), bf16),
        ],
        [at, inputs, *attended, *sides, *packs, gains],
        scratch=[
            pltpu.VMEM((width, 2 * ff), bf16),
            pltpu.VMEM((width, ff), bf16),
            pltpu.VMEM((rows, width), bf16),
            pltpu.VMEM((width, 2 * ff), f32),
            pltpu.VMEM((width, ff), f32),
            pltpu.VMEM((nz, d_rows, lanes), bf16),
            pltpu.VMEM((nz, d_rows, lanes), f32),
        ],
        limit=48,
        cost=18.0,
    )


def add_crossed(keep, crossed, count):
    local, width = keep.shape[0] // count, keep.shape[1]

    def kernel(keep_ref, cross_ref, own_ref, *sends):
        for j in range(count):
            at = pl.ds(j * local, local)
            target = own_ref if j == 0 else sends[j - 1]
            target[...] = (
                keep_ref[at, :] + cross_ref[at, pl.ds(0, width)].astype(f32)
            ).astype(target.dtype)

    return call(
        kernel,
        [shape((local, width), f32)] + [shape((local, width), bf16)] * (count - 1),
        [keep, crossed],
        scalars=0,
        limit=12,
        cost=1.0,
    )


def branch_gradient(at, sums, resid, cotangent, w_out, gains):
    local, width = resid.shape

    def kernel(at_ref, *refs):
        parts, refs = refs[: len(sums)], refs[len(sums) :]
        resid_ref, cot_ref, wo_ref, gain_ref, grad_ref, keep_ref, pass_ref, ga_ref, gb_ref = refs
        tp = at_ref[0]
        grad_hidden = parts[0][...]
        for part in parts[1:]:
            grad_hidden = grad_hidden + part[...].astype(f32)
        resid = resid_ref[...]
        scale = norm_scale(resid)
        normal = resid * scale
        grad = grad_hidden * gain_ref[pl.ds(1, 1), :]
        grad = scale * (grad - normal * jnp.mean(grad * normal, axis=1, keepdims=True))
        grad = grad + cot_ref[...].astype(f32)
        grad_ref[...] = grad
        low = grad.astype(bf16)
        gb_ref[...] = jnp.zeros_like(gb_ref)
        gb_ref[:, pl.ds(0, width)] = low
        ga_ref[...] = jnp.zeros_like(ga_ref)
        ga_ref[:, pl.ds(0, width)] = nn(low, wo_ref[pl.ds(0, width), :]).astype(bf16)
        for j in range(TP):
            columns = pl.ds(pl.multiple_of((tp ^ j) * OWN, OWN), OWN)
            target = keep_ref if j % 2 == 0 else pass_ref
            rows = pl.ds((j // 2) * local, local)
            target[rows, pl.ds(0, OWN)] = ga_ref[:, columns]
            target[rows, pl.ds(OWN, OWN)] = gb_ref[:, columns]

    blocks = shape((TP // 2 * local, 2 * OWN), bf16)
    return call(
        kernel,
        [shape((local, width), f32), blocks, blocks],
        [at, *sums, resid, cotangent, w_out, gains],
        scratch=[pltpu.VMEM((local, TP * OWN), bf16), pltpu.VMEM((local, TP * OWN), bf16)],
        limit=16,
        cost=3.0,
    )


def pair_up(keep, crossed, count):
    local, width = keep.shape[0] // count, keep.shape[1]

    def kernel(keep_ref, cross_ref, *outs):
        for j in range(1, count):
            at = pl.ds(j * local, local)
            outs[j - 1][pl.ds(0, local), :] = keep_ref[at, :]
            outs[j - 1][pl.ds(local, local), :] = cross_ref[at, :]

    return call(
        kernel,
        [shape((2 * local, width), bf16)] * (count - 1),
        [keep, crossed],
        scalars=0,
        limit=8,
        cost=0.7,
    )


def projection_gradient(
    at, grad_query, grad_kv, inputs, hidden, w_qkv, gain_sums, cosine, sine, grad_out, nz
):
    rows, width = inputs.shape
    local = rows // TP
    half_rows = local // 2
    d_rows = width // nz
    per = 4
    tile_rows = per * half_rows
    pieces = len(grad_kv)

    def kernel(at_ref, dq_ref, *refs):
        kvs, refs = refs[:pieces], refs[pieces:]
        x_ref, hid_ref, w_ref, gain_two_ref, cos_ref, sin_ref, wo_ref = refs[:7]
        keep_ref, pass_ref, own_ref = refs[7:10]
        sends, refs = refs[10 : 10 + nz - 1], refs[10 + nz - 1 :]
        turn_ref, acc_ref, gain_acc, hold = refs
        z = at_ref[1]
        turn_ref[...] = dq_ref[...].T * HEAD**-0.5
        acc_ref[...] = jnp.zeros_like(acc_ref)
        gain_acc[...] = jnp.zeros_like(gain_acc)

        def one_tile(tile, unused):
            at_rows = pl.ds(pl.multiple_of(tile * tile_rows, tile_rows), tile_rows)
            cos, sin = cos_ref[at_rows, :], sin_ref[at_rows, :]
            query = turn_ref[at_rows, :]
            query = query * cos - swap_halves(query) * sin
            pair = kvs[0][at_rows, :].astype(f32)
            for piece in kvs[1:]:
                pair = pair + piece[at_rows, :].astype(f32)
            turned = pair * cos - swap_halves(pair) * sin
            lane = lax.broadcasted_iota(i32, pair.shape, 1)
            pair = jnp.where(lane < HEAD, turned, pair)
            grad = jnp.concatenate([query, pair], axis=1).astype(bf16)
            partial = nt(grad, w_ref[...])
            x = x_ref[at_rows, :].astype(f32)
            gain_acc[pl.ds(0, 1), :] += jnp.sum(partial * (x * norm_scale(x)), axis=0, keepdims=True)
            store_blocks(partial, tile, per, half_rows, keep_ref, pass_ref)
            acc_ref[...] += tn(hid_ref[at_rows, :], grad)
            return unused

        lax.fori_loop(0, 2 * TP // per, one_tile, 0)
        hold[...] = jnp.zeros_like(hold)
        for s in range(nz):
            columns = slice(s * d_rows, (s + 1) * d_rows)
            hold[s, pl.ds(0, 1), pl.ds(0, d_rows)] = gain_acc[pl.ds(0, 1), :][:, columns]
            hold[s, pl.ds(1, 1), pl.ds(0, d_rows)] = gain_two_ref[pl.ds(0, 1), :][:, columns]
        for s in range(nz):
            block = z ^ s
            target = own_ref if s == 0 else sends[s - 1]
            rows_at = pl.ds(pl.multiple_of(block * d_rows, 8), d_rows)
            part = pl.ds(0, d_rows)
            target[part, pl.ds(0, 2 * OWN)] = acc_ref[rows_at, :].astype(target.dtype)
            target[part, pl.ds(2 * OWN, OWN)] = wo_ref[rows_at, :].astype(target.dtype)
            target[pl.ds(d_rows, 16), :] = hold[block].astype(target.dtype)

    return call(
        kernel,
        [
            shape((TP // 2 * local, width), f32),
            shape((TP // 2 * local, TP * OWN), bf16),
            shape((d_rows + 16, 3 * OWN), f32),
        ]
        + [shape((d_rows + 16, 3 * OWN), bf16)] * (nz - 1),
        [at, grad_query, *grad_kv, inputs, hidden, w_qkv, gain_sums, cosine, sine, grad_out],
        scratch=[
            pltpu.VMEM((rows, OWN), f32),
            pltpu.VMEM((width, 2 * OWN), f32),
            pltpu.VMEM((8, width), f32),
            pltpu.VMEM((nz, 16, 3 * OWN), f32),
        ],
        limit=32,
        cost=8.0,
    )


def token_gradient(sums, tokens, grad_resid, gains):
    local, width = tokens.shape

    def kernel(*refs):
        parts, refs = refs[: len(sums)], refs[len(sums) :]
        x_ref, grad_ref, gain_ref, out_ref = refs
        grad_hidden = parts[0][...]
        for part in parts[1:]:
            grad_hidden = grad_hidden + part[...].astype(f32)
        x = x_ref[...].astype(f32)
        scale = norm_scale(x)
        normal = x * scale
        grad = grad_hidden * gain_ref[pl.ds(0, 1), :]
        grad = scale * (grad - normal * jnp.mean(grad * normal, axis=1, keepdims=True))
        out_ref[...] = (grad + grad_ref[...]).T

    return call(
        kernel,
        [shape((width, local), f32)],
        [*sums, tokens, grad_resid, gains],
        scalars=0,
        limit=8,
        cost=1.0,
    )[0].T


def layer_output(sums, resid):
    def kernel(*refs):
        parts, (resid_ref, out_ref) = refs[: len(sums)], refs[len(sums) :]
        total = resid_ref[...]
        for part in parts:
            total = total + part[...].astype(f32)
        out_ref[...] = total.T.astype(bf16)

    turned = shape(resid.shape[::-1], bf16)
    return call(kernel, [turned], [*sums, resid], scalars=0, limit=8, cost=1.0)[0].T


def split_rows(rows):
    first = (rows // 2 + 15) // 16 * 16
    return first, rows - first


def first_sum(keep, arrived):
    rows, lanes = keep.shape[0] // 2, keep.shape[1]

    def kernel(keep_ref, in_ref, own_ref, send_ref):
        for ref, start in ((own_ref, 0), (send_ref, rows)):
            at = pl.ds(start, rows)
            ref[...] = (keep_ref[at, :] + in_ref[at, :].astype(f32)).astype(ref.dtype)

    return call(
        kernel,
        [shape((rows, lanes), f32), shape((rows, lanes), bf16)],
        [keep, arrived],
        scalars=0,
        limit=8,
        cost=1.0,
    )


def last_sum(own, arrived):
    rows, lanes = own.shape
    first, second = split_rows(rows)

    def kernel(own_ref, in_ref, a_ref, b_ref):
        for ref, start, count in ((a_ref, 0, first), (b_ref, first, second)):
            at = pl.ds(start, count)
            ref[:, pl.ds(0, lanes)] = (own_ref[at, :] + in_ref[at, :].astype(f32)).astype(bf16)

    return call(
        kernel,
        [shape((first, TP * OWN), bf16), shape((second, TP * OWN), bf16)],
        [own, arrived],
        scalars=0,
        limit=8,
        cost=1.0,
    )


def ff_outputs(at, even_a, even_b, odd, d_rows, ff_z, nz):
    part = ff_z // TP
    ff = part * nz
    first, second = split_rows(d_rows)

    def kernel(at_ref, a_ref, b_ref, odd_ref, gate_ref, up_ref, down_ref, hold):
        tp = at_ref[0]
        for j in range(TP):
            from_a, from_b = (odd_ref, odd_ref) if j % 2 else (a_ref, b_ref)
            row_b = (first * TP // 2 if j % 2 else 0) + second * (2 * (j // 2 % 2) + j // 4)
            hold[tp ^ j, pl.ds(0, first), :] = from_a[pl.ds(first * (j // 2), first), pl.ds(0, 3 * ff)]
            hold[tp ^ j, pl.ds(first, second), :] = from_b[pl.ds(row_b, second), pl.ds(0, 3 * ff)]
        for s in range(nz):
            for start in (s * part, ff + s * part, 2 * ff + s * part):
                block = jnp.concatenate(
                    [hold[c][:, start : start + part] for c in range(TP)], axis=1
                ).astype(f32)
                if start < ff:
                    gate_ref[:, pl.ds(s * ff_z, ff_z)] = block
                elif start < 2 * ff:
                    up_ref[:, pl.ds(s * ff_z, ff_z)] = block
                else:
                    down_ref[pl.ds(s * d_rows, d_rows), :] = block

    gate, up, down = call(
        kernel,
        [
            shape((d_rows, nz * ff_z), f32),
            shape((d_rows, nz * ff_z), f32),
            shape((nz * d_rows, ff_z), f32),
        ],
        [at, even_a, even_b, odd],
        scratch=[pltpu.VMEM((TP, d_rows, 3 * ff), bf16)],
        limit=32,
        cost=7.0,
    )
    return gate, up, down.T


def projection_outputs(at, slots, width):
    d_rows = slots[0].shape[0] - 16

    def kernel(at_ref, *refs):
        parts, (q_ref, k_ref, v_ref, o_ref, one_ref, two_ref, hold) = refs[:TP], refs[TP:]
        tp = at_ref[0]
        total = jnp.zeros((16, 3 * OWN), f32)
        for j in range(TP):
            hold[tp ^ j] = parts[j][...].astype(f32)
            total = total + parts[j][pl.ds(d_rows, 16), :].astype(f32)
        one_ref[...] = total[0:1, :d_rows]
        two_ref[...] = total[1:2, :d_rows]
        heads = [hold[c][:d_rows, :OWN] for c in range(TP)]
        q_ref[...] = jnp.concatenate(heads, axis=1)[:, :width]
        heads = [hold[c][:d_rows, 2 * OWN :] for c in range(TP)]
        o_ref[...] = jnp.concatenate(heads, axis=1)[:, :width]
        kv = [hold[c][:d_rows, OWN : 2 * OWN] for c in range(TP)]
        kv = [kv[0], kv[1] + kv[2], kv[3] + kv[4], kv[5], kv[6]]
        for c in range(KV_HEADS):
            turned = kv[c].T
            k_ref[pl.ds(c * HEAD, HEAD), :] = turned[:HEAD]
            v_ref[pl.ds(c * HEAD, HEAD), :] = turned[HEAD:]

    query, key, value, out, one, two = call(
        kernel,
        [
            shape((d_rows, width), f32),
            shape((KV_HEADS * HEAD, d_rows), f32),
            shape((KV_HEADS * HEAD, d_rows), f32),
            shape((d_rows, width), f32),
            shape((1, d_rows), f32),
            shape((1, d_rows), f32),
        ],
        [at, *slots],
        scratch=[pltpu.VMEM((TP, d_rows + 16, 3 * OWN), f32)],
        limit=12,
        cost=2.0,
    )
    return query, key.T, value.T, out, one, two


def body(
    tokens,
    pair_order,
    gain_attn,
    gain_mlp,
    w_query,
    w_key,
    w_value,
    w_out,
    w_gate,
    w_up,
    w_down,
    cotangent,
):
    local_rows, width = tokens.shape
    half_rows = local_rows // 2
    nz = lax.axis_size("fsdp")
    outer = lax.axis_size("ctx") // TP
    count = lax.axis_size(AXES)
    groups = outer * nz
    me = lax.axis_index(AXES)
    z = lax.axis_index("fsdp")
    tp = lax.axis_index("ctx") % TP
    kv_index = (4 * (tp // 2)) // GROUP + tp % 2
    at = jnp.stack([tp, z, kv_index]).astype(i32)
    send = functools.partial(exchange, count=count)
    group_mask = [(g // nz) * TP * nz + g % nz for g in range(groups)]

    def after(value, *others):
        return lax.optimization_barrier((value, *others))[0]

    def both(left, right):
        return jnp.concatenate([left, right], axis=0)

    def plane_gather(block):
        even = [block] + [send(block, j * nz) for j in range(2, TP, 2)]
        odd = [send(e, nz) for e in even]
        return [piece for pair in zip(even, odd) for piece in pair]

    def plane_scatter(keep, passed):
        first, *rest = add_crossed(keep, send(passed, nz), TP // 2)
        return [first] + [send(piece, 2 * (j + 1) * nz) for j, piece in enumerate(rest)]

    def from_z(block):
        return [block] + [send(block, s) for s in range(1, nz)]

    pack_one = slice_attention_weights(at, w_query, w_key, w_value, w_out, gain_attn, gain_mlp)
    token_slots = plane_gather(tokens)
    pack_one = from_z(pack_one)

    slot_of = jnp.array([[m | (j * nz) for j in range(TP)] for m in group_mask], dtype=i32)
    low = pair_order[me ^ slot_of]
    base = jnp.stack([low, 2 * count - 1 - low], axis=1) * half_rows
    query_base = base[0].reshape(2 * TP)
    partner = jnp.array([j ^ 1 for j in range(TP)], dtype=i32)
    key_base = jnp.stack([base, base[:, :, partner]]).reshape(2 * groups, 2 * TP)
    places = (query_base[:, None] + jnp.arange(half_rows, dtype=i32)[None, :]).reshape(-1)
    lane = jnp.arange(OWN)
    freqs = base_theta ** (-2.0 * (lane % (HEAD // 2)).astype(f32) / HEAD)
    angles = places.astype(f32)[:, None] * freqs[None, :]
    cosine = jnp.cos(angles)
    sine = jnp.sin(angles) * jnp.where(lane % HEAD < HEAD // 2, -1.0, 1.0)[None, :]
    select = jnp.where((2 * tp + jnp.arange(2)) // GROUP == kv_index, 0, 1).astype(i32)

    inputs, hidden_one, turned_query, kv, w_qkv, cot_own, w_out_own, gains = project(
        at, token_slots, pack_one, cosine, sine, cotangent
    )
    own_kv = [kv] + [send(kv, m) for m in group_mask[1:]]
    other_kv = [send(slot, nz) for slot in own_kv]
    pack_two = slice_ff_weights(after(at, kv), w_gate, w_up, w_down, nz)
    mask_x, mask_y = 2 * nz, 4 * nz
    cot_even = both(cot_own, send(cot_own, mask_x))
    w_out_even = both(w_out_own, send(w_out_own, mask_y))
    attended, attended_own, log_mass = attention_forward(
        after(select, cot_even, w_out_even),
        key_base,
        query_base,
        turned_query,
        own_kv,
        other_kv,
        half_rows,
    )
    cot_even = both(cot_even, send(cot_even, mask_y))
    w_out_even = both(w_out_even, send(w_out_even, mask_x))
    pack_two = after(pack_two, *own_kv)
    pack_near = both(pack_two, send(pack_two, 2))
    attended_own = after(attended_own, cot_even, w_out_even, pack_near)
    pack_far = send(pack_near, 1)
    side_odd = send(both(cot_even, w_out_even), nz)
    attended_slots = plane_gather(attended_own)

    (
        attended_low,
        w_out_all,
        resid,
        grad_keep,
        grad_pass,
        out_keep,
        out_pass,
        gain_sums,
        ff_keep,
        ff_send,
    ) = feed_forward(
        at,
        inputs,
        attended_slots,
        [cot_even, w_out_even, side_odd],
        [pack_near, pack_far],
        gains,
        nz,
    )
    sums = plane_scatter(grad_keep, grad_pass)
    ff_own, ff_send = first_sum(ff_keep, send(ff_send, 1))
    out_first, *out_rest = add_crossed(
        out_keep, send(after(out_pass, sums[0]), nz), TP // 2
    )
    grad_resid, trade_keep, trade_pass = branch_gradient(
        at, sums, resid, cotangent, w_out_all, gains
    )
    crossed = send(after(trade_pass, ff_own), nz)
    pairs = [
        send(pair, 2 * (j + 1) * nz)
        for j, pair in enumerate(pair_up(trade_keep, crossed, TP // 2))
    ]
    ff_arrived = send(ff_send, 2)
    out_sums = [out_first] + [
        send(after(piece, pairs[0]), 2 * (j + 1) * nz) for j, piece in enumerate(out_rest)
    ]

    grad_query, kv_keep, kv_pass, branch_columns = attention_backward(
        after(select, out_first),
        key_base,
        query_base,
        turned_query,
        own_kv,
        other_kv,
        [trade_keep, crossed, *pairs],
        attended,
        log_mass,
        half_rows,
    )
    kv_crossed = send(after(kv_pass, *out_sums), nz)
    ff_a, ff_b = last_sum(ff_own, ff_arrived)
    first, *rest = add_crossed(kv_keep, after(kv_crossed, ff_a), groups)
    grad_kv = [first] + [send(piece, m) for piece, m in zip(rest, group_mask[1:])]

    for step in range(outer.bit_length() - 1):
        far = TP * nz << step
        ff_a, ff_b = (
            (part.astype(f32) + send(part, far).astype(f32)).astype(bf16) for part in (ff_a, ff_b)
        )
    ff_a, ff_b = after(ff_a, rest[0]), after(ff_b, rest[0])
    layer_out = layer_output(out_sums, after(resid, rest[0]))
    ff_even_a = both(ff_a, send(ff_a, mask_x))
    ff_even_b = both(ff_b, send(ff_b, mask_y))
    ff_even_a = both(ff_even_a, send(ff_even_a, mask_y))
    ff_even_b = both(ff_even_b, send(ff_even_b, mask_x))
    grad_out = tn(attended_low[:, :width], after(branch_columns, rest[0]))

    last_keep, last_pass, last_own, *last_sends = projection_gradient(
        at,
        grad_query,
        [after(first, ff_even_a, ff_even_b), *grad_kv[1:]],
        inputs,
        hidden_one,
        w_qkv,
        gain_sums,
        cosine,
        sine,
        grad_out,
        nz,
    )
    ff_odd = send(both(ff_even_a, ff_even_b), nz)
    sums = plane_scatter(last_keep, last_pass)
    last_total = last_own
    for s, piece in enumerate(last_sends):
        last_total = last_total + send(piece, s + 1).astype(f32)
    for step in range(outer.bit_length() - 1):
        last_total = last_total + send(last_total.astype(bf16), TP * nz << step).astype(f32)
    last_slots = plane_gather(last_total.astype(bf16))
    grad_gate, grad_up, grad_down = ff_outputs(
        at, ff_even_a, ff_even_b, ff_odd, w_gate.shape[0], w_down.shape[0], nz
    )
    grad_w_query, grad_w_key, grad_w_value, grad_out, gain_one, gain_two = projection_outputs(
        at, last_slots, width
    )
    grad_tokens = token_gradient(sums, tokens, grad_resid, gains)
    return (
        layer_out,
        grad_tokens,
        gain_one.reshape(-1),
        gain_two.reshape(-1),
        grad_w_query,
        grad_w_key,
        grad_w_value,
        grad_out,
        grad_gate,
        grad_up,
        grad_down,
    )


def solution(mesh):
    return jax.shard_map(
        body,
        mesh=mesh,
        in_specs=(
            P(("ctx", "fsdp"), None),
            P(),
            P("fsdp"),
            P("fsdp"),
            P("fsdp", None),
            P("fsdp", None),
            P("fsdp", None),
            P("fsdp", None),
            P("fsdp", None),
            P("fsdp", None),
            P("fsdp", None),
            P(("ctx", "fsdp"), None),
        ),
        out_specs=(
            P(("ctx", "fsdp"), None),
            P(("ctx", "fsdp"), None),
            P("fsdp"),
            P("fsdp"),
            P("fsdp", None),
            P("fsdp", None),
            P("fsdp", None),
            P("fsdp", None),
            P("fsdp", None),
            P("fsdp", None),
            P("fsdp", None),
        ),
        check_vma=False,
    )
```

```python
import functools

import jax
import jax.numpy as jnp
from jax import lax
from jax.experimental import pallas as pl
from jax.experimental.pallas import tpu as pltpu
from jax.sharding import PartitionSpec as P

HEADS = 15
KV_HEADS = 5
HEAD = 64
TP = 8
GROUP = HEADS // KV_HEADS
OWN = 2 * HEAD
epsilon = 1e-05
base_theta = 100000.0
far_below = -1e30
f32 = jnp.float32
bf16 = jnp.bfloat16
i32 = jnp.int32
AXES = ("ctx", "fsdp")
MIB = 1024 * 1024
smem = pl.BlockSpec(memory_space=pltpu.SMEM)
vmem = pl.BlockSpec(memory_space=pltpu.VMEM)


def exchange(array, mask, count):
    return lax.ppermute(array, AXES, [(i, i ^ mask) for i in range(count)])


def nn(left, right):
    return lax.dot_general(left, right, (((1,), (0,)), ((), ())), preferred_element_type=f32)


def tn(left, right):
    return lax.dot_general(left, right, (((0,), (0,)), ((), ())), preferred_element_type=f32)


def nt(left, right):
    return lax.dot_general(left, right, (((1,), (1,)), ((), ())), preferred_element_type=f32)


def shape(dims, dtype):
    return jax.ShapeDtypeStruct(dims, dtype)


def call(kernel, outs, inputs, scalars=1, scratch=(), limit=56, cost=1.0, far=()):
    specs = [smem] * scalars + [vmem] * (len(inputs) - scalars)
    for i in far:
        specs[i] = pl.BlockSpec(memory_space=pltpu.HBM)
    return pl.pallas_call(
        kernel,
        out_shape=tuple(outs),
        in_specs=specs,
        out_specs=tuple(vmem for unused in outs),
        scratch_shapes=list(scratch),
        compiler_params=pltpu.CompilerParams(vmem_limit_bytes=limit * MIB),
        cost_estimate=pl.CostEstimate(
            flops=int(cost * 1e9), bytes_accessed=int(cost * 1e6), transcendentals=0
        ),
    )(*inputs)


def early_rows(rows):
    return rows // 4 // 16 * 16 + 16


def one_hot(rows, columns, start):
    row = lax.broadcasted_iota(i32, (rows, columns), 0)
    column = lax.broadcasted_iota(i32, (rows, columns), 1)
    return jnp.where(row == column + start, 1.0, 0.0).astype(bf16)


def query_positions(base_ref, at, width, half_rows):
    lane = lax.broadcasted_iota(i32, (1, width), 1)
    place = jnp.zeros((1, width), i32)
    for block in range(width // half_rows):
        start = base_ref[at + block] - block * half_rows
        place = jnp.where(lane >= block * half_rows, start + lane, place)
    return place


def key_positions(base_ref, row, at, count, half_rows, width):
    offset = lax.broadcasted_iota(i32, (half_rows, width), 0)
    return jnp.concatenate([offset + base_ref[row, at + b] for b in range(count)], axis=0)


def swap_halves(matrix):
    lane = lax.broadcasted_iota(i32, matrix.shape, 1)
    ahead = pltpu.roll(matrix, matrix.shape[1] - HEAD // 2, 1)
    behind = pltpu.roll(matrix, HEAD // 2, 1)
    return jnp.where(lane % HEAD < HEAD // 2, ahead, behind)


def norm_scale(matrix):
    return lax.rsqrt(jnp.mean(matrix * matrix, axis=1, keepdims=True) + epsilon)


def slice_attention_weights(at, w_query, w_key, w_value, w_out, gain_one, gain_two):
    d_rows, width = w_query.shape
    lanes = 2 * OWN + OWN
    rest = width - (TP - 1) * OWN

    def kernel(at_ref, q_ref, k_ref, v_ref, o_ref, g1_ref, g2_ref, out_ref, cols, heads, whole, sems):
        tp = at_ref[0]
        kv = at_ref[2]
        wides, narrows = (q_ref, o_ref), (k_ref, v_ref)

        @pl.when(tp < TP - 1)
        def most():
            columns = pl.ds(pl.multiple_of(tp * OWN, OWN), OWN)
            copies = [
                pltpu.make_async_copy(ref.at[:, columns], cols.at[i], sems.at[i])
                for i, ref in enumerate(wides)
            ]
            for copy in copies:
                copy.start()
            for copy in copies:
                copy.wait()

        @pl.when(tp == TP - 1)
        def last():
            copies = [
                pltpu.make_async_copy(ref, whole.at[i], sems.at[i]) for i, ref in enumerate(wides)
            ]
            for copy in copies:
                copy.start()
            for copy in copies:
                copy.wait()
            for i in range(2):
                cols[i] = jnp.zeros((d_rows, OWN), bf16)
                cols[i, :, pl.ds(0, rest)] = whole[i, :, pl.ds(width - rest, rest)]

        @pl.when(kv < KV_HEADS)
        def real():
            rows = pl.ds(pl.multiple_of(kv * HEAD, HEAD), HEAD)
            copies = [
                pltpu.make_async_copy(ref.at[rows, :], heads.at[i], sems.at[2 + i])
                for i, ref in enumerate(narrows)
            ]
            for copy in copies:
                copy.start()
            for copy in copies:
                copy.wait()

        @pl.when(kv >= KV_HEADS)
        def none():
            heads[...] = jnp.zeros_like(heads)

        out_ref[pl.ds(0, d_rows), pl.ds(0, OWN)] = cols[0]
        turned = jnp.concatenate([heads[0], heads[1]], axis=0).astype(f32).T
        out_ref[pl.ds(0, d_rows), pl.ds(OWN, OWN)] = turned.astype(bf16)
        out_ref[pl.ds(0, d_rows), pl.ds(2 * OWN, OWN)] = cols[1]
        out_ref[pl.ds(d_rows, 16), :] = jnp.zeros((16, lanes), bf16)
        out_ref[d_rows, pl.ds(0, d_rows)] = g1_ref[...]
        out_ref[d_rows + 1, pl.ds(0, d_rows)] = g2_ref[...]

    return call(
        kernel,
        [shape((d_rows + 16, lanes), bf16)],
        [at, w_query, w_key.T, w_value.T, w_out, gain_one, gain_two],
        scratch=[
            pltpu.VMEM((2, d_rows, OWN), bf16),
            pltpu.VMEM((2, HEAD, d_rows), bf16),
            pltpu.VMEM((2, d_rows, width), bf16),
            pltpu.SemaphoreType.DMA((4,)),
        ],
        limit=60,
        cost=2.0,
        far=(1, 2, 3, 4),
    )[0]


def slice_ff_weights(at, w_gate, w_up, w_down, nz):
    d_rows = w_gate.shape[0]
    ff_z, width = w_down.shape
    part = ff_z // TP
    own = part * nz

    upper = early_rows(d_rows)
    lower = d_rows - upper

    def kernel(at_ref, g_ref, u_ref, d_ref, out_ref, upper_ref, lower_ref):
        pick = one_hot(ff_z, part, at_ref[0] * part)
        for ref, start in ((g_ref, 0), (u_ref, own)):
            pieces = [nn(ref[:, pl.ds(s * ff_z, ff_z)], pick) for s in range(nz)]
            out_ref[:, pl.ds(start, own)] = jnp.concatenate(pieces, axis=1).astype(bf16)
        pieces = [nn(d_ref[pl.ds(s * d_rows, d_rows), :], pick) for s in range(nz)]
        out_ref[:, pl.ds(2 * own, own)] = jnp.concatenate(pieces, axis=1).astype(bf16)
        upper_ref[...] = out_ref[pl.ds(0, upper), :]
        lower_ref[...] = out_ref[pl.ds(upper, lower), :]

    return call(
        kernel,
        [shape((rows, 3 * own), bf16) for rows in (d_rows, upper, lower)],
        [at, w_gate, w_up, w_down.T],
        limit=16,
        cost=4.0,
    )


def project(at, tokens, packs, cosine, sine, cotangent):
    local, width = tokens[0].shape
    half_rows = local // 2
    rows = TP * local
    nz = len(packs)
    pack_rows, lanes = packs[0].shape
    d_rows = pack_rows - 16

    def kernel(at_ref, *refs):
        toks, refs = refs[:TP], refs[TP:]
        pack, refs = refs[:nz], refs[nz:]
        cos_ref, sin_ref, cot_ref, x_ref, hid_ref, qt_ref, kv_ref, w_ref, side_ref, gain_ref, hold = refs
        z = at_ref[1]
        for s in range(nz):
            hold[z ^ s] = pack[s][...]
        for s in range(nz):
            w_ref[pl.ds(s * d_rows, d_rows), :] = hold[s, pl.ds(0, d_rows), pl.ds(0, 2 * OWN)]
        gains = [hold[s, pl.ds(d_rows, 16), pl.ds(0, d_rows)].astype(f32) for s in range(nz)]
        gain_ref[...] = jnp.concatenate(gains, axis=1)[:8]
        gain = gain_ref[pl.ds(0, 1), :]
        side_ref[pl.ds(0, local), pl.ds(0, width)] = cot_ref[...]
        turned = [
            hold[s, pl.ds(0, d_rows), pl.ds(2 * OWN, OWN)].astype(f32) for s in range(nz)
        ]
        side_ref[pl.ds(local, OWN), pl.ds(0, width)] = jnp.concatenate(turned, axis=0).T.astype(bf16)
        per = 4
        for tile in range(2 * TP // per):
            side, first = (tile * per) // TP, (tile * per) % TP
            at_rows = pl.ds(tile * per * half_rows, per * half_rows)
            block = jnp.concatenate(
                [toks[first + j][pl.ds(side * half_rows, half_rows), :] for j in range(per)], axis=0
            )
            x_ref[at_rows, :] = block
            inputs = block.astype(f32)
            hidden = (inputs * norm_scale(inputs) * gain).astype(bf16)
            hid_ref[at_rows, :] = hidden
            out = nn(hidden, w_ref[...])
            cos, sin = cos_ref[at_rows, :], sin_ref[at_rows, :]
            query = out[:, :OWN]
            query = query * cos + swap_halves(query) * sin
            qt_ref[:, at_rows] = (query.astype(bf16).astype(f32) * HEAD**-0.5).T.astype(bf16)
            pair = out[:, OWN:]
            turned = pair * cos + swap_halves(pair) * sin
            lane = lax.broadcasted_iota(i32, pair.shape, 1)
            kv_ref[at_rows, :] = jnp.where(lane < HEAD, turned, pair).astype(bf16)

    return call(
        kernel,
        [
            shape((rows, width), bf16),
            shape((rows, width), bf16),
            shape((OWN, rows), bf16),
            shape((rows, OWN), bf16),
            shape((width, 2 * OWN), bf16),
            shape((local + OWN, TP * OWN), bf16),
            shape((8, width), f32),
        ],
        [at, *tokens, *packs, cosine, sine, cotangent],
        scratch=[pltpu.VMEM((nz, pack_rows, lanes), bf16)],
        limit=60,
        cost=6.0,
    )


def attention_forward(select, key_base, query_base, turned_query, own_kv, other_kv, half_rows):
    groups = len(own_kv)
    rows = own_kv[0].shape[0]
    half = rows // 2
    blocks = half // half_rows
    wide, deep = 128, 128

    def kernel(sel_ref, key_ref, query_ref, q_ref, *refs):
        own, other = refs[:groups], refs[groups : 2 * groups]
        out_ref, low_ref, lse_ref, kv_ref, kvt_ref, top_ref, mass_ref, place_ref = refs[2 * groups :]
        for head in range(2):
            chosen = sel_ref[head] == 0
            for group in range(groups):

                @pl.when(chosen)
                def take_own():
                    kv_ref[head, group] = own[group][...]
                    kvt_ref[head, group] = own[group][...].T

                @pl.when(jnp.logical_not(chosen))
                def take_other():
                    kv_ref[head, group] = other[group][...]
                    kvt_ref[head, group] = other[group][...].T

        top_ref[...] = jnp.full_like(top_ref, far_below)
        mass_ref[...] = jnp.zeros_like(mass_ref)
        out_ref[...] = jnp.zeros_like(out_ref)

        def one_group(group, unused):
            for head in range(2):
                row = sel_ref[head] * groups + group
                own_rows = pl.ds(head * HEAD, HEAD)
                stat = pl.ds(head, 1)
                place_ref[...] = key_positions(key_ref, row, 0, 2 * blocks, half_rows, 128)
                for k_start in range(0, rows, deep):
                    keys_at = pl.ds(k_start, deep)
                    k_side = k_start // half
                    block = kv_ref[head, group, keys_at, :]
                    values = kvt_ref[head, group, pl.ds(HEAD, HEAD), keys_at]
                    for start in range(k_side * half, rows, wide):
                        lanes = pl.ds(start, wide)
                        turned = q_ref[own_rows, lanes]
                        padded = jnp.concatenate([turned, jnp.zeros_like(turned)], axis=0)
                        scores = nn(block, padded)
                        if start // half == k_side:
                            places = query_positions(
                                query_ref, start // half_rows, wide, half_rows
                            )
                            scores = jnp.where(place_ref[keys_at, :] <= places, scores, far_below)
                        before = top_ref[stat, lanes]
                        top = jnp.maximum(before, jnp.max(scores, axis=0, keepdims=True))
                        weights = jnp.exp(scores - top)
                        fade = jnp.exp(before - top)
                        top_ref[stat, lanes] = top
                        mass_ref[stat, lanes] = mass_ref[stat, lanes] * fade + jnp.sum(
                            weights, axis=0, keepdims=True
                        )
                        out_ref[own_rows, lanes] = out_ref[own_rows, lanes] * fade + nn(
                            values, weights.astype(bf16)
                        )
            return unused

        lax.fori_loop(0, groups, one_group, 0)
        for head in range(2):
            own_rows = pl.ds(head * HEAD, HEAD)
            mass = mass_ref[pl.ds(head, 1), :]
            out_ref[own_rows, :] = out_ref[own_rows, :] / mass
            lse_ref[pl.ds(head, 1), :] = top_ref[pl.ds(head, 1), :] + jnp.log(mass)
        low_ref[...] = out_ref[...].T.astype(bf16)

    return call(
        kernel,
        [shape((OWN, rows), f32), shape((rows, OWN), bf16), shape((2, rows), f32)],
        [select, key_base, query_base, turned_query, *own_kv, *other_kv],
        scalars=3,
        scratch=[
            pltpu.VMEM((2, groups, rows, OWN), bf16),
            pltpu.VMEM((2, groups, OWN, rows), bf16),
            pltpu.VMEM((2, rows), f32),
            pltpu.VMEM((2, rows), f32),
            pltpu.VMEM((rows, 128), i32),
        ],
        limit=24,
        cost=14.0,
    )


def attention_backward(
    select, key_base, query_base, turned_query, own_kv, other_kv, traded, attended, log_mass, half_rows
):
    groups = len(own_kv)
    rows = own_kv[0].shape[0]
    half = rows // 2
    blocks = half // half_rows
    wide, deep = 512, 256

    def kernel(sel_ref, key_ref, query_ref, q_ref, *refs):
        own, other = refs[:groups], refs[groups : 2 * groups]
        refs = refs[2 * groups :]
        local = 2 * half_rows
        parts = [refs[0], refs[1]] + [
            refs[2 + j].at[pl.ds(k * local, local), :] for j in range(TP // 2 - 1) for k in range(2)
        ]
        refs = refs[1 + TP // 2 :]
        att_ref, lse_ref, dq_ref, keep_ref, pass_ref, gb_ref = refs[:6]
        kv_ref, sum_ref, g_ref, rq_ref, rg_ref, delta_ref, pos_ref = refs[6:]
        for group in range(groups):
            kv_ref[0, group] = own[group][...]
            kv_ref[1, group] = other[group][...]
        sum_ref[...] = jnp.zeros_like(sum_ref)
        dq_ref[...] = jnp.zeros_like(dq_ref)
        zeros = jnp.zeros((rows, HEAD), bf16)
        for j in range(0, TP, 2):
            for side in range(2):
                at = pl.ds(side * half + j * half_rows, 2 * half_rows)
                pair = jnp.concatenate(
                    [parts[j + k][pl.ds(side * half_rows, half_rows), :] for k in range(2)], axis=0
                )
                g_ref[:, at] = pair[:, :OWN].T
                gb_ref[at, :] = pair[:, OWN:]
        for head in range(2):
            own_rows = pl.ds(head * HEAD, HEAD)
            rq_ref[head] = jnp.concatenate([q_ref[own_rows, :].T, zeros], axis=1)
            grad = g_ref[own_rows, :]
            rg_ref[head] = jnp.concatenate([zeros, grad.T], axis=1)
            delta_ref[pl.ds(head, 1), :] = jnp.sum(
                grad.astype(f32) * att_ref[own_rows, :], axis=0, keepdims=True
            )

        def one_group(group, unused):
            for head in range(2):
                which = sel_ref[head]
                own_rows = pl.ds(head * HEAD, HEAD)
                stat = pl.ds(head, 1)
                pos_ref[...] = key_positions(
                    key_ref, which * groups + group, 0, 2 * blocks, half_rows, 128
                )
                for k_start in range(0, rows, deep):
                    keys_at = pl.ds(k_start, deep)
                    k_side = k_start // half
                    block = kv_ref[which, group, keys_at, :]
                    turned_keys = block.T[:HEAD]
                    for start in range(k_side * half, rows, wide):
                        lanes = pl.ds(start, wide)
                        turned = q_ref[own_rows, lanes]
                        padded = jnp.concatenate([turned, jnp.zeros_like(turned)], axis=0)
                        scores = nn(block, padded)
                        if start // half == k_side:
                            places = query_positions(
                                query_ref, start // half_rows, wide, half_rows
                            )
                            at = jnp.concatenate([pos_ref[keys_at, :]] * (wide // 128), axis=1)
                            scores = jnp.where(at <= places, scores, far_below)
                        probs = jnp.exp(scores - lse_ref[stat, lanes])
                        grads = g_ref[own_rows, lanes]
                        padded = jnp.concatenate([jnp.zeros_like(grads), grads], axis=0)
                        grad_probs = nn(block, padded)
                        grad_scores = probs * (grad_probs - delta_ref[stat, lanes])
                        probs = probs.astype(bf16)
                        grad_scores = grad_scores.astype(bf16)
                        sum_ref[which, group, keys_at, :] += nn(
                            grad_scores, rq_ref[head, lanes, :]
                        ) + nn(probs, rg_ref[head, lanes, :])
                        dq_ref[own_rows, lanes] += nn(turned_keys, grad_scores)
            return unused

        lax.fori_loop(0, groups, one_group, 0)
        for group in range(groups):
            keep_ref[pl.ds(group * rows, rows), :] = sum_ref[0, group]
            pass_ref[pl.ds(group * rows, rows), :] = sum_ref[1, group].astype(bf16)

    return call(
        kernel,
        [
            shape((OWN, rows), f32),
            shape((groups * rows, OWN), f32),
            shape((groups * rows, OWN), bf16),
            shape((rows, OWN), bf16),
        ],
        [
            select,
            key_base,
            query_base,
            turned_query,
            *own_kv,
            *other_kv,
            *traded,
            attended,
            log_mass,
        ],
        scalars=3,
        scratch=[
            pltpu.VMEM((2, groups, rows, OWN), bf16),
            pltpu.VMEM((2, groups, rows, OWN), f32),
            pltpu.VMEM((OWN, rows), bf16),
            pltpu.VMEM((2, rows, OWN), bf16),
            pltpu.VMEM((2, rows, OWN), bf16),
            pltpu.VMEM((2, rows), f32),
            pltpu.VMEM((rows, 128), i32),
        ],
        limit=28,
        cost=18.0,
    )


def store_blocks(part, tile, per, half_rows, keep_ref, pass_ref):
    side = (tile * per) // TP
    first = lax.rem(tile * per, TP) // 2
    for j in range(per):
        piece = part[j * half_rows : (j + 1) * half_rows]
        row = (2 * (first + j // 2) + side) * half_rows
        at = pl.ds(pl.multiple_of(row, half_rows), half_rows)
        target = keep_ref if j % 2 == 0 else pass_ref
        target[at, pl.ds(0, piece.shape[1])] = piece.astype(target.dtype)


def feed_forward(at, inputs, attended, sides, packs, gains, nz):
    rows, width = inputs.shape
    local = rows // TP
    half_rows = local // 2
    half = rows // 2
    d_rows, lanes = packs[0].shape
    upper, lower = packs[2].shape[0], packs[3].shape[0]
    ff = lanes // 3
    part_rows = ff // nz
    per = 4
    tile_rows = per * half_rows

    def kernel(at_ref, x_ref, *refs):
        att, refs = refs[:TP], refs[TP:]
        mine, by_x, by_y, by_xy, odd, last_odd = refs[:6]
        own_pack, one_pack, near_a, near_b, far_a, far_b = refs[6:12]
        refs = refs[12:]
        cot_at = pl.ds(0, local)
        wo_at = pl.ds(local, OWN)
        gain_ref, refs = refs[0], refs[1:]
        att_out, wo_out, resid_out, gk_ref, gp_ref, lk_ref, lp_ref, gain_out = refs[:8]
        targets, refs = refs[8:12], refs[12:]
        gu_w, dn_w, cot_ref, acc_gu, acc_dn, hold, blocks = refs
        tp = at_ref[0]
        z = at_ref[1]
        for j in range(TP):
            columns = pl.ds(pl.multiple_of((tp ^ j) * OWN, OWN), OWN)
            even = (mine, by_x, by_y, by_xy)[j // 2]
            from_cot, from_wo = even.at[cot_at, :], even.at[wo_at, :]
            if j % 2:
                source, start = (odd, (local + OWN) * (j // 2)) if j < TP - 1 else (last_odd, 0)
                from_cot = source.at[pl.ds(start, local), :]
                from_wo = source.at[pl.ds(start + local, OWN), :]
            wo_out[columns, :] = from_wo[:, pl.ds(0, width)]
            for side in range(2):
                for k in range(TP):
                    att_out[pl.ds(side * half + k * half_rows, half_rows), columns] = att[j][
                        pl.ds(side * half + (k ^ j) * half_rows, half_rows), :
                    ]
                cot_ref[pl.ds(side * half + j * half_rows, half_rows), :] = from_cot[
                    pl.ds(side * half_rows, half_rows), pl.ds(0, width)
                ]
        hold[z] = own_pack[...]
        hold[z ^ 1] = one_pack[...]
        for s, first, second in ((2, near_a, near_b), (3, far_a, far_b)):
            hold[z ^ s, pl.ds(0, upper), :] = first[...]
            hold[z ^ s, pl.ds(upper, lower), :] = second[...]
        for s in range(nz):
            rows_at = pl.ds(s * d_rows, d_rows)
            gu_w[rows_at, :] = hold[s, :, pl.ds(0, 2 * ff)]
            dn_w[rows_at, :] = jnp.concatenate(
                [
                    hold[b][:, 2 * ff + s * part_rows : 2 * ff + (s + 1) * part_rows]
                    for b in range(nz)
                ],
                axis=1,
            )
        gain = gain_ref[pl.ds(1, 1), :]
        gain_out[...] = jnp.zeros_like(gain_out)
        acc_gu[...] = jnp.zeros_like(acc_gu)
        acc_dn[...] = jnp.zeros_like(acc_dn)

        def one_tile(tile, unused):
            at_rows = pl.ds(pl.multiple_of(tile * tile_rows, tile_rows), tile_rows)
            branch = nt(att_out[at_rows, :][:, :width], wo_out[pl.ds(0, width), :])
            resid = x_ref[at_rows, :].astype(f32) + branch
            side = (tile * per) // TP

            @pl.when(lax.rem(tile * per, TP) == 0)
            def keep_own():
                resid_out[pl.ds(pl.multiple_of(side * half_rows, half_rows), half_rows), :] = resid[
                    :half_rows
                ]

            normal = resid * norm_scale(resid)
            hidden = (normal * gain).astype(bf16)
            gate_up = nn(hidden, gu_w[...])
            gate, up = gate_up[:, :ff], gate_up[:, ff:]
            sigmoid = 1.0 / (1.0 + jnp.exp(-gate))
            activated = gate * sigmoid
            product = (activated * up).astype(bf16)
            cotangent = cot_ref[at_rows, :]
            grad_product = nn(cotangent, dn_w[...])
            grad_gate = grad_product * up * sigmoid * (1.0 + gate * (1.0 - sigmoid))
            grad_gu = jnp.concatenate([grad_gate, grad_product * activated], axis=1).astype(bf16)
            partial = nt(grad_gu, gu_w[...])
            gain_out[pl.ds(0, 1), :] += jnp.sum(partial * normal, axis=0, keepdims=True)
            store_blocks(partial, tile, per, half_rows, gk_ref, gp_ref)
            store_blocks(nt(product, dn_w[...]), tile, per, half_rows, lk_ref, lp_ref)
            acc_gu[...] += tn(hidden, grad_gu)
            acc_dn[...] += tn(cotangent, product)
            return unused

        lax.fori_loop(0, 2 * TP // per, one_tile, 0)
        for b in range(nz):
            blocks[b, :, pl.ds(0, 2 * ff)] = acc_gu[pl.ds(b * d_rows, d_rows), :]
            blocks[b, :, pl.ds(2 * ff, ff)] = jnp.concatenate(
                [
                    acc_dn[pl.ds(s * d_rows, d_rows), :][:, b * part_rows : (b + 1) * part_rows]
                    for s in range(nz)
                ],
                axis=1,
            )
        for s in range(nz):
            targets[s][...] = blocks[z ^ s].astype(targets[s].dtype)

    keep = shape((TP // 2 * local, width), bf16)
    passed = shape((TP // 2 * local, TP * OWN), bf16)
    return call(
        kernel,
        [
            shape((rows, TP * OWN), bf16),
            shape((TP * OWN, width), bf16),
            shape((local, width), f32),
            keep,
            passed,
            keep,
            passed,
            shape((8, width), f32),
            shape((d_rows, lanes), f32),
            shape((d_rows, lanes), bf16),
            shape((d_rows, lanes), f32),
            shape((d_rows, lanes), bf16),
        ],
        [at, inputs, *attended, *sides, *packs, gains],
        scratch=[
            pltpu.VMEM((width, 2 * ff), bf16),
            pltpu.VMEM((width, ff), bf16),
            pltpu.VMEM((rows, width), bf16),
            pltpu.VMEM((width, 2 * ff), f32),
            pltpu.VMEM((width, ff), f32),
            pltpu.VMEM((nz, d_rows, lanes), bf16),
            pltpu.VMEM((nz, d_rows, lanes), f32),
        ],
        limit=44,
        cost=18.0,
    )


def add_crossed(keep, crossed, count):
    local, width = keep.shape[0] // count, keep.shape[1]

    def kernel(keep_ref, cross_ref, own_ref, *sends):
        for j in range(count):
            at = pl.ds(j * local, local)
            target = own_ref if j == 0 else sends[j - 1]
            target[...] = (
                keep_ref[at, :].astype(f32) + cross_ref[at, pl.ds(0, width)].astype(f32)
            ).astype(target.dtype)

    return call(
        kernel,
        [shape((local, width), f32)] + [shape((local, width), bf16)] * (count - 1),
        [keep, crossed],
        scalars=0,
        limit=12,
        cost=1.0,
    )


def branch_gradient(at, sums, resid, cotangent, w_out, gains):
    local, width = resid.shape

    def kernel(at_ref, *refs):
        parts, refs = refs[: len(sums)], refs[len(sums) :]
        resid_ref, cot_ref, wo_ref, gain_ref, grad_ref, keep_ref, pass_ref, ga_ref, gb_ref = refs
        tp = at_ref[0]
        grad_hidden = parts[0][...]
        for part in parts[1:]:
            grad_hidden = grad_hidden + part[...].astype(f32)
        resid = resid_ref[...]
        scale = norm_scale(resid)
        normal = resid * scale
        grad = grad_hidden * gain_ref[pl.ds(1, 1), :]
        grad = scale * (grad - normal * jnp.mean(grad * normal, axis=1, keepdims=True))
        grad = grad + cot_ref[...].astype(f32)
        grad_ref[...] = grad
        low = grad.astype(bf16)
        gb_ref[...] = jnp.zeros_like(gb_ref)
        gb_ref[:, pl.ds(0, width)] = low
        ga_ref[...] = jnp.zeros_like(ga_ref)
        ga_ref[:, pl.ds(0, width)] = nn(low, wo_ref[pl.ds(0, width), :]).astype(bf16)
        for j in range(TP):
            columns = pl.ds(pl.multiple_of((tp ^ j) * OWN, OWN), OWN)
            target = keep_ref if j % 2 == 0 else pass_ref
            rows = pl.ds((j // 2) * local, local)
            target[rows, pl.ds(0, OWN)] = ga_ref[:, columns]
            target[rows, pl.ds(OWN, OWN)] = gb_ref[:, columns]

    blocks = shape((TP // 2 * local, 2 * OWN), bf16)
    return call(
        kernel,
        [shape((local, width), f32), blocks, blocks],
        [at, *sums, resid, cotangent, w_out, gains],
        scratch=[pltpu.VMEM((local, TP * OWN), bf16), pltpu.VMEM((local, TP * OWN), bf16)],
        limit=16,
        cost=3.0,
    )


def pair_up(keep, crossed, count):
    local, width = keep.shape[0] // count, keep.shape[1]

    def kernel(keep_ref, cross_ref, *outs):
        for j in range(1, count):
            at = pl.ds(j * local, local)
            outs[j - 1][pl.ds(0, local), :] = keep_ref[at, :]
            outs[j - 1][pl.ds(local, local), :] = cross_ref[at, :]

    return call(
        kernel,
        [shape((2 * local, width), bf16)] * (count - 1),
        [keep, crossed],
        scalars=0,
        limit=8,
        cost=0.7,
    )


def projection_gradient(
    at, grad_query, grad_kv, inputs, hidden, w_qkv, gain_sums, cosine, sine, grad_out, nz
):
    rows, width = inputs.shape
    local = rows // TP
    half_rows = local // 2
    d_rows = width // nz
    per = 4
    tile_rows = per * half_rows
    pieces = len(grad_kv)

    def kernel(at_ref, dq_ref, *refs):
        kvs, refs = refs[:pieces], refs[pieces:]
        x_ref, hid_ref, w_ref, gain_two_ref, cos_ref, sin_ref, wo_ref = refs[:7]
        keep_ref, pass_ref, own_ref = refs[7:10]
        sends, refs = refs[10 : 10 + nz - 1], refs[10 + nz - 1 :]
        turn_ref, acc_ref, gain_acc, hold = refs
        z = at_ref[1]
        turn_ref[...] = dq_ref[...].T * HEAD**-0.5
        acc_ref[...] = jnp.zeros_like(acc_ref)
        gain_acc[...] = jnp.zeros_like(gain_acc)

        def one_tile(tile, unused):
            at_rows = pl.ds(pl.multiple_of(tile * tile_rows, tile_rows), tile_rows)
            cos, sin = cos_ref[at_rows, :], sin_ref[at_rows, :]
            query = turn_ref[at_rows, :]
            query = query * cos - swap_halves(query) * sin
            pair = kvs[0][at_rows, :].astype(f32)
            for piece in kvs[1:]:
                pair = pair + piece[at_rows, :].astype(f32)
            turned = pair * cos - swap_halves(pair) * sin
            lane = lax.broadcasted_iota(i32, pair.shape, 1)
            pair = jnp.where(lane < HEAD, turned, pair)
            grad = jnp.concatenate([query, pair], axis=1).astype(bf16)
            partial = nt(grad, w_ref[...])
            x = x_ref[at_rows, :].astype(f32)
            gain_acc[pl.ds(0, 1), :] += jnp.sum(partial * (x * norm_scale(x)), axis=0, keepdims=True)
            store_blocks(partial, tile, per, half_rows, keep_ref, pass_ref)
            acc_ref[...] += tn(hid_ref[at_rows, :], grad)
            return unused

        lax.fori_loop(0, 2 * TP // per, one_tile, 0)
        hold[...] = jnp.zeros_like(hold)
        for s in range(nz):
            columns = slice(s * d_rows, (s + 1) * d_rows)
            hold[s, pl.ds(0, 1), pl.ds(0, d_rows)] = gain_acc[pl.ds(0, 1), :][:, columns]
            hold[s, pl.ds(1, 1), pl.ds(0, d_rows)] = gain_two_ref[pl.ds(0, 1), :][:, columns]
        for s in range(nz):
            block = z ^ s
            target = own_ref if s == 0 else sends[s - 1]
            rows_at = pl.ds(pl.multiple_of(block * d_rows, 8), d_rows)
            part = pl.ds(0, d_rows)
            target[part, pl.ds(0, 2 * OWN)] = acc_ref[rows_at, :].astype(target.dtype)
            target[part, pl.ds(2 * OWN, OWN)] = wo_ref[rows_at, :].astype(target.dtype)
            target[pl.ds(d_rows, 16), :] = hold[block].astype(target.dtype)

    return call(
        kernel,
        [
            shape((TP // 2 * local, width), bf16),
            shape((TP // 2 * local, TP * OWN), bf16),
            shape((d_rows + 16, 3 * OWN), f32),
        ]
        + [shape((d_rows + 16, 3 * OWN), bf16)] * (nz - 1),
        [at, grad_query, *grad_kv, inputs, hidden, w_qkv, gain_sums, cosine, sine, grad_out],
        scratch=[
            pltpu.VMEM((rows, OWN), f32),
            pltpu.VMEM((width, 2 * OWN), f32),
            pltpu.VMEM((8, width), f32),
            pltpu.VMEM((nz, 16, 3 * OWN), f32),
        ],
        limit=32,
        cost=8.0,
    )


def token_gradient(sums, tokens, grad_resid, gains):
    local, width = tokens.shape

    def kernel(*refs):
        parts, refs = refs[: len(sums)], refs[len(sums) :]
        x_ref, grad_ref, gain_ref, out_ref = refs
        grad_hidden = parts[0][...]
        for part in parts[1:]:
            grad_hidden = grad_hidden + part[...].astype(f32)
        x = x_ref[...].astype(f32)
        scale = norm_scale(x)
        normal = x * scale
        grad = grad_hidden * gain_ref[pl.ds(0, 1), :]
        grad = scale * (grad - normal * jnp.mean(grad * normal, axis=1, keepdims=True))
        out_ref[...] = (grad + grad_ref[...]).T

    return call(
        kernel,
        [shape((width, local), f32)],
        [*sums, tokens, grad_resid, gains],
        scalars=0,
        limit=8,
        cost=1.0,
    )[0].T


def layer_output(sums, resid):
    def kernel(*refs):
        parts, (resid_ref, out_ref) = refs[: len(sums)], refs[len(sums) :]
        total = resid_ref[...]
        for part in parts:
            total = total + part[...].astype(f32)
        out_ref[...] = total.T.astype(bf16)

    turned = shape(resid.shape[::-1], bf16)
    return call(kernel, [turned], [*sums, resid], scalars=0, limit=8, cost=1.0)[0].T


def first_sum(own, arrived):
    def kernel(own_ref, in_ref, out_ref):
        out_ref[...] = (own_ref[...] + in_ref[...].astype(f32)).astype(bf16)

    return call(
        kernel, [shape(own.shape, bf16)], [own, arrived], scalars=0, limit=8, cost=1.0
    )[0]


def last_sum(own, *arrived):
    rows, lanes = own.shape

    def kernel(own_ref, *refs):
        total = own_ref[...]
        for ref in refs[:-1]:
            total = total + ref[...].astype(f32)
        refs[-1][:, pl.ds(0, lanes)] = total.astype(bf16)

    return call(
        kernel, [shape((rows, TP * OWN), bf16)], [own, *arrived], scalars=0, limit=8, cost=1.0
    )[0]


def ff_outputs(at, mine, by_x, by_y, by_xy, odd, ff_z, nz):
    d_rows = mine.shape[0]
    part = ff_z // TP
    ff = part * nz

    def kernel(at_ref, m_ref, x_ref, y_ref, xy_ref, odd_ref, gate_ref, up_ref, down_ref, hold):
        tp = at_ref[0]
        lanes = pl.ds(0, 3 * ff)
        for j, ref in enumerate((m_ref, x_ref, y_ref, xy_ref)):
            hold[tp ^ (2 * j)] = ref[:, lanes]
        for j in range(TP // 2):
            hold[tp ^ (2 * j + 1)] = odd_ref[pl.ds(d_rows * j, d_rows), lanes]
        for s in range(nz):
            for start in (s * part, ff + s * part, 2 * ff + s * part):
                block = jnp.concatenate(
                    [hold[c][:, start : start + part] for c in range(TP)], axis=1
                ).astype(f32)
                if start < ff:
                    gate_ref[:, pl.ds(s * ff_z, ff_z)] = block
                elif start < 2 * ff:
                    up_ref[:, pl.ds(s * ff_z, ff_z)] = block
                else:
                    down_ref[pl.ds(s * d_rows, d_rows), :] = block

    gate, up, down = call(
        kernel,
        [
            shape((d_rows, nz * ff_z), f32),
            shape((d_rows, nz * ff_z), f32),
            shape((nz * d_rows, ff_z), f32),
        ],
        [at, mine, by_x, by_y, by_xy, odd],
        scratch=[pltpu.VMEM((TP, d_rows, 3 * ff), bf16)],
        limit=32,
        cost=7.0,
    )
    return gate, up, down.T


def projection_outputs(at, slots, width):
    d_rows = slots[0].shape[0] - 16

    def kernel(at_ref, *refs):
        parts, (q_ref, k_ref, v_ref, o_ref, one_ref, two_ref, hold) = refs[:TP], refs[TP:]
        tp = at_ref[0]
        total = jnp.zeros((16, 3 * OWN), f32)
        for j in range(TP):
            hold[tp ^ j] = parts[j][...].astype(f32)
            total = total + parts[j][pl.ds(d_rows, 16), :].astype(f32)
        one_ref[...] = total[0:1, :d_rows]
        two_ref[...] = total[1:2, :d_rows]
        heads = [hold[c][:d_rows, :OWN] for c in range(TP)]
        q_ref[...] = jnp.concatenate(heads, axis=1)[:, :width]
        heads = [hold[c][:d_rows, 2 * OWN :] for c in range(TP)]
        o_ref[...] = jnp.concatenate(heads, axis=1)[:, :width]
        kv = [hold[c][:d_rows, OWN : 2 * OWN] for c in range(TP)]
        kv = [kv[0], kv[1] + kv[2], kv[3] + kv[4], kv[5], kv[6]]
        for c in range(KV_HEADS):
            turned = kv[c].T
            k_ref[pl.ds(c * HEAD, HEAD), :] = turned[:HEAD]
            v_ref[pl.ds(c * HEAD, HEAD), :] = turned[HEAD:]

    query, key, value, out, one, two = call(
        kernel,
        [
            shape((d_rows, width), f32),
            shape((KV_HEADS * HEAD, d_rows), f32),
            shape((KV_HEADS * HEAD, d_rows), f32),
            shape((d_rows, width), f32),
            shape((1, d_rows), f32),
            shape((1, d_rows), f32),
        ],
        [at, *slots],
        scratch=[pltpu.VMEM((TP, d_rows + 16, 3 * OWN), f32)],
        limit=12,
        cost=2.0,
    )
    return query, key.T, value.T, out, one, two


def body(
    tokens,
    pair_order,
    gain_attn,
    gain_mlp,
    w_query,
    w_key,
    w_value,
    w_out,
    w_gate,
    w_up,
    w_down,
    cotangent,
):
    local_rows, width = tokens.shape
    half_rows = local_rows // 2
    nz = lax.axis_size("fsdp")
    outer = lax.axis_size("ctx") // TP
    count = lax.axis_size(AXES)
    groups = outer * nz
    me = lax.axis_index(AXES)
    z = lax.axis_index("fsdp")
    tp = lax.axis_index("ctx") % TP
    kv_index = (4 * (tp // 2)) // GROUP + tp % 2
    at = jnp.stack([tp, z, kv_index]).astype(i32)
    send = functools.partial(exchange, count=count)
    group_mask = [(g // nz) * TP * nz + g % nz for g in range(groups)]

    def after(value, *others):
        return lax.optimization_barrier((value, *others))[0]

    def level(*arrays):
        return list(lax.optimization_barrier(arrays))

    def gather_even(block):
        return [block] + [send(block, j * nz) for j in range(2, TP, 2)]

    def gather_odd(even):
        return [piece for e in even for piece in (e, send(e, nz))]

    def scatter_far(pieces):
        return [send(piece, 2 * (j + 1) * nz) for j, piece in enumerate(pieces)]

    def from_z(block):
        return [block] + [send(block, s) for s in range(1, nz)]

    pack_one = slice_attention_weights(at, w_query, w_key, w_value, w_out, gain_attn, gain_mlp)
    token_slots = gather_odd(level(*gather_even(tokens)))
    pack_two = slice_ff_weights(after(at, pack_one), w_gate, w_up, w_down, nz)
    pack_one = from_z(pack_one)

    slot_of = jnp.array([[m | (j * nz) for j in range(TP)] for m in group_mask], dtype=i32)
    low = pair_order[me ^ slot_of]
    base = jnp.stack([low, 2 * count - 1 - low], axis=1) * half_rows
    query_base = base[0].reshape(2 * TP)
    partner = jnp.array([j ^ 1 for j in range(TP)], dtype=i32)
    key_base = jnp.stack([base, base[:, :, partner]]).reshape(2 * groups, 2 * TP)
    places = (query_base[:, None] + jnp.arange(half_rows, dtype=i32)[None, :]).reshape(-1)
    lane = jnp.arange(OWN)
    freqs = base_theta ** (-2.0 * (lane % (HEAD // 2)).astype(f32) / HEAD)
    angles = places.astype(f32)[:, None] * freqs[None, :]
    cosine = jnp.cos(angles)
    sine = jnp.sin(angles) * jnp.where(lane % HEAD < HEAD // 2, -1.0, 1.0)[None, :]
    select = jnp.where((2 * tp + jnp.arange(2)) // GROUP == kv_index, 0, 1).astype(i32)

    mask_x, mask_y = 2 * nz, 4 * nz
    pack_two, pack_a, pack_b = pack_two
    near_a = send(after(pack_a, *pack_one), 2)
    inputs, hidden_one, turned_query, kv, w_qkv, side, gains = project(
        after(at, pack_two), token_slots, pack_one, cosine, sine, cotangent
    )
    kv, side, near_a = level(kv, side, near_a)
    own_kv = [kv] + [send(kv, m) for m in group_mask[1:]]
    side_x, side_y = send(side, mask_x), send(side, mask_y)
    side_x, side_y, *own_kv = level(side_x, side_y, *own_kv)
    other_kv = level(*[send(slot, nz) for slot in own_kv])
    one, near_b = send(after(pack_two, *own_kv), 1), send(after(pack_b, *own_kv), 2)
    side_xy = send(side_x, mask_y)
    side_odd = send(jnp.concatenate([side, side_x, side_y], axis=0), nz)
    attended, attended_own, log_mass = attention_forward(
        select, key_base, query_base, turned_query, own_kv, other_kv, half_rows
    )
    attended_own, near_b, one, side_xy, side_odd = level(
        attended_own, near_b, one, side_xy, side_odd
    )
    far_a, far_b, side_xy, *even = level(
        send(after(near_a, attended_own), 1), send(near_b, 1), side_xy, *gather_even(attended_own)
    )
    attended_slots = gather_odd(even)
    packs = [pack_two, one, near_a, near_b, far_a, far_b]
    sides = [side, side_x, side_y, side_xy, side_odd, send(side_xy, nz)]

    (
        attended_low,
        w_out_all,
        resid,
        grad_keep,
        grad_pass,
        out_keep,
        out_pass,
        gain_sums,
        ff_own,
        ff_one,
        ff_two,
        ff_three,
    ) = feed_forward(
        at,
        inputs,
        attended_slots,
        sides,
        packs,
        gains,
        nz,
    )
    first, *rest = add_crossed(grad_keep, send(grad_pass, nz), TP // 2)
    ff_three, first, *rest = level(send(after(ff_three, first), 1), first, *scatter_far(rest))
    grad_resid, trade_keep, trade_pass = branch_gradient(
        at, [first, *rest], resid, cotangent, w_out_all, gains
    )
    crossed, out_crossed = level(send(trade_pass, nz), send(after(out_pass, first), nz))
    ff_one, *pairs = level(
        send(after(ff_one, crossed), 1),
        *scatter_far(pair_up(trade_keep, crossed, TP // 2)),
    )
    out_first, *out_rest = add_crossed(out_keep, out_crossed, TP // 2)
    ff_two = send(after(first_sum(ff_two, ff_three), *pairs), 2)
    out_rest = scatter_far([after(piece, *pairs) for piece in out_rest])

    grad_query, kv_keep, kv_pass, branch_columns = attention_backward(
        after(select, out_first),
        key_base,
        query_base,
        turned_query,
        own_kv,
        other_kv,
        [trade_keep, crossed, *pairs],
        attended,
        log_mass,
        half_rows,
    )
    kv_pass, ff_two, *out_rest = level(kv_pass, ff_two, *out_rest)
    kv_crossed = send(kv_pass, nz)
    first, *rest = add_crossed(kv_keep, kv_crossed, groups)
    ff_total = last_sum(after(ff_own, rest[0]), ff_one, ff_two)

    for step in range(outer.bit_length() - 1):
        crossing = send(ff_total, TP * nz << step).astype(f32)
        ff_total = (ff_total.astype(f32) + crossing).astype(bf16)
    layer_out = layer_output([after(out_first, rest[0]), *out_rest], resid)
    ff_x, ff_y, *grad_kv = level(
        send(ff_total, mask_x),
        send(ff_total, mask_y),
        *[send(piece, m) for piece, m in zip(rest, group_mask[1:])],
    )
    grad_out = tn(attended_low[:, :width], after(branch_columns, rest[0]))

    last_keep, last_pass, last_own, *last_sends = projection_gradient(
        at,
        grad_query,
        [first, *grad_kv],
        inputs,
        hidden_one,
        w_qkv,
        gain_sums,
        cosine,
        sine,
        grad_out,
        nz,
    )
    near, far = add_crossed(last_keep, send(last_pass, nz), 2)
    ff_xy, far, *arrived = level(
        send(after(ff_x, last_own), mask_y),
        send(far, mask_y),
        *[send(piece, s + 1) for s, piece in enumerate(last_sends)],
    )
    near, far = add_crossed(near, far, 2)
    last_total = last_own
    for piece in arrived:
        last_total = last_total + piece.astype(f32)
    for step in range(outer.bit_length() - 1):
        last_total = last_total + send(last_total.astype(bf16), TP * nz << step).astype(f32)
    last_total = last_total.astype(bf16)
    ff_slots = [ff_total, ff_x, ff_y, ff_xy]
    ff_slots.append(send(jnp.concatenate(ff_slots, axis=0), nz))
    grad_gate, grad_up, grad_down = ff_outputs(at, *ff_slots, w_down.shape[0], nz)
    far, grad_gate, *even = level(send(far, mask_x), grad_gate, *gather_even(last_total))
    last_slots = gather_odd(even)
    grad_w_query, grad_w_key, grad_w_value, grad_out, gain_one, gain_two = projection_outputs(
        at, last_slots, width
    )
    grad_tokens = token_gradient([near, far], tokens, grad_resid, gains)
    return (
        layer_out,
        grad_tokens,
        gain_one.reshape(-1),
        gain_two.reshape(-1),
        grad_w_query,
        grad_w_key,
        grad_w_value,
        grad_out,
        grad_gate,
        grad_up,
        grad_down,
    )


def solution(mesh):
    return jax.shard_map(
        body,
        mesh=mesh,
        in_specs=(
            P(("ctx", "fsdp"), None),
            P(),
            P("fsdp"),
            P("fsdp"),
            P("fsdp", None),
            P("fsdp", None),
            P("fsdp", None),
            P("fsdp", None),
            P("fsdp", None),
            P("fsdp", None),
            P("fsdp", None),
            P(("ctx", "fsdp"), None),
        ),
        out_specs=(
            P(("ctx", "fsdp"), None),
            P(("ctx", "fsdp"), None),
            P("fsdp"),
            P("fsdp"),
            P("fsdp", None),
            P("fsdp", None),
            P("fsdp", None),
            P("fsdp", None),
            P("fsdp", None),
            P("fsdp", None),
            P("fsdp", None),
        ),
        check_vma=False,
    )
```

```python
import functools

import jax
import jax.numpy as jnp
from jax import lax
from jax.experimental import pallas as pl
from jax.experimental.pallas import tpu as pltpu
from jax.sharding import PartitionSpec as P

HEADS = 15
KV_HEADS = 5
HEAD = 64
TP = 8
GROUP = HEADS // KV_HEADS
OWN = 2 * HEAD
epsilon = 1e-05
base_theta = 100000.0
far_below = -1e30
f32 = jnp.float32
bf16 = jnp.bfloat16
i32 = jnp.int32
AXES = ("ctx", "fsdp")
MIB = 1024 * 1024
smem = pl.BlockSpec(memory_space=pltpu.SMEM)
vmem = pl.BlockSpec(memory_space=pltpu.VMEM)


def exchange(array, mask, count):
    return lax.ppermute(array, AXES, [(i, i ^ mask) for i in range(count)])


def nn(left, right):
    return lax.dot_general(left, right, (((1,), (0,)), ((), ())), preferred_element_type=f32)


def tn(left, right):
    return lax.dot_general(left, right, (((0,), (0,)), ((), ())), preferred_element_type=f32)


def nt(left, right):
    return lax.dot_general(left, right, (((1,), (1,)), ((), ())), preferred_element_type=f32)


def shape(dims, dtype):
    return jax.ShapeDtypeStruct(dims, dtype)


def call(kernel, outs, inputs, scalars=1, scratch=(), limit=56, cost=1.0, far=(), far_out=()):
    specs = [smem] * scalars + [vmem] * (len(inputs) - scalars)
    for i in far:
        specs[i] = pl.BlockSpec(memory_space=pltpu.HBM)
    out_specs = [vmem for unused in outs]
    for i in far_out:
        out_specs[i] = pl.BlockSpec(memory_space=pltpu.HBM)
    return pl.pallas_call(
        kernel,
        out_shape=tuple(outs),
        in_specs=specs,
        out_specs=tuple(out_specs),
        scratch_shapes=list(scratch),
        compiler_params=pltpu.CompilerParams(vmem_limit_bytes=limit * MIB),
        cost_estimate=pl.CostEstimate(
            flops=int(cost * 1e9), bytes_accessed=int(cost * 1e6), transcendentals=0
        ),
    )(*inputs)


def one_hot(rows, columns, start):
    row = lax.broadcasted_iota(i32, (rows, columns), 0)
    column = lax.broadcasted_iota(i32, (rows, columns), 1)
    return jnp.where(row == column + start, 1.0, 0.0).astype(bf16)


def query_positions(base_ref, at, width, half_rows):
    lane = lax.broadcasted_iota(i32, (1, width), 1)
    place = jnp.zeros((1, width), i32)
    for block in range(width // half_rows):
        start = base_ref[at + block] - block * half_rows
        place = jnp.where(lane >= block * half_rows, start + lane, place)
    return place


def key_positions(base_ref, row, at, count, half_rows, width):
    offset = lax.broadcasted_iota(i32, (half_rows, width), 0)
    return jnp.concatenate([offset + base_ref[row, at + b] for b in range(count)], axis=0)


def swap_halves(matrix):
    lane = lax.broadcasted_iota(i32, matrix.shape, 1)
    ahead = pltpu.roll(matrix, matrix.shape[1] - HEAD // 2, 1)
    behind = pltpu.roll(matrix, HEAD // 2, 1)
    return jnp.where(lane % HEAD < HEAD // 2, ahead, behind)


def norm_scale(matrix):
    return lax.rsqrt(jnp.mean(matrix * matrix, axis=1, keepdims=True) + epsilon)


def slice_attention_weights(at, w_query, w_key, w_value, w_out, gain_one, gain_two):
    d_rows, width = w_query.shape
    lanes = 2 * OWN + OWN
    rest = width - (TP - 1) * OWN

    def kernel(at_ref, q_ref, k_ref, v_ref, o_ref, g1_ref, g2_ref, out_ref, cols, heads, whole, sems):
        tp = at_ref[0]
        kv = at_ref[2]
        wides, narrows = (q_ref, o_ref), (k_ref, v_ref)

        @pl.when(tp < TP - 1)
        def most():
            columns = pl.ds(pl.multiple_of(tp * OWN, OWN), OWN)
            copies = [
                pltpu.make_async_copy(ref.at[:, columns], cols.at[i], sems.at[i])
                for i, ref in enumerate(wides)
            ]
            for copy in copies:
                copy.start()
            for copy in copies:
                copy.wait()

        @pl.when(tp == TP - 1)
        def last():
            copies = [
                pltpu.make_async_copy(ref, whole.at[i], sems.at[i]) for i, ref in enumerate(wides)
            ]
            for copy in copies:
                copy.start()
            for copy in copies:
                copy.wait()
            for i in range(2):
                cols[i] = jnp.zeros((d_rows, OWN), bf16)
                cols[i, :, pl.ds(0, rest)] = whole[i, :, pl.ds(width - rest, rest)]

        @pl.when(kv < KV_HEADS)
        def real():
            rows = pl.ds(pl.multiple_of(kv * HEAD, HEAD), HEAD)
            copies = [
                pltpu.make_async_copy(ref.at[rows, :], heads.at[i], sems.at[2 + i])
                for i, ref in enumerate(narrows)
            ]
            for copy in copies:
                copy.start()
            for copy in copies:
                copy.wait()

        @pl.when(kv >= KV_HEADS)
        def none():
            heads[...] = jnp.zeros_like(heads)

        out_ref[pl.ds(0, d_rows), pl.ds(0, OWN)] = cols[0]
        turned = jnp.concatenate([heads[0], heads[1]], axis=0).astype(f32).T
        out_ref[pl.ds(0, d_rows), pl.ds(OWN, OWN)] = turned.astype(bf16)
        out_ref[pl.ds(0, d_rows), pl.ds(2 * OWN, OWN)] = cols[1]
        out_ref[pl.ds(d_rows, 16), :] = jnp.zeros((16, lanes), bf16)
        out_ref[d_rows, pl.ds(0, d_rows)] = g1_ref[...]
        out_ref[d_rows + 1, pl.ds(0, d_rows)] = g2_ref[...]

    return call(
        kernel,
        [shape((d_rows + 16, lanes), bf16)],
        [at, w_query, w_key.T, w_value.T, w_out, gain_one, gain_two],
        scratch=[
            pltpu.VMEM((2, d_rows, OWN), bf16),
            pltpu.VMEM((2, HEAD, d_rows), bf16),
            pltpu.VMEM((2, d_rows, width), bf16),
            pltpu.SemaphoreType.DMA((4,)),
        ],
        limit=60,
        cost=2.0,
        far=(1, 2, 3, 4),
    )[0]


def slice_ff_weights(at, w_gate, w_up, w_down, nz):
    d_rows = w_gate.shape[0]
    ff_z, width = w_down.shape
    part = ff_z // TP
    own = part * nz


    def kernel(at_ref, g_ref, u_ref, d_ref, out_ref):
        pick = one_hot(ff_z, part, at_ref[0] * part)
        for ref, start in ((g_ref, 0), (u_ref, own)):
            pieces = [nn(ref[:, pl.ds(s * ff_z, ff_z)], pick) for s in range(nz)]
            out_ref[:, pl.ds(start, own)] = jnp.concatenate(pieces, axis=1).astype(bf16)
        pieces = [nn(d_ref[pl.ds(s * d_rows, d_rows), :], pick) for s in range(nz)]
        out_ref[:, pl.ds(2 * own, own)] = jnp.concatenate(pieces, axis=1).astype(bf16)

    return call(
        kernel,
        [shape((d_rows, 3 * own), bf16)],
        [at, w_gate, w_up, w_down.T],
        limit=16,
        cost=4.0,
    )[0]


def project_keys(at, tokens, packs, cosine, sine, cotangent):
    local, width = tokens[0].shape
    half_rows = local // 2
    rows = TP * local
    nz = len(packs)
    pack_rows, lanes = packs[0].shape
    d_rows = pack_rows - 16
    per = 4
    tiles = 2 * TP // per

    def kernel(at_ref, *refs):
        toks, refs = refs[:TP], refs[TP:]
        pack, refs = refs[:nz], refs[nz:]
        cos_ref, sin_ref, cot_ref, hid_ref, kv_ref, w_ref, side_ref, gain_ref, hold, kept, sems = refs
        z = at_ref[1]
        for s in range(nz):
            hold[z ^ s] = pack[s][...]
        for s in range(nz):
            w_ref[pl.ds(s * d_rows, d_rows), :] = hold[s, pl.ds(0, d_rows), pl.ds(0, 2 * OWN)]
        gains = [hold[s, pl.ds(d_rows, 16), pl.ds(0, d_rows)].astype(f32) for s in range(nz)]
        gain_ref[...] = jnp.concatenate(gains, axis=1)[:8]
        gain = gain_ref[pl.ds(0, 1), :]
        side_ref[pl.ds(0, local), pl.ds(0, width)] = cot_ref[...]
        turned = [
            hold[s, pl.ds(0, d_rows), pl.ds(2 * OWN, OWN)].astype(f32) for s in range(nz)
        ]
        side_ref[pl.ds(local, OWN), pl.ds(0, width)] = jnp.concatenate(turned, axis=0).T.astype(bf16)
        copies = []
        for tile in range(tiles):
            side, first = (tile * per) // TP, (tile * per) % TP
            at_rows = pl.ds(tile * per * half_rows, per * half_rows)
            block = jnp.concatenate(
                [toks[first + j][pl.ds(side * half_rows, half_rows), :] for j in range(per)], axis=0
            )
            inputs = block.astype(f32)
            hidden = (inputs * norm_scale(inputs) * gain).astype(bf16)
            kept[at_rows, :] = hidden
            copy = pltpu.make_async_copy(kept.at[at_rows, :], hid_ref.at[at_rows, :], sems.at[tile])
            copy.start()
            copies.append(copy)
            pair = nn(hidden, w_ref[:, pl.ds(OWN, OWN)])
            turned = pair * cos_ref[at_rows, :] + swap_halves(pair) * sin_ref[at_rows, :]
            lane = lax.broadcasted_iota(i32, pair.shape, 1)
            kv_ref[at_rows, :] = jnp.where(lane < HEAD, turned, pair).astype(bf16)
        for copy in copies:
            copy.wait()

    return call(
        kernel,
        [
            shape((rows, width), bf16),
            shape((rows, OWN), bf16),
            shape((width, 2 * OWN), bf16),
            shape((local + OWN, TP * OWN), bf16),
            shape((8, width), f32),
        ],
        [at, *tokens, *packs, cosine, sine, cotangent],
        scratch=[
            pltpu.VMEM((nz, pack_rows, lanes), bf16),
            pltpu.VMEM((rows, width), bf16),
            pltpu.SemaphoreType.DMA((tiles,)),
        ],
        limit=60,
        cost=4.0,
        far_out=(0,),
    )


def project_queries(tokens, hidden, w_qkv, cosine, sine):
    local, width = tokens[0].shape
    half_rows = local // 2
    rows = TP * local
    per = 4

    def kernel(*refs):
        toks, refs = refs[:TP], refs[TP:]
        hid_ref, w_ref, cos_ref, sin_ref, x_ref, qt_ref = refs
        for tile in range(2 * TP // per):
            side, first = (tile * per) // TP, (tile * per) % TP
            at_rows = pl.ds(tile * per * half_rows, per * half_rows)
            for j in range(per):
                x_ref[pl.ds((tile * per + j) * half_rows, half_rows), :] = toks[first + j][
                    pl.ds(side * half_rows, half_rows), :
                ]
            query = nn(hid_ref[at_rows, :], w_ref[:, pl.ds(0, OWN)])
            query = query * cos_ref[at_rows, :] + swap_halves(query) * sin_ref[at_rows, :]
            qt_ref[:, at_rows] = (query.astype(bf16).astype(f32) * HEAD**-0.5).T.astype(bf16)

    return call(
        kernel,
        [shape((rows, width), bf16), shape((OWN, rows), bf16)],
        [*tokens, hidden, w_qkv, cosine, sine],
        scalars=0,
        limit=60,
        cost=4.0,
    )


def attention_forward(select, key_base, query_base, turned_query, own_kv, other_kv, half_rows):
    groups = len(own_kv)
    rows = own_kv[0].shape[0]
    half = rows // 2
    blocks = half // half_rows
    wide, deep = 128, 128

    def kernel(sel_ref, key_ref, query_ref, q_ref, *refs):
        own, other = refs[:groups], refs[groups : 2 * groups]
        out_ref, low_ref, lse_ref, kv_ref, kvt_ref, top_ref, mass_ref, place_ref = refs[2 * groups :]
        for head in range(2):
            chosen = sel_ref[head] == 0
            for group in range(groups):

                @pl.when(chosen)
                def take_own():
                    kv_ref[head, group] = own[group][...]
                    kvt_ref[head, group] = own[group][...].T

                @pl.when(jnp.logical_not(chosen))
                def take_other():
                    kv_ref[head, group] = other[group][...]
                    kvt_ref[head, group] = other[group][...].T

        top_ref[...] = jnp.full_like(top_ref, far_below)
        mass_ref[...] = jnp.zeros_like(mass_ref)
        out_ref[...] = jnp.zeros_like(out_ref)

        def one_group(group, unused):
            for head in range(2):
                row = sel_ref[head] * groups + group
                own_rows = pl.ds(head * HEAD, HEAD)
                stat = pl.ds(head, 1)
                place_ref[...] = key_positions(key_ref, row, 0, 2 * blocks, half_rows, 128)
                for k_start in range(0, rows, deep):
                    keys_at = pl.ds(k_start, deep)
                    k_side = k_start // half
                    block = kv_ref[head, group, keys_at, :]
                    values = kvt_ref[head, group, pl.ds(HEAD, HEAD), keys_at]
                    for start in range(k_side * half, rows, wide):
                        lanes = pl.ds(start, wide)
                        turned = q_ref[own_rows, lanes]
                        padded = jnp.concatenate([turned, jnp.zeros_like(turned)], axis=0)
                        scores = nn(block, padded)
                        if start // half == k_side:
                            places = query_positions(
                                query_ref, start // half_rows, wide, half_rows
                            )
                            scores = jnp.where(place_ref[keys_at, :] <= places, scores, far_below)
                        before = top_ref[stat, lanes]
                        top = jnp.maximum(before, jnp.max(scores, axis=0, keepdims=True))
                        weights = jnp.exp(scores - top)
                        fade = jnp.exp(before - top)
                        top_ref[stat, lanes] = top
                        mass_ref[stat, lanes] = mass_ref[stat, lanes] * fade + jnp.sum(
                            weights, axis=0, keepdims=True
                        )
                        out_ref[own_rows, lanes] = out_ref[own_rows, lanes] * fade + nn(
                            values, weights.astype(bf16)
                        )
            return unused

        lax.fori_loop(0, groups, one_group, 0)
        for head in range(2):
            own_rows = pl.ds(head * HEAD, HEAD)
            mass = mass_ref[pl.ds(head, 1), :]
            out_ref[own_rows, :] = out_ref[own_rows, :] / mass
            lse_ref[pl.ds(head, 1), :] = top_ref[pl.ds(head, 1), :] + jnp.log(mass)
        low_ref[...] = out_ref[...].T.astype(bf16)

    return call(
        kernel,
        [shape((OWN, rows), f32), shape((rows, OWN), bf16), shape((2, rows), f32)],
        [select, key_base, query_base, turned_query, *own_kv, *other_kv],
        scalars=3,
        scratch=[
            pltpu.VMEM((2, groups, rows, OWN), bf16),
            pltpu.VMEM((2, groups, OWN, rows), bf16),
            pltpu.VMEM((2, rows), f32),
            pltpu.VMEM((2, rows), f32),
            pltpu.VMEM((rows, 128), i32),
        ],
        limit=60,
        cost=14.0,
    )


def attention_backward(
    select, key_base, query_base, turned_query, own_kv, other_kv, traded, attended, log_mass, half_rows
):
    groups = len(own_kv)
    rows = own_kv[0].shape[0]
    half = rows // 2
    blocks = half // half_rows
    wide, deep = 512, 256

    def kernel(sel_ref, key_ref, query_ref, q_ref, *refs):
        own, other = refs[:groups], refs[groups : 2 * groups]
        refs = refs[2 * groups :]
        local = 2 * half_rows
        parts = [refs[0], refs[1]] + [
            refs[2 + j].at[pl.ds(k * local, local), :] for j in range(TP // 2 - 1) for k in range(2)
        ]
        refs = refs[1 + TP // 2 :]
        att_ref, lse_ref, dq_ref, keep_ref, pass_ref, gb_ref = refs[:6]
        kv_ref, sum_ref, g_ref, rq_ref, rg_ref, delta_ref, pos_ref = refs[6:]
        for group in range(groups):
            kv_ref[0, group] = own[group][...]
            kv_ref[1, group] = other[group][...]
        sum_ref[...] = jnp.zeros_like(sum_ref)
        dq_ref[...] = jnp.zeros_like(dq_ref)
        zeros = jnp.zeros((rows, HEAD), bf16)
        for j in range(0, TP, 2):
            for side in range(2):
                at = pl.ds(side * half + j * half_rows, 2 * half_rows)
                pair = jnp.concatenate(
                    [parts[j + k][pl.ds(side * half_rows, half_rows), :] for k in range(2)], axis=0
                )
                g_ref[:, at] = pair[:, :OWN].T
                gb_ref[at, :] = pair[:, OWN:]
        for head in range(2):
            own_rows = pl.ds(head * HEAD, HEAD)
            rq_ref[head] = jnp.concatenate([q_ref[own_rows, :].T, zeros], axis=1)
            grad = g_ref[own_rows, :]
            rg_ref[head] = jnp.concatenate([zeros, grad.T], axis=1)
            delta_ref[pl.ds(head, 1), :] = jnp.sum(
                grad.astype(f32) * att_ref[own_rows, :], axis=0, keepdims=True
            )

        def one_group(group, unused):
            for head in range(2):
                which = sel_ref[head]
                own_rows = pl.ds(head * HEAD, HEAD)
                stat = pl.ds(head, 1)
                pos_ref[...] = key_positions(
                    key_ref, which * groups + group, 0, 2 * blocks, half_rows, 128
                )
                for k_start in range(0, rows, deep):
                    keys_at = pl.ds(k_start, deep)
                    k_side = k_start // half
                    block = kv_ref[which, group, keys_at, :]
                    turned_keys = block.T[:HEAD]
                    for start in range(k_side * half, rows, wide):
                        lanes = pl.ds(start, wide)
                        turned = q_ref[own_rows, lanes]
                        padded = jnp.concatenate([turned, jnp.zeros_like(turned)], axis=0)
                        scores = nn(block, padded)
                        if start // half == k_side:
                            places = query_positions(
                                query_ref, start // half_rows, wide, half_rows
                            )
                            at = jnp.concatenate([pos_ref[keys_at, :]] * (wide // 128), axis=1)
                            scores = jnp.where(at <= places, scores, far_below)
                        probs = jnp.exp(scores - lse_ref[stat, lanes])
                        grads = g_ref[own_rows, lanes]
                        padded = jnp.concatenate([jnp.zeros_like(grads), grads], axis=0)
                        grad_probs = nn(block, padded)
                        grad_scores = probs * (grad_probs - delta_ref[stat, lanes])
                        probs = probs.astype(bf16)
                        grad_scores = grad_scores.astype(bf16)
                        sum_ref[which, group, keys_at, :] += nn(
                            grad_scores, rq_ref[head, lanes, :]
                        ) + nn(probs, rg_ref[head, lanes, :])
                        dq_ref[own_rows, lanes] += nn(turned_keys, grad_scores)
            return unused

        lax.fori_loop(0, groups, one_group, 0)
        for group in range(groups):
            keep_ref[pl.ds(group * rows, rows), :] = sum_ref[0, group]
            pass_ref[pl.ds(group * rows, rows), :] = sum_ref[1, group].astype(bf16)

    return call(
        kernel,
        [
            shape((OWN, rows), f32),
            shape((groups * rows, OWN), f32),
            shape((groups * rows, OWN), bf16),
            shape((rows, OWN), bf16),
        ],
        [
            select,
            key_base,
            query_base,
            turned_query,
            *own_kv,
            *other_kv,
            *traded,
            attended,
            log_mass,
        ],
        scalars=3,
        scratch=[
            pltpu.VMEM((2, groups, rows, OWN), bf16),
            pltpu.VMEM((2, groups, rows, OWN), f32),
            pltpu.VMEM((OWN, rows), bf16),
            pltpu.VMEM((2, rows, OWN), bf16),
            pltpu.VMEM((2, rows, OWN), bf16),
            pltpu.VMEM((2, rows), f32),
            pltpu.VMEM((rows, 128), i32),
        ],
        limit=28,
        cost=18.0,
    )


def store_blocks(part, tile, per, half_rows, keep_ref, pass_ref):
    side = (tile * per) // TP
    first = lax.rem(tile * per, TP) // 2
    for j in range(per):
        piece = part[j * half_rows : (j + 1) * half_rows]
        row = (2 * (first + j // 2) + side) * half_rows
        at = pl.ds(pl.multiple_of(row, half_rows), half_rows)
        target = keep_ref if j % 2 == 0 else pass_ref
        target[at, pl.ds(0, piece.shape[1])] = piece.astype(target.dtype)


def feed_forward(at, inputs, attended, sides, packs, gains, nz):
    rows, width = inputs.shape
    local = rows // TP
    half_rows = local // 2
    half = rows // 2
    d_rows, lanes = packs[0].shape
    ff = lanes // 3
    part_rows = ff // nz
    per = 4
    tile_rows = per * half_rows
    tiles = 2 * TP // per

    def kernel(at_ref, x_ref, *refs):
        att, refs = refs[:TP], refs[TP:]
        extra, refs = refs[:TP], refs[TP:]
        pack, refs = refs[:nz], refs[nz:]
        gain_ref, refs = refs[0], refs[1:]
        resid_out, gk_ref, gp_ref, gain_out, dn_w = refs[:5]
        targets, prod_out, refs = refs[5 : 5 + nz], refs[5 + nz], refs[6 + nz :]
        att_ref, wo_ref, gu_w, cot_ref, hold, acc_gu, acc_dn, blocks, prod_ref, sems = refs
        tp = at_ref[0]
        z = at_ref[1]
        for j in range(TP):
            columns = pl.ds(pl.multiple_of((tp ^ j) * OWN, OWN), OWN)
            wo_ref[columns, :] = extra[j][pl.ds(local, OWN), pl.ds(0, width)]
            for side in range(2):
                for k in range(TP):
                    att_ref[pl.ds(side * half + k * half_rows, half_rows), columns] = att[j][
                        pl.ds(side * half + (k ^ j) * half_rows, half_rows), :
                    ]
                cot_ref[pl.ds(side * half + j * half_rows, half_rows), :] = extra[j][
                    pl.ds(side * half_rows, half_rows), pl.ds(0, width)
                ]
        for s in range(nz):
            hold[z ^ s] = pack[s][...]
        for s in range(nz):
            rows_at = pl.ds(s * d_rows, d_rows)
            gu_w[rows_at, :] = hold[s, :, pl.ds(0, 2 * ff)]
            dn_w[rows_at, :] = jnp.concatenate(
                [
                    hold[b][:, 2 * ff + s * part_rows : 2 * ff + (s + 1) * part_rows]
                    for b in range(nz)
                ],
                axis=1,
            )
        gain = gain_ref[pl.ds(1, 1), :]
        gain_out[...] = jnp.zeros_like(gain_out)
        acc_gu[...] = jnp.zeros_like(acc_gu)
        acc_dn[...] = jnp.zeros_like(acc_dn)

        def copy_of(tile):
            at_rows = pl.ds(pl.multiple_of(tile * tile_rows, tile_rows), tile_rows)
            return pltpu.make_async_copy(
                prod_ref.at[at_rows, :], prod_out.at[at_rows, :], sems.at[tile]
            )

        def one_tile(tile, unused):
            at_rows = pl.ds(pl.multiple_of(tile * tile_rows, tile_rows), tile_rows)
            branch = nt(att_ref[at_rows, :][:, :width], wo_ref[pl.ds(0, width), :])
            resid = x_ref[at_rows, :].astype(f32) + branch
            side = (tile * per) // TP

            @pl.when(lax.rem(tile * per, TP) == 0)
            def keep_own():
                resid_out[pl.ds(pl.multiple_of(side * half_rows, half_rows), half_rows), :] = resid[
                    :half_rows
                ]

            normal = resid * norm_scale(resid)
            hidden = (normal * gain).astype(bf16)
            gate_up = nn(hidden, gu_w[...])
            gate, up = gate_up[:, :ff], gate_up[:, ff:]
            sigmoid = 1.0 / (1.0 + jnp.exp(-gate))
            activated = gate * sigmoid
            product = (activated * up).astype(bf16)
            prod_ref[at_rows, :] = product
            copy_of(tile).start()
            cotangent = cot_ref[at_rows, :]
            grad_product = nn(cotangent, dn_w[...])
            grad_gate = grad_product * up * sigmoid * (1.0 + gate * (1.0 - sigmoid))
            grad_gu = jnp.concatenate([grad_gate, grad_product * activated], axis=1).astype(bf16)
            partial = nt(grad_gu, gu_w[...])
            gain_out[pl.ds(0, 1), :] += jnp.sum(partial * normal, axis=0, keepdims=True)
            store_blocks(partial, tile, per, half_rows, gk_ref, gp_ref)
            acc_gu[...] += tn(hidden, grad_gu)
            acc_dn[...] += tn(cotangent, product)
            return unused

        lax.fori_loop(0, tiles, one_tile, 0)
        for b in range(nz):
            blocks[b, :, pl.ds(0, 2 * ff)] = acc_gu[pl.ds(b * d_rows, d_rows), :]
            blocks[b, :, pl.ds(2 * ff, ff)] = jnp.concatenate(
                [
                    acc_dn[pl.ds(s * d_rows, d_rows), :][:, b * part_rows : (b + 1) * part_rows]
                    for s in range(nz)
                ],
                axis=1,
            )
        for s in range(nz):
            targets[s][...] = blocks[z ^ s].astype(targets[s].dtype)
        for tile in range(tiles):
            copy_of(tile).wait()

    return call(
        kernel,
        [
            shape((local, width), f32),
            shape((TP // 2 * local, width), bf16),
            shape((TP // 2 * local, TP * OWN), bf16),
            shape((8, width), f32),
            shape((width, ff), bf16),
        ]
        + [shape((d_rows, lanes), f32 if s % 2 == 0 else bf16) for s in range(nz)]
        + [shape((rows, ff), bf16)],
        [at, inputs, *attended, *sides, *packs, gains],
        scratch=[
            pltpu.VMEM((rows, TP * OWN), bf16),
            pltpu.VMEM((TP * OWN, width), bf16),
            pltpu.VMEM((width, 2 * ff), bf16),
            pltpu.VMEM((rows, width), bf16),
            pltpu.VMEM((nz, d_rows, lanes), bf16),
            pltpu.VMEM((width, 2 * ff), f32),
            pltpu.VMEM((width, ff), f32),
            pltpu.VMEM((nz, d_rows, lanes), f32),
            pltpu.VMEM((rows, ff), bf16),
            pltpu.SemaphoreType.DMA((tiles,)),
        ],
        limit=44,
        cost=17.0,
        far_out=(5 + nz,),
    )


def feed_forward_rest(at, attended, sides, product, w_down):
    rows = attended[0].shape[0]
    width, ff = w_down.shape
    local = rows // TP
    half_rows = local // 2
    half = rows // 2
    per = 4
    tile_rows = per * half_rows

    def kernel(at_ref, *refs):
        att, refs = refs[:TP], refs[TP:]
        extra, refs = refs[:TP], refs[TP:]
        prod_ref, dn_w, att_out, wo_out, lk_ref, lp_ref = refs
        tp = at_ref[0]
        for j in range(TP):
            columns = pl.ds(pl.multiple_of((tp ^ j) * OWN, OWN), OWN)
            wo_out[columns, :] = extra[j][pl.ds(local, OWN), pl.ds(0, width)]
            for side in range(2):
                for k in range(TP):
                    att_out[pl.ds(side * half + k * half_rows, half_rows), columns] = att[j][
                        pl.ds(side * half + (k ^ j) * half_rows, half_rows), :
                    ]

        def one_tile(tile, unused):
            at_rows = pl.ds(pl.multiple_of(tile * tile_rows, tile_rows), tile_rows)
            part = nt(prod_ref[at_rows, :], dn_w[...])
            store_blocks(part, tile, per, half_rows, lk_ref, lp_ref)
            return unused

        lax.fori_loop(0, 2 * TP // per, one_tile, 0)

    return call(
        kernel,
        [
            shape((rows, TP * OWN), bf16),
            shape((TP * OWN, width), bf16),
            shape((TP // 2 * local, width), bf16),
            shape((TP // 2 * local, TP * OWN), bf16),
        ],
        [at, *attended, *sides, product, w_down],
        limit=24,
        cost=5.0,
    )


def add_crossed(keep, crossed, count):
    local, width = keep.shape[0] // count, keep.shape[1]

    def kernel(keep_ref, cross_ref, own_ref, *sends):
        for j in range(count):
            at = pl.ds(j * local, local)
            target = own_ref if j == 0 else sends[j - 1]
            target[...] = (
                keep_ref[at, :].astype(f32) + cross_ref[at, pl.ds(0, width)].astype(f32)
            ).astype(target.dtype)

    return call(
        kernel,
        [shape((local, width), f32)] + [shape((local, width), bf16)] * (count - 1),
        [keep, crossed],
        scalars=0,
        limit=12,
        cost=1.0,
    )


def branch_gradient(at, sums, resid, cotangent, w_out, gains):
    local, width = resid.shape

    def kernel(at_ref, *refs):
        parts, refs = refs[: len(sums)], refs[len(sums) :]
        resid_ref, cot_ref, wo_ref, gain_ref, grad_ref, keep_ref, pass_ref, ga_ref, gb_ref = refs
        tp = at_ref[0]
        grad_hidden = parts[0][...]
        for part in parts[1:]:
            grad_hidden = grad_hidden + part[...].astype(f32)
        resid = resid_ref[...]
        scale = norm_scale(resid)
        normal = resid * scale
        grad = grad_hidden * gain_ref[pl.ds(1, 1), :]
        grad = scale * (grad - normal * jnp.mean(grad * normal, axis=1, keepdims=True))
        grad = grad + cot_ref[...].astype(f32)
        grad_ref[...] = grad
        low = grad.astype(bf16)
        gb_ref[...] = jnp.zeros_like(gb_ref)
        gb_ref[:, pl.ds(0, width)] = low
        ga_ref[...] = jnp.zeros_like(ga_ref)
        ga_ref[:, pl.ds(0, width)] = nn(low, wo_ref[pl.ds(0, width), :]).astype(bf16)
        for j in range(TP):
            columns = pl.ds(pl.multiple_of((tp ^ j) * OWN, OWN), OWN)
            target = keep_ref if j % 2 == 0 else pass_ref
            rows = pl.ds((j // 2) * local, local)
            target[rows, pl.ds(0, OWN)] = ga_ref[:, columns]
            target[rows, pl.ds(OWN, OWN)] = gb_ref[:, columns]

    blocks = shape((TP // 2 * local, 2 * OWN), bf16)
    return call(
        kernel,
        [shape((local, width), f32), blocks, blocks],
        [at, *sums, resid, cotangent, w_out, gains],
        scratch=[pltpu.VMEM((local, TP * OWN), bf16), pltpu.VMEM((local, TP * OWN), bf16)],
        limit=16,
        cost=3.0,
    )


def pair_up(keep, crossed, count):
    local, width = keep.shape[0] // count, keep.shape[1]

    def kernel(keep_ref, cross_ref, *outs):
        for j in range(1, count):
            at = pl.ds(j * local, local)
            outs[j - 1][pl.ds(0, local), :] = keep_ref[at, :]
            outs[j - 1][pl.ds(local, local), :] = cross_ref[at, :]

    return call(
        kernel,
        [shape((2 * local, width), bf16)] * (count - 1),
        [keep, crossed],
        scalars=0,
        limit=8,
        cost=0.7,
    )


def projection_gradient(
    at, grad_query, grad_kv, inputs, hidden, w_qkv, gain_sums, cosine, sine, grad_out, nz
):
    rows, width = inputs.shape
    local = rows // TP
    half_rows = local // 2
    d_rows = width // nz
    per = 4
    tile_rows = per * half_rows
    pieces = len(grad_kv)

    def kernel(at_ref, dq_ref, *refs):
        kvs, refs = refs[:pieces], refs[pieces:]
        x_ref, hid_ref, w_ref, gain_two_ref, cos_ref, sin_ref, wo_ref = refs[:7]
        keep_ref, pass_ref, own_ref = refs[7:10]
        sends, refs = refs[10 : 10 + nz - 1], refs[10 + nz - 1 :]
        turn_ref, acc_ref, gain_acc, hold = refs
        z = at_ref[1]
        turn_ref[...] = dq_ref[...].T * HEAD**-0.5
        acc_ref[...] = jnp.zeros_like(acc_ref)
        gain_acc[...] = jnp.zeros_like(gain_acc)

        def one_tile(tile, unused):
            at_rows = pl.ds(pl.multiple_of(tile * tile_rows, tile_rows), tile_rows)
            cos, sin = cos_ref[at_rows, :], sin_ref[at_rows, :]
            query = turn_ref[at_rows, :]
            query = query * cos - swap_halves(query) * sin
            pair = kvs[0][at_rows, :].astype(f32)
            for piece in kvs[1:]:
                pair = pair + piece[at_rows, :].astype(f32)
            turned = pair * cos - swap_halves(pair) * sin
            lane = lax.broadcasted_iota(i32, pair.shape, 1)
            pair = jnp.where(lane < HEAD, turned, pair)
            grad = jnp.concatenate([query, pair], axis=1).astype(bf16)
            partial = nt(grad, w_ref[...])
            x = x_ref[at_rows, :].astype(f32)
            gain_acc[pl.ds(0, 1), :] += jnp.sum(partial * (x * norm_scale(x)), axis=0, keepdims=True)
            store_blocks(partial, tile, per, half_rows, keep_ref, pass_ref)
            acc_ref[...] += tn(hid_ref[at_rows, :], grad)
            return unused

        lax.fori_loop(0, 2 * TP // per, one_tile, 0)
        hold[...] = jnp.zeros_like(hold)
        for s in range(nz):
            columns = slice(s * d_rows, (s + 1) * d_rows)
            hold[s, pl.ds(0, 1), pl.ds(0, d_rows)] = gain_acc[pl.ds(0, 1), :][:, columns]
            hold[s, pl.ds(1, 1), pl.ds(0, d_rows)] = gain_two_ref[pl.ds(0, 1), :][:, columns]
        for s in range(nz):
            block = z ^ s
            target = own_ref if s == 0 else sends[s - 1]
            rows_at = pl.ds(pl.multiple_of(block * d_rows, 8), d_rows)
            part = pl.ds(0, d_rows)
            target[part, pl.ds(0, 2 * OWN)] = acc_ref[rows_at, :].astype(target.dtype)
            target[part, pl.ds(2 * OWN, OWN)] = wo_ref[rows_at, :].astype(target.dtype)
            target[pl.ds(d_rows, 16), :] = hold[block].astype(target.dtype)

    return call(
        kernel,
        [
            shape((TP // 2 * local, width), bf16),
            shape((TP // 2 * local, TP * OWN), bf16),
            shape((d_rows + 16, 3 * OWN), f32),
        ]
        + [shape((d_rows + 16, 3 * OWN), bf16)] * (nz - 1),
        [at, grad_query, *grad_kv, inputs, hidden, w_qkv, gain_sums, cosine, sine, grad_out],
        scratch=[
            pltpu.VMEM((rows, OWN), f32),
            pltpu.VMEM((width, 2 * OWN), f32),
            pltpu.VMEM((8, width), f32),
            pltpu.VMEM((nz, 16, 3 * OWN), f32),
        ],
        limit=32,
        cost=8.0,
    )


def token_gradient(sums, tokens, grad_resid, gains):
    local, width = tokens.shape

    def kernel(*refs):
        parts, refs = refs[: len(sums)], refs[len(sums) :]
        x_ref, grad_ref, gain_ref, out_ref = refs
        grad_hidden = parts[0][...]
        for part in parts[1:]:
            grad_hidden = grad_hidden + part[...].astype(f32)
        x = x_ref[...].astype(f32)
        scale = norm_scale(x)
        normal = x * scale
        grad = grad_hidden * gain_ref[pl.ds(0, 1), :]
        grad = scale * (grad - normal * jnp.mean(grad * normal, axis=1, keepdims=True))
        out_ref[...] = (grad + grad_ref[...]).T

    return call(
        kernel,
        [shape((width, local), f32)],
        [*sums, tokens, grad_resid, gains],
        scalars=0,
        limit=8,
        cost=1.0,
    )[0].T


def layer_output(sums, resid):
    def kernel(*refs):
        parts, (resid_ref, out_ref) = refs[: len(sums)], refs[len(sums) :]
        total = resid_ref[...]
        for part in parts:
            total = total + part[...].astype(f32)
        out_ref[...] = total.T.astype(bf16)

    turned = shape(resid.shape[::-1], bf16)
    return call(kernel, [turned], [*sums, resid], scalars=0, limit=8, cost=1.0)[0].T


def first_sum(own, arrived):
    def kernel(own_ref, in_ref, out_ref):
        out_ref[...] = (own_ref[...] + in_ref[...].astype(f32)).astype(bf16)

    return call(
        kernel, [shape(own.shape, bf16)], [own, arrived], scalars=0, limit=8, cost=1.0
    )[0]


def last_sum(own, *arrived):
    rows, lanes = own.shape

    def kernel(own_ref, *refs):
        total = own_ref[...]
        for ref in refs[:-1]:
            total = total + ref[...].astype(f32)
        refs[-1][:, pl.ds(0, lanes)] = total.astype(bf16)

    return call(
        kernel, [shape((rows, TP * OWN), bf16)], [own, *arrived], scalars=0, limit=8, cost=1.0
    )[0]


def ff_outputs(at, mine, by_x, by_y, by_xy, odd, ff_z, nz):
    d_rows = mine.shape[0]
    part = ff_z // TP
    ff = part * nz

    def kernel(at_ref, m_ref, x_ref, y_ref, xy_ref, odd_ref, gate_ref, up_ref, down_ref, hold):
        tp = at_ref[0]
        lanes = pl.ds(0, 3 * ff)
        for j, ref in enumerate((m_ref, x_ref, y_ref, xy_ref)):
            hold[tp ^ (2 * j)] = ref[:, lanes]
        for j in range(TP // 2):
            hold[tp ^ (2 * j + 1)] = odd_ref[pl.ds(d_rows * j, d_rows), lanes]
        for s in range(nz):
            for start in (s * part, ff + s * part, 2 * ff + s * part):
                block = jnp.concatenate(
                    [hold[c][:, start : start + part] for c in range(TP)], axis=1
                ).astype(f32)
                if start < ff:
                    gate_ref[:, pl.ds(s * ff_z, ff_z)] = block
                elif start < 2 * ff:
                    up_ref[:, pl.ds(s * ff_z, ff_z)] = block
                else:
                    down_ref[pl.ds(s * d_rows, d_rows), :] = block

    gate, up, down = call(
        kernel,
        [
            shape((d_rows, nz * ff_z), f32),
            shape((d_rows, nz * ff_z), f32),
            shape((nz * d_rows, ff_z), f32),
        ],
        [at, mine, by_x, by_y, by_xy, odd],
        scratch=[pltpu.VMEM((TP, d_rows, 3 * ff), bf16)],
        limit=32,
        cost=7.0,
    )
    return gate, up, down.T


def projection_outputs(at, slots, width):
    d_rows = slots[0].shape[0] - 16

    def kernel(at_ref, *refs):
        parts, (q_ref, k_ref, v_ref, o_ref, one_ref, two_ref, hold) = refs[:TP], refs[TP:]
        tp = at_ref[0]
        total = jnp.zeros((16, 3 * OWN), f32)
        for j in range(TP):
            hold[tp ^ j] = parts[j][...].astype(f32)
            total = total + parts[j][pl.ds(d_rows, 16), :].astype(f32)
        one_ref[...] = total[0:1, :d_rows]
        two_ref[...] = total[1:2, :d_rows]
        heads = [hold[c][:d_rows, :OWN] for c in range(TP)]
        q_ref[...] = jnp.concatenate(heads, axis=1)[:, :width]
        heads = [hold[c][:d_rows, 2 * OWN :] for c in range(TP)]
        o_ref[...] = jnp.concatenate(heads, axis=1)[:, :width]
        kv = [hold[c][:d_rows, OWN : 2 * OWN] for c in range(TP)]
        kv = [kv[0], kv[1] + kv[2], kv[3] + kv[4], kv[5], kv[6]]
        for c in range(KV_HEADS):
            turned = kv[c].T
            k_ref[pl.ds(c * HEAD, HEAD), :] = turned[:HEAD]
            v_ref[pl.ds(c * HEAD, HEAD), :] = turned[HEAD:]

    query, key, value, out, one, two = call(
        kernel,
        [
            shape((d_rows, width), f32),
            shape((KV_HEADS * HEAD, d_rows), f32),
            shape((KV_HEADS * HEAD, d_rows), f32),
            shape((d_rows, width), f32),
            shape((1, d_rows), f32),
            shape((1, d_rows), f32),
        ],
        [at, *slots],
        scratch=[pltpu.VMEM((TP, d_rows + 16, 3 * OWN), f32)],
        limit=12,
        cost=2.0,
    )
    return query, key.T, value.T, out, one, two


def body(
    tokens,
    pair_order,
    gain_attn,
    gain_mlp,
    w_query,
    w_key,
    w_value,
    w_out,
    w_gate,
    w_up,
    w_down,
    cotangent,
):
    local_rows, width = tokens.shape
    half_rows = local_rows // 2
    nz = lax.axis_size("fsdp")
    outer = lax.axis_size("ctx") // TP
    count = lax.axis_size(AXES)
    groups = outer * nz
    me = lax.axis_index(AXES)
    z = lax.axis_index("fsdp")
    tp = lax.axis_index("ctx") % TP
    kv_index = (4 * (tp // 2)) // GROUP + tp % 2
    at = jnp.stack([tp, z, kv_index]).astype(i32)
    send = functools.partial(exchange, count=count)
    group_mask = [(g // nz) * TP * nz + g % nz for g in range(groups)]

    def after(value, *others):
        return lax.optimization_barrier((value, *others))[0]

    def level(*arrays):
        return list(lax.optimization_barrier(arrays))

    def gather_even(block):
        return [block] + [send(block, j * nz) for j in range(2, TP, 2)]

    def gather_odd(even):
        return [piece for e in even for piece in (e, send(e, nz))]

    def scatter_far(pieces):
        return [send(piece, 2 * (j + 1) * nz) for j, piece in enumerate(pieces)]

    def from_z(block):
        return [block] + [send(block, s) for s in range(1, nz)]

    pack_one = slice_attention_weights(at, w_query, w_key, w_value, w_out, gain_attn, gain_mlp)
    token_slots = gather_odd(level(*gather_even(tokens)))
    pack_two = slice_ff_weights(after(at, pack_one), w_gate, w_up, w_down, nz)
    pack_one = from_z(pack_one)

    slot_of = jnp.array([[m | (j * nz) for j in range(TP)] for m in group_mask], dtype=i32)
    low = pair_order[me ^ slot_of]
    base = jnp.stack([low, 2 * count - 1 - low], axis=1) * half_rows
    query_base = base[0].reshape(2 * TP)
    partner = jnp.array([j ^ 1 for j in range(TP)], dtype=i32)
    key_base = jnp.stack([base, base[:, :, partner]]).reshape(2 * groups, 2 * TP)
    places = (query_base[:, None] + jnp.arange(half_rows, dtype=i32)[None, :]).reshape(-1)
    lane = jnp.arange(OWN)
    freqs = base_theta ** (-2.0 * (lane % (HEAD // 2)).astype(f32) / HEAD)
    angles = places.astype(f32)[:, None] * freqs[None, :]
    cosine = jnp.cos(angles)
    sine = jnp.sin(angles) * jnp.where(lane % HEAD < HEAD // 2, -1.0, 1.0)[None, :]
    select = jnp.where((2 * tp + jnp.arange(2)) // GROUP == kv_index, 0, 1).astype(i32)

    mask_x, mask_y = 2 * nz, 4 * nz
    hidden_one, kv, w_qkv, side, gains = project_keys(
        after(at, pack_two, select, key_base, query_base),
        token_slots,
        pack_one,
        cosine,
        sine,
        cotangent,
    )
    own_kv = [kv] + [send(kv, m) for m in group_mask[1:]]
    side_x, side_y = send(side, mask_x), send(side, mask_y)
    inputs, turned_query = project_queries(
        token_slots, after(hidden_one, kv), w_qkv, cosine, sine
    )
    side_x, side_y, inputs, turned_query, *own_kv = level(
        side_x, side_y, inputs, turned_query, *own_kv
    )
    side_odd, *other_kv = level(send(after(side, *own_kv), nz), *[send(slot, nz) for slot in own_kv])
    one, near = send(after(pack_two, *own_kv), 1), send(after(pack_two, *own_kv), 2)
    side_xy = send(side_x, mask_y)
    odd_x, odd_y = send(after(side_x, *other_kv), nz), send(after(side_y, *other_kv), nz)
    attended, attended_own, log_mass = attention_forward(
        select, key_base, query_base, turned_query, own_kv, other_kv, half_rows
    )
    attended_own, near, one, side_xy, odd_x, odd_y = level(
        attended_own, near, one, side_xy, odd_x, odd_y
    )
    far, side_xy, *even = level(send(near, 1), side_xy, *gather_even(attended_own))
    attended_slots = gather_odd(even)
    packs = [pack_two, one, near, far]
    sides = [side, side_odd, side_x, odd_x, side_y, odd_y, side_xy, send(side_xy, nz)]

    resid, grad_keep, grad_pass, gain_sums, w_down_own, *ff_blocks, product = feed_forward(
        at, inputs, attended_slots, sides, packs, gains, nz
    )
    ff_own, ff_one, ff_two, ff_three = ff_blocks
    first, *rest = add_crossed(grad_keep, send(grad_pass, nz), TP // 2)
    attended_low, w_out_all, out_keep, out_pass, ff_three, first, *rest = level(
        *feed_forward_rest(after(at, first), attended_slots, sides, product, w_down_own),
        send(after(ff_three, first), 1),
        first,
        *scatter_far(rest),
    )
    grad_resid, trade_keep, trade_pass = branch_gradient(
        at, [first, *rest], resid, cotangent, w_out_all, gains
    )
    crossed, out_crossed = level(send(trade_pass, nz), send(after(out_pass, first), nz))
    pairs = level(*scatter_far(pair_up(trade_keep, crossed, TP // 2)))
    out_first, *out_rest = add_crossed(out_keep, out_crossed, TP // 2)
    ff_one = send(after(ff_one, crossed), 1)
    ff_two = send(first_sum(ff_two, ff_three), 2)
    out_rest = scatter_far([after(piece, *pairs) for piece in out_rest])

    grad_query, kv_keep, kv_pass, branch_columns = attention_backward(
        after(select, out_first),
        key_base,
        query_base,
        turned_query,
        own_kv,
        other_kv,
        [trade_keep, crossed, *pairs],
        attended,
        log_mass,
        half_rows,
    )
    kv_pass, ff_one, ff_two, *out_rest = level(kv_pass, ff_one, ff_two, *out_rest)
    kv_crossed = send(kv_pass, nz)
    first, *rest = add_crossed(kv_keep, kv_crossed, groups)
    grad_out = tn(attended_low[:, :width], after(branch_columns, rest[0]))
    ff_total = last_sum(after(ff_own, grad_out), ff_one, ff_two)

    for step in range(outer.bit_length() - 1):
        crossing = send(ff_total, TP * nz << step).astype(f32)
        ff_total = (ff_total.astype(f32) + crossing).astype(bf16)
    layer_out = layer_output([after(out_first, rest[0]), *out_rest], resid)
    ff_x, ff_y, *grad_kv = level(
        send(ff_total, mask_x),
        send(ff_total, mask_y),
        *[send(piece, m) for piece, m in zip(rest, group_mask[1:])],
    )

    last_keep, last_pass, last_own, *last_sends = projection_gradient(
        at,
        grad_query,
        [first, *grad_kv],
        inputs,
        hidden_one,
        w_qkv,
        gain_sums,
        cosine,
        sine,
        grad_out,
        nz,
    )
    near, far = add_crossed(last_keep, send(last_pass, nz), 2)
    ff_xy, far, *arrived = level(
        send(after(ff_x, last_own), mask_y),
        send(far, mask_y),
        *[send(piece, s + 1) for s, piece in enumerate(last_sends)],
    )
    near, far = add_crossed(near, far, 2)
    last_total = last_own
    for piece in arrived:
        last_total = last_total + piece.astype(f32)
    for step in range(outer.bit_length() - 1):
        last_total = last_total + send(last_total.astype(bf16), TP * nz << step).astype(f32)
    last_total = last_total.astype(bf16)
    ff_slots = [ff_total, ff_x, ff_y, ff_xy]
    ff_slots.append(send(jnp.concatenate(ff_slots, axis=0), nz))
    grad_gate, grad_up, grad_down = ff_outputs(at, *ff_slots, w_down.shape[0], nz)
    far, grad_gate, *even = level(send(far, mask_x), grad_gate, *gather_even(last_total))
    last_slots = gather_odd(even)
    grad_w_query, grad_w_key, grad_w_value, grad_out, gain_one, gain_two = projection_outputs(
        at, last_slots, width
    )
    grad_tokens = token_gradient([near, far], tokens, grad_resid, gains)
    return (
        layer_out,
        grad_tokens,
        gain_one.reshape(-1),
        gain_two.reshape(-1),
        grad_w_query,
        grad_w_key,
        grad_w_value,
        grad_out,
        grad_gate,
        grad_up,
        grad_down,
    )


def solution(mesh):
    return jax.shard_map(
        body,
        mesh=mesh,
        in_specs=(
            P(("ctx", "fsdp"), None),
            P(),
            P("fsdp"),
            P("fsdp"),
            P("fsdp", None),
            P("fsdp", None),
            P("fsdp", None),
            P("fsdp", None),
            P("fsdp", None),
            P("fsdp", None),
            P("fsdp", None),
            P(("ctx", "fsdp"), None),
        ),
        out_specs=(
            P(("ctx", "fsdp"), None),
            P(("ctx", "fsdp"), None),
            P("fsdp"),
            P("fsdp"),
            P("fsdp", None),
            P("fsdp", None),
            P("fsdp", None),
            P("fsdp", None),
            P("fsdp", None),
            P("fsdp", None),
            P("fsdp", None),
        ),
        check_vma=False,
    )
```

```python
import functools

import jax
import jax.numpy as jnp
from jax import lax
from jax.experimental import pallas as pl
from jax.experimental.pallas import tpu as pltpu
from jax.sharding import PartitionSpec as P

HEADS = 15
KV_HEADS = 5
HEAD = 64
TP = 8
GROUP = HEADS // KV_HEADS
OWN = 2 * HEAD
epsilon = 1e-05
base_theta = 100000.0
far_below = -1e30
f32 = jnp.float32
bf16 = jnp.bfloat16
i32 = jnp.int32
AXES = ("ctx", "fsdp")
MIB = 1024 * 1024
smem = pl.BlockSpec(memory_space=pltpu.SMEM)
vmem = pl.BlockSpec(memory_space=pltpu.VMEM)


def exchange(array, mask, count):
    return lax.ppermute(array, AXES, [(i, i ^ mask) for i in range(count)])


def nn(left, right):
    return lax.dot_general(left, right, (((1,), (0,)), ((), ())), preferred_element_type=f32)


def tn(left, right):
    return lax.dot_general(left, right, (((0,), (0,)), ((), ())), preferred_element_type=f32)


def nt(left, right):
    return lax.dot_general(left, right, (((1,), (1,)), ((), ())), preferred_element_type=f32)


def shape(dims, dtype):
    return jax.ShapeDtypeStruct(dims, dtype)


def call(kernel, outs, inputs, scalars=1, scratch=(), limit=56, cost=1.0, far=(), far_out=()):
    specs = [smem] * scalars + [vmem] * (len(inputs) - scalars)
    for i in far:
        specs[i] = pl.BlockSpec(memory_space=pltpu.HBM)
    out_specs = [vmem for unused in outs]
    for i in far_out:
        out_specs[i] = pl.BlockSpec(memory_space=pltpu.HBM)
    return pl.pallas_call(
        kernel,
        out_shape=tuple(outs),
        in_specs=specs,
        out_specs=tuple(out_specs),
        scratch_shapes=list(scratch),
        compiler_params=pltpu.CompilerParams(vmem_limit_bytes=limit * MIB),
        cost_estimate=pl.CostEstimate(
            flops=int(cost * 1e9), bytes_accessed=int(cost * 1e6), transcendentals=0
        ),
    )(*inputs)


def one_hot(rows, columns, start):
    row = lax.broadcasted_iota(i32, (rows, columns), 0)
    column = lax.broadcasted_iota(i32, (rows, columns), 1)
    return jnp.where(row == column + start, 1.0, 0.0).astype(bf16)


def query_positions(base_ref, at, width, half_rows):
    lane = lax.broadcasted_iota(i32, (1, width), 1)
    place = jnp.zeros((1, width), i32)
    for block in range(width // half_rows):
        start = base_ref[at + block] - block * half_rows
        place = jnp.where(lane >= block * half_rows, start + lane, place)
    return place


def key_positions(base_ref, row, at, count, half_rows, width):
    offset = lax.broadcasted_iota(i32, (half_rows, width), 0)
    return jnp.concatenate([offset + base_ref[row, at + b] for b in range(count)], axis=0)


def swap_halves(matrix):
    lane = lax.broadcasted_iota(i32, matrix.shape, 1)
    ahead = pltpu.roll(matrix, matrix.shape[1] - HEAD // 2, 1)
    behind = pltpu.roll(matrix, HEAD // 2, 1)
    return jnp.where(lane % HEAD < HEAD // 2, ahead, behind)


def norm_scale(matrix):
    return lax.rsqrt(jnp.mean(matrix * matrix, axis=1, keepdims=True) + epsilon)


def slice_attention_weights(at, w_query, w_key, w_value, w_out, gain_one, gain_two):
    d_rows, width = w_query.shape
    lanes = 2 * OWN + OWN
    rest = width - (TP - 1) * OWN

    def kernel(at_ref, q_ref, k_ref, v_ref, o_ref, g1_ref, g2_ref, out_ref, cols, heads, whole, sems):
        tp = at_ref[0]
        kv = at_ref[2]
        wides, narrows = (q_ref, o_ref), (k_ref, v_ref)

        columns = pl.ds(pl.multiple_of(tp * OWN, OWN), OWN)
        rows = pl.ds(pl.multiple_of(kv * HEAD, HEAD), HEAD)

        def wide_copies():
            return [
                pltpu.make_async_copy(ref.at[:, columns], cols.at[i], sems.at[i])
                for i, ref in enumerate(wides)
            ]

        def whole_copies():
            return [
                pltpu.make_async_copy(ref, whole.at[i], sems.at[i]) for i, ref in enumerate(wides)
            ]

        def head_copies():
            return [
                pltpu.make_async_copy(ref.at[rows, :], heads.at[i], sems.at[2 + i])
                for i, ref in enumerate(narrows)
            ]

        @pl.when(tp < TP - 1)
        def most():
            for copy in wide_copies():
                copy.start()

        @pl.when(tp == TP - 1)
        def last():
            for copy in whole_copies():
                copy.start()

        @pl.when(kv < KV_HEADS)
        def real():
            for copy in head_copies():
                copy.start()

        @pl.when(kv >= KV_HEADS)
        def none():
            heads[...] = jnp.zeros_like(heads)

        @pl.when(tp < TP - 1)
        def most_came():
            for copy in wide_copies():
                copy.wait()

        @pl.when(tp == TP - 1)
        def last_came():
            for copy in whole_copies():
                copy.wait()
            for i in range(2):
                cols[i] = jnp.zeros((d_rows, OWN), bf16)
                cols[i, :, pl.ds(0, rest)] = whole[i, :, pl.ds(width - rest, rest)]

        @pl.when(kv < KV_HEADS)
        def real_came():
            for copy in head_copies():
                copy.wait()

        out_ref[pl.ds(0, d_rows), pl.ds(0, OWN)] = cols[0]
        turned = jnp.concatenate([heads[0], heads[1]], axis=0).astype(f32).T
        out_ref[pl.ds(0, d_rows), pl.ds(OWN, OWN)] = turned.astype(bf16)
        out_ref[pl.ds(0, d_rows), pl.ds(2 * OWN, OWN)] = cols[1]
        out_ref[pl.ds(d_rows, 16), :] = jnp.zeros((16, lanes), bf16)
        out_ref[d_rows, pl.ds(0, d_rows)] = g1_ref[...]
        out_ref[d_rows + 1, pl.ds(0, d_rows)] = g2_ref[...]

    return call(
        kernel,
        [shape((d_rows + 16, lanes), bf16)],
        [at, w_query, w_key.T, w_value.T, w_out, gain_one, gain_two],
        scratch=[
            pltpu.VMEM((2, d_rows, OWN), bf16),
            pltpu.VMEM((2, HEAD, d_rows), bf16),
            pltpu.VMEM((2, d_rows, width), bf16),
            pltpu.SemaphoreType.DMA((4,)),
        ],
        limit=60,
        cost=2.0,
        far=(1, 2, 3, 4),
    )[0]


def slice_ff_weights(at, w_gate, w_up, w_down, nz):
    d_rows = w_gate.shape[0]
    ff_z, width = w_down.shape
    part = ff_z // TP
    own = part * nz


    def kernel(at_ref, g_ref, u_ref, d_ref, out_ref):
        pick = one_hot(ff_z, part, at_ref[0] * part)
        for ref, start in ((g_ref, 0), (u_ref, own)):
            pieces = [nn(ref[:, pl.ds(s * ff_z, ff_z)], pick) for s in range(nz)]
            out_ref[:, pl.ds(start, own)] = jnp.concatenate(pieces, axis=1).astype(bf16)
        pieces = [nn(d_ref[pl.ds(s * d_rows, d_rows), :], pick) for s in range(nz)]
        out_ref[:, pl.ds(2 * own, own)] = jnp.concatenate(pieces, axis=1).astype(bf16)

    return call(
        kernel,
        [shape((d_rows, 3 * own), bf16)],
        [at, w_gate, w_up, w_down.T],
        limit=16,
        cost=4.0,
    )[0]


def project_keys(at, tokens, packs, cosine, sine, cotangent):
    local, width = tokens[0].shape
    half_rows = local // 2
    rows = TP * local
    nz = len(packs)
    pack_rows, lanes = packs[0].shape
    d_rows = pack_rows - 16
    per = 4
    tiles = 2 * TP // per

    def kernel(at_ref, *refs):
        toks, refs = refs[:TP], refs[TP:]
        pack, refs = refs[:nz], refs[nz:]
        cos_ref, sin_ref, cot_ref, hid_ref, kv_ref, w_ref, side_ref, gain_ref, hold, kept, sems = refs
        z = at_ref[1]
        for s in range(nz):
            hold[z ^ s] = pack[s][...]
        for s in range(nz):
            w_ref[pl.ds(s * d_rows, d_rows), :] = hold[s, pl.ds(0, d_rows), pl.ds(0, 2 * OWN)]
        gains = [hold[s, pl.ds(d_rows, 16), pl.ds(0, d_rows)].astype(f32) for s in range(nz)]
        gain_ref[...] = jnp.concatenate(gains, axis=1)[:8]
        gain = gain_ref[pl.ds(0, 1), :]
        side_ref[pl.ds(0, local), pl.ds(0, width)] = cot_ref[...]
        turned = [
            hold[s, pl.ds(0, d_rows), pl.ds(2 * OWN, OWN)].astype(f32) for s in range(nz)
        ]
        side_ref[pl.ds(local, OWN), pl.ds(0, width)] = jnp.concatenate(turned, axis=0).T.astype(bf16)
        copies = []
        for tile in range(tiles):
            side, first = (tile * per) // TP, (tile * per) % TP
            at_rows = pl.ds(tile * per * half_rows, per * half_rows)
            block = jnp.concatenate(
                [toks[first + j][pl.ds(side * half_rows, half_rows), :] for j in range(per)], axis=0
            )
            inputs = block.astype(f32)
            hidden = (inputs * norm_scale(inputs) * gain).astype(bf16)
            kept[at_rows, :] = hidden
            copy = pltpu.make_async_copy(kept.at[at_rows, :], hid_ref.at[at_rows, :], sems.at[tile])
            copy.start()
            copies.append(copy)
            pair = nn(hidden, w_ref[:, pl.ds(OWN, OWN)])
            turned = pair * cos_ref[at_rows, :] + swap_halves(pair) * sin_ref[at_rows, :]
            lane = lax.broadcasted_iota(i32, pair.shape, 1)
            kv_ref[at_rows, :] = jnp.where(lane < HEAD, turned, pair).astype(bf16)
        for copy in copies:
            copy.wait()

    return call(
        kernel,
        [
            shape((rows, width), bf16),
            shape((rows, OWN), bf16),
            shape((width, 2 * OWN), bf16),
            shape((local + OWN, TP * OWN), bf16),
            shape((8, width), f32),
        ],
        [at, *tokens, *packs, cosine, sine, cotangent],
        scratch=[
            pltpu.VMEM((nz, pack_rows, lanes), bf16),
            pltpu.VMEM((rows, width), bf16),
            pltpu.SemaphoreType.DMA((tiles,)),
        ],
        limit=60,
        cost=4.0,
        far_out=(0,),
    )


def project_queries(tokens, hidden, w_qkv, cosine, sine):
    local, width = tokens[0].shape
    half_rows = local // 2
    rows = TP * local
    per = 4

    def kernel(*refs):
        toks, refs = refs[:TP], refs[TP:]
        hid_ref, w_ref, cos_ref, sin_ref, x_ref, qt_ref = refs
        for tile in range(2 * TP // per):
            side, first = (tile * per) // TP, (tile * per) % TP
            at_rows = pl.ds(tile * per * half_rows, per * half_rows)
            for j in range(per):
                x_ref[pl.ds((tile * per + j) * half_rows, half_rows), :] = toks[first + j][
                    pl.ds(side * half_rows, half_rows), :
                ]
            query = nn(hid_ref[at_rows, :], w_ref[:, pl.ds(0, OWN)])
            query = query * cos_ref[at_rows, :] + swap_halves(query) * sin_ref[at_rows, :]
            qt_ref[:, at_rows] = (query.astype(bf16).astype(f32) * HEAD**-0.5).T.astype(bf16)

    return call(
        kernel,
        [shape((rows, width), bf16), shape((OWN, rows), bf16)],
        [*tokens, hidden, w_qkv, cosine, sine],
        scalars=0,
        limit=60,
        cost=4.0,
    )


def attention_forward(select, key_base, query_base, turned_query, own_kv, other_kv, half_rows):
    groups = len(own_kv)
    rows = own_kv[0].shape[0]
    half = rows // 2
    blocks = half // half_rows
    wide, deep = 128, 128

    def kernel(sel_ref, key_ref, query_ref, q_ref, *refs):
        own, other = refs[:groups], refs[groups : 2 * groups]
        out_ref, low_ref, lse_ref, kv_ref, kvt_ref, top_ref, mass_ref, place_ref = refs[2 * groups :]
        for head in range(2):
            chosen = sel_ref[head] == 0
            for group in range(groups):

                @pl.when(chosen)
                def take_own():
                    kv_ref[head, group] = own[group][...]
                    kvt_ref[head, group] = own[group][...].T

                @pl.when(jnp.logical_not(chosen))
                def take_other():
                    kv_ref[head, group] = other[group][...]
                    kvt_ref[head, group] = other[group][...].T

        top_ref[...] = jnp.full_like(top_ref, far_below)
        mass_ref[...] = jnp.zeros_like(mass_ref)
        out_ref[...] = jnp.zeros_like(out_ref)

        def one_group(group, unused):
            for head in range(2):
                row = sel_ref[head] * groups + group
                own_rows = pl.ds(head * HEAD, HEAD)
                stat = pl.ds(head, 1)
                place_ref[...] = key_positions(key_ref, row, 0, 2 * blocks, half_rows, 128)
                for k_start in range(0, rows, deep):
                    keys_at = pl.ds(k_start, deep)
                    k_side = k_start // half
                    block = kv_ref[head, group, keys_at, :]
                    values = kvt_ref[head, group, pl.ds(HEAD, HEAD), keys_at]
                    for start in range(k_side * half, rows, wide):
                        lanes = pl.ds(start, wide)
                        turned = q_ref[own_rows, lanes]
                        padded = jnp.concatenate([turned, jnp.zeros_like(turned)], axis=0)
                        scores = nn(block, padded)
                        if start // half == k_side:
                            places = query_positions(
                                query_ref, start // half_rows, wide, half_rows
                            )
                            scores = jnp.where(place_ref[keys_at, :] <= places, scores, far_below)
                        before = top_ref[stat, lanes]
                        top = jnp.maximum(before, jnp.max(scores, axis=0, keepdims=True))
                        weights = jnp.exp(scores - top)
                        fade = jnp.exp(before - top)
                        top_ref[stat, lanes] = top
                        mass_ref[stat, lanes] = mass_ref[stat, lanes] * fade + jnp.sum(
                            weights, axis=0, keepdims=True
                        )
                        out_ref[own_rows, lanes] = out_ref[own_rows, lanes] * fade + nn(
                            values, weights.astype(bf16)
                        )
            return unused

        lax.fori_loop(0, groups, one_group, 0)
        for head in range(2):
            own_rows = pl.ds(head * HEAD, HEAD)
            mass = mass_ref[pl.ds(head, 1), :]
            out_ref[own_rows, :] = out_ref[own_rows, :] / mass
            lse_ref[pl.ds(head, 1), :] = top_ref[pl.ds(head, 1), :] + jnp.log(mass)
        low_ref[...] = out_ref[...].T.astype(bf16)

    return call(
        kernel,
        [shape((OWN, rows), f32), shape((rows, OWN), bf16), shape((2, rows), f32)],
        [select, key_base, query_base, turned_query, *own_kv, *other_kv],
        scalars=3,
        scratch=[
            pltpu.VMEM((2, groups, rows, OWN), bf16),
            pltpu.VMEM((2, groups, OWN, rows), bf16),
            pltpu.VMEM((2, rows), f32),
            pltpu.VMEM((2, rows), f32),
            pltpu.VMEM((rows, 128), i32),
        ],
        limit=60,
        cost=14.0,
    )


def attention_backward(
    select, key_base, query_base, turned_query, own_kv, other_kv, traded, attended, log_mass, half_rows
):
    groups = len(own_kv)
    rows = own_kv[0].shape[0]
    half = rows // 2
    blocks = half // half_rows
    wide, deep = 512, 256

    def kernel(sel_ref, key_ref, query_ref, q_ref, *refs):
        own, other = refs[:groups], refs[groups : 2 * groups]
        refs = refs[2 * groups :]
        local = 2 * half_rows
        parts = [refs[0], refs[1]] + [
            refs[2 + j].at[pl.ds(k * local, local), :] for j in range(TP // 2 - 1) for k in range(2)
        ]
        refs = refs[1 + TP // 2 :]
        att_ref, lse_ref, dq_ref, keep_ref, pass_ref, gb_ref = refs[:6]
        kv_ref, sum_ref, g_ref, rq_ref, rg_ref, delta_ref, pos_ref = refs[6:]
        for group in range(groups):
            kv_ref[0, group] = own[group][...]
            kv_ref[1, group] = other[group][...]
        sum_ref[...] = jnp.zeros_like(sum_ref)
        dq_ref[...] = jnp.zeros_like(dq_ref)
        zeros = jnp.zeros((rows, HEAD), bf16)
        for j in range(0, TP, 2):
            for side in range(2):
                at = pl.ds(side * half + j * half_rows, 2 * half_rows)
                pair = jnp.concatenate(
                    [parts[j + k][pl.ds(side * half_rows, half_rows), :] for k in range(2)], axis=0
                )
                g_ref[:, at] = pair[:, :OWN].T
                gb_ref[at, :] = pair[:, OWN:]
        for head in range(2):
            own_rows = pl.ds(head * HEAD, HEAD)
            rq_ref[head] = jnp.concatenate([q_ref[own_rows, :].T, zeros], axis=1)
            grad = g_ref[own_rows, :]
            rg_ref[head] = jnp.concatenate([zeros, grad.T], axis=1)
            delta_ref[pl.ds(head, 1), :] = jnp.sum(
                grad.astype(f32) * att_ref[own_rows, :], axis=0, keepdims=True
            )

        def one_group(group, unused):
            for head in range(2):
                which = sel_ref[head]
                own_rows = pl.ds(head * HEAD, HEAD)
                stat = pl.ds(head, 1)
                pos_ref[...] = key_positions(
                    key_ref, which * groups + group, 0, 2 * blocks, half_rows, 128
                )
                for k_start in range(0, rows, deep):
                    keys_at = pl.ds(k_start, deep)
                    k_side = k_start // half
                    block = kv_ref[which, group, keys_at, :]
                    turned_keys = block.T[:HEAD]
                    for start in range(k_side * half, rows, wide):
                        lanes = pl.ds(start, wide)
                        turned = q_ref[own_rows, lanes]
                        padded = jnp.concatenate([turned, jnp.zeros_like(turned)], axis=0)
                        scores = nn(block, padded)
                        if start // half == k_side:
                            places = query_positions(
                                query_ref, start // half_rows, wide, half_rows
                            )
                            at = jnp.concatenate([pos_ref[keys_at, :]] * (wide // 128), axis=1)
                            scores = jnp.where(at <= places, scores, far_below)
                        probs = jnp.exp(scores - lse_ref[stat, lanes])
                        grads = g_ref[own_rows, lanes]
                        padded = jnp.concatenate([jnp.zeros_like(grads), grads], axis=0)
                        grad_probs = nn(block, padded)
                        grad_scores = probs * (grad_probs - delta_ref[stat, lanes])
                        probs = probs.astype(bf16)
                        grad_scores = grad_scores.astype(bf16)
                        sum_ref[which, group, keys_at, :] += nn(
                            grad_scores, rq_ref[head, lanes, :]
                        ) + nn(probs, rg_ref[head, lanes, :])
                        dq_ref[own_rows, lanes] += nn(turned_keys, grad_scores)
            return unused

        lax.fori_loop(0, groups, one_group, 0)
        for group in range(groups):
            keep_ref[pl.ds(group * rows, rows), :] = sum_ref[0, group]
            pass_ref[pl.ds(group * rows, rows), :] = sum_ref[1, group].astype(bf16)

    return call(
        kernel,
        [
            shape((OWN, rows), f32),
            shape((groups * rows, OWN), f32),
            shape((groups * rows, OWN), bf16),
            shape((rows, OWN), bf16),
        ],
        [
            select,
            key_base,
            query_base,
            turned_query,
            *own_kv,
            *other_kv,
            *traded,
            attended,
            log_mass,
        ],
        scalars=3,
        scratch=[
            pltpu.VMEM((2, groups, rows, OWN), bf16),
            pltpu.VMEM((2, groups, rows, OWN), f32),
            pltpu.VMEM((OWN, rows), bf16),
            pltpu.VMEM((2, rows, OWN), bf16),
            pltpu.VMEM((2, rows, OWN), bf16),
            pltpu.VMEM((2, rows), f32),
            pltpu.VMEM((rows, 128), i32),
        ],
        limit=28,
        cost=18.0,
    )


def store_blocks(part, tile, per, half_rows, keep_ref, pass_ref, x_first=False):
    side = (tile * per) // TP
    first = lax.rem(tile * per, TP) // 2
    for j in range(per):
        piece = part[j * half_rows : (j + 1) * half_rows]
        place = first // 2 + j if x_first else first + j // 2
        if x_first and j % 2:
            place = first // 2 + j - 1
        row = (2 * place + side) * half_rows
        at = pl.ds(pl.multiple_of(row, half_rows), half_rows)
        target = keep_ref if j % 2 == 0 else pass_ref
        target[at, pl.ds(0, piece.shape[1])] = piece.astype(target.dtype)


def feed_forward(at, inputs, attended, sides, packs, gains, nz):
    rows, width = inputs.shape
    local = rows // TP
    half_rows = local // 2
    half = rows // 2
    d_rows, lanes = packs[0].shape
    ff = lanes // 3
    part_rows = ff // nz
    per = 8
    tile_rows = per * half_rows
    tiles = 2 * TP // per

    def kernel(at_ref, x_ref, *refs):
        att, refs = refs[:TP], refs[TP:]
        extra, refs = refs[:TP], refs[TP:]
        pack, refs = refs[:nz], refs[nz:]
        gain_ref, refs = refs[0], refs[1:]
        resid_out, gk_ref, gp_ref, gain_out, dn_w = refs[:5]
        targets, prod_out, refs = refs[5 : 5 + nz], refs[5 + nz], refs[6 + nz :]
        att_ref, wo_ref, gu_w, cot_ref, hold, acc_gu, acc_dn, blocks, prod_ref, sems = refs
        tp = at_ref[0]
        z = at_ref[1]
        for j in range(TP):
            columns = pl.ds(pl.multiple_of((tp ^ j) * OWN, OWN), OWN)
            wo_ref[columns, :] = extra[j][pl.ds(local, OWN), pl.ds(0, width)]
            for side in range(2):
                for k in range(TP):
                    att_ref[pl.ds(side * half + k * half_rows, half_rows), columns] = att[j][
                        pl.ds(side * half + (k ^ j) * half_rows, half_rows), :
                    ]
                cot_ref[pl.ds(side * half + j * half_rows, half_rows), :] = extra[j][
                    pl.ds(side * half_rows, half_rows), pl.ds(0, width)
                ]
        for s in range(nz):
            hold[z ^ s] = pack[s][...]
        for s in range(nz):
            rows_at = pl.ds(s * d_rows, d_rows)
            gu_w[rows_at, :] = hold[s, :, pl.ds(0, 2 * ff)]
            dn_w[rows_at, :] = jnp.concatenate(
                [
                    hold[b][:, 2 * ff + s * part_rows : 2 * ff + (s + 1) * part_rows]
                    for b in range(nz)
                ],
                axis=1,
            )
        gain = gain_ref[pl.ds(1, 1), :]
        gain_out[...] = jnp.zeros_like(gain_out)
        acc_gu[...] = jnp.zeros_like(acc_gu)
        acc_dn[...] = jnp.zeros_like(acc_dn)

        def copy_of(tile):
            at_rows = pl.ds(pl.multiple_of(tile * tile_rows, tile_rows), tile_rows)
            return pltpu.make_async_copy(
                prod_ref.at[at_rows, :], prod_out.at[at_rows, :], sems.at[tile]
            )

        def one_tile(tile, unused):
            at_rows = pl.ds(pl.multiple_of(tile * tile_rows, tile_rows), tile_rows)
            branch = nt(att_ref[at_rows, :][:, :width], wo_ref[pl.ds(0, width), :])
            resid = x_ref[at_rows, :].astype(f32) + branch
            side = (tile * per) // TP

            @pl.when(lax.rem(tile * per, TP) == 0)
            def keep_own():
                resid_out[pl.ds(pl.multiple_of(side * half_rows, half_rows), half_rows), :] = resid[
                    :half_rows
                ]

            normal = resid * norm_scale(resid)
            hidden = (normal * gain).astype(bf16)
            gate_up = nn(hidden, gu_w[...])
            gate, up = gate_up[:, :ff], gate_up[:, ff:]
            sigmoid = 1.0 / (1.0 + jnp.exp(-gate))
            activated = gate * sigmoid
            product = (activated * up).astype(bf16)
            prod_ref[at_rows, :] = product
            copy_of(tile).start()
            cotangent = cot_ref[at_rows, :]
            grad_product = nn(cotangent, dn_w[...])
            grad_gate = grad_product * up * sigmoid * (1.0 + gate * (1.0 - sigmoid))
            grad_gu = jnp.concatenate([grad_gate, grad_product * activated], axis=1).astype(bf16)
            partial = nt(grad_gu, gu_w[...])
            gain_out[pl.ds(0, 1), :] += jnp.sum(partial * normal, axis=0, keepdims=True)
            store_blocks(partial, tile, per, half_rows, gk_ref, gp_ref)
            acc_gu[...] += tn(hidden, grad_gu)
            acc_dn[...] += tn(cotangent, product)
            return unused

        lax.fori_loop(0, tiles, one_tile, 0)
        for b in range(nz):
            blocks[b, :, pl.ds(0, 2 * ff)] = acc_gu[pl.ds(b * d_rows, d_rows), :]
            blocks[b, :, pl.ds(2 * ff, ff)] = jnp.concatenate(
                [
                    acc_dn[pl.ds(s * d_rows, d_rows), :][:, b * part_rows : (b + 1) * part_rows]
                    for s in range(nz)
                ],
                axis=1,
            )
        for s in range(nz):
            targets[s][...] = blocks[z ^ s].astype(targets[s].dtype)
        for tile in range(tiles):
            copy_of(tile).wait()

    return call(
        kernel,
        [
            shape((local, width), f32),
            shape((TP // 2 * local, width), bf16),
            shape((TP // 2 * local, TP * OWN), bf16),
            shape((8, width), f32),
            shape((width, ff), bf16),
        ]
        + [shape((d_rows, lanes), f32 if s % 2 == 0 else bf16) for s in range(nz)]
        + [shape((rows, ff), bf16)],
        [at, inputs, *attended, *sides, *packs, gains],
        scratch=[
            pltpu.VMEM((rows, TP * OWN), bf16),
            pltpu.VMEM((TP * OWN, width), bf16),
            pltpu.VMEM((width, 2 * ff), bf16),
            pltpu.VMEM((rows, width), bf16),
            pltpu.VMEM((nz, d_rows, lanes), bf16),
            pltpu.VMEM((width, 2 * ff), f32),
            pltpu.VMEM((width, ff), f32),
            pltpu.VMEM((nz, d_rows, lanes), f32),
            pltpu.VMEM((rows, ff), bf16),
            pltpu.SemaphoreType.DMA((tiles,)),
        ],
        limit=44,
        cost=17.0,
        far_out=(5 + nz,),
    )


def feed_forward_rest(at, attended, sides, product, w_down):
    rows = attended[0].shape[0]
    width, ff = w_down.shape
    local = rows // TP
    half_rows = local // 2
    half = rows // 2
    per = 4
    tile_rows = per * half_rows

    def kernel(at_ref, *refs):
        att, refs = refs[:TP], refs[TP:]
        extra, refs = refs[:TP], refs[TP:]
        prod_ref, dn_w, att_out, wo_out, lk_ref, lp_ref = refs
        tp = at_ref[0]
        for j in range(TP):
            columns = pl.ds(pl.multiple_of((tp ^ j) * OWN, OWN), OWN)
            wo_out[columns, :] = extra[j][pl.ds(local, OWN), pl.ds(0, width)]
            for side in range(2):
                for k in range(TP):
                    att_out[pl.ds(side * half + k * half_rows, half_rows), columns] = att[j][
                        pl.ds(side * half + (k ^ j) * half_rows, half_rows), :
                    ]

        def one_tile(tile, unused):
            at_rows = pl.ds(pl.multiple_of(tile * tile_rows, tile_rows), tile_rows)
            part = nt(prod_ref[at_rows, :], dn_w[...])
            store_blocks(part, tile, per, half_rows, lk_ref, lp_ref)
            return unused

        lax.fori_loop(0, 2 * TP // per, one_tile, 0)

    return call(
        kernel,
        [
            shape((rows, TP * OWN), bf16),
            shape((TP * OWN, width), bf16),
            shape((TP // 2 * local, width), bf16),
            shape((TP // 2 * local, TP * OWN), bf16),
        ],
        [at, *attended, *sides, product, w_down],
        limit=24,
        cost=5.0,
    )


def add_crossed(keep, crossed, count, tail=None):
    local, width = keep.shape[0] // count, keep.shape[1]
    tails = [] if tail is None else [tail]
    more = 0 if tail is None else tail.shape[0]

    def kernel(keep_ref, cross_ref, *refs):
        own_ref, *sends = refs[len(tails) :]
        for j in range(count):
            at = pl.ds(j * local, local)
            target = own_ref if j == 0 else sends[j - 1]
            target[pl.ds(0, local), pl.ds(0, width)] = (
                keep_ref[at, :].astype(f32) + cross_ref[at, pl.ds(0, width)].astype(f32)
            ).astype(target.dtype)
        if tails:
            sends[-1][pl.ds(local, more), pl.ds(0, width)] = refs[0][...]

    return call(
        kernel,
        [shape((local, width), f32)]
        + [shape((local, width), bf16)] * (count - 2)
        + [shape((local + more, TP * OWN if tails else width), bf16)],
        [keep, crossed, *tails],
        scalars=0,
        limit=12,
        cost=1.0,
    )


def branch_gradient(at, sums, resid, cotangent, w_out, gains):
    local, width = resid.shape

    def kernel(at_ref, *refs):
        parts, refs = refs[: len(sums)], refs[len(sums) :]
        resid_ref, cot_ref, wo_ref, gain_ref, grad_ref, keep_ref, pass_ref, ga_ref, gb_ref = refs
        tp = at_ref[0]
        grad_hidden = parts[0][...]
        for part in parts[1:]:
            grad_hidden = grad_hidden + part[...].astype(f32)
        resid = resid_ref[...]
        scale = norm_scale(resid)
        normal = resid * scale
        grad = grad_hidden * gain_ref[pl.ds(1, 1), :]
        grad = scale * (grad - normal * jnp.mean(grad * normal, axis=1, keepdims=True))
        grad = grad + cot_ref[...].astype(f32)
        grad_ref[...] = grad
        low = grad.astype(bf16)
        gb_ref[...] = jnp.zeros_like(gb_ref)
        gb_ref[:, pl.ds(0, width)] = low
        ga_ref[...] = jnp.zeros_like(ga_ref)
        ga_ref[:, pl.ds(0, width)] = nn(low, wo_ref[pl.ds(0, width), :]).astype(bf16)
        for j in range(TP):
            columns = pl.ds(pl.multiple_of((tp ^ j) * OWN, OWN), OWN)
            target = keep_ref if j % 2 == 0 else pass_ref
            rows = pl.ds((j // 2) * local, local)
            target[rows, pl.ds(0, OWN)] = ga_ref[:, columns]
            target[rows, pl.ds(OWN, OWN)] = gb_ref[:, columns]

    blocks = shape((TP // 2 * local, 2 * OWN), bf16)
    return call(
        kernel,
        [shape((local, width), f32), blocks, blocks],
        [at, *sums, resid, cotangent, w_out, gains],
        scratch=[pltpu.VMEM((local, TP * OWN), bf16), pltpu.VMEM((local, TP * OWN), bf16)],
        limit=16,
        cost=3.0,
    )


def pair_up(keep, crossed, count):
    local, width = keep.shape[0] // count, keep.shape[1]

    def kernel(keep_ref, cross_ref, *outs):
        for j in range(1, count):
            at = pl.ds(j * local, local)
            outs[j - 1][pl.ds(0, local), :] = keep_ref[at, :]
            outs[j - 1][pl.ds(local, local), :] = cross_ref[at, :]

    return call(
        kernel,
        [shape((2 * local, width), bf16)] * (count - 1),
        [keep, crossed],
        scalars=0,
        limit=8,
        cost=0.7,
    )


def projection_gradient(
    at, grad_query, grad_kv, inputs, hidden, w_qkv, gain_sums, cosine, sine, grad_out, nz
):
    rows, width = inputs.shape
    local = rows // TP
    half_rows = local // 2
    d_rows = width // nz
    per = 4
    tile_rows = per * half_rows
    pieces = len(grad_kv)

    def kernel(at_ref, dq_ref, *refs):
        kvs, refs = refs[:pieces], refs[pieces:]
        x_ref, hid_ref, w_ref, gain_two_ref, cos_ref, sin_ref, wo_ref = refs[:7]
        keep_ref, pass_ref, own_ref = refs[7:10]
        sends, refs = refs[10 : 10 + nz - 1], refs[10 + nz - 1 :]
        turn_ref, acc_ref, gain_acc, hold = refs
        z = at_ref[1]
        turn_ref[...] = dq_ref[...].T * HEAD**-0.5
        acc_ref[...] = jnp.zeros_like(acc_ref)
        gain_acc[...] = jnp.zeros_like(gain_acc)

        def one_tile(tile, unused):
            at_rows = pl.ds(pl.multiple_of(tile * tile_rows, tile_rows), tile_rows)
            cos, sin = cos_ref[at_rows, :], sin_ref[at_rows, :]
            query = turn_ref[at_rows, :]
            query = query * cos - swap_halves(query) * sin
            pair = kvs[0][at_rows, :].astype(f32)
            for piece in kvs[1:]:
                pair = pair + piece[at_rows, :].astype(f32)
            turned = pair * cos - swap_halves(pair) * sin
            lane = lax.broadcasted_iota(i32, pair.shape, 1)
            pair = jnp.where(lane < HEAD, turned, pair)
            grad = jnp.concatenate([query, pair], axis=1).astype(bf16)
            partial = nt(grad, w_ref[...])
            x = x_ref[at_rows, :].astype(f32)
            gain_acc[pl.ds(0, 1), :] += jnp.sum(partial * (x * norm_scale(x)), axis=0, keepdims=True)
            store_blocks(partial, tile, per, half_rows, keep_ref, pass_ref, True)
            acc_ref[...] += tn(hid_ref[at_rows, :], grad)
            return unused

        lax.fori_loop(0, 2 * TP // per, one_tile, 0)
        hold[...] = jnp.zeros_like(hold)
        for s in range(nz):
            columns = slice(s * d_rows, (s + 1) * d_rows)
            hold[s, pl.ds(0, 1), pl.ds(0, d_rows)] = gain_acc[pl.ds(0, 1), :][:, columns]
            hold[s, pl.ds(1, 1), pl.ds(0, d_rows)] = gain_two_ref[pl.ds(0, 1), :][:, columns]
        for s in range(nz):
            block = z ^ s
            target = own_ref if s == 0 else sends[s - 1]
            rows_at = pl.ds(pl.multiple_of(block * d_rows, 8), d_rows)
            part = pl.ds(0, d_rows)
            target[part, pl.ds(0, 2 * OWN)] = acc_ref[rows_at, :].astype(target.dtype)
            target[part, pl.ds(2 * OWN, OWN)] = wo_ref[rows_at, :].astype(target.dtype)
            target[pl.ds(d_rows, 16), :] = hold[block].astype(target.dtype)

    return call(
        kernel,
        [
            shape((TP // 2 * local, width), bf16),
            shape((TP // 2 * local, TP * OWN), bf16),
            shape((d_rows + 16, 3 * OWN), f32),
        ]
        + [shape((d_rows + 16, 3 * OWN), bf16)] * (nz - 1),
        [at, grad_query, *grad_kv, inputs, hidden, w_qkv, gain_sums, cosine, sine, grad_out],
        scratch=[
            pltpu.VMEM((rows, OWN), f32),
            pltpu.VMEM((width, 2 * OWN), f32),
            pltpu.VMEM((8, width), f32),
            pltpu.VMEM((nz, 16, 3 * OWN), f32),
        ],
        limit=32,
        cost=8.0,
    )


def token_gradient(sums, tokens, grad_resid, gains):
    local, width = tokens.shape

    def kernel(*refs):
        parts, refs = refs[: len(sums)], refs[len(sums) :]
        x_ref, grad_ref, gain_ref, out_ref = refs
        grad_hidden = parts[0][...]
        for part in parts[1:]:
            grad_hidden = grad_hidden + part[...].astype(f32)
        x = x_ref[...].astype(f32)
        scale = norm_scale(x)
        normal = x * scale
        grad = grad_hidden * gain_ref[pl.ds(0, 1), :]
        grad = scale * (grad - normal * jnp.mean(grad * normal, axis=1, keepdims=True))
        out_ref[...] = (grad + grad_ref[...]).T

    return call(
        kernel,
        [shape((width, local), f32)],
        [*sums, tokens, grad_resid, gains],
        scalars=0,
        limit=8,
        cost=1.0,
    )[0].T


def layer_output(near, arrived, resid):
    local, width = resid.shape
    start = arrived.shape[0] - local

    def kernel(near_ref, in_ref, resid_ref, out_ref):
        total = resid_ref[...] + near_ref[...] + in_ref[pl.ds(start, local), pl.ds(0, width)].astype(f32)
        out_ref[...] = total.T.astype(bf16)

    turned = shape(resid.shape[::-1], bf16)
    return call(kernel, [turned], [near, arrived, resid], scalars=0, limit=8, cost=1.0)[0].T


def first_sum(own, arrived):
    def kernel(own_ref, in_ref, out_ref):
        out_ref[...] = (own_ref[...] + in_ref[...].astype(f32)).astype(bf16)

    return call(
        kernel, [shape(own.shape, bf16)], [own, arrived], scalars=0, limit=8, cost=1.0
    )[0]


def last_sum(own, *arrived):
    rows, lanes = own.shape

    def kernel(own_ref, *refs):
        total = own_ref[...]
        for ref in refs[:-1]:
            total = total + ref[...].astype(f32)
        refs[-1][:, pl.ds(0, lanes)] = total.astype(bf16)

    return call(
        kernel, [shape((rows, TP * OWN), bf16)], [own, *arrived], scalars=0, limit=8, cost=1.0
    )[0]


def ff_outputs(at, mine, by_x, by_y, by_xy, odd, ff_z, nz):
    d_rows = mine.shape[0]
    part = ff_z // TP
    ff = part * nz

    def kernel(at_ref, m_ref, x_ref, y_ref, xy_ref, odd_ref, gate_ref, up_ref, down_ref, hold):
        tp = at_ref[0]
        lanes = pl.ds(0, 3 * ff)
        for j, ref in enumerate((m_ref, x_ref, y_ref, xy_ref)):
            hold[tp ^ (2 * j)] = ref[:, lanes]
        for j in range(TP // 2):
            hold[tp ^ (2 * j + 1)] = odd_ref[pl.ds(d_rows * j, d_rows), lanes]
        for s in range(nz):
            for start in (s * part, ff + s * part, 2 * ff + s * part):
                block = jnp.concatenate(
                    [hold[c][:, start : start + part] for c in range(TP)], axis=1
                ).astype(f32)
                if start < ff:
                    gate_ref[:, pl.ds(s * ff_z, ff_z)] = block
                elif start < 2 * ff:
                    up_ref[:, pl.ds(s * ff_z, ff_z)] = block
                else:
                    down_ref[pl.ds(s * d_rows, d_rows), :] = block

    gate, up, down = call(
        kernel,
        [
            shape((d_rows, nz * ff_z), f32),
            shape((d_rows, nz * ff_z), f32),
            shape((nz * d_rows, ff_z), f32),
        ],
        [at, mine, by_x, by_y, by_xy, odd],
        scratch=[pltpu.VMEM((TP, d_rows, 3 * ff), bf16)],
        limit=32,
        cost=7.0,
    )
    return gate, up, down.T


def projection_outputs(at, slots, width):
    d_rows = slots[0].shape[0] - 16

    def kernel(at_ref, *refs):
        parts, (q_ref, k_ref, v_ref, o_ref, one_ref, two_ref, hold) = refs[:TP], refs[TP:]
        tp = at_ref[0]
        total = jnp.zeros((16, 3 * OWN), f32)
        for j in range(TP):
            hold[tp ^ j] = parts[j][...].astype(f32)
            total = total + parts[j][pl.ds(d_rows, 16), :].astype(f32)
        one_ref[...] = total[0:1, :d_rows]
        two_ref[...] = total[1:2, :d_rows]
        heads = [hold[c][:d_rows, :OWN] for c in range(TP)]
        q_ref[...] = jnp.concatenate(heads, axis=1)[:, :width]
        heads = [hold[c][:d_rows, 2 * OWN :] for c in range(TP)]
        o_ref[...] = jnp.concatenate(heads, axis=1)[:, :width]
        kv = [hold[c][:d_rows, OWN : 2 * OWN] for c in range(TP)]
        kv = [kv[0], kv[1] + kv[2], kv[3] + kv[4], kv[5], kv[6]]
        for c in range(KV_HEADS):
            turned = kv[c].T
            k_ref[pl.ds(c * HEAD, HEAD), :] = turned[:HEAD]
            v_ref[pl.ds(c * HEAD, HEAD), :] = turned[HEAD:]

    query, key, value, out, one, two = call(
        kernel,
        [
            shape((d_rows, width), f32),
            shape((KV_HEADS * HEAD, d_rows), f32),
            shape((KV_HEADS * HEAD, d_rows), f32),
            shape((d_rows, width), f32),
            shape((1, d_rows), f32),
            shape((1, d_rows), f32),
        ],
        [at, *slots],
        scratch=[pltpu.VMEM((TP, d_rows + 16, 3 * OWN), f32)],
        limit=12,
        cost=0.01,
    )
    return query, key.T, value.T, out, one, two


def body(
    tokens,
    pair_order,
    gain_attn,
    gain_mlp,
    w_query,
    w_key,
    w_value,
    w_out,
    w_gate,
    w_up,
    w_down,
    cotangent,
):
    local_rows, width = tokens.shape
    half_rows = local_rows // 2
    nz = lax.axis_size("fsdp")
    outer = lax.axis_size("ctx") // TP
    count = lax.axis_size(AXES)
    groups = outer * nz
    me = lax.axis_index(AXES)
    z = lax.axis_index("fsdp")
    tp = lax.axis_index("ctx") % TP
    kv_index = (4 * (tp // 2)) // GROUP + tp % 2
    at = jnp.stack([tp, z, kv_index]).astype(i32)
    send = functools.partial(exchange, count=count)
    group_mask = [(g // nz) * TP * nz + g % nz for g in range(groups)]

    def after(value, *others):
        return lax.optimization_barrier((value, *others))[0]

    def level(*arrays):
        return list(lax.optimization_barrier(arrays))

    def gather_even(block):
        return [block] + [send(block, j * nz) for j in range(2, TP, 2)]

    def gather_odd(even):
        return [piece for e in even for piece in (e, send(e, nz))]

    def scatter_far(pieces):
        return [send(piece, 2 * (j + 1) * nz) for j, piece in enumerate(pieces)]

    def from_z(block):
        return [block] + [send(block, s) for s in range(1, nz)]

    pack_one = slice_attention_weights(at, w_query, w_key, w_value, w_out, gain_attn, gain_mlp)
    token_slots = gather_odd(level(*gather_even(tokens)))
    pack_two = slice_ff_weights(after(at, pack_one), w_gate, w_up, w_down, nz)
    pack_one = from_z(pack_one)

    slot_of = jnp.array([[m | (j * nz) for j in range(TP)] for m in group_mask], dtype=i32)
    low = pair_order[me ^ slot_of]
    base = jnp.stack([low, 2 * count - 1 - low], axis=1) * half_rows
    query_base = base[0].reshape(2 * TP)
    partner = jnp.array([j ^ 1 for j in range(TP)], dtype=i32)
    key_base = jnp.stack([base, base[:, :, partner]]).reshape(2 * groups, 2 * TP)
    places = (query_base[:, None] + jnp.arange(half_rows, dtype=i32)[None, :]).reshape(-1)
    lane = jnp.arange(OWN)
    freqs = base_theta ** (-2.0 * (lane % (HEAD // 2)).astype(f32) / HEAD)
    angles = places.astype(f32)[:, None] * freqs[None, :]
    cosine = jnp.cos(angles)
    sine = jnp.sin(angles) * jnp.where(lane % HEAD < HEAD // 2, -1.0, 1.0)[None, :]
    select = jnp.where((2 * tp + jnp.arange(2)) // GROUP == kv_index, 0, 1).astype(i32)

    mask_x, mask_y = 2 * nz, 4 * nz
    hidden_one, kv, w_qkv, side, gains = project_keys(
        after(at, pack_two, select, key_base, query_base),
        token_slots,
        pack_one,
        cosine,
        sine,
        cotangent,
    )
    own_kv = [kv] + [send(kv, m) for m in group_mask[1:]]
    side_x, side_y = send(side, mask_x), send(side, mask_y)
    inputs, turned_query = project_queries(
        token_slots, after(hidden_one, kv), w_qkv, cosine, sine
    )
    side_x, side_y, inputs, turned_query, *own_kv = level(
        side_x, side_y, inputs, turned_query, *own_kv
    )
    other_kv = level(*[send(slot, nz) for slot in own_kv])
    one, near = send(after(pack_two, *own_kv), 1), send(after(pack_two, *own_kv), 2)
    side_xy = send(side_x, mask_y)
    side_odd, odd_x = send(after(side, *other_kv), nz), send(after(side_x, *other_kv), nz)
    attended, attended_own, log_mass = attention_forward(
        select, key_base, query_base, turned_query, own_kv, other_kv, half_rows
    )
    attended_own, near, one, side_xy, side_odd, odd_x = level(
        attended_own, near, one, side_xy, side_odd, odd_x
    )
    far, side_xy, *even = level(send(near, 1), side_xy, *gather_even(attended_own))
    attended_slots = gather_odd(even)
    packs = [pack_two, one, near, far]
    odd_y = send(after(side_y, side_xy), nz)
    sides = [side, side_odd, side_x, odd_x, side_y, odd_y, side_xy, send(side_xy, nz)]

    resid, grad_keep, grad_pass, gain_sums, w_down_own, *ff_blocks, product = feed_forward(
        at, inputs, attended_slots, sides, packs, gains, nz
    )
    ff_own, ff_one, ff_two, ff_three = ff_blocks
    first, *rest = add_crossed(grad_keep, send(grad_pass, nz), TP // 2)
    attended_low, w_out_all, out_keep, out_pass, ff_three, first, *rest = level(
        *feed_forward_rest(after(at, first), attended_slots, sides, product, w_down_own),
        send(after(ff_three, first), 1),
        first,
        *scatter_far(rest),
    )
    grad_resid, trade_keep, trade_pass = branch_gradient(
        at, [first, *rest], resid, cotangent, w_out_all, gains
    )
    crossed, out_crossed = level(send(trade_pass, nz), send(after(out_pass, first), nz))
    pairs = level(*scatter_far(pair_up(trade_keep, crossed, TP // 2)))
    out_near, out_far = add_crossed(out_keep, out_crossed, 2)
    ff_one = send(after(ff_one, crossed), 1)
    ff_two = send(first_sum(ff_two, ff_three), 2)
    out_far = send(after(out_far, *pairs), mask_y)

    grad_query, kv_keep, kv_pass, branch_columns = attention_backward(
        after(select, out_near),
        key_base,
        query_base,
        turned_query,
        own_kv,
        other_kv,
        [trade_keep, crossed, *pairs],
        attended,
        log_mass,
        half_rows,
    )
    kv_pass, ff_one, ff_two, out_far = level(kv_pass, ff_one, ff_two, out_far)
    kv_crossed = send(kv_pass, nz)
    first, *rest = add_crossed(kv_keep, kv_crossed, groups)
    grad_out = tn(attended_low[:, :width], after(branch_columns, rest[0]))
    ff_total = last_sum(after(ff_own, grad_out), ff_one, ff_two)

    for step in range(outer.bit_length() - 1):
        crossing = send(ff_total, TP * nz << step).astype(f32)
        ff_total = (ff_total.astype(f32) + crossing).astype(bf16)
    out_near, out_far = add_crossed(after(out_near, rest[0]), out_far, 2)
    ff_x, ff_y, *grad_kv = level(
        send(ff_total, mask_x),
        send(ff_total, mask_y),
        *[send(piece, m) for piece, m in zip(rest, group_mask[1:])],
    )

    last_keep, last_pass, last_own, *last_sends = projection_gradient(
        at,
        grad_query,
        [first, *grad_kv],
        inputs,
        hidden_one,
        w_qkv,
        gain_sums,
        cosine,
        sine,
        grad_out,
        nz,
    )
    near, far = add_crossed(last_keep, send(last_pass, nz), 2, out_far)
    ff_xy, far, *arrived = level(
        send(after(ff_x, last_own), mask_y),
        send(far, mask_x),
        *[send(piece, s + 1) for s, piece in enumerate(last_sends)],
    )
    layer_out = layer_output(out_near, far, resid)
    near, far = add_crossed(near, far, 2)
    last_total = last_own
    for piece in arrived:
        last_total = last_total + piece.astype(f32)
    for step in range(outer.bit_length() - 1):
        last_total = last_total + send(last_total.astype(bf16), TP * nz << step).astype(f32)
    last_total = last_total.astype(bf16)
    ff_slots = [ff_total, ff_x, ff_y, ff_xy]
    ff_slots.append(send(jnp.concatenate(ff_slots, axis=0), nz))
    grad_gate, grad_up, grad_down = ff_outputs(at, *ff_slots, w_down.shape[0], nz)
    far = send(far, mask_y)
    grad_gate, *even = level(grad_gate, *gather_even(last_total))
    last_slots = gather_odd(even)
    grad_w_query, grad_w_key, grad_w_value, grad_out, gain_one, gain_two = projection_outputs(
        at, last_slots, width
    )
    grad_tokens = token_gradient([after(near, grad_w_query), far], tokens, grad_resid, gains)
    return (
        layer_out,
        grad_tokens,
        gain_one.reshape(-1),
        gain_two.reshape(-1),
        grad_w_query,
        grad_w_key,
        grad_w_value,
        grad_out,
        grad_gate,
        grad_up,
        grad_down,
    )


def solution(mesh):
    return jax.shard_map(
        body,
        mesh=mesh,
        in_specs=(
            P(("ctx", "fsdp"), None),
            P(),
            P("fsdp"),
            P("fsdp"),
            P("fsdp", None),
            P("fsdp", None),
            P("fsdp", None),
            P("fsdp", None),
            P("fsdp", None),
            P("fsdp", None),
            P("fsdp", None),
            P(("ctx", "fsdp"), None),
        ),
        out_specs=(
            P(("ctx", "fsdp"), None),
            P(("ctx", "fsdp"), None),
            P("fsdp"),
            P("fsdp"),
            P("fsdp", None),
            P("fsdp", None),
            P("fsdp", None),
            P("fsdp", None),
            P("fsdp", None),
            P("fsdp", None),
            P("fsdp", None),
        ),
        check_vma=False,
    )
```

```python
import functools

import jax
import jax.numpy as jnp
from jax import lax
from jax.experimental import pallas as pl
from jax.experimental.pallas import tpu as pltpu
from jax.sharding import PartitionSpec as P

HEADS = 15
KV_HEADS = 5
HEAD = 64
TP = 8
GROUP = HEADS // KV_HEADS
OWN = 2 * HEAD
epsilon = 1e-05
base_theta = 100000.0
far_below = -1e30
f32 = jnp.float32
bf16 = jnp.bfloat16
i32 = jnp.int32
AXES = ("ctx", "fsdp")
MIB = 1024 * 1024
smem = pl.BlockSpec(memory_space=pltpu.SMEM)
vmem = pl.BlockSpec(memory_space=pltpu.VMEM)


def exchange(array, mask, count):
    return lax.ppermute(array, AXES, [(i, i ^ mask) for i in range(count)])


def nn(left, right):
    return lax.dot_general(left, right, (((1,), (0,)), ((), ())), preferred_element_type=f32)


def tn(left, right):
    return lax.dot_general(left, right, (((0,), (0,)), ((), ())), preferred_element_type=f32)


def nt(left, right):
    return lax.dot_general(left, right, (((1,), (1,)), ((), ())), preferred_element_type=f32)


def shape(dims, dtype):
    return jax.ShapeDtypeStruct(dims, dtype)


def call(kernel, outs, inputs, scalars=1, scratch=(), limit=56, cost=1.0, far=(), far_out=()):
    specs = [smem] * scalars + [vmem] * (len(inputs) - scalars)
    for i in far:
        specs[i] = pl.BlockSpec(memory_space=pltpu.HBM)
    out_specs = [vmem for unused in outs]
    for i in far_out:
        out_specs[i] = pl.BlockSpec(memory_space=pltpu.HBM)
    return pl.pallas_call(
        kernel,
        out_shape=tuple(outs),
        in_specs=specs,
        out_specs=tuple(out_specs),
        scratch_shapes=list(scratch),
        compiler_params=pltpu.CompilerParams(vmem_limit_bytes=limit * MIB),
        cost_estimate=pl.CostEstimate(
            flops=int(cost * 1e9), bytes_accessed=int(cost * 1e6), transcendentals=0
        ),
    )(*inputs)


def one_hot(rows, columns, start):
    row = lax.broadcasted_iota(i32, (rows, columns), 0)
    column = lax.broadcasted_iota(i32, (rows, columns), 1)
    return jnp.where(row == column + start, 1.0, 0.0).astype(bf16)


def query_positions(base_ref, at, width, half_rows):
    lane = lax.broadcasted_iota(i32, (1, width), 1)
    place = jnp.zeros((1, width), i32)
    for block in range(width // half_rows):
        start = base_ref[at + block] - block * half_rows
        place = jnp.where(lane >= block * half_rows, start + lane, place)
    return place


def key_positions(base_ref, row, at, count, half_rows, width):
    offset = lax.broadcasted_iota(i32, (half_rows, width), 0)
    return jnp.concatenate([offset + base_ref[row, at + b] for b in range(count)], axis=0)


def swap_halves(matrix):
    lane = lax.broadcasted_iota(i32, matrix.shape, 1)
    ahead = pltpu.roll(matrix, matrix.shape[1] - HEAD // 2, 1)
    behind = pltpu.roll(matrix, HEAD // 2, 1)
    return jnp.where(lane % HEAD < HEAD // 2, ahead, behind)


def norm_scale(matrix):
    return lax.rsqrt(jnp.mean(matrix * matrix, axis=1, keepdims=True) + epsilon)


def slice_attention_weights(at, w_query, w_key, w_value, w_out, gain_one, gain_two):
    d_rows, width = w_query.shape
    lanes = 2 * OWN + OWN
    rest = width - (TP - 1) * OWN

    def kernel(at_ref, q_ref, k_ref, v_ref, o_ref, g1_ref, g2_ref, out_ref, cols, heads, whole, sems):
        tp = at_ref[0]
        kv = at_ref[2]
        wides, narrows = (q_ref, o_ref), (k_ref, v_ref)

        columns = pl.ds(pl.multiple_of(tp * OWN, OWN), OWN)
        rows = pl.ds(pl.multiple_of(kv * HEAD, HEAD), HEAD)

        def wide_copies():
            return [
                pltpu.make_async_copy(ref.at[:, columns], cols.at[i], sems.at[i])
                for i, ref in enumerate(wides)
            ]

        def whole_copies():
            return [
                pltpu.make_async_copy(ref, whole.at[i], sems.at[i]) for i, ref in enumerate(wides)
            ]

        def head_copies():
            return [
                pltpu.make_async_copy(ref.at[rows, :], heads.at[i], sems.at[2 + i])
                for i, ref in enumerate(narrows)
            ]

        @pl.when(tp < TP - 1)
        def most():
            for copy in wide_copies():
                copy.start()

        @pl.when(tp == TP - 1)
        def last():
            for copy in whole_copies():
                copy.start()

        @pl.when(kv < KV_HEADS)
        def real():
            for copy in head_copies():
                copy.start()

        @pl.when(kv >= KV_HEADS)
        def none():
            heads[...] = jnp.zeros_like(heads)

        @pl.when(tp < TP - 1)
        def most_came():
            for copy in wide_copies():
                copy.wait()

        @pl.when(tp == TP - 1)
        def last_came():
            for copy in whole_copies():
                copy.wait()
            for i in range(2):
                cols[i] = jnp.zeros((d_rows, OWN), bf16)
                cols[i, :, pl.ds(0, rest)] = whole[i, :, pl.ds(width - rest, rest)]

        @pl.when(kv < KV_HEADS)
        def real_came():
            for copy in head_copies():
                copy.wait()

        out_ref[pl.ds(0, d_rows), pl.ds(0, OWN)] = cols[0]
        turned = jnp.concatenate([heads[0], heads[1]], axis=0).astype(f32).T
        out_ref[pl.ds(0, d_rows), pl.ds(OWN, OWN)] = turned.astype(bf16)
        out_ref[pl.ds(0, d_rows), pl.ds(2 * OWN, OWN)] = cols[1]
        out_ref[pl.ds(d_rows, 16), :] = jnp.zeros((16, lanes), bf16)
        out_ref[d_rows, pl.ds(0, d_rows)] = g1_ref[...]
        out_ref[d_rows + 1, pl.ds(0, d_rows)] = g2_ref[...]

    return call(
        kernel,
        [shape((d_rows + 16, lanes), bf16)],
        [at, w_query, w_key.T, w_value.T, w_out, gain_one, gain_two],
        scratch=[
            pltpu.VMEM((2, d_rows, OWN), bf16),
            pltpu.VMEM((2, HEAD, d_rows), bf16),
            pltpu.VMEM((2, d_rows, width), bf16),
            pltpu.SemaphoreType.DMA((4,)),
        ],
        limit=60,
        cost=2.0,
        far=(1, 2, 3, 4),
    )[0]


def slice_ff_weights(at, w_gate, w_up, w_down, nz):
    d_rows = w_gate.shape[0]
    ff_z, width = w_down.shape
    part = ff_z // TP
    own = part * nz


    def kernel(at_ref, g_ref, u_ref, d_ref, out_ref):
        pick = one_hot(ff_z, part, at_ref[0] * part)
        for ref, start in ((g_ref, 0), (u_ref, own)):
            pieces = [nn(ref[:, pl.ds(s * ff_z, ff_z)], pick) for s in range(nz)]
            out_ref[:, pl.ds(start, own)] = jnp.concatenate(pieces, axis=1).astype(bf16)
        pieces = [nn(d_ref[pl.ds(s * d_rows, d_rows), :], pick) for s in range(nz)]
        out_ref[:, pl.ds(2 * own, own)] = jnp.concatenate(pieces, axis=1).astype(bf16)

    return call(
        kernel,
        [shape((d_rows, 3 * own), bf16)],
        [at, w_gate, w_up, w_down.T],
        limit=16,
        cost=4.0,
    )[0]


def project_keys(at, tokens, packs, cosine, sine, cotangent):
    local, width = tokens[0].shape
    half_rows = local // 2
    rows = TP * local
    nz = len(packs)
    pack_rows, lanes = packs[0].shape
    d_rows = pack_rows - 16
    per = 4
    tiles = 2 * TP // per

    def kernel(at_ref, *refs):
        toks, refs = refs[:TP], refs[TP:]
        pack, refs = refs[:nz], refs[nz:]
        cos_ref, sin_ref, cot_ref, hid_ref, kv_ref, w_ref, side_ref, gain_ref, hold, kept, sems = refs
        z = at_ref[1]
        for s in range(nz):
            hold[z ^ s] = pack[s][...]
        for s in range(nz):
            w_ref[pl.ds(s * d_rows, d_rows), :] = hold[s, pl.ds(0, d_rows), pl.ds(0, 2 * OWN)]
        gains = [hold[s, pl.ds(d_rows, 16), pl.ds(0, d_rows)].astype(f32) for s in range(nz)]
        gain_ref[...] = jnp.concatenate(gains, axis=1)[:8]
        gain = gain_ref[pl.ds(0, 1), :]
        side_ref[pl.ds(0, local), pl.ds(0, width)] = cot_ref[...]
        turned = [
            hold[s, pl.ds(0, d_rows), pl.ds(2 * OWN, OWN)].astype(f32) for s in range(nz)
        ]
        side_ref[pl.ds(local, OWN), pl.ds(0, width)] = jnp.concatenate(turned, axis=0).T.astype(bf16)
        copies = []
        for tile in range(tiles):
            side, first = (tile * per) // TP, (tile * per) % TP
            at_rows = pl.ds(tile * per * half_rows, per * half_rows)
            block = jnp.concatenate(
                [toks[first + j][pl.ds(side * half_rows, half_rows), :] for j in range(per)], axis=0
            )
            inputs = block.astype(f32)
            hidden = (inputs * norm_scale(inputs) * gain).astype(bf16)
            kept[at_rows, :] = hidden
            copy = pltpu.make_async_copy(kept.at[at_rows, :], hid_ref.at[at_rows, :], sems.at[tile])
            copy.start()
            copies.append(copy)
            pair = nn(hidden, w_ref[:, pl.ds(OWN, OWN)])
            turned = pair * cos_ref[at_rows, :] + swap_halves(pair) * sin_ref[at_rows, :]
            lane = lax.broadcasted_iota(i32, pair.shape, 1)
            kv_ref[at_rows, :] = jnp.where(lane < HEAD, turned, pair).astype(bf16)
        for copy in copies:
            copy.wait()

    return call(
        kernel,
        [
            shape((rows, width), bf16),
            shape((rows, OWN), bf16),
            shape((width, 2 * OWN), bf16),
            shape((local + OWN, TP * OWN), bf16),
            shape((8, width), f32),
        ],
        [at, *tokens, *packs, cosine, sine, cotangent],
        scratch=[
            pltpu.VMEM((nz, pack_rows, lanes), bf16),
            pltpu.VMEM((rows, width), bf16),
            pltpu.SemaphoreType.DMA((tiles,)),
        ],
        limit=60,
        cost=4.0,
        far_out=(0,),
    )


def project_queries(tokens, hidden, w_qkv, cosine, sine):
    local, width = tokens[0].shape
    half_rows = local // 2
    rows = TP * local
    per = 4

    def kernel(*refs):
        toks, refs = refs[:TP], refs[TP:]
        hid_ref, w_ref, cos_ref, sin_ref, x_ref, qt_ref = refs
        for tile in range(2 * TP // per):
            side, first = (tile * per) // TP, (tile * per) % TP
            at_rows = pl.ds(tile * per * half_rows, per * half_rows)
            for j in range(per):
                x_ref[pl.ds((tile * per + j) * half_rows, half_rows), :] = toks[first + j][
                    pl.ds(side * half_rows, half_rows), :
                ]
            query = nn(hid_ref[at_rows, :], w_ref[:, pl.ds(0, OWN)])
            query = query * cos_ref[at_rows, :] + swap_halves(query) * sin_ref[at_rows, :]
            qt_ref[:, at_rows] = (query.astype(bf16).astype(f32) * HEAD**-0.5).T.astype(bf16)

    return call(
        kernel,
        [shape((rows, width), bf16), shape((OWN, rows), bf16)],
        [*tokens, hidden, w_qkv, cosine, sine],
        scalars=0,
        limit=60,
        cost=4.0,
    )


def attention_forward(select, key_base, query_base, turned_query, own_kv, other_kv, half_rows):
    groups = len(own_kv)
    rows = own_kv[0].shape[0]
    half = rows // 2
    blocks = half // half_rows
    wide, deep = 128, 128

    def kernel(sel_ref, key_ref, query_ref, q_ref, *refs):
        own, other = refs[:groups], refs[groups : 2 * groups]
        out_ref, low_ref, lse_ref, kv_ref, kvt_ref, top_ref, mass_ref, place_ref = refs[2 * groups :]
        for head in range(2):
            chosen = sel_ref[head] == 0
            for group in range(groups):

                @pl.when(chosen)
                def take_own():
                    kv_ref[head, group] = own[group][...]
                    kvt_ref[head, group] = own[group][...].T

                @pl.when(jnp.logical_not(chosen))
                def take_other():
                    kv_ref[head, group] = other[group][...]
                    kvt_ref[head, group] = other[group][...].T

        top_ref[...] = jnp.full_like(top_ref, far_below)
        mass_ref[...] = jnp.zeros_like(mass_ref)
        out_ref[...] = jnp.zeros_like(out_ref)

        def one_group(group, unused):
            for head in range(2):
                row = sel_ref[head] * groups + group
                own_rows = pl.ds(head * HEAD, HEAD)
                stat = pl.ds(head, 1)
                place_ref[...] = key_positions(key_ref, row, 0, 2 * blocks, half_rows, 128)
                for k_start in range(0, rows, deep):
                    keys_at = pl.ds(k_start, deep)
                    k_side = k_start // half
                    block = kv_ref[head, group, keys_at, :]
                    values = kvt_ref[head, group, pl.ds(HEAD, HEAD), keys_at]
                    for start in range(k_side * half, rows, wide):
                        lanes = pl.ds(start, wide)
                        turned = q_ref[own_rows, lanes]
                        padded = jnp.concatenate([turned, jnp.zeros_like(turned)], axis=0)
                        scores = nn(block, padded)
                        if start // half == k_side:
                            places = query_positions(
                                query_ref, start // half_rows, wide, half_rows
                            )
                            scores = jnp.where(place_ref[keys_at, :] <= places, scores, far_below)
                        before = top_ref[stat, lanes]
                        top = jnp.maximum(before, jnp.max(scores, axis=0, keepdims=True))
                        weights = jnp.exp(scores - top)
                        fade = jnp.exp(before - top)
                        top_ref[stat, lanes] = top
                        mass_ref[stat, lanes] = mass_ref[stat, lanes] * fade + jnp.sum(
                            weights, axis=0, keepdims=True
                        )
                        out_ref[own_rows, lanes] = out_ref[own_rows, lanes] * fade + nn(
                            values, weights.astype(bf16)
                        )
            return unused

        lax.fori_loop(0, groups, one_group, 0)
        for head in range(2):
            own_rows = pl.ds(head * HEAD, HEAD)
            mass = mass_ref[pl.ds(head, 1), :]
            out_ref[own_rows, :] = out_ref[own_rows, :] / mass
            lse_ref[pl.ds(head, 1), :] = top_ref[pl.ds(head, 1), :] + jnp.log(mass)
        low_ref[...] = out_ref[...].T.astype(bf16)

    return call(
        kernel,
        [shape((OWN, rows), f32), shape((rows, OWN), bf16), shape((2, rows), f32)],
        [select, key_base, query_base, turned_query, *own_kv, *other_kv],
        scalars=3,
        scratch=[
            pltpu.VMEM((2, groups, rows, OWN), bf16),
            pltpu.VMEM((2, groups, OWN, rows), bf16),
            pltpu.VMEM((2, rows), f32),
            pltpu.VMEM((2, rows), f32),
            pltpu.VMEM((rows, 128), i32),
        ],
        limit=60,
        cost=14.0,
    )


def attention_backward(
    select, key_base, query_base, turned_query, own_kv, other_kv, traded, attended, log_mass, half_rows
):
    groups = len(own_kv)
    rows = own_kv[0].shape[0]
    half = rows // 2
    blocks = half // half_rows
    wide, deep = 512, 256

    def kernel(sel_ref, key_ref, query_ref, q_ref, *refs):
        own, other = refs[:groups], refs[groups : 2 * groups]
        refs = refs[2 * groups :]
        local = 2 * half_rows
        parts = [refs[0], refs[1]] + [
            refs[2 + j].at[pl.ds(k * local, local), :] for j in range(TP // 2 - 1) for k in range(2)
        ]
        refs = refs[1 + TP // 2 :]
        att_ref, lse_ref, dq_ref, keep_ref, pass_ref, gb_ref = refs[:6]
        kv_ref, sum_ref, g_ref, rq_ref, rg_ref, delta_ref, pos_ref = refs[6:]
        for group in range(groups):
            kv_ref[0, group] = own[group][...]
            kv_ref[1, group] = other[group][...]
        sum_ref[...] = jnp.zeros_like(sum_ref)
        dq_ref[...] = jnp.zeros_like(dq_ref)
        zeros = jnp.zeros((rows, HEAD), bf16)
        for j in range(0, TP, 2):
            for side in range(2):
                at = pl.ds(side * half + j * half_rows, 2 * half_rows)
                pair = jnp.concatenate(
                    [parts[j + k][pl.ds(side * half_rows, half_rows), :] for k in range(2)], axis=0
                )
                g_ref[:, at] = pair[:, :OWN].T
                gb_ref[at, :] = pair[:, OWN:]
        for head in range(2):
            own_rows = pl.ds(head * HEAD, HEAD)
            rq_ref[head] = jnp.concatenate([q_ref[own_rows, :].T, zeros], axis=1)
            grad = g_ref[own_rows, :]
            rg_ref[head] = jnp.concatenate([zeros, grad.T], axis=1)
            delta_ref[pl.ds(head, 1), :] = jnp.sum(
                grad.astype(f32) * att_ref[own_rows, :], axis=0, keepdims=True
            )

        def one_group(group, unused):
            for head in range(2):
                which = sel_ref[head]
                own_rows = pl.ds(head * HEAD, HEAD)
                stat = pl.ds(head, 1)
                pos_ref[...] = key_positions(
                    key_ref, which * groups + group, 0, 2 * blocks, half_rows, 128
                )
                for k_start in range(0, rows, deep):
                    keys_at = pl.ds(k_start, deep)
                    k_side = k_start // half
                    block = kv_ref[which, group, keys_at, :]
                    turned_keys = block.T[:HEAD]
                    for start in range(k_side * half, rows, wide):
                        lanes = pl.ds(start, wide)
                        turned = q_ref[own_rows, lanes]
                        padded = jnp.concatenate([turned, jnp.zeros_like(turned)], axis=0)
                        scores = nn(block, padded)
                        if start // half == k_side:
                            places = query_positions(
                                query_ref, start // half_rows, wide, half_rows
                            )
                            at = jnp.concatenate([pos_ref[keys_at, :]] * (wide // 128), axis=1)
                            scores = jnp.where(at <= places, scores, far_below)
                        probs = jnp.exp(scores - lse_ref[stat, lanes])
                        grads = g_ref[own_rows, lanes]
                        padded = jnp.concatenate([jnp.zeros_like(grads), grads], axis=0)
                        grad_probs = nn(block, padded)
                        grad_scores = probs * (grad_probs - delta_ref[stat, lanes])
                        probs = probs.astype(bf16)
                        grad_scores = grad_scores.astype(bf16)
                        sum_ref[which, group, keys_at, :] += nn(
                            grad_scores, rq_ref[head, lanes, :]
                        ) + nn(probs, rg_ref[head, lanes, :])
                        dq_ref[own_rows, lanes] += nn(turned_keys, grad_scores)
            return unused

        lax.fori_loop(0, groups, one_group, 0)
        for group in range(groups):
            keep_ref[pl.ds(group * rows, rows), :] = sum_ref[0, group]
            pass_ref[pl.ds(group * rows, rows), :] = sum_ref[1, group].astype(bf16)

    return call(
        kernel,
        [
            shape((OWN, rows), f32),
            shape((groups * rows, OWN), f32),
            shape((groups * rows, OWN), bf16),
            shape((rows, OWN), bf16),
        ],
        [
            select,
            key_base,
            query_base,
            turned_query,
            *own_kv,
            *other_kv,
            *traded,
            attended,
            log_mass,
        ],
        scalars=3,
        scratch=[
            pltpu.VMEM((2, groups, rows, OWN), bf16),
            pltpu.VMEM((2, groups, rows, OWN), f32),
            pltpu.VMEM((OWN, rows), bf16),
            pltpu.VMEM((2, rows, OWN), bf16),
            pltpu.VMEM((2, rows, OWN), bf16),
            pltpu.VMEM((2, rows), f32),
            pltpu.VMEM((rows, 128), i32),
        ],
        limit=28,
        cost=18.0,
    )


def store_blocks(part, tile, per, half_rows, keep_ref, pass_ref, x_first=False):
    side = (tile * per) // TP
    first = lax.rem(tile * per, TP) // 2
    for j in range(per):
        piece = part[j * half_rows : (j + 1) * half_rows]
        place = first // 2 + j if x_first else first + j // 2
        if x_first and j % 2:
            place = first // 2 + j - 1
        row = (2 * place + side) * half_rows
        at = pl.ds(pl.multiple_of(row, half_rows), half_rows)
        target = keep_ref if j % 2 == 0 else pass_ref
        target[at, pl.ds(0, piece.shape[1])] = piece.astype(target.dtype)


def feed_forward(at, inputs, attended, sides, packs, gains, nz):
    rows, width = inputs.shape
    local = rows // TP
    half_rows = local // 2
    half = rows // 2
    d_rows, lanes = packs[0].shape
    ff = lanes // 3
    part_rows = ff // nz
    per = 8
    tile_rows = per * half_rows
    tiles = 2 * TP // per

    def kernel(at_ref, x_ref, *refs):
        att, refs = refs[:TP], refs[TP:]
        extra, refs = refs[:TP], refs[TP:]
        pack, refs = refs[:nz], refs[nz:]
        gain_ref, refs = refs[0], refs[1:]
        resid_out, gk_ref, gp_ref, gain_out, dn_w = refs[:5]
        targets, prod_out, refs = refs[5 : 5 + nz], refs[5 + nz], refs[6 + nz :]
        att_ref, wo_ref, gu_w, cot_ref, hold, acc_gu, acc_dn, blocks, prod_ref, sems = refs
        tp = at_ref[0]
        z = at_ref[1]
        for j in range(TP):
            columns = pl.ds(pl.multiple_of((tp ^ j) * OWN, OWN), OWN)
            wo_ref[columns, :] = extra[j][pl.ds(local, OWN), pl.ds(0, width)]
            for side in range(2):
                for k in range(TP):
                    att_ref[pl.ds(side * half + k * half_rows, half_rows), columns] = att[j][
                        pl.ds(side * half + (k ^ j) * half_rows, half_rows), :
                    ]
                cot_ref[pl.ds(side * half + j * half_rows, half_rows), :] = extra[j][
                    pl.ds(side * half_rows, half_rows), pl.ds(0, width)
                ]
        for s in range(nz):
            hold[z ^ s] = pack[s][...]
        for s in range(nz):
            rows_at = pl.ds(s * d_rows, d_rows)
            gu_w[rows_at, :] = hold[s, :, pl.ds(0, 2 * ff)]
            dn_w[rows_at, :] = jnp.concatenate(
                [
                    hold[b][:, 2 * ff + s * part_rows : 2 * ff + (s + 1) * part_rows]
                    for b in range(nz)
                ],
                axis=1,
            )
        gain = gain_ref[pl.ds(1, 1), :]
        gain_out[...] = jnp.zeros_like(gain_out)
        acc_gu[...] = jnp.zeros_like(acc_gu)
        acc_dn[...] = jnp.zeros_like(acc_dn)

        def copy_of(tile):
            at_rows = pl.ds(pl.multiple_of(tile * tile_rows, tile_rows), tile_rows)
            return pltpu.make_async_copy(
                prod_ref.at[at_rows, :], prod_out.at[at_rows, :], sems.at[tile]
            )

        def one_tile(tile, unused):
            at_rows = pl.ds(pl.multiple_of(tile * tile_rows, tile_rows), tile_rows)
            branch = nt(att_ref[at_rows, :][:, :width], wo_ref[pl.ds(0, width), :])
            resid = x_ref[at_rows, :].astype(f32) + branch
            side = (tile * per) // TP

            @pl.when(lax.rem(tile * per, TP) == 0)
            def keep_own():
                resid_out[pl.ds(pl.multiple_of(side * half_rows, half_rows), half_rows), :] = resid[
                    :half_rows
                ]

            normal = resid * norm_scale(resid)
            hidden = (normal * gain).astype(bf16)
            gate_up = nn(hidden, gu_w[...])
            gate, up = gate_up[:, :ff], gate_up[:, ff:]
            sigmoid = 1.0 / (1.0 + jnp.exp(-gate))
            activated = gate * sigmoid
            product = (activated * up).astype(bf16)
            prod_ref[at_rows, :] = product
            copy_of(tile).start()
            cotangent = cot_ref[at_rows, :]
            grad_product = nn(cotangent, dn_w[...])
            grad_gate = grad_product * up * sigmoid * (1.0 + gate * (1.0 - sigmoid))
            grad_gu = jnp.concatenate([grad_gate, grad_product * activated], axis=1).astype(bf16)
            partial = nt(grad_gu, gu_w[...])
            gain_out[pl.ds(0, 1), :] += jnp.sum(partial * normal, axis=0, keepdims=True)
            store_blocks(partial, tile, per, half_rows, gk_ref, gp_ref)
            acc_gu[...] += tn(hidden, grad_gu)
            acc_dn[...] += tn(cotangent, product)
            return unused

        lax.fori_loop(0, tiles, one_tile, 0)
        for b in range(nz):
            blocks[b, :, pl.ds(0, 2 * ff)] = acc_gu[pl.ds(b * d_rows, d_rows), :]
            blocks[b, :, pl.ds(2 * ff, ff)] = jnp.concatenate(
                [
                    acc_dn[pl.ds(s * d_rows, d_rows), :][:, b * part_rows : (b + 1) * part_rows]
                    for s in range(nz)
                ],
                axis=1,
            )
        for s in range(nz):
            targets[s][...] = blocks[z ^ s].astype(targets[s].dtype)
        for tile in range(tiles):
            copy_of(tile).wait()

    return call(
        kernel,
        [
            shape((local, width), f32),
            shape((TP // 2 * local, width), bf16),
            shape((TP // 2 * local, TP * OWN), bf16),
            shape((8, width), f32),
            shape((width, ff), bf16),
        ]
        + [shape((d_rows, lanes), f32 if s % 2 == 0 else bf16) for s in range(nz)]
        + [shape((rows, ff), bf16)],
        [at, inputs, *attended, *sides, *packs, gains],
        scratch=[
            pltpu.VMEM((rows, TP * OWN), bf16),
            pltpu.VMEM((TP * OWN, width), bf16),
            pltpu.VMEM((width, 2 * ff), bf16),
            pltpu.VMEM((rows, width), bf16),
            pltpu.VMEM((nz, d_rows, lanes), bf16),
            pltpu.VMEM((width, 2 * ff), f32),
            pltpu.VMEM((width, ff), f32),
            pltpu.VMEM((nz, d_rows, lanes), f32),
            pltpu.VMEM((rows, ff), bf16),
            pltpu.SemaphoreType.DMA((tiles,)),
        ],
        limit=44,
        cost=17.0,
        far_out=(5 + nz,),
    )


def feed_forward_rest(at, attended, sides, product, w_down):
    rows = attended[0].shape[0]
    width, ff = w_down.shape
    local = rows // TP
    half_rows = local // 2
    half = rows // 2
    per = 4
    tile_rows = per * half_rows

    def kernel(at_ref, *refs):
        att, refs = refs[:TP], refs[TP:]
        extra, refs = refs[:TP], refs[TP:]
        prod_ref, dn_w, att_out, wo_out, lk_ref, lp_ref = refs
        tp = at_ref[0]
        for j in range(TP):
            columns = pl.ds(pl.multiple_of((tp ^ j) * OWN, OWN), OWN)
            wo_out[columns, :] = extra[j][pl.ds(local, OWN), pl.ds(0, width)]
            for side in range(2):
                for k in range(TP):
                    att_out[pl.ds(side * half + k * half_rows, half_rows), columns] = att[j][
                        pl.ds(side * half + (k ^ j) * half_rows, half_rows), :
                    ]

        def one_tile(tile, unused):
            at_rows = pl.ds(pl.multiple_of(tile * tile_rows, tile_rows), tile_rows)
            part = nt(prod_ref[at_rows, :], dn_w[...])
            store_blocks(part, tile, per, half_rows, lk_ref, lp_ref)
            return unused

        lax.fori_loop(0, 2 * TP // per, one_tile, 0)

    return call(
        kernel,
        [
            shape((rows, TP * OWN), bf16),
            shape((TP * OWN, width), bf16),
            shape((TP // 2 * local, width), bf16),
            shape((TP // 2 * local, TP * OWN), bf16),
        ],
        [at, *attended, *sides, product, w_down],
        limit=24,
        cost=5.0,
    )


def add_crossed(keep, crossed, count, tail=None):
    local, width = keep.shape[0] // count, keep.shape[1]
    tails = [] if tail is None else [tail]
    more = 0 if tail is None else tail.shape[0]

    def kernel(keep_ref, cross_ref, *refs):
        own_ref, *sends = refs[len(tails) :]
        for j in range(count):
            at = pl.ds(j * local, local)
            target = own_ref if j == 0 else sends[j - 1]
            target[pl.ds(0, local), pl.ds(0, width)] = (
                keep_ref[at, :].astype(f32) + cross_ref[at, pl.ds(0, width)].astype(f32)
            ).astype(target.dtype)
        if tails:
            sends[-1][pl.ds(local, more), pl.ds(0, width)] = refs[0][...]

    return call(
        kernel,
        [shape((local, width), f32)]
        + [shape((local, width), bf16)] * (count - 2)
        + [shape((local + more, TP * OWN if tails else width), bf16)],
        [keep, crossed, *tails],
        scalars=0,
        limit=12,
        cost=1.0,
    )


def branch_gradient(at, sums, resid, cotangent, w_out, gains):
    local, width = resid.shape

    def kernel(at_ref, *refs):
        parts, refs = refs[: len(sums)], refs[len(sums) :]
        resid_ref, cot_ref, wo_ref, gain_ref, grad_ref, keep_ref, pass_ref, ga_ref, gb_ref = refs
        tp = at_ref[0]
        grad_hidden = parts[0][...]
        for part in parts[1:]:
            grad_hidden = grad_hidden + part[...].astype(f32)
        resid = resid_ref[...]
        scale = norm_scale(resid)
        normal = resid * scale
        grad = grad_hidden * gain_ref[pl.ds(1, 1), :]
        grad = scale * (grad - normal * jnp.mean(grad * normal, axis=1, keepdims=True))
        grad = grad + cot_ref[...].astype(f32)
        grad_ref[...] = grad
        low = grad.astype(bf16)
        gb_ref[...] = jnp.zeros_like(gb_ref)
        gb_ref[:, pl.ds(0, width)] = low
        ga_ref[...] = jnp.zeros_like(ga_ref)
        ga_ref[:, pl.ds(0, width)] = nn(low, wo_ref[pl.ds(0, width), :]).astype(bf16)
        for j in range(TP):
            columns = pl.ds(pl.multiple_of((tp ^ j) * OWN, OWN), OWN)
            target = keep_ref if j % 2 == 0 else pass_ref
            rows = pl.ds((j // 2) * local, local)
            target[rows, pl.ds(0, OWN)] = ga_ref[:, columns]
            target[rows, pl.ds(OWN, OWN)] = gb_ref[:, columns]

    blocks = shape((TP // 2 * local, 2 * OWN), bf16)
    return call(
        kernel,
        [shape((local, width), f32), blocks, blocks],
        [at, *sums, resid, cotangent, w_out, gains],
        scratch=[pltpu.VMEM((local, TP * OWN), bf16), pltpu.VMEM((local, TP * OWN), bf16)],
        limit=16,
        cost=3.0,
    )


def pair_up(keep, crossed, count):
    local, width = keep.shape[0] // count, keep.shape[1]

    def kernel(keep_ref, cross_ref, *outs):
        for j in range(1, count):
            at = pl.ds(j * local, local)
            outs[j - 1][pl.ds(0, local), :] = keep_ref[at, :]
            outs[j - 1][pl.ds(local, local), :] = cross_ref[at, :]

    return call(
        kernel,
        [shape((2 * local, width), bf16)] * (count - 1),
        [keep, crossed],
        scalars=0,
        limit=8,
        cost=0.7,
    )


def projection_gradient(
    at, grad_query, grad_kv, inputs, hidden, w_qkv, gain_sums, cosine, sine, grad_out, nz
):
    rows, width = inputs.shape
    local = rows // TP
    half_rows = local // 2
    d_rows = width // nz
    per = 4
    tile_rows = per * half_rows
    pieces = len(grad_kv)

    def kernel(at_ref, dq_ref, *refs):
        kvs, refs = refs[:pieces], refs[pieces:]
        x_ref, hid_ref, w_ref, gain_two_ref, cos_ref, sin_ref, wo_ref = refs[:7]
        keep_ref, pass_ref, own_ref = refs[7:10]
        sends, refs = refs[10 : 10 + nz - 1], refs[10 + nz - 1 :]
        turn_ref, acc_ref, gain_acc, hold = refs
        z = at_ref[1]
        turn_ref[...] = dq_ref[...].T * HEAD**-0.5
        acc_ref[...] = jnp.zeros_like(acc_ref)
        gain_acc[...] = jnp.zeros_like(gain_acc)

        def one_tile(tile, unused):
            at_rows = pl.ds(pl.multiple_of(tile * tile_rows, tile_rows), tile_rows)
            cos, sin = cos_ref[at_rows, :], sin_ref[at_rows, :]
            query = turn_ref[at_rows, :]
            query = query * cos - swap_halves(query) * sin
            pair = kvs[0][at_rows, :].astype(f32)
            for piece in kvs[1:]:
                pair = pair + piece[at_rows, :].astype(f32)
            turned = pair * cos - swap_halves(pair) * sin
            lane = lax.broadcasted_iota(i32, pair.shape, 1)
            pair = jnp.where(lane < HEAD, turned, pair)
            grad = jnp.concatenate([query, pair], axis=1).astype(bf16)
            partial = nt(grad, w_ref[...])
            x = x_ref[at_rows, :].astype(f32)
            gain_acc[pl.ds(0, 1), :] += jnp.sum(partial * (x * norm_scale(x)), axis=0, keepdims=True)
            store_blocks(partial, tile, per, half_rows, keep_ref, pass_ref, True)
            acc_ref[...] += tn(hid_ref[at_rows, :], grad)
            return unused

        lax.fori_loop(0, 2 * TP // per, one_tile, 0)
        hold[...] = jnp.zeros_like(hold)
        for s in range(nz):
            columns = slice(s * d_rows, (s + 1) * d_rows)
            hold[s, pl.ds(0, 1), pl.ds(0, d_rows)] = gain_acc[pl.ds(0, 1), :][:, columns]
            hold[s, pl.ds(1, 1), pl.ds(0, d_rows)] = gain_two_ref[pl.ds(0, 1), :][:, columns]
        for s in range(nz):
            block = z ^ s
            target = own_ref if s == 0 else sends[s - 1]
            rows_at = pl.ds(pl.multiple_of(block * d_rows, 8), d_rows)
            part = pl.ds(0, d_rows)
            target[part, pl.ds(0, 2 * OWN)] = acc_ref[rows_at, :].astype(target.dtype)
            target[part, pl.ds(2 * OWN, OWN)] = wo_ref[rows_at, :].astype(target.dtype)
            target[pl.ds(d_rows, 16), :] = hold[block].astype(target.dtype)

    return call(
        kernel,
        [
            shape((TP // 2 * local, width), bf16),
            shape((TP // 2 * local, TP * OWN), bf16),
            shape((d_rows + 16, 3 * OWN), f32),
        ]
        + [shape((d_rows + 16, 3 * OWN), bf16)] * (nz - 1),
        [at, grad_query, *grad_kv, inputs, hidden, w_qkv, gain_sums, cosine, sine, grad_out],
        scratch=[
            pltpu.VMEM((rows, OWN), f32),
            pltpu.VMEM((width, 2 * OWN), f32),
            pltpu.VMEM((8, width), f32),
            pltpu.VMEM((nz, 16, 3 * OWN), f32),
        ],
        limit=32,
        cost=8.0,
    )


def token_gradient(sums, tokens, grad_resid, gains):
    local, width = tokens.shape

    def kernel(*refs):
        parts, refs = refs[: len(sums)], refs[len(sums) :]
        x_ref, grad_ref, gain_ref, out_ref = refs
        grad_hidden = parts[0][...]
        for part in parts[1:]:
            grad_hidden = grad_hidden + part[...].astype(f32)
        x = x_ref[...].astype(f32)
        scale = norm_scale(x)
        normal = x * scale
        grad = grad_hidden * gain_ref[pl.ds(0, 1), :]
        grad = scale * (grad - normal * jnp.mean(grad * normal, axis=1, keepdims=True))
        out_ref[...] = (grad + grad_ref[...]).T

    return call(
        kernel,
        [shape((width, local), f32)],
        [*sums, tokens, grad_resid, gains],
        scalars=0,
        limit=8,
        cost=1.0,
    )[0].T


def layer_output(near, arrived, resid):
    local, width = resid.shape
    start = arrived.shape[0] - local

    def kernel(near_ref, in_ref, resid_ref, out_ref):
        total = resid_ref[...] + near_ref[...] + in_ref[pl.ds(start, local), pl.ds(0, width)].astype(f32)
        out_ref[...] = total.T.astype(bf16)

    turned = shape(resid.shape[::-1], bf16)
    return call(kernel, [turned], [near, arrived, resid], scalars=0, limit=8, cost=1.0)[0].T


def first_sum(own, arrived):
    def kernel(own_ref, in_ref, out_ref):
        out_ref[...] = (own_ref[...] + in_ref[...].astype(f32)).astype(bf16)

    return call(
        kernel, [shape(own.shape, bf16)], [own, arrived], scalars=0, limit=8, cost=1.0
    )[0]


def last_sum(own, *arrived):
    rows, lanes = own.shape

    def kernel(own_ref, *refs):
        total = own_ref[...]
        for ref in refs[:-1]:
            total = total + ref[...].astype(f32)
        refs[-1][:, pl.ds(0, lanes)] = total.astype(bf16)

    return call(
        kernel, [shape((rows, TP * OWN), bf16)], [own, *arrived], scalars=0, limit=8, cost=1.0
    )[0]


def ff_outputs(at, mine, by_x, by_y, by_xy, odd, ff_z, nz):
    d_rows = mine.shape[0]
    part = ff_z // TP
    ff = part * nz

    def kernel(at_ref, m_ref, x_ref, y_ref, xy_ref, odd_ref, gate_ref, up_ref, down_ref, hold):
        tp = at_ref[0]
        lanes = pl.ds(0, 3 * ff)
        for j, ref in enumerate((m_ref, x_ref, y_ref, xy_ref)):
            hold[tp ^ (2 * j)] = ref[:, lanes]
        for j in range(TP // 2):
            hold[tp ^ (2 * j + 1)] = odd_ref[pl.ds(d_rows * j, d_rows), lanes]
        for s in range(nz):
            for start in (s * part, ff + s * part, 2 * ff + s * part):
                block = jnp.concatenate(
                    [hold[c][:, start : start + part] for c in range(TP)], axis=1
                ).astype(f32)
                if start < ff:
                    gate_ref[:, pl.ds(s * ff_z, ff_z)] = block
                elif start < 2 * ff:
                    up_ref[:, pl.ds(s * ff_z, ff_z)] = block
                else:
                    down_ref[pl.ds(s * d_rows, d_rows), :] = block

    gate, up, down = call(
        kernel,
        [
            shape((d_rows, nz * ff_z), f32),
            shape((d_rows, nz * ff_z), f32),
            shape((nz * d_rows, ff_z), f32),
        ],
        [at, mine, by_x, by_y, by_xy, odd],
        scratch=[pltpu.VMEM((TP, d_rows, 3 * ff), bf16)],
        limit=32,
        cost=7.0,
    )
    return gate, up, down.T


def wide_outputs(at, slots, width):
    d_rows = slots[0].shape[0] - 16

    def kernel(at_ref, *refs):
        parts, (q_ref, o_ref, hold) = refs[:TP], refs[TP:]
        tp = at_ref[0]
        for j in range(TP):
            hold[tp ^ j] = parts[j][...]
        for ref, start in ((q_ref, 0), (o_ref, 2 * OWN)):
            heads = [hold[c][:d_rows, start : start + OWN] for c in range(TP)]
            ref[...] = jnp.concatenate(heads, axis=1)[:, :width].astype(f32)

    return call(
        kernel,
        [shape((d_rows, width), f32), shape((d_rows, width), f32)],
        [at, *slots],
        scratch=[pltpu.VMEM((TP, d_rows + 16, 3 * OWN), bf16)],
        limit=12,
        cost=0.01,
    )


def narrow_outputs(at, slots):
    d_rows = slots[0].shape[0] - 16

    def kernel(at_ref, *refs):
        parts, (k_ref, v_ref, one_ref, two_ref, hold) = refs[:TP], refs[TP:]
        tp = at_ref[0]
        total = jnp.zeros((16, d_rows), f32)
        for j in range(TP):
            hold[tp ^ j] = parts[j][pl.ds(0, d_rows), pl.ds(OWN, OWN)].astype(f32)
            total = total + parts[j][pl.ds(d_rows, 16), pl.ds(0, d_rows)].astype(f32)
        one_ref[...] = total[0:1]
        two_ref[...] = total[1:2]
        kv = [hold[c] for c in range(TP)]
        kv = [kv[0], kv[1] + kv[2], kv[3] + kv[4], kv[5], kv[6]]
        for c in range(KV_HEADS):
            turned = kv[c].T
            k_ref[pl.ds(c * HEAD, HEAD), :] = turned[:HEAD]
            v_ref[pl.ds(c * HEAD, HEAD), :] = turned[HEAD:]

    key, value, one, two = call(
        kernel,
        [
            shape((KV_HEADS * HEAD, d_rows), f32),
            shape((KV_HEADS * HEAD, d_rows), f32),
            shape((1, d_rows), f32),
            shape((1, d_rows), f32),
        ],
        [at, *slots],
        scratch=[pltpu.VMEM((TP, d_rows, OWN), f32)],
        limit=12,
        cost=0.01,
    )
    return key.T, value.T, one, two


def body(
    tokens,
    pair_order,
    gain_attn,
    gain_mlp,
    w_query,
    w_key,
    w_value,
    w_out,
    w_gate,
    w_up,
    w_down,
    cotangent,
):
    local_rows, width = tokens.shape
    half_rows = local_rows // 2
    nz = lax.axis_size("fsdp")
    outer = lax.axis_size("ctx") // TP
    count = lax.axis_size(AXES)
    groups = outer * nz
    me = lax.axis_index(AXES)
    z = lax.axis_index("fsdp")
    tp = lax.axis_index("ctx") % TP
    kv_index = (4 * (tp // 2)) // GROUP + tp % 2
    at = jnp.stack([tp, z, kv_index]).astype(i32)
    send = functools.partial(exchange, count=count)
    group_mask = [(g // nz) * TP * nz + g % nz for g in range(groups)]

    def after(value, *others):
        return lax.optimization_barrier((value, *others))[0]

    def level(*arrays):
        return list(lax.optimization_barrier(arrays))

    def gather_even(block):
        return [block] + [send(block, j * nz) for j in range(2, TP, 2)]

    def gather_odd(even):
        return [piece for e in even for piece in (e, send(e, nz))]

    def scatter_far(pieces):
        return [send(piece, 2 * (j + 1) * nz) for j, piece in enumerate(pieces)]

    def from_z(block):
        return [block] + [send(block, s) for s in range(1, nz)]

    pack_one = slice_attention_weights(at, w_query, w_key, w_value, w_out, gain_attn, gain_mlp)
    token_slots = gather_odd(level(*gather_even(tokens)))
    pack_two = slice_ff_weights(after(at, pack_one), w_gate, w_up, w_down, nz)
    pack_one = from_z(pack_one)

    slot_of = jnp.array([[m | (j * nz) for j in range(TP)] for m in group_mask], dtype=i32)
    low = pair_order[me ^ slot_of]
    base = jnp.stack([low, 2 * count - 1 - low], axis=1) * half_rows
    query_base = base[0].reshape(2 * TP)
    partner = jnp.array([j ^ 1 for j in range(TP)], dtype=i32)
    key_base = jnp.stack([base, base[:, :, partner]]).reshape(2 * groups, 2 * TP)
    places = (query_base[:, None] + jnp.arange(half_rows, dtype=i32)[None, :]).reshape(-1)
    lane = jnp.arange(OWN)
    freqs = base_theta ** (-2.0 * (lane % (HEAD // 2)).astype(f32) / HEAD)
    angles = places.astype(f32)[:, None] * freqs[None, :]
    cosine = jnp.cos(angles)
    sine = jnp.sin(angles) * jnp.where(lane % HEAD < HEAD // 2, -1.0, 1.0)[None, :]
    select = jnp.where((2 * tp + jnp.arange(2)) // GROUP == kv_index, 0, 1).astype(i32)

    mask_x, mask_y = 2 * nz, 4 * nz
    hidden_one, kv, w_qkv, side, gains = project_keys(
        after(at, pack_two, select, key_base, query_base),
        token_slots,
        pack_one,
        cosine,
        sine,
        cotangent,
    )
    own_kv = [kv] + [send(kv, m) for m in group_mask[1:]]
    side_x, side_y = send(side, mask_x), send(side, mask_y)
    inputs, turned_query = project_queries(
        token_slots, after(hidden_one, kv), w_qkv, cosine, sine
    )
    side_x, side_y, inputs, turned_query, *own_kv = level(
        side_x, side_y, inputs, turned_query, *own_kv
    )
    other_kv = level(*[send(slot, nz) for slot in own_kv])
    one, near = send(after(pack_two, *own_kv), 1), send(after(pack_two, *own_kv), 2)
    side_xy = send(side_x, mask_y)
    side_odd, odd_x = send(after(side, *other_kv), nz), send(after(side_x, *other_kv), nz)
    attended, attended_own, log_mass = attention_forward(
        select, key_base, query_base, turned_query, own_kv, other_kv, half_rows
    )
    attended_own, near, one, side_xy, side_odd, odd_x = level(
        attended_own, near, one, side_xy, side_odd, odd_x
    )
    far, side_xy, *even = level(send(near, 1), side_xy, *gather_even(attended_own))
    attended_slots = gather_odd(even)
    packs = [pack_two, one, near, far]
    odd_y = send(after(side_y, side_xy), nz)
    sides = [side, side_odd, side_x, odd_x, side_y, odd_y, side_xy, send(side_xy, nz)]

    resid, grad_keep, grad_pass, gain_sums, w_down_own, *ff_blocks, product = feed_forward(
        at, inputs, attended_slots, sides, packs, gains, nz
    )
    ff_own, ff_one, ff_two, ff_three = ff_blocks
    first, *rest = add_crossed(grad_keep, send(grad_pass, nz), TP // 2)
    attended_low, w_out_all, out_keep, out_pass, ff_three, first, *rest = level(
        *feed_forward_rest(after(at, first), attended_slots, sides, product, w_down_own),
        send(after(ff_three, first), 1),
        first,
        *scatter_far(rest),
    )
    grad_resid, trade_keep, trade_pass = branch_gradient(
        at, [first, *rest], resid, cotangent, w_out_all, gains
    )
    crossed, out_crossed = level(send(trade_pass, nz), send(after(out_pass, first), nz))
    pairs = level(*scatter_far(pair_up(trade_keep, crossed, TP // 2)))
    out_near, out_far = add_crossed(out_keep, out_crossed, 2)
    ff_one = send(after(ff_one, crossed), 1)
    ff_two = send(first_sum(ff_two, ff_three), 2)
    out_far = send(after(out_far, *pairs), mask_y)

    grad_query, kv_keep, kv_pass, branch_columns = attention_backward(
        after(select, out_near),
        key_base,
        query_base,
        turned_query,
        own_kv,
        other_kv,
        [trade_keep, crossed, *pairs],
        attended,
        log_mass,
        half_rows,
    )
    kv_pass, ff_one, ff_two, out_far = level(kv_pass, ff_one, ff_two, out_far)
    kv_crossed = send(kv_pass, nz)
    first, *rest = add_crossed(kv_keep, kv_crossed, groups)
    grad_out = tn(attended_low[:, :width], after(branch_columns, rest[0]))
    ff_total = last_sum(after(ff_own, grad_out), ff_one, ff_two)

    for step in range(outer.bit_length() - 1):
        crossing = send(ff_total, TP * nz << step).astype(f32)
        ff_total = (ff_total.astype(f32) + crossing).astype(bf16)
    out_near, out_far = add_crossed(after(out_near, rest[0]), out_far, 2)
    ff_x, ff_y, *grad_kv = level(
        send(ff_total, mask_x),
        send(ff_total, mask_y),
        *[send(piece, m) for piece, m in zip(rest, group_mask[1:])],
    )

    last_keep, last_pass, last_own, *last_sends = projection_gradient(
        at,
        grad_query,
        [first, *grad_kv],
        inputs,
        hidden_one,
        w_qkv,
        gain_sums,
        cosine,
        sine,
        grad_out,
        nz,
    )
    near, far = add_crossed(last_keep, send(last_pass, nz), 2, out_far)
    ff_xy, far, *arrived = level(
        send(after(ff_x, last_own), mask_y),
        send(far, mask_x),
        *[send(piece, s + 1) for s, piece in enumerate(last_sends)],
    )
    layer_out = layer_output(out_near, far, resid)
    near, far = add_crossed(near, far, 2)
    last_total = last_own
    for piece in arrived:
        last_total = last_total + piece.astype(f32)
    for step in range(outer.bit_length() - 1):
        last_total = last_total + send(last_total.astype(bf16), TP * nz << step).astype(f32)
    last_total = last_total.astype(bf16)
    ff_slots = [ff_total, ff_x, ff_y, ff_xy]
    ff_slots.append(send(jnp.concatenate(ff_slots, axis=0), nz))
    grad_gate, grad_up, grad_down = ff_outputs(at, *ff_slots, w_down.shape[0], nz)
    far = send(far, mask_y)
    grad_gate, *even = level(grad_gate, *gather_even(last_total))
    last_slots = gather_odd(even)
    grad_w_query, grad_out = wide_outputs(at, last_slots, width)
    near = after(near, grad_w_query, grad_out)
    grad_tokens = token_gradient([near, far], tokens, grad_resid, gains)
    grad_w_key, grad_w_value, gain_one, gain_two = narrow_outputs(
        after(at, grad_tokens, layer_out), last_slots
    )
    return (
        layer_out,
        grad_tokens,
        gain_one.reshape(-1),
        gain_two.reshape(-1),
        grad_w_query,
        grad_w_key,
        grad_w_value,
        grad_out,
        grad_gate,
        grad_up,
        grad_down,
    )


def solution(mesh):
    return jax.shard_map(
        body,
        mesh=mesh,
        in_specs=(
            P(("ctx", "fsdp"), None),
            P(),
            P("fsdp"),
            P("fsdp"),
            P("fsdp", None),
            P("fsdp", None),
            P("fsdp", None),
            P("fsdp", None),
            P("fsdp", None),
            P("fsdp", None),
            P("fsdp", None),
            P(("ctx", "fsdp"), None),
        ),
        out_specs=(
            P(("ctx", "fsdp"), None),
            P(("ctx", "fsdp"), None),
            P("fsdp"),
            P("fsdp"),
            P("fsdp", None),
            P("fsdp", None),
            P("fsdp", None),
            P("fsdp", None),
            P("fsdp", None),
            P("fsdp", None),
            P("fsdp", None),
        ),
        check_vma=False,
    )
```

```python
import functools

import jax
import jax.numpy as jnp
from jax import lax
from jax.experimental import pallas as pl
from jax.experimental.pallas import tpu as pltpu
from jax.sharding import PartitionSpec as P

HEADS = 15
KV_HEADS = 5
HEAD = 64
TP = 8
GROUP = HEADS // KV_HEADS
OWN = 2 * HEAD
epsilon = 1e-05
base_theta = 100000.0
far_below = -1e30
f32 = jnp.float32
bf16 = jnp.bfloat16
i32 = jnp.int32
AXES = ("ctx", "fsdp")
MIB = 1024 * 1024
smem = pl.BlockSpec(memory_space=pltpu.SMEM)
vmem = pl.BlockSpec(memory_space=pltpu.VMEM)


def exchange(array, mask, count):
    return lax.ppermute(array, AXES, [(i, i ^ mask) for i in range(count)])


def nn(left, right):
    return lax.dot_general(left, right, (((1,), (0,)), ((), ())), preferred_element_type=f32)


def tn(left, right):
    return lax.dot_general(left, right, (((0,), (0,)), ((), ())), preferred_element_type=f32)


def nt(left, right):
    return lax.dot_general(left, right, (((1,), (1,)), ((), ())), preferred_element_type=f32)


def shape(dims, dtype):
    return jax.ShapeDtypeStruct(dims, dtype)


def call(kernel, outs, inputs, scalars=1, scratch=(), limit=56, cost=1.0, far=(), far_out=()):
    specs = [smem] * scalars + [vmem] * (len(inputs) - scalars)
    for i in far:
        specs[i] = pl.BlockSpec(memory_space=pltpu.HBM)
    out_specs = [vmem for unused in outs]
    for i in far_out:
        out_specs[i] = pl.BlockSpec(memory_space=pltpu.HBM)
    return pl.pallas_call(
        kernel,
        out_shape=tuple(outs),
        in_specs=specs,
        out_specs=tuple(out_specs),
        scratch_shapes=list(scratch),
        compiler_params=pltpu.CompilerParams(vmem_limit_bytes=limit * MIB),
        cost_estimate=pl.CostEstimate(
            flops=int(cost * 1e9), bytes_accessed=int(cost * 1e6), transcendentals=0
        ),
    )(*inputs)


def one_hot(rows, columns, start):
    row = lax.broadcasted_iota(i32, (rows, columns), 0)
    column = lax.broadcasted_iota(i32, (rows, columns), 1)
    return jnp.where(row == column + start, 1.0, 0.0).astype(bf16)


def query_positions(base_ref, at, width, half_rows):
    lane = lax.broadcasted_iota(i32, (1, width), 1)
    place = jnp.zeros((1, width), i32)
    for block in range(width // half_rows):
        start = base_ref[at + block] - block * half_rows
        place = jnp.where(lane >= block * half_rows, start + lane, place)
    return place


def key_positions(base_ref, row, at, count, half_rows, width):
    offset = lax.broadcasted_iota(i32, (half_rows, width), 0)
    return jnp.concatenate([offset + base_ref[row, at + b] for b in range(count)], axis=0)


def swap_halves(matrix):
    lane = lax.broadcasted_iota(i32, matrix.shape, 1)
    ahead = pltpu.roll(matrix, matrix.shape[1] - HEAD // 2, 1)
    behind = pltpu.roll(matrix, HEAD // 2, 1)
    return jnp.where(lane % HEAD < HEAD // 2, ahead, behind)


def norm_scale(matrix):
    return lax.rsqrt(jnp.mean(matrix * matrix, axis=1, keepdims=True) + epsilon)


def slice_attention_weights(at, w_query, w_key, w_value, w_out, gain_one, gain_two):
    d_rows, width = w_query.shape
    lanes = 2 * OWN + OWN
    rest = width - (TP - 1) * OWN

    def kernel(at_ref, q_ref, k_ref, v_ref, o_ref, g1_ref, g2_ref, out_ref, cols, heads, whole, sems):
        tp = at_ref[0]
        kv = at_ref[2]
        wides, narrows = (q_ref, o_ref), (k_ref, v_ref)

        columns = pl.ds(pl.multiple_of(tp * OWN, OWN), OWN)
        rows = pl.ds(pl.multiple_of(kv * HEAD, HEAD), HEAD)

        def wide_copies():
            return [
                pltpu.make_async_copy(ref.at[:, columns], cols.at[i], sems.at[i])
                for i, ref in enumerate(wides)
            ]

        def whole_copies():
            return [
                pltpu.make_async_copy(ref, whole.at[i], sems.at[i]) for i, ref in enumerate(wides)
            ]

        def head_copies():
            return [
                pltpu.make_async_copy(ref.at[rows, :], heads.at[i], sems.at[2 + i])
                for i, ref in enumerate(narrows)
            ]

        @pl.when(tp < TP - 1)
        def most():
            for copy in wide_copies():
                copy.start()

        @pl.when(tp == TP - 1)
        def last():
            for copy in whole_copies():
                copy.start()

        @pl.when(kv < KV_HEADS)
        def real():
            for copy in head_copies():
                copy.start()

        @pl.when(kv >= KV_HEADS)
        def none():
            heads[...] = jnp.zeros_like(heads)

        @pl.when(tp < TP - 1)
        def most_came():
            for copy in wide_copies():
                copy.wait()

        @pl.when(tp == TP - 1)
        def last_came():
            for copy in whole_copies():
                copy.wait()
            for i in range(2):
                cols[i] = jnp.zeros((d_rows, OWN), bf16)
                cols[i, :, pl.ds(0, rest)] = whole[i, :, pl.ds(width - rest, rest)]

        @pl.when(kv < KV_HEADS)
        def real_came():
            for copy in head_copies():
                copy.wait()

        out_ref[pl.ds(0, d_rows), pl.ds(0, OWN)] = cols[0]
        turned = jnp.concatenate([heads[0], heads[1]], axis=0).astype(f32).T
        out_ref[pl.ds(0, d_rows), pl.ds(OWN, OWN)] = turned.astype(bf16)
        out_ref[pl.ds(0, d_rows), pl.ds(2 * OWN, OWN)] = cols[1]
        out_ref[pl.ds(d_rows, 16), :] = jnp.zeros((16, lanes), bf16)
        out_ref[d_rows, pl.ds(0, d_rows)] = g1_ref[...]
        out_ref[d_rows + 1, pl.ds(0, d_rows)] = g2_ref[...]

    return call(
        kernel,
        [shape((d_rows + 16, lanes), bf16)],
        [at, w_query, w_key.T, w_value.T, w_out, gain_one, gain_two],
        scratch=[
            pltpu.VMEM((2, d_rows, OWN), bf16),
            pltpu.VMEM((2, HEAD, d_rows), bf16),
            pltpu.VMEM((2, d_rows, width), bf16),
            pltpu.SemaphoreType.DMA((4,)),
        ],
        limit=60,
        cost=2.0,
        far=(1, 2, 3, 4),
    )[0]


def slice_ff_weights(at, w_gate, w_up, w_down, nz):
    d_rows = w_gate.shape[0]
    ff_z, width = w_down.shape
    part = ff_z // TP
    own = part * nz


    def kernel(at_ref, g_ref, u_ref, d_ref, out_ref):
        pick = one_hot(ff_z, part, at_ref[0] * part)
        for ref, start in ((g_ref, 0), (u_ref, own)):
            pieces = [nn(ref[:, pl.ds(s * ff_z, ff_z)], pick) for s in range(nz)]
            out_ref[:, pl.ds(start, own)] = jnp.concatenate(pieces, axis=1).astype(bf16)
        pieces = [nn(d_ref[pl.ds(s * d_rows, d_rows), :], pick) for s in range(nz)]
        out_ref[:, pl.ds(2 * own, own)] = jnp.concatenate(pieces, axis=1).astype(bf16)

    return call(
        kernel,
        [shape((d_rows, 3 * own), bf16)],
        [at, w_gate, w_up, w_down.T],
        limit=16,
        cost=4.0,
    )[0]


def project_keys(at, tokens, packs, cosine, sine, cotangent):
    local, width = tokens[0].shape
    half_rows = local // 2
    rows = TP * local
    nz = len(packs)
    pack_rows, lanes = packs[0].shape
    d_rows = pack_rows - 16
    per = 4
    tiles = 2 * TP // per

    def kernel(at_ref, *refs):
        toks, refs = refs[:TP], refs[TP:]
        pack, refs = refs[:nz], refs[nz:]
        cos_ref, sin_ref, cot_ref, hid_ref, kv_ref, w_ref, side_ref, gain_ref, hold, kept, sems = refs
        z = at_ref[1]
        for s in range(nz):
            hold[z ^ s] = pack[s][...]
        for s in range(nz):
            w_ref[pl.ds(s * d_rows, d_rows), :] = hold[s, pl.ds(0, d_rows), pl.ds(0, 2 * OWN)]
        gains = [hold[s, pl.ds(d_rows, 16), pl.ds(0, d_rows)].astype(f32) for s in range(nz)]
        gain_ref[...] = jnp.concatenate(gains, axis=1)[:8]
        gain = gain_ref[pl.ds(0, 1), :]
        side_ref[pl.ds(0, local), pl.ds(0, width)] = cot_ref[...]
        turned = [
            hold[s, pl.ds(0, d_rows), pl.ds(2 * OWN, OWN)].astype(f32) for s in range(nz)
        ]
        side_ref[pl.ds(local, OWN), pl.ds(0, width)] = jnp.concatenate(turned, axis=0).T.astype(bf16)
        copies = []
        for tile in range(tiles):
            side, first = (tile * per) // TP, (tile * per) % TP
            at_rows = pl.ds(tile * per * half_rows, per * half_rows)
            block = jnp.concatenate(
                [toks[first + j][pl.ds(side * half_rows, half_rows), :] for j in range(per)], axis=0
            )
            inputs = block.astype(f32)
            hidden = (inputs * norm_scale(inputs) * gain).astype(bf16)
            kept[at_rows, :] = hidden
            copy = pltpu.make_async_copy(kept.at[at_rows, :], hid_ref.at[at_rows, :], sems.at[tile])
            copy.start()
            copies.append(copy)
            pair = nn(hidden, w_ref[:, pl.ds(OWN, OWN)])
            turned = pair * cos_ref[at_rows, :] + swap_halves(pair) * sin_ref[at_rows, :]
            lane = lax.broadcasted_iota(i32, pair.shape, 1)
            kv_ref[at_rows, :] = jnp.where(lane < HEAD, turned, pair).astype(bf16)
        for copy in copies:
            copy.wait()

    return call(
        kernel,
        [
            shape((rows, width), bf16),
            shape((rows, OWN), bf16),
            shape((width, 2 * OWN), bf16),
            shape((local + OWN, TP * OWN), bf16),
            shape((8, width), f32),
        ],
        [at, *tokens, *packs, cosine, sine, cotangent],
        scratch=[
            pltpu.VMEM((nz, pack_rows, lanes), bf16),
            pltpu.VMEM((rows, width), bf16),
            pltpu.SemaphoreType.DMA((tiles,)),
        ],
        limit=60,
        cost=4.0,
        far_out=(0,),
    )


def project_queries(tokens, hidden, w_qkv, cosine, sine):
    local, width = tokens[0].shape
    half_rows = local // 2
    rows = TP * local
    per = 4

    def kernel(*refs):
        toks, refs = refs[:TP], refs[TP:]
        hid_ref, w_ref, cos_ref, sin_ref, x_ref, qt_ref = refs
        for tile in range(2 * TP // per):
            side, first = (tile * per) // TP, (tile * per) % TP
            at_rows = pl.ds(tile * per * half_rows, per * half_rows)
            for j in range(per):
                x_ref[pl.ds((tile * per + j) * half_rows, half_rows), :] = toks[first + j][
                    pl.ds(side * half_rows, half_rows), :
                ]
            query = nn(hid_ref[at_rows, :], w_ref[:, pl.ds(0, OWN)])
            query = query * cos_ref[at_rows, :] + swap_halves(query) * sin_ref[at_rows, :]
            qt_ref[:, at_rows] = (query.astype(bf16).astype(f32) * HEAD**-0.5).T.astype(bf16)

    return call(
        kernel,
        [shape((rows, width), bf16), shape((OWN, rows), bf16)],
        [*tokens, hidden, w_qkv, cosine, sine],
        scalars=0,
        limit=60,
        cost=4.0,
    )


def attention_forward(select, key_base, query_base, turned_query, own_kv, other_kv, half_rows):
    groups = len(own_kv)
    rows = own_kv[0].shape[0]
    half = rows // 2
    blocks = half // half_rows
    wide, deep = 128, 128

    def kernel(sel_ref, key_ref, query_ref, q_ref, *refs):
        own, other = refs[:groups], refs[groups : 2 * groups]
        out_ref, low_ref, lse_ref, kv_ref, kvt_ref, top_ref, mass_ref, place_ref = refs[2 * groups :]
        for head in range(2):
            chosen = sel_ref[head] == 0
            for group in range(groups):

                @pl.when(chosen)
                def take_own():
                    kv_ref[head, group] = own[group][...]
                    kvt_ref[head, group] = own[group][...].T

                @pl.when(jnp.logical_not(chosen))
                def take_other():
                    kv_ref[head, group] = other[group][...]
                    kvt_ref[head, group] = other[group][...].T

        top_ref[...] = jnp.full_like(top_ref, far_below)
        mass_ref[...] = jnp.zeros_like(mass_ref)
        out_ref[...] = jnp.zeros_like(out_ref)

        def one_group(group, unused):
            for head in range(2):
                row = sel_ref[head] * groups + group
                own_rows = pl.ds(head * HEAD, HEAD)
                stat = pl.ds(head, 1)
                place_ref[...] = key_positions(key_ref, row, 0, 2 * blocks, half_rows, 128)
                for k_start in range(0, rows, deep):
                    keys_at = pl.ds(k_start, deep)
                    k_side = k_start // half
                    block = kv_ref[head, group, keys_at, :]
                    values = kvt_ref[head, group, pl.ds(HEAD, HEAD), keys_at]
                    for start in range(k_side * half, rows, wide):
                        lanes = pl.ds(start, wide)
                        turned = q_ref[own_rows, lanes]
                        padded = jnp.concatenate([turned, jnp.zeros_like(turned)], axis=0)
                        scores = nn(block, padded)
                        if start // half == k_side:
                            places = query_positions(
                                query_ref, start // half_rows, wide, half_rows
                            )
                            scores = jnp.where(place_ref[keys_at, :] <= places, scores, far_below)
                        before = top_ref[stat, lanes]
                        top = jnp.maximum(before, jnp.max(scores, axis=0, keepdims=True))
                        weights = jnp.exp(scores - top)
                        fade = jnp.exp(before - top)
                        top_ref[stat, lanes] = top
                        mass_ref[stat, lanes] = mass_ref[stat, lanes] * fade + jnp.sum(
                            weights, axis=0, keepdims=True
                        )
                        out_ref[own_rows, lanes] = out_ref[own_rows, lanes] * fade + nn(
                            values, weights.astype(bf16)
                        )
            return unused

        lax.fori_loop(0, groups, one_group, 0)
        for head in range(2):
            own_rows = pl.ds(head * HEAD, HEAD)
            mass = mass_ref[pl.ds(head, 1), :]
            out_ref[own_rows, :] = out_ref[own_rows, :] / mass
            lse_ref[pl.ds(head, 1), :] = top_ref[pl.ds(head, 1), :] + jnp.log(mass)
        low_ref[...] = out_ref[...].T.astype(bf16)

    return call(
        kernel,
        [shape((OWN, rows), f32), shape((rows, OWN), bf16), shape((2, rows), f32)],
        [select, key_base, query_base, turned_query, *own_kv, *other_kv],
        scalars=3,
        scratch=[
            pltpu.VMEM((2, groups, rows, OWN), bf16),
            pltpu.VMEM((2, groups, OWN, rows), bf16),
            pltpu.VMEM((2, rows), f32),
            pltpu.VMEM((2, rows), f32),
            pltpu.VMEM((rows, 128), i32),
        ],
        limit=60,
        cost=14.0,
    )


def attention_backward(
    select, key_base, query_base, turned_query, own_kv, other_kv, traded, attended, log_mass, half_rows
):
    groups = len(own_kv)
    rows = own_kv[0].shape[0]
    half = rows // 2
    blocks = half // half_rows
    wide, deep = 512, 256

    def kernel(sel_ref, key_ref, query_ref, q_ref, *refs):
        own, other = refs[:groups], refs[groups : 2 * groups]
        refs = refs[2 * groups :]
        local = 2 * half_rows
        parts = [refs[0], refs[1]] + [
            refs[2 + j].at[pl.ds(k * local, local), :] for j in range(TP // 2 - 1) for k in range(2)
        ]
        refs = refs[1 + TP // 2 :]
        att_ref, lse_ref, dq_ref, keep_ref, pass_ref, gb_ref = refs[:6]
        kv_ref, sum_ref, g_ref, rq_ref, rg_ref, delta_ref, pos_ref = refs[6:]
        for group in range(groups):
            kv_ref[0, group] = own[group][...]
            kv_ref[1, group] = other[group][...]
        sum_ref[...] = jnp.zeros_like(sum_ref)
        dq_ref[...] = jnp.zeros_like(dq_ref)
        zeros = jnp.zeros((rows, HEAD), bf16)
        for j in range(0, TP, 2):
            for side in range(2):
                at = pl.ds(side * half + j * half_rows, 2 * half_rows)
                pair = jnp.concatenate(
                    [parts[j + k][pl.ds(side * half_rows, half_rows), :] for k in range(2)], axis=0
                )
                g_ref[:, at] = pair[:, :OWN].T
                gb_ref[at, :] = pair[:, OWN:]
        for head in range(2):
            own_rows = pl.ds(head * HEAD, HEAD)
            rq_ref[head] = jnp.concatenate([q_ref[own_rows, :].T, zeros], axis=1)
            grad = g_ref[own_rows, :]
            rg_ref[head] = jnp.concatenate([zeros, grad.T], axis=1)
            delta_ref[pl.ds(head, 1), :] = jnp.sum(
                grad.astype(f32) * att_ref[own_rows, :], axis=0, keepdims=True
            )

        def one_group(group, unused):
            for head in range(2):
                which = sel_ref[head]
                own_rows = pl.ds(head * HEAD, HEAD)
                stat = pl.ds(head, 1)
                pos_ref[...] = key_positions(
                    key_ref, which * groups + group, 0, 2 * blocks, half_rows, 128
                )
                for k_start in range(0, rows, deep):
                    keys_at = pl.ds(k_start, deep)
                    k_side = k_start // half
                    block = kv_ref[which, group, keys_at, :]
                    turned_keys = block.T[:HEAD]
                    for start in range(k_side * half, rows, wide):
                        lanes = pl.ds(start, wide)
                        turned = q_ref[own_rows, lanes]
                        padded = jnp.concatenate([turned, jnp.zeros_like(turned)], axis=0)
                        scores = nn(block, padded)
                        if start // half == k_side:
                            places = query_positions(
                                query_ref, start // half_rows, wide, half_rows
                            )
                            at = jnp.concatenate([pos_ref[keys_at, :]] * (wide // 128), axis=1)
                            scores = jnp.where(at <= places, scores, far_below)
                        probs = jnp.exp(scores - lse_ref[stat, lanes])
                        grads = g_ref[own_rows, lanes]
                        padded = jnp.concatenate([jnp.zeros_like(grads), grads], axis=0)
                        grad_probs = nn(block, padded)
                        grad_scores = probs * (grad_probs - delta_ref[stat, lanes])
                        probs = probs.astype(bf16)
                        grad_scores = grad_scores.astype(bf16)
                        sum_ref[which, group, keys_at, :] += nn(
                            grad_scores, rq_ref[head, lanes, :]
                        ) + nn(probs, rg_ref[head, lanes, :])
                        dq_ref[own_rows, lanes] += nn(turned_keys, grad_scores)
            return unused

        lax.fori_loop(0, groups, one_group, 0)
        for group in range(groups):
            keep_ref[pl.ds(group * rows, rows), :] = sum_ref[0, group]
            pass_ref[pl.ds(group * rows, rows), :] = sum_ref[1, group].astype(bf16)

    return call(
        kernel,
        [
            shape((OWN, rows), f32),
            shape((groups * rows, OWN), f32),
            shape((groups * rows, OWN), bf16),
            shape((rows, OWN), bf16),
        ],
        [
            select,
            key_base,
            query_base,
            turned_query,
            *own_kv,
            *other_kv,
            *traded,
            attended,
            log_mass,
        ],
        scalars=3,
        scratch=[
            pltpu.VMEM((2, groups, rows, OWN), bf16),
            pltpu.VMEM((2, groups, rows, OWN), f32),
            pltpu.VMEM((OWN, rows), bf16),
            pltpu.VMEM((2, rows, OWN), bf16),
            pltpu.VMEM((2, rows, OWN), bf16),
            pltpu.VMEM((2, rows), f32),
            pltpu.VMEM((rows, 128), i32),
        ],
        limit=28,
        cost=18.0,
    )


def store_blocks(part, tile, per, half_rows, keep_ref, pass_ref, x_first=False):
    side = (tile * per) // TP
    first = lax.rem(tile * per, TP) // 2
    for j in range(per):
        piece = part[j * half_rows : (j + 1) * half_rows]
        place = first // 2 + j if x_first else first + j // 2
        if x_first and j % 2:
            place = first // 2 + j - 1
        row = (2 * place + side) * half_rows
        at = pl.ds(pl.multiple_of(row, half_rows), half_rows)
        target = keep_ref if j % 2 == 0 else pass_ref
        target[at, pl.ds(0, piece.shape[1])] = piece.astype(target.dtype)


def feed_forward(at, inputs, attended, sides, packs, gains, nz):
    rows, width = inputs.shape
    local = rows // TP
    half_rows = local // 2
    half = rows // 2
    d_rows, lanes = packs[0].shape
    ff = lanes // 3
    part_rows = ff // nz
    per = 8
    tile_rows = per * half_rows
    tiles = 2 * TP // per

    def kernel(at_ref, x_ref, *refs):
        att, refs = refs[:TP], refs[TP:]
        extra, refs = refs[:TP], refs[TP:]
        pack, refs = refs[:nz], refs[nz:]
        gain_ref, refs = refs[0], refs[1:]
        resid_out, gk_ref, gp_ref, gain_out, dn_w = refs[:5]
        targets, prod_out, refs = refs[5 : 5 + nz], refs[5 + nz], refs[6 + nz :]
        att_ref, wo_ref, gu_w, cot_ref, hold, acc_gu, acc_dn, blocks, prod_ref, sems = refs
        tp = at_ref[0]
        z = at_ref[1]
        for j in range(TP):
            columns = pl.ds(pl.multiple_of((tp ^ j) * OWN, OWN), OWN)
            wo_ref[columns, :] = extra[j][pl.ds(local, OWN), pl.ds(0, width)]
            for side in range(2):
                for k in range(TP):
                    att_ref[pl.ds(side * half + k * half_rows, half_rows), columns] = att[j][
                        pl.ds(side * half + (k ^ j) * half_rows, half_rows), :
                    ]
                cot_ref[pl.ds(side * half + j * half_rows, half_rows), :] = extra[j][
                    pl.ds(side * half_rows, half_rows), pl.ds(0, width)
                ]
        for s in range(nz):
            hold[z ^ s] = pack[s][...]
        for s in range(nz):
            rows_at = pl.ds(s * d_rows, d_rows)
            gu_w[rows_at, :] = hold[s, :, pl.ds(0, 2 * ff)]
            dn_w[rows_at, :] = jnp.concatenate(
                [
                    hold[b][:, 2 * ff + s * part_rows : 2 * ff + (s + 1) * part_rows]
                    for b in range(nz)
                ],
                axis=1,
            )
        gain = gain_ref[pl.ds(1, 1), :]
        gain_out[...] = jnp.zeros_like(gain_out)
        acc_gu[...] = jnp.zeros_like(acc_gu)
        acc_dn[...] = jnp.zeros_like(acc_dn)

        def copy_of(tile):
            at_rows = pl.ds(pl.multiple_of(tile * tile_rows, tile_rows), tile_rows)
            return pltpu.make_async_copy(
                prod_ref.at[at_rows, :], prod_out.at[at_rows, :], sems.at[tile]
            )

        def one_tile(tile, unused):
            at_rows = pl.ds(pl.multiple_of(tile * tile_rows, tile_rows), tile_rows)
            branch = nt(att_ref[at_rows, :][:, :width], wo_ref[pl.ds(0, width), :])
            resid = x_ref[at_rows, :].astype(f32) + branch
            side = (tile * per) // TP

            @pl.when(lax.rem(tile * per, TP) == 0)
            def keep_own():
                resid_out[pl.ds(pl.multiple_of(side * half_rows, half_rows), half_rows), :] = resid[
                    :half_rows
                ]

            normal = resid * norm_scale(resid)
            hidden = (normal * gain).astype(bf16)
            gate_up = nn(hidden, gu_w[...])
            gate, up = gate_up[:, :ff], gate_up[:, ff:]
            sigmoid = 1.0 / (1.0 + jnp.exp(-gate))
            activated = gate * sigmoid
            product = (activated * up).astype(bf16)
            prod_ref[at_rows, :] = product
            copy_of(tile).start()
            cotangent = cot_ref[at_rows, :]
            grad_product = nn(cotangent, dn_w[...])
            grad_gate = grad_product * up * sigmoid * (1.0 + gate * (1.0 - sigmoid))
            grad_gu = jnp.concatenate([grad_gate, grad_product * activated], axis=1).astype(bf16)
            partial = nt(grad_gu, gu_w[...])
            gain_out[pl.ds(0, 1), :] += jnp.sum(partial * normal, axis=0, keepdims=True)
            store_blocks(partial, tile, per, half_rows, gk_ref, gp_ref)
            acc_gu[...] += tn(hidden, grad_gu)
            acc_dn[...] += tn(cotangent, product)
            return unused

        lax.fori_loop(0, tiles, one_tile, 0)
        for b in range(nz):
            blocks[b, :, pl.ds(0, 2 * ff)] = acc_gu[pl.ds(b * d_rows, d_rows), :]
            blocks[b, :, pl.ds(2 * ff, ff)] = jnp.concatenate(
                [
                    acc_dn[pl.ds(s * d_rows, d_rows), :][:, b * part_rows : (b + 1) * part_rows]
                    for s in range(nz)
                ],
                axis=1,
            )
        for s in range(nz):
            targets[s][...] = blocks[z ^ s].astype(targets[s].dtype)
        for tile in range(tiles):
            copy_of(tile).wait()

    return call(
        kernel,
        [
            shape((local, width), f32),
            shape((TP // 2 * local, width), bf16),
            shape((TP // 2 * local, TP * OWN), bf16),
            shape((8, width), f32),
            shape((width, ff), bf16),
        ]
        + [shape((d_rows, lanes), f32 if s % 2 == 0 else bf16) for s in range(nz)]
        + [shape((rows, ff), bf16)],
        [at, inputs, *attended, *sides, *packs, gains],
        scratch=[
            pltpu.VMEM((rows, TP * OWN), bf16),
            pltpu.VMEM((TP * OWN, width), bf16),
            pltpu.VMEM((width, 2 * ff), bf16),
            pltpu.VMEM((rows, width), bf16),
            pltpu.VMEM((nz, d_rows, lanes), bf16),
            pltpu.VMEM((width, 2 * ff), f32),
            pltpu.VMEM((width, ff), f32),
            pltpu.VMEM((nz, d_rows, lanes), f32),
            pltpu.VMEM((rows, ff), bf16),
            pltpu.SemaphoreType.DMA((tiles,)),
        ],
        limit=44,
        cost=17.0,
        far_out=(5 + nz,),
    )


def feed_forward_rest(at, attended, sides, product, w_down):
    rows = attended[0].shape[0]
    width, ff = w_down.shape
    local = rows // TP
    half_rows = local // 2
    half = rows // 2
    per = 4
    tile_rows = per * half_rows

    def kernel(at_ref, *refs):
        att, refs = refs[:TP], refs[TP:]
        extra, refs = refs[:TP], refs[TP:]
        prod_ref, dn_w, att_out, wo_out, lk_ref, lp_ref = refs
        tp = at_ref[0]
        for j in range(TP):
            columns = pl.ds(pl.multiple_of((tp ^ j) * OWN, OWN), OWN)
            wo_out[columns, :] = extra[j][pl.ds(local, OWN), pl.ds(0, width)]
            for side in range(2):
                for k in range(TP):
                    att_out[pl.ds(side * half + k * half_rows, half_rows), columns] = att[j][
                        pl.ds(side * half + (k ^ j) * half_rows, half_rows), :
                    ]

        def one_tile(tile, unused):
            at_rows = pl.ds(pl.multiple_of(tile * tile_rows, tile_rows), tile_rows)
            part = nt(prod_ref[at_rows, :], dn_w[...])
            store_blocks(part, tile, per, half_rows, lk_ref, lp_ref)
            return unused

        lax.fori_loop(0, 2 * TP // per, one_tile, 0)

    return call(
        kernel,
        [
            shape((rows, TP * OWN), bf16),
            shape((TP * OWN, width), bf16),
            shape((TP // 2 * local, width), bf16),
            shape((TP // 2 * local, TP * OWN), bf16),
        ],
        [at, *attended, *sides, product, w_down],
        limit=24,
        cost=5.0,
    )


def add_crossed(keep, crossed, count, tail=None):
    local, width = keep.shape[0] // count, keep.shape[1]
    tails = [] if tail is None else [tail]
    more = 0 if tail is None else tail.shape[0]

    def kernel(keep_ref, cross_ref, *refs):
        own_ref, *sends = refs[len(tails) :]
        for j in range(count):
            at = pl.ds(j * local, local)
            target = own_ref if j == 0 else sends[j - 1]
            target[pl.ds(0, local), pl.ds(0, width)] = (
                keep_ref[at, :].astype(f32) + cross_ref[at, pl.ds(0, width)].astype(f32)
            ).astype(target.dtype)
        if tails:
            sends[-1][pl.ds(local, more), pl.ds(0, width)] = refs[0][...]

    return call(
        kernel,
        [shape((local, width), f32)]
        + [shape((local, width), bf16)] * (count - 2)
        + [shape((local + more, TP * OWN if tails else width), bf16)],
        [keep, crossed, *tails],
        scalars=0,
        limit=12,
        cost=1.0,
    )


def branch_gradient(at, sums, resid, cotangent, w_out, gains):
    local, width = resid.shape

    def kernel(at_ref, *refs):
        parts, refs = refs[: len(sums)], refs[len(sums) :]
        resid_ref, cot_ref, wo_ref, gain_ref, grad_ref, keep_ref, pass_ref, ga_ref, gb_ref = refs
        tp = at_ref[0]
        grad_hidden = parts[0][...]
        for part in parts[1:]:
            grad_hidden = grad_hidden + part[...].astype(f32)
        resid = resid_ref[...]
        scale = norm_scale(resid)
        normal = resid * scale
        grad = grad_hidden * gain_ref[pl.ds(1, 1), :]
        grad = scale * (grad - normal * jnp.mean(grad * normal, axis=1, keepdims=True))
        grad = grad + cot_ref[...].astype(f32)
        grad_ref[...] = grad
        low = grad.astype(bf16)
        gb_ref[...] = jnp.zeros_like(gb_ref)
        gb_ref[:, pl.ds(0, width)] = low
        ga_ref[...] = jnp.zeros_like(ga_ref)
        ga_ref[:, pl.ds(0, width)] = nn(low, wo_ref[pl.ds(0, width), :]).astype(bf16)
        for j in range(TP):
            columns = pl.ds(pl.multiple_of((tp ^ j) * OWN, OWN), OWN)
            target = keep_ref if j % 2 == 0 else pass_ref
            rows = pl.ds((j // 2) * local, local)
            target[rows, pl.ds(0, OWN)] = ga_ref[:, columns]
            target[rows, pl.ds(OWN, OWN)] = gb_ref[:, columns]

    blocks = shape((TP // 2 * local, 2 * OWN), bf16)
    return call(
        kernel,
        [shape((local, width), f32), blocks, blocks],
        [at, *sums, resid, cotangent, w_out, gains],
        scratch=[pltpu.VMEM((local, TP * OWN), bf16), pltpu.VMEM((local, TP * OWN), bf16)],
        limit=16,
        cost=3.0,
    )


def pair_up(keep, crossed, count):
    local, width = keep.shape[0] // count, keep.shape[1]

    def kernel(keep_ref, cross_ref, *outs):
        for j in range(1, count):
            at = pl.ds(j * local, local)
            outs[j - 1][pl.ds(0, local), :] = keep_ref[at, :]
            outs[j - 1][pl.ds(local, local), :] = cross_ref[at, :]

    return call(
        kernel,
        [shape((2 * local, width), bf16)] * (count - 1),
        [keep, crossed],
        scalars=0,
        limit=8,
        cost=0.7,
    )


def projection_gradient(
    at, grad_query, grad_kv, inputs, hidden, w_qkv, gain_sums, cosine, sine, grad_out, nz
):
    rows, width = inputs.shape
    local = rows // TP
    half_rows = local // 2
    d_rows = width // nz
    per = 4
    tile_rows = per * half_rows
    pieces = len(grad_kv)

    def kernel(at_ref, dq_ref, *refs):
        kvs, refs = refs[:pieces], refs[pieces:]
        x_ref, hid_ref, w_ref, gain_two_ref, cos_ref, sin_ref, wo_ref = refs[:7]
        keep_ref, pass_ref, own_ref = refs[7:10]
        sends, refs = refs[10 : 10 + nz - 1], refs[10 + nz - 1 :]
        turn_ref, acc_ref, gain_acc, hold = refs
        z = at_ref[1]
        turn_ref[...] = dq_ref[...].T * HEAD**-0.5
        acc_ref[...] = jnp.zeros_like(acc_ref)
        gain_acc[...] = jnp.zeros_like(gain_acc)

        def one_tile(tile, unused):
            at_rows = pl.ds(pl.multiple_of(tile * tile_rows, tile_rows), tile_rows)
            cos, sin = cos_ref[at_rows, :], sin_ref[at_rows, :]
            query = turn_ref[at_rows, :]
            query = query * cos - swap_halves(query) * sin
            pair = kvs[0][at_rows, :].astype(f32)
            for piece in kvs[1:]:
                pair = pair + piece[at_rows, :].astype(f32)
            turned = pair * cos - swap_halves(pair) * sin
            lane = lax.broadcasted_iota(i32, pair.shape, 1)
            pair = jnp.where(lane < HEAD, turned, pair)
            grad = jnp.concatenate([query, pair], axis=1).astype(bf16)
            partial = nt(grad, w_ref[...])
            x = x_ref[at_rows, :].astype(f32)
            gain_acc[pl.ds(0, 1), :] += jnp.sum(partial * (x * norm_scale(x)), axis=0, keepdims=True)
            store_blocks(partial, tile, per, half_rows, keep_ref, pass_ref, True)
            acc_ref[...] += tn(hid_ref[at_rows, :], grad)
            return unused

        lax.fori_loop(0, 2 * TP // per, one_tile, 0)
        hold[...] = jnp.zeros_like(hold)
        for s in range(nz):
            columns = slice(s * d_rows, (s + 1) * d_rows)
            hold[s, pl.ds(0, 1), pl.ds(0, d_rows)] = gain_acc[pl.ds(0, 1), :][:, columns]
            hold[s, pl.ds(1, 1), pl.ds(0, d_rows)] = gain_two_ref[pl.ds(0, 1), :][:, columns]
        for s in range(nz):
            block = z ^ s
            target = own_ref if s == 0 else sends[s - 1]
            rows_at = pl.ds(pl.multiple_of(block * d_rows, 8), d_rows)
            part = pl.ds(0, d_rows)
            target[part, pl.ds(0, 2 * OWN)] = acc_ref[rows_at, :].astype(target.dtype)
            target[part, pl.ds(2 * OWN, OWN)] = wo_ref[rows_at, :].astype(target.dtype)
            target[pl.ds(d_rows, 16), :] = hold[block].astype(target.dtype)

    return call(
        kernel,
        [
            shape((TP // 2 * local, width), bf16),
            shape((TP // 2 * local, TP * OWN), bf16),
            shape((d_rows + 16, 3 * OWN), f32),
        ]
        + [shape((d_rows + 16, 3 * OWN), bf16)] * (nz - 1),
        [at, grad_query, *grad_kv, inputs, hidden, w_qkv, gain_sums, cosine, sine, grad_out],
        scratch=[
            pltpu.VMEM((rows, OWN), f32),
            pltpu.VMEM((width, 2 * OWN), f32),
            pltpu.VMEM((8, width), f32),
            pltpu.VMEM((nz, 16, 3 * OWN), f32),
        ],
        limit=32,
        cost=8.0,
    )


def token_gradient(sums, tokens, grad_resid, gains):
    local, width = tokens.shape

    def kernel(*refs):
        parts, refs = refs[: len(sums)], refs[len(sums) :]
        x_ref, grad_ref, gain_ref, out_ref = refs
        grad_hidden = parts[0][...]
        for part in parts[1:]:
            grad_hidden = grad_hidden + part[...].astype(f32)
        x = x_ref[...].astype(f32)
        scale = norm_scale(x)
        normal = x * scale
        grad = grad_hidden * gain_ref[pl.ds(0, 1), :]
        grad = scale * (grad - normal * jnp.mean(grad * normal, axis=1, keepdims=True))
        out_ref[...] = (grad + grad_ref[...]).T

    return call(
        kernel,
        [shape((width, local), f32)],
        [*sums, tokens, grad_resid, gains],
        scalars=0,
        limit=8,
        cost=1.0,
    )[0].T


def layer_output(near, arrived, resid):
    local, width = resid.shape
    start = arrived.shape[0] - local

    def kernel(near_ref, in_ref, resid_ref, out_ref):
        total = resid_ref[...] + near_ref[...] + in_ref[pl.ds(start, local), pl.ds(0, width)].astype(f32)
        out_ref[...] = total.T.astype(bf16)

    turned = shape(resid.shape[::-1], bf16)
    return call(kernel, [turned], [near, arrived, resid], scalars=0, limit=8, cost=1.0)[0].T


def first_sum(own, arrived):
    def kernel(own_ref, in_ref, out_ref):
        out_ref[...] = (own_ref[...] + in_ref[...].astype(f32)).astype(bf16)

    return call(
        kernel, [shape(own.shape, bf16)], [own, arrived], scalars=0, limit=8, cost=1.0
    )[0]


def last_sum(own, *arrived):
    rows, lanes = own.shape

    def kernel(own_ref, *refs):
        total = own_ref[...]
        for ref in refs[:-1]:
            total = total + ref[...].astype(f32)
        refs[-1][:, pl.ds(0, lanes)] = total.astype(bf16)

    return call(
        kernel, [shape((rows, TP * OWN), bf16)], [own, *arrived], scalars=0, limit=8, cost=1.0
    )[0]


def ff_outputs(at, mine, by_x, by_y, by_xy, odd, ff_z, nz):
    d_rows = mine.shape[0]
    part = ff_z // TP
    ff = part * nz

    def kernel(at_ref, m_ref, x_ref, y_ref, xy_ref, odd_ref, gate_ref, up_ref, down_ref, hold):
        tp = at_ref[0]
        lanes = pl.ds(0, 3 * ff)
        for j, ref in enumerate((m_ref, x_ref, y_ref, xy_ref)):
            hold[tp ^ (2 * j)] = ref[:, lanes]
        for j in range(TP // 2):
            hold[tp ^ (2 * j + 1)] = odd_ref[pl.ds(d_rows * j, d_rows), lanes]
        for s in range(nz):
            for start in (s * part, ff + s * part, 2 * ff + s * part):
                block = jnp.concatenate(
                    [hold[c][:, start : start + part] for c in range(TP)], axis=1
                ).astype(f32)
                if start < ff:
                    gate_ref[:, pl.ds(s * ff_z, ff_z)] = block
                elif start < 2 * ff:
                    up_ref[:, pl.ds(s * ff_z, ff_z)] = block
                else:
                    down_ref[pl.ds(s * d_rows, d_rows), :] = block

    gate, up, down = call(
        kernel,
        [
            shape((d_rows, nz * ff_z), f32),
            shape((d_rows, nz * ff_z), f32),
            shape((nz * d_rows, ff_z), f32),
        ],
        [at, mine, by_x, by_y, by_xy, odd],
        scratch=[pltpu.VMEM((TP, d_rows, 3 * ff), bf16)],
        limit=32,
        cost=7.0,
    )
    return gate, up, down.T


def projection_outputs(at, slots, width):
    d_rows = slots[0].shape[0] - 16

    def kernel(at_ref, *refs):
        parts, (q_ref, k_ref, v_ref, o_ref, one_ref, two_ref, hold) = refs[:TP], refs[TP:]
        tp = at_ref[0]
        total = jnp.zeros((16, 3 * OWN), f32)
        for j in range(TP):
            hold[tp ^ j] = parts[j][...].astype(f32)
            total = total + parts[j][pl.ds(d_rows, 16), :].astype(f32)
        one_ref[...] = total[0:1, :d_rows]
        two_ref[...] = total[1:2, :d_rows]
        heads = [hold[c][:d_rows, :OWN] for c in range(TP)]
        q_ref[...] = jnp.concatenate(heads, axis=1)[:, :width]
        heads = [hold[c][:d_rows, 2 * OWN :] for c in range(TP)]
        o_ref[...] = jnp.concatenate(heads, axis=1)[:, :width]
        kv = [hold[c][:d_rows, OWN : 2 * OWN] for c in range(TP)]
        kv = [kv[0], kv[1] + kv[2], kv[3] + kv[4], kv[5], kv[6]]
        for c in range(KV_HEADS):
            turned = kv[c].T
            k_ref[pl.ds(c * HEAD, HEAD), :] = turned[:HEAD]
            v_ref[pl.ds(c * HEAD, HEAD), :] = turned[HEAD:]

    query, key, value, out, one, two = call(
        kernel,
        [
            shape((d_rows, width), f32),
            shape((KV_HEADS * HEAD, d_rows), f32),
            shape((KV_HEADS * HEAD, d_rows), f32),
            shape((d_rows, width), f32),
            shape((1, d_rows), f32),
            shape((1, d_rows), f32),
        ],
        [at, *slots],
        scratch=[pltpu.VMEM((TP, d_rows + 16, 3 * OWN), f32)],
        limit=12,
        cost=0.01,
    )
    return query, key.T, value.T, out, one, two


def body(
    tokens,
    pair_order,
    gain_attn,
    gain_mlp,
    w_query,
    w_key,
    w_value,
    w_out,
    w_gate,
    w_up,
    w_down,
    cotangent,
):
    local_rows, width = tokens.shape
    half_rows = local_rows // 2
    nz = lax.axis_size("fsdp")
    outer = lax.axis_size("ctx") // TP
    count = lax.axis_size(AXES)
    groups = outer * nz
    me = lax.axis_index(AXES)
    z = lax.axis_index("fsdp")
    tp = lax.axis_index("ctx") % TP
    kv_index = (4 * (tp // 2)) // GROUP + tp % 2
    at = jnp.stack([tp, z, kv_index]).astype(i32)
    send = functools.partial(exchange, count=count)
    group_mask = [(g // nz) * TP * nz + g % nz for g in range(groups)]

    def after(value, *others):
        return lax.optimization_barrier((value, *others))[0]

    def level(*arrays):
        return list(lax.optimization_barrier(arrays))

    def gather_even(block):
        return [block] + [send(block, j * nz) for j in range(2, TP, 2)]

    def gather_odd(even):
        return [piece for e in even for piece in (e, send(e, nz))]

    def scatter_far(pieces):
        return [send(piece, 2 * (j + 1) * nz) for j, piece in enumerate(pieces)]

    def from_z(block):
        return [block] + [send(block, s) for s in range(1, nz)]

    pack_one = slice_attention_weights(at, w_query, w_key, w_value, w_out, gain_attn, gain_mlp)
    token_slots = gather_odd(level(*gather_even(tokens)))
    pack_two = slice_ff_weights(after(at, pack_one), w_gate, w_up, w_down, nz)
    pack_one = from_z(pack_one)

    slot_of = jnp.array([[m | (j * nz) for j in range(TP)] for m in group_mask], dtype=i32)
    low = pair_order[me ^ slot_of]
    base = jnp.stack([low, 2 * count - 1 - low], axis=1) * half_rows
    query_base = base[0].reshape(2 * TP)
    partner = jnp.array([j ^ 1 for j in range(TP)], dtype=i32)
    key_base = jnp.stack([base, base[:, :, partner]]).reshape(2 * groups, 2 * TP)
    places = (query_base[:, None] + jnp.arange(half_rows, dtype=i32)[None, :]).reshape(-1)
    lane = jnp.arange(OWN)
    freqs = base_theta ** (-2.0 * (lane % (HEAD // 2)).astype(f32) / HEAD)
    angles = places.astype(f32)[:, None] * freqs[None, :]
    cosine = jnp.cos(angles)
    sine = jnp.sin(angles) * jnp.where(lane % HEAD < HEAD // 2, -1.0, 1.0)[None, :]
    select = jnp.where((2 * tp + jnp.arange(2)) // GROUP == kv_index, 0, 1).astype(i32)

    mask_x, mask_y = 2 * nz, 4 * nz
    hidden_one, kv, w_qkv, side, gains = project_keys(
        after(at, pack_two, select, key_base, query_base),
        token_slots,
        pack_one,
        cosine,
        sine,
        cotangent,
    )
    own_kv = [kv] + [send(kv, m) for m in group_mask[1:]]
    side_x, side_y = send(side, mask_x), send(side, mask_y)
    inputs, turned_query = project_queries(
        token_slots, after(hidden_one, kv), w_qkv, cosine, sine
    )
    side_x, side_y, inputs, turned_query, *own_kv = level(
        side_x, side_y, inputs, turned_query, *own_kv
    )
    other_kv = level(*[send(slot, nz) for slot in own_kv])
    one, near = send(after(pack_two, *own_kv), 1), send(after(pack_two, *own_kv), 2)
    side_xy = send(side_x, mask_y)
    side_odd, odd_x = send(after(side, *other_kv), nz), send(after(side_x, *other_kv), nz)
    attended, attended_own, log_mass = attention_forward(
        select, key_base, query_base, turned_query, own_kv, other_kv, half_rows
    )
    attended_own, near, one, side_xy, side_odd, odd_x = level(
        attended_own, near, one, side_xy, side_odd, odd_x
    )
    far, side_xy, *even = level(send(near, 1), side_xy, *gather_even(attended_own))
    attended_slots = gather_odd(even)
    packs = [pack_two, one, near, far]
    odd_y = send(after(side_y, side_xy), nz)
    sides = [side, side_odd, side_x, odd_x, side_y, odd_y, side_xy, send(side_xy, nz)]

    resid, grad_keep, grad_pass, gain_sums, w_down_own, *ff_blocks, product = feed_forward(
        at, inputs, attended_slots, sides, packs, gains, nz
    )
    ff_own, ff_one, ff_two, ff_three = ff_blocks
    first, *rest = add_crossed(grad_keep, send(grad_pass, nz), TP // 2)
    attended_low, w_out_all, out_keep, out_pass, ff_three, first, *rest = level(
        *feed_forward_rest(after(at, first), attended_slots, sides, product, w_down_own),
        send(after(ff_three, first), 1),
        first,
        *scatter_far(rest),
    )
    grad_resid, trade_keep, trade_pass = branch_gradient(
        at, [first, *rest], resid, cotangent, w_out_all, gains
    )
    crossed, out_crossed = level(send(trade_pass, nz), send(after(out_pass, first), nz))
    pairs = level(*scatter_far(pair_up(trade_keep, crossed, TP // 2)))
    out_near, out_far = add_crossed(out_keep, out_crossed, 2)
    ff_one = send(after(ff_one, crossed), 1)
    ff_two = send(first_sum(ff_two, ff_three), 2)
    out_far = send(after(out_far, *pairs), mask_y)

    grad_query, kv_keep, kv_pass, branch_columns = attention_backward(
        after(select, out_near),
        key_base,
        query_base,
        turned_query,
        own_kv,
        other_kv,
        [trade_keep, crossed, *pairs],
        attended,
        log_mass,
        half_rows,
    )
    kv_pass, ff_one, ff_two, out_far = level(kv_pass, ff_one, ff_two, out_far)
    kv_crossed = send(kv_pass, nz)
    first, *rest = add_crossed(kv_keep, kv_crossed, groups)
    grad_out = tn(attended_low[:, :width], after(branch_columns, rest[0]))
    ff_total = last_sum(after(ff_own, grad_out), ff_one, ff_two)

    for step in range(outer.bit_length() - 1):
        crossing = send(ff_total, TP * nz << step).astype(f32)
        ff_total = (ff_total.astype(f32) + crossing).astype(bf16)
    out_near, out_far = add_crossed(after(out_near, rest[0]), out_far, 2)
    ff_x, ff_y, *grad_kv = level(
        send(ff_total, mask_x),
        send(ff_total, mask_y),
        *[send(piece, m) for piece, m in zip(rest, group_mask[1:])],
    )

    last_keep, last_pass, last_own, *last_sends = projection_gradient(
        at,
        grad_query,
        [first, *grad_kv],
        inputs,
        hidden_one,
        w_qkv,
        gain_sums,
        cosine,
        sine,
        grad_out,
        nz,
    )
    near, far = add_crossed(last_keep, send(last_pass, nz), 2, out_far)
    ff_xy, far, *arrived = level(
        send(after(ff_x, last_own), mask_y),
        send(far, mask_x),
        *[send(piece, s + 1) for s, piece in enumerate(last_sends)],
    )
    layer_out = layer_output(out_near, far, resid)
    near, far = add_crossed(near, far, 2)
    last_total = last_own
    for piece in arrived:
        last_total = last_total + piece.astype(f32)
    for step in range(outer.bit_length() - 1):
        last_total = last_total + send(last_total.astype(bf16), TP * nz << step).astype(f32)
    last_total = last_total.astype(bf16)
    ff_slots = [ff_total, ff_x, ff_y, ff_xy]
    ff_slots.append(send(jnp.concatenate(ff_slots, axis=0), nz))
    grad_gate, grad_up, grad_down = ff_outputs(at, *ff_slots, w_down.shape[0], nz)
    far, grad_gate, *even = level(send(far, mask_y), grad_gate, *gather_even(last_total))
    grad_tokens = token_gradient([near, far], tokens, grad_resid, gains)
    last_slots = gather_odd(even)
    grad_w_query, grad_w_key, grad_w_value, grad_out, gain_one, gain_two = projection_outputs(
        after(at, grad_tokens, layer_out), last_slots, width
    )
    return (
        layer_out,
        grad_tokens,
        gain_one.reshape(-1),
        gain_two.reshape(-1),
        grad_w_query,
        grad_w_key,
        grad_w_value,
        grad_out,
        grad_gate,
        grad_up,
        grad_down,
    )


def solution(mesh):
    return jax.shard_map(
        body,
        mesh=mesh,
        in_specs=(
            P(("ctx", "fsdp"), None),
            P(),
            P("fsdp"),
            P("fsdp"),
            P("fsdp", None),
            P("fsdp", None),
            P("fsdp", None),
            P("fsdp", None),
            P("fsdp", None),
            P("fsdp", None),
            P("fsdp", None),
            P(("ctx", "fsdp"), None),
        ),
        out_specs=(
            P(("ctx", "fsdp"), None),
            P(("ctx", "fsdp"), None),
            P("fsdp"),
            P("fsdp"),
            P("fsdp", None),
            P("fsdp", None),
            P("fsdp", None),
            P("fsdp", None),
            P("fsdp", None),
            P("fsdp", None),
            P("fsdp", None),
        ),
        check_vma=False,
    )
```

```python
import functools

import jax
import jax.numpy as jnp
from jax import lax
from jax.experimental import pallas as pl
from jax.experimental.pallas import tpu as pltpu
from jax.sharding import PartitionSpec as P

HEADS = 15
KV_HEADS = 5
HEAD = 64
TP = 8
GROUP = HEADS // KV_HEADS
OWN = 2 * HEAD
epsilon = 1e-05
base_theta = 100000.0
far_below = -1e30
f32 = jnp.float32
bf16 = jnp.bfloat16
i32 = jnp.int32
AXES = ("ctx", "fsdp")
MIB = 1024 * 1024
smem = pl.BlockSpec(memory_space=pltpu.SMEM)
vmem = pl.BlockSpec(memory_space=pltpu.VMEM)


def exchange(array, mask, count):
    return lax.ppermute(array, AXES, [(i, i ^ mask) for i in range(count)])


def nn(left, right):
    return lax.dot_general(left, right, (((1,), (0,)), ((), ())), preferred_element_type=f32)


def tn(left, right):
    return lax.dot_general(left, right, (((0,), (0,)), ((), ())), preferred_element_type=f32)


def nt(left, right):
    return lax.dot_general(left, right, (((1,), (1,)), ((), ())), preferred_element_type=f32)


def shape(dims, dtype):
    return jax.ShapeDtypeStruct(dims, dtype)


def call(kernel, outs, inputs, scalars=1, scratch=(), limit=56, cost=1.0, far=(), far_out=()):
    specs = [smem] * scalars + [vmem] * (len(inputs) - scalars)
    for i in far:
        specs[i] = pl.BlockSpec(memory_space=pltpu.HBM)
    out_specs = [vmem for unused in outs]
    for i in far_out:
        out_specs[i] = pl.BlockSpec(memory_space=pltpu.HBM)
    return pl.pallas_call(
        kernel,
        out_shape=tuple(outs),
        in_specs=specs,
        out_specs=tuple(out_specs),
        scratch_shapes=list(scratch),
        compiler_params=pltpu.CompilerParams(vmem_limit_bytes=limit * MIB),
        cost_estimate=pl.CostEstimate(
            flops=int(cost * 1e9), bytes_accessed=int(cost * 1e6), transcendentals=0
        ),
    )(*inputs)


def one_hot(rows, columns, start):
    row = lax.broadcasted_iota(i32, (rows, columns), 0)
    column = lax.broadcasted_iota(i32, (rows, columns), 1)
    return jnp.where(row == column + start, 1.0, 0.0).astype(bf16)


def query_positions(base_ref, at, width, half_rows):
    lane = lax.broadcasted_iota(i32, (1, width), 1)
    place = jnp.zeros((1, width), i32)
    for block in range(width // half_rows):
        start = base_ref[at + block] - block * half_rows
        place = jnp.where(lane >= block * half_rows, start + lane, place)
    return place


def key_positions(base_ref, row, at, count, half_rows, width):
    offset = lax.broadcasted_iota(i32, (half_rows, width), 0)
    return jnp.concatenate([offset + base_ref[row, at + b] for b in range(count)], axis=0)


def swap_halves(matrix):
    lane = lax.broadcasted_iota(i32, matrix.shape, 1)
    ahead = pltpu.roll(matrix, matrix.shape[1] - HEAD // 2, 1)
    behind = pltpu.roll(matrix, HEAD // 2, 1)
    return jnp.where(lane % HEAD < HEAD // 2, ahead, behind)


def norm_scale(matrix):
    return lax.rsqrt(jnp.mean(matrix * matrix, axis=1, keepdims=True) + epsilon)


def slice_attention_weights(at, w_query, w_key, w_value, w_out, gain_one, gain_two):
    d_rows, width = w_query.shape
    lanes = 2 * OWN + OWN
    rest = width - (TP - 1) * OWN

    def kernel(at_ref, q_ref, k_ref, v_ref, o_ref, g1_ref, g2_ref, out_ref, cols, heads, whole, sems):
        tp = at_ref[0]
        kv = at_ref[2]
        wides, narrows = (q_ref, o_ref), (k_ref, v_ref)

        columns = pl.ds(pl.multiple_of(tp * OWN, OWN), OWN)
        rows = pl.ds(pl.multiple_of(kv * HEAD, HEAD), HEAD)

        def wide_copies():
            return [
                pltpu.make_async_copy(ref.at[:, columns], cols.at[i], sems.at[i])
                for i, ref in enumerate(wides)
            ]

        def whole_copies():
            return [
                pltpu.make_async_copy(ref, whole.at[i], sems.at[i]) for i, ref in enumerate(wides)
            ]

        def head_copies():
            return [
                pltpu.make_async_copy(ref.at[rows, :], heads.at[i], sems.at[2 + i])
                for i, ref in enumerate(narrows)
            ]

        @pl.when(tp < TP - 1)
        def most():
            for copy in wide_copies():
                copy.start()

        @pl.when(tp == TP - 1)
        def last():
            for copy in whole_copies():
                copy.start()

        @pl.when(kv < KV_HEADS)
        def real():
            for copy in head_copies():
                copy.start()

        @pl.when(kv >= KV_HEADS)
        def none():
            heads[...] = jnp.zeros_like(heads)

        @pl.when(tp < TP - 1)
        def most_came():
            for copy in wide_copies():
                copy.wait()

        @pl.when(tp == TP - 1)
        def last_came():
            for copy in whole_copies():
                copy.wait()
            for i in range(2):
                cols[i] = jnp.zeros((d_rows, OWN), bf16)
                cols[i, :, pl.ds(0, rest)] = whole[i, :, pl.ds(width - rest, rest)]

        @pl.when(kv < KV_HEADS)
        def real_came():
            for copy in head_copies():
                copy.wait()

        out_ref[pl.ds(0, d_rows), pl.ds(0, OWN)] = cols[0]
        turned = jnp.concatenate([heads[0], heads[1]], axis=0).astype(f32).T
        out_ref[pl.ds(0, d_rows), pl.ds(OWN, OWN)] = turned.astype(bf16)
        out_ref[pl.ds(0, d_rows), pl.ds(2 * OWN, OWN)] = cols[1]
        out_ref[pl.ds(d_rows, 16), :] = jnp.zeros((16, lanes), bf16)
        out_ref[d_rows, pl.ds(0, d_rows)] = g1_ref[...]
        out_ref[d_rows + 1, pl.ds(0, d_rows)] = g2_ref[...]

    return call(
        kernel,
        [shape((d_rows + 16, lanes), bf16)],
        [at, w_query, w_key.T, w_value.T, w_out, gain_one, gain_two],
        scratch=[
            pltpu.VMEM((2, d_rows, OWN), bf16),
            pltpu.VMEM((2, HEAD, d_rows), bf16),
            pltpu.VMEM((2, d_rows, width), bf16),
            pltpu.SemaphoreType.DMA((4,)),
        ],
        limit=60,
        cost=2.0,
        far=(1, 2, 3, 4),
    )[0]


def slice_ff_weights(at, w_gate, w_up, w_down, nz):
    d_rows = w_gate.shape[0]
    ff_z, width = w_down.shape
    part = ff_z // TP
    own = part * nz


    def kernel(at_ref, g_ref, u_ref, d_ref, out_ref):
        pick = one_hot(ff_z, part, at_ref[0] * part)
        for ref, start in ((g_ref, 0), (u_ref, own)):
            pieces = [nn(ref[:, pl.ds(s * ff_z, ff_z)], pick) for s in range(nz)]
            out_ref[:, pl.ds(start, own)] = jnp.concatenate(pieces, axis=1).astype(bf16)
        pieces = [nn(d_ref[pl.ds(s * d_rows, d_rows), :], pick) for s in range(nz)]
        out_ref[:, pl.ds(2 * own, own)] = jnp.concatenate(pieces, axis=1).astype(bf16)

    return call(
        kernel,
        [shape((d_rows, 3 * own), bf16)],
        [at, w_gate, w_up, w_down.T],
        limit=16,
        cost=4.0,
    )[0]


def project_keys(at, tokens, packs, cosine, sine, cotangent):
    local, width = tokens[0].shape
    half_rows = local // 2
    rows = TP * local
    nz = len(packs)
    pack_rows, lanes = packs[0].shape
    d_rows = pack_rows - 16
    per = 4
    tiles = 2 * TP // per

    def kernel(at_ref, *refs):
        toks, refs = refs[:TP], refs[TP:]
        pack, refs = refs[:nz], refs[nz:]
        cos_ref, sin_ref, cot_ref, hid_ref, kv_ref, w_ref, side_ref, gain_ref, hold, kept, sems = refs
        z = at_ref[1]
        for s in range(nz):
            hold[z ^ s] = pack[s][...]
        for s in range(nz):
            w_ref[pl.ds(s * d_rows, d_rows), :] = hold[s, pl.ds(0, d_rows), pl.ds(0, 2 * OWN)]
        gains = [hold[s, pl.ds(d_rows, 16), pl.ds(0, d_rows)].astype(f32) for s in range(nz)]
        gain_ref[...] = jnp.concatenate(gains, axis=1)[:8]
        gain = gain_ref[pl.ds(0, 1), :]
        side_ref[pl.ds(0, local), pl.ds(0, width)] = cot_ref[...]
        turned = [
            hold[s, pl.ds(0, d_rows), pl.ds(2 * OWN, OWN)].astype(f32) for s in range(nz)
        ]
        side_ref[pl.ds(local, OWN), pl.ds(0, width)] = jnp.concatenate(turned, axis=0).T.astype(bf16)
        copies = []
        for tile in range(tiles):
            side, first = (tile * per) // TP, (tile * per) % TP
            at_rows = pl.ds(tile * per * half_rows, per * half_rows)
            block = jnp.concatenate(
                [toks[first + j][pl.ds(side * half_rows, half_rows), :] for j in range(per)], axis=0
            )
            inputs = block.astype(f32)
            hidden = (inputs * norm_scale(inputs) * gain).astype(bf16)
            kept[at_rows, :] = hidden
            copy = pltpu.make_async_copy(kept.at[at_rows, :], hid_ref.at[at_rows, :], sems.at[tile])
            copy.start()
            copies.append(copy)
            pair = nn(hidden, w_ref[:, pl.ds(OWN, OWN)])
            turned = pair * cos_ref[at_rows, :] + swap_halves(pair) * sin_ref[at_rows, :]
            lane = lax.broadcasted_iota(i32, pair.shape, 1)
            kv_ref[at_rows, :] = jnp.where(lane < HEAD, turned, pair).astype(bf16)
        for copy in copies:
            copy.wait()

    return call(
        kernel,
        [
            shape((rows, width), bf16),
            shape((rows, OWN), bf16),
            shape((width, 2 * OWN), bf16),
            shape((local + OWN, TP * OWN), bf16),
            shape((8, width), f32),
        ],
        [at, *tokens, *packs, cosine, sine, cotangent],
        scratch=[
            pltpu.VMEM((nz, pack_rows, lanes), bf16),
            pltpu.VMEM((rows, width), bf16),
            pltpu.SemaphoreType.DMA((tiles,)),
        ],
        limit=60,
        cost=4.0,
        far_out=(0,),
    )


def project_queries(tokens, hidden, w_qkv, cosine, sine):
    local, width = tokens[0].shape
    half_rows = local // 2
    rows = TP * local
    per = 4

    def kernel(*refs):
        toks, refs = refs[:TP], refs[TP:]
        hid_ref, w_ref, cos_ref, sin_ref, x_ref, qt_ref = refs
        for tile in range(2 * TP // per):
            side, first = (tile * per) // TP, (tile * per) % TP
            at_rows = pl.ds(tile * per * half_rows, per * half_rows)
            for j in range(per):
                x_ref[pl.ds((tile * per + j) * half_rows, half_rows), :] = toks[first + j][
                    pl.ds(side * half_rows, half_rows), :
                ]
            query = nn(hid_ref[at_rows, :], w_ref[:, pl.ds(0, OWN)])
            query = query * cos_ref[at_rows, :] + swap_halves(query) * sin_ref[at_rows, :]
            qt_ref[:, at_rows] = (query.astype(bf16).astype(f32) * HEAD**-0.5).T.astype(bf16)

    return call(
        kernel,
        [shape((rows, width), bf16), shape((OWN, rows), bf16)],
        [*tokens, hidden, w_qkv, cosine, sine],
        scalars=0,
        limit=60,
        cost=4.0,
    )


def attention_forward(select, key_base, query_base, turned_query, own_kv, other_kv, half_rows):
    groups = len(own_kv)
    rows = own_kv[0].shape[0]
    half = rows // 2
    blocks = half // half_rows
    wide, deep = 128, 128

    def kernel(sel_ref, key_ref, query_ref, q_ref, *refs):
        own, other = refs[:groups], refs[groups : 2 * groups]
        out_ref, low_ref, lse_ref, kv_ref, kvt_ref, top_ref, mass_ref, place_ref = refs[2 * groups :]
        for head in range(2):
            chosen = sel_ref[head] == 0
            for group in range(groups):

                @pl.when(chosen)
                def take_own():
                    kv_ref[head, group] = own[group][...]
                    kvt_ref[head, group] = own[group][...].T

                @pl.when(jnp.logical_not(chosen))
                def take_other():
                    kv_ref[head, group] = other[group][...]
                    kvt_ref[head, group] = other[group][...].T

        top_ref[...] = jnp.full_like(top_ref, far_below)
        mass_ref[...] = jnp.zeros_like(mass_ref)
        out_ref[...] = jnp.zeros_like(out_ref)

        def one_group(group, unused):
            for head in range(2):
                row = sel_ref[head] * groups + group
                own_rows = pl.ds(head * HEAD, HEAD)
                stat = pl.ds(head, 1)
                place_ref[...] = key_positions(key_ref, row, 0, 2 * blocks, half_rows, 128)
                for k_start in range(0, rows, deep):
                    keys_at = pl.ds(k_start, deep)
                    k_side = k_start // half
                    block = kv_ref[head, group, keys_at, :]
                    values = kvt_ref[head, group, pl.ds(HEAD, HEAD), keys_at]
                    for start in range(k_side * half, rows, wide):
                        lanes = pl.ds(start, wide)
                        turned = q_ref[own_rows, lanes]
                        padded = jnp.concatenate([turned, jnp.zeros_like(turned)], axis=0)
                        scores = nn(block, padded)
                        if start // half == k_side:
                            places = query_positions(
                                query_ref, start // half_rows, wide, half_rows
                            )
                            scores = jnp.where(place_ref[keys_at, :] <= places, scores, far_below)
                        before = top_ref[stat, lanes]
                        top = jnp.maximum(before, jnp.max(scores, axis=0, keepdims=True))
                        weights = jnp.exp(scores - top)
                        fade = jnp.exp(before - top)
                        top_ref[stat, lanes] = top
                        mass_ref[stat, lanes] = mass_ref[stat, lanes] * fade + jnp.sum(
                            weights, axis=0, keepdims=True
                        )
                        out_ref[own_rows, lanes] = out_ref[own_rows, lanes] * fade + nn(
                            values, weights.astype(bf16)
                        )
            return unused

        lax.fori_loop(0, groups, one_group, 0)
        for head in range(2):
            own_rows = pl.ds(head * HEAD, HEAD)
            mass = mass_ref[pl.ds(head, 1), :]
            out_ref[own_rows, :] = out_ref[own_rows, :] / mass
            lse_ref[pl.ds(head, 1), :] = top_ref[pl.ds(head, 1), :] + jnp.log(mass)
        low_ref[...] = out_ref[...].T.astype(bf16)

    return call(
        kernel,
        [shape((OWN, rows), f32), shape((rows, OWN), bf16), shape((2, rows), f32)],
        [select, key_base, query_base, turned_query, *own_kv, *other_kv],
        scalars=3,
        scratch=[
            pltpu.VMEM((2, groups, rows, OWN), bf16),
            pltpu.VMEM((2, groups, OWN, rows), bf16),
            pltpu.VMEM((2, rows), f32),
            pltpu.VMEM((2, rows), f32),
            pltpu.VMEM((rows, 128), i32),
        ],
        limit=60,
        cost=14.0,
    )


def attention_backward(
    select, key_base, query_base, turned_query, own_kv, other_kv, traded, attended, log_mass, half_rows
):
    groups = len(own_kv)
    rows = own_kv[0].shape[0]
    half = rows // 2
    blocks = half // half_rows
    wide, deep = 512, 256

    def kernel(sel_ref, key_ref, query_ref, q_ref, *refs):
        own, other = refs[:groups], refs[groups : 2 * groups]
        refs = refs[2 * groups :]
        local = 2 * half_rows
        parts = [refs[0], refs[1]] + [
            refs[2 + j].at[pl.ds(k * local, local), :] for j in range(TP // 2 - 1) for k in range(2)
        ]
        refs = refs[1 + TP // 2 :]
        att_ref, lse_ref, dq_ref, keep_ref, pass_ref, gb_ref = refs[:6]
        kv_ref, sum_ref, g_ref, rq_ref, rg_ref, delta_ref, pos_ref = refs[6:]
        for group in range(groups):
            kv_ref[0, group] = own[group][...]
            kv_ref[1, group] = other[group][...]
        sum_ref[...] = jnp.zeros_like(sum_ref)
        dq_ref[...] = jnp.zeros_like(dq_ref)
        zeros = jnp.zeros((rows, HEAD), bf16)
        for j in range(0, TP, 2):
            for side in range(2):
                at = pl.ds(side * half + j * half_rows, 2 * half_rows)
                pair = jnp.concatenate(
                    [parts[j + k][pl.ds(side * half_rows, half_rows), :] for k in range(2)], axis=0
                )
                g_ref[:, at] = pair[:, :OWN].T
                gb_ref[at, :] = pair[:, OWN:]
        for head in range(2):
            own_rows = pl.ds(head * HEAD, HEAD)
            rq_ref[head] = jnp.concatenate([q_ref[own_rows, :].T, zeros], axis=1)
            grad = g_ref[own_rows, :]
            rg_ref[head] = jnp.concatenate([zeros, grad.T], axis=1)
            delta_ref[pl.ds(head, 1), :] = jnp.sum(
                grad.astype(f32) * att_ref[own_rows, :], axis=0, keepdims=True
            )

        def one_group(group, unused):
            for head in range(2):
                which = sel_ref[head]
                own_rows = pl.ds(head * HEAD, HEAD)
                stat = pl.ds(head, 1)
                pos_ref[...] = key_positions(
                    key_ref, which * groups + group, 0, 2 * blocks, half_rows, 128
                )
                for k_start in range(0, rows, deep):
                    keys_at = pl.ds(k_start, deep)
                    k_side = k_start // half
                    block = kv_ref[which, group, keys_at, :]
                    turned_keys = block.T[:HEAD]
                    for start in range(k_side * half, rows, wide):
                        lanes = pl.ds(start, wide)
                        turned = q_ref[own_rows, lanes]
                        padded = jnp.concatenate([turned, jnp.zeros_like(turned)], axis=0)
                        scores = nn(block, padded)
                        if start // half == k_side:
                            places = query_positions(
                                query_ref, start // half_rows, wide, half_rows
                            )
                            at = jnp.concatenate([pos_ref[keys_at, :]] * (wide // 128), axis=1)
                            scores = jnp.where(at <= places, scores, far_below)
                        probs = jnp.exp(scores - lse_ref[stat, lanes])
                        grads = g_ref[own_rows, lanes]
                        padded = jnp.concatenate([jnp.zeros_like(grads), grads], axis=0)
                        grad_probs = nn(block, padded)
                        grad_scores = probs * (grad_probs - delta_ref[stat, lanes])
                        probs = probs.astype(bf16)
                        grad_scores = grad_scores.astype(bf16)
                        sum_ref[which, group, keys_at, :] += nn(
                            grad_scores, rq_ref[head, lanes, :]
                        ) + nn(probs, rg_ref[head, lanes, :])
                        dq_ref[own_rows, lanes] += nn(turned_keys, grad_scores)
            return unused

        lax.fori_loop(0, groups, one_group, 0)
        for group in range(groups):
            keep_ref[pl.ds(group * rows, rows), :] = sum_ref[0, group]
            pass_ref[pl.ds(group * rows, rows), :] = sum_ref[1, group].astype(bf16)

    return call(
        kernel,
        [
            shape((OWN, rows), f32),
            shape((groups * rows, OWN), f32),
            shape((groups * rows, OWN), bf16),
            shape((rows, OWN), bf16),
        ],
        [
            select,
            key_base,
            query_base,
            turned_query,
            *own_kv,
            *other_kv,
            *traded,
            attended,
            log_mass,
        ],
        scalars=3,
        scratch=[
            pltpu.VMEM((2, groups, rows, OWN), bf16),
            pltpu.VMEM((2, groups, rows, OWN), f32),
            pltpu.VMEM((OWN, rows), bf16),
            pltpu.VMEM((2, rows, OWN), bf16),
            pltpu.VMEM((2, rows, OWN), bf16),
            pltpu.VMEM((2, rows), f32),
            pltpu.VMEM((rows, 128), i32),
        ],
        limit=28,
        cost=18.0,
    )


def store_blocks(part, tile, per, half_rows, keep_ref, pass_ref, x_first=False):
    side = (tile * per) // TP
    first = lax.rem(tile * per, TP) // 2
    for j in range(per):
        piece = part[j * half_rows : (j + 1) * half_rows]
        place = first // 2 + j if x_first else first + j // 2
        if x_first and j % 2:
            place = first // 2 + j - 1
        row = (2 * place + side) * half_rows
        at = pl.ds(pl.multiple_of(row, half_rows), half_rows)
        target = keep_ref if j % 2 == 0 else pass_ref
        target[at, pl.ds(0, piece.shape[1])] = piece.astype(target.dtype)


def feed_forward(at, inputs, attended, sides, packs, gains, nz):
    rows, width = inputs.shape
    local = rows // TP
    half_rows = local // 2
    half = rows // 2
    d_rows, lanes = packs[0].shape
    ff = lanes // 3
    part_rows = ff // nz
    per = 4
    tile_rows = per * half_rows
    tiles = 2 * TP // per

    def kernel(at_ref, x_ref, *refs):
        att, refs = refs[:TP], refs[TP:]
        extra, refs = refs[:TP], refs[TP:]
        pack, refs = refs[:nz], refs[nz:]
        gain_ref, refs = refs[0], refs[1:]
        resid_out, gk_ref, gp_ref, gain_out, dn_w = refs[:5]
        targets, prod_out, refs = refs[5 : 5 + nz], refs[5 + nz], refs[6 + nz :]
        att_ref, wo_ref, gu_w, cot_ref, hold, acc_gu, acc_dn, blocks, prod_ref, sems = refs
        tp = at_ref[0]
        z = at_ref[1]
        for j in range(TP):
            columns = pl.ds(pl.multiple_of((tp ^ j) * OWN, OWN), OWN)
            wo_ref[columns, :] = extra[j][pl.ds(local, OWN), pl.ds(0, width)]
            for side in range(2):
                for k in range(TP):
                    att_ref[pl.ds(side * half + k * half_rows, half_rows), columns] = att[j][
                        pl.ds(side * half + (k ^ j) * half_rows, half_rows), :
                    ]
                cot_ref[pl.ds(side * half + j * half_rows, half_rows), :] = extra[j][
                    pl.ds(side * half_rows, half_rows), pl.ds(0, width)
                ]
        for s in range(nz):
            hold[z ^ s] = pack[s][...]
        for s in range(nz):
            rows_at = pl.ds(s * d_rows, d_rows)
            gu_w[rows_at, :] = hold[s, :, pl.ds(0, 2 * ff)]
            dn_w[rows_at, :] = jnp.concatenate(
                [
                    hold[b][:, 2 * ff + s * part_rows : 2 * ff + (s + 1) * part_rows]
                    for b in range(nz)
                ],
                axis=1,
            )
        gain = gain_ref[pl.ds(1, 1), :]
        gain_out[...] = jnp.zeros_like(gain_out)
        acc_gu[...] = jnp.zeros_like(acc_gu)
        acc_dn[...] = jnp.zeros_like(acc_dn)

        def copy_of(tile):
            at_rows = pl.ds(pl.multiple_of(tile * tile_rows, tile_rows), tile_rows)
            return pltpu.make_async_copy(
                prod_ref.at[at_rows, :], prod_out.at[at_rows, :], sems.at[tile]
            )

        def one_tile(tile, unused):
            at_rows = pl.ds(pl.multiple_of(tile * tile_rows, tile_rows), tile_rows)
            branch = nt(att_ref[at_rows, :][:, :width], wo_ref[pl.ds(0, width), :])
            resid = x_ref[at_rows, :].astype(f32) + branch
            side = (tile * per) // TP

            @pl.when(lax.rem(tile * per, TP) == 0)
            def keep_own():
                resid_out[pl.ds(pl.multiple_of(side * half_rows, half_rows), half_rows), :] = resid[
                    :half_rows
                ]

            normal = resid * norm_scale(resid)
            hidden = (normal * gain).astype(bf16)
            gate_up = nn(hidden, gu_w[...])
            gate, up = gate_up[:, :ff], gate_up[:, ff:]
            sigmoid = 1.0 / (1.0 + jnp.exp(-gate))
            activated = gate * sigmoid
            product = (activated * up).astype(bf16)
            prod_ref[at_rows, :] = product
            copy_of(tile).start()
            cotangent = cot_ref[at_rows, :]
            grad_product = nn(cotangent, dn_w[...])
            grad_gate = grad_product * up * sigmoid * (1.0 + gate * (1.0 - sigmoid))
            grad_gu = jnp.concatenate([grad_gate, grad_product * activated], axis=1).astype(bf16)
            partial = nt(grad_gu, gu_w[...])
            gain_out[pl.ds(0, 1), :] += jnp.sum(partial * normal, axis=0, keepdims=True)
            store_blocks(partial, tile, per, half_rows, gk_ref, gp_ref)
            acc_gu[...] += tn(hidden, grad_gu)
            acc_dn[...] += tn(cotangent, product)
            return unused

        lax.fori_loop(0, tiles, one_tile, 0)
        for b in range(nz):
            blocks[b, :, pl.ds(0, 2 * ff)] = acc_gu[pl.ds(b * d_rows, d_rows), :]
            blocks[b, :, pl.ds(2 * ff, ff)] = jnp.concatenate(
                [
                    acc_dn[pl.ds(s * d_rows, d_rows), :][:, b * part_rows : (b + 1) * part_rows]
                    for s in range(nz)
                ],
                axis=1,
            )
        for s in range(nz):
            targets[s][...] = blocks[z ^ s].astype(targets[s].dtype)
        for tile in range(tiles):
            copy_of(tile).wait()

    return call(
        kernel,
        [
            shape((local, width), f32),
            shape((TP // 2 * local, width), bf16),
            shape((TP // 2 * local, TP * OWN), bf16),
            shape((8, width), f32),
            shape((width, ff), bf16),
        ]
        + [shape((d_rows, lanes), f32 if s % 2 == 0 else bf16) for s in range(nz)]
        + [shape((rows, ff), bf16)],
        [at, inputs, *attended, *sides, *packs, gains],
        scratch=[
            pltpu.VMEM((rows, TP * OWN), bf16),
            pltpu.VMEM((TP * OWN, width), bf16),
            pltpu.VMEM((width, 2 * ff), bf16),
            pltpu.VMEM((rows, width), bf16),
            pltpu.VMEM((nz, d_rows, lanes), bf16),
            pltpu.VMEM((width, 2 * ff), f32),
            pltpu.VMEM((width, ff), f32),
            pltpu.VMEM((nz, d_rows, lanes), f32),
            pltpu.VMEM((rows, ff), bf16),
            pltpu.SemaphoreType.DMA((tiles,)),
        ],
        limit=44,
        cost=17.0,
        far_out=(5 + nz,),
    )


def feed_forward_rest(at, attended, sides, product, w_down):
    rows = attended[0].shape[0]
    width, ff = w_down.shape
    local = rows // TP
    half_rows = local // 2
    half = rows // 2
    per = 4
    tile_rows = per * half_rows

    def kernel(at_ref, *refs):
        att, refs = refs[:TP], refs[TP:]
        extra, refs = refs[:TP], refs[TP:]
        prod_ref, dn_w, att_out, wo_out, lk_ref, lp_ref = refs
        tp = at_ref[0]
        for j in range(TP):
            columns = pl.ds(pl.multiple_of((tp ^ j) * OWN, OWN), OWN)
            wo_out[columns, :] = extra[j][pl.ds(local, OWN), pl.ds(0, width)]
            for side in range(2):
                for k in range(TP):
                    att_out[pl.ds(side * half + k * half_rows, half_rows), columns] = att[j][
                        pl.ds(side * half + (k ^ j) * half_rows, half_rows), :
                    ]

        def one_tile(tile, unused):
            at_rows = pl.ds(pl.multiple_of(tile * tile_rows, tile_rows), tile_rows)
            part = nt(prod_ref[at_rows, :], dn_w[...])
            store_blocks(part, tile, per, half_rows, lk_ref, lp_ref)
            return unused

        lax.fori_loop(0, 2 * TP // per, one_tile, 0)

    return call(
        kernel,
        [
            shape((rows, TP * OWN), bf16),
            shape((TP * OWN, width), bf16),
            shape((TP // 2 * local, width), bf16),
            shape((TP // 2 * local, TP * OWN), bf16),
        ],
        [at, *attended, *sides, product, w_down],
        limit=24,
        cost=5.0,
    )


def add_crossed(keep, crossed, count, tail=None):
    local, width = keep.shape[0] // count, keep.shape[1]
    tails = [] if tail is None else [tail]
    more = 0 if tail is None else tail.shape[0]

    def kernel(keep_ref, cross_ref, *refs):
        own_ref, *sends = refs[len(tails) :]
        for j in range(count):
            at = pl.ds(j * local, local)
            target = own_ref if j == 0 else sends[j - 1]
            target[pl.ds(0, local), pl.ds(0, width)] = (
                keep_ref[at, :].astype(f32) + cross_ref[at, pl.ds(0, width)].astype(f32)
            ).astype(target.dtype)
        if tails:
            sends[-1][pl.ds(local, more), pl.ds(0, width)] = refs[0][...]

    return call(
        kernel,
        [shape((local, width), f32)]
        + [shape((local, width), bf16)] * (count - 2)
        + [shape((local + more, TP * OWN if tails else width), bf16)],
        [keep, crossed, *tails],
        scalars=0,
        limit=12,
        cost=1.0,
    )


def branch_gradient(at, sums, resid, cotangent, w_out, gains):
    local, width = resid.shape

    def kernel(at_ref, *refs):
        parts, refs = refs[: len(sums)], refs[len(sums) :]
        resid_ref, cot_ref, wo_ref, gain_ref, grad_ref, keep_ref, pass_ref, ga_ref, gb_ref = refs
        tp = at_ref[0]
        grad_hidden = parts[0][...]
        for part in parts[1:]:
            grad_hidden = grad_hidden + part[...].astype(f32)
        resid = resid_ref[...]
        scale = norm_scale(resid)
        normal = resid * scale
        grad = grad_hidden * gain_ref[pl.ds(1, 1), :]
        grad = scale * (grad - normal * jnp.mean(grad * normal, axis=1, keepdims=True))
        grad = grad + cot_ref[...].astype(f32)
        grad_ref[...] = grad
        low = grad.astype(bf16)
        gb_ref[...] = jnp.zeros_like(gb_ref)
        gb_ref[:, pl.ds(0, width)] = low
        ga_ref[...] = jnp.zeros_like(ga_ref)
        ga_ref[:, pl.ds(0, width)] = nn(low, wo_ref[pl.ds(0, width), :]).astype(bf16)
        for j in range(TP):
            columns = pl.ds(pl.multiple_of((tp ^ j) * OWN, OWN), OWN)
            target = keep_ref if j % 2 == 0 else pass_ref
            rows = pl.ds((j // 2) * local, local)
            target[rows, pl.ds(0, OWN)] = ga_ref[:, columns]
            target[rows, pl.ds(OWN, OWN)] = gb_ref[:, columns]

    blocks = shape((TP // 2 * local, 2 * OWN), bf16)
    return call(
        kernel,
        [shape((local, width), f32), blocks, blocks],
        [at, *sums, resid, cotangent, w_out, gains],
        scratch=[pltpu.VMEM((local, TP * OWN), bf16), pltpu.VMEM((local, TP * OWN), bf16)],
        limit=16,
        cost=3.0,
    )


def pair_up(keep, crossed, count):
    local, width = keep.shape[0] // count, keep.shape[1]

    def kernel(keep_ref, cross_ref, *outs):
        for j in range(1, count):
            at = pl.ds(j * local, local)
            outs[j - 1][pl.ds(0, local), :] = keep_ref[at, :]
            outs[j - 1][pl.ds(local, local), :] = cross_ref[at, :]

    return call(
        kernel,
        [shape((2 * local, width), bf16)] * (count - 1),
        [keep, crossed],
        scalars=0,
        limit=8,
        cost=0.7,
    )


def projection_gradient(
    at, grad_query, grad_kv, inputs, hidden, w_qkv, gain_sums, cosine, sine, grad_out, nz
):
    rows, width = inputs.shape
    local = rows // TP
    half_rows = local // 2
    d_rows = width // nz
    per = 4
    tile_rows = per * half_rows
    pieces = len(grad_kv)

    def kernel(at_ref, dq_ref, *refs):
        kvs, refs = refs[:pieces], refs[pieces:]
        x_ref, hid_ref, w_ref, gain_two_ref, cos_ref, sin_ref, wo_ref = refs[:7]
        keep_ref, pass_ref, own_ref = refs[7:10]
        sends, refs = refs[10 : 10 + nz - 1], refs[10 + nz - 1 :]
        turn_ref, acc_ref, gain_acc, hold = refs
        z = at_ref[1]
        turn_ref[...] = dq_ref[...].T * HEAD**-0.5
        acc_ref[...] = jnp.zeros_like(acc_ref)
        gain_acc[...] = jnp.zeros_like(gain_acc)

        def one_tile(tile, unused):
            at_rows = pl.ds(pl.multiple_of(tile * tile_rows, tile_rows), tile_rows)
            cos, sin = cos_ref[at_rows, :], sin_ref[at_rows, :]
            query = turn_ref[at_rows, :]
            query = query * cos - swap_halves(query) * sin
            pair = kvs[0][at_rows, :].astype(f32)
            for piece in kvs[1:]:
                pair = pair + piece[at_rows, :].astype(f32)
            turned = pair * cos - swap_halves(pair) * sin
            lane = lax.broadcasted_iota(i32, pair.shape, 1)
            pair = jnp.where(lane < HEAD, turned, pair)
            grad = jnp.concatenate([query, pair], axis=1).astype(bf16)
            partial = nt(grad, w_ref[...])
            x = x_ref[at_rows, :].astype(f32)
            gain_acc[pl.ds(0, 1), :] += jnp.sum(partial * (x * norm_scale(x)), axis=0, keepdims=True)
            store_blocks(partial, tile, per, half_rows, keep_ref, pass_ref, True)
            acc_ref[...] += tn(hid_ref[at_rows, :], grad)
            return unused

        lax.fori_loop(0, 2 * TP // per, one_tile, 0)
        hold[...] = jnp.zeros_like(hold)
        for s in range(nz):
            columns = slice(s * d_rows, (s + 1) * d_rows)
            hold[s, pl.ds(0, 1), pl.ds(0, d_rows)] = gain_acc[pl.ds(0, 1), :][:, columns]
            hold[s, pl.ds(1, 1), pl.ds(0, d_rows)] = gain_two_ref[pl.ds(0, 1), :][:, columns]
        for s in range(nz):
            block = z ^ s
            target = own_ref if s == 0 else sends[s - 1]
            rows_at = pl.ds(pl.multiple_of(block * d_rows, 8), d_rows)
            part = pl.ds(0, d_rows)
            target[part, pl.ds(0, 2 * OWN)] = acc_ref[rows_at, :].astype(target.dtype)
            target[part, pl.ds(2 * OWN, OWN)] = wo_ref[rows_at, :].astype(target.dtype)
            target[pl.ds(d_rows, 16), :] = hold[block].astype(target.dtype)

    return call(
        kernel,
        [
            shape((TP // 2 * local, width), bf16),
            shape((TP // 2 * local, TP * OWN), bf16),
            shape((d_rows + 16, 3 * OWN), f32),
        ]
        + [shape((d_rows + 16, 3 * OWN), bf16)] * (nz - 1),
        [at, grad_query, *grad_kv, inputs, hidden, w_qkv, gain_sums, cosine, sine, grad_out],
        scratch=[
            pltpu.VMEM((rows, OWN), f32),
            pltpu.VMEM((width, 2 * OWN), f32),
            pltpu.VMEM((8, width), f32),
            pltpu.VMEM((nz, 16, 3 * OWN), f32),
        ],
        limit=32,
        cost=8.0,
    )


def token_gradient(sums, tokens, grad_resid, gains):
    local, width = tokens.shape

    def kernel(*refs):
        parts, refs = refs[: len(sums)], refs[len(sums) :]
        x_ref, grad_ref, gain_ref, out_ref = refs
        grad_hidden = parts[0][...]
        for part in parts[1:]:
            grad_hidden = grad_hidden + part[...].astype(f32)
        x = x_ref[...].astype(f32)
        scale = norm_scale(x)
        normal = x * scale
        grad = grad_hidden * gain_ref[pl.ds(0, 1), :]
        grad = scale * (grad - normal * jnp.mean(grad * normal, axis=1, keepdims=True))
        out_ref[...] = (grad + grad_ref[...]).T

    return call(
        kernel,
        [shape((width, local), f32)],
        [*sums, tokens, grad_resid, gains],
        scalars=0,
        limit=8,
        cost=1.0,
    )[0].T


def layer_output(near, arrived, resid):
    local, width = resid.shape
    start = arrived.shape[0] - local

    def kernel(near_ref, in_ref, resid_ref, out_ref):
        total = resid_ref[...] + near_ref[...] + in_ref[pl.ds(start, local), pl.ds(0, width)].astype(f32)
        out_ref[...] = total.T.astype(bf16)

    turned = shape(resid.shape[::-1], bf16)
    return call(kernel, [turned], [near, arrived, resid], scalars=0, limit=8, cost=1.0)[0].T


def first_sum(own, arrived):
    def kernel(own_ref, in_ref, out_ref):
        out_ref[...] = (own_ref[...] + in_ref[...].astype(f32)).astype(bf16)

    return call(
        kernel, [shape(own.shape, bf16)], [own, arrived], scalars=0, limit=8, cost=1.0
    )[0]


def last_sum(own, *arrived):
    rows, lanes = own.shape

    def kernel(own_ref, *refs):
        total = own_ref[...]
        for ref in refs[:-1]:
            total = total + ref[...].astype(f32)
        refs[-1][:, pl.ds(0, lanes)] = total.astype(bf16)

    return call(
        kernel, [shape((rows, TP * OWN), bf16)], [own, *arrived], scalars=0, limit=8, cost=1.0
    )[0]


def ff_outputs(at, mine, by_x, by_y, by_xy, odd, ff_z, nz):
    d_rows = mine.shape[0]
    part = ff_z // TP
    ff = part * nz

    def kernel(at_ref, m_ref, x_ref, y_ref, xy_ref, odd_ref, gate_ref, up_ref, down_ref, hold):
        tp = at_ref[0]
        lanes = pl.ds(0, 3 * ff)
        for j, ref in enumerate((m_ref, x_ref, y_ref, xy_ref)):
            hold[tp ^ (2 * j)] = ref[:, lanes]
        for j in range(TP // 2):
            hold[tp ^ (2 * j + 1)] = odd_ref[pl.ds(d_rows * j, d_rows), lanes]
        for s in range(nz):
            for start in (s * part, ff + s * part, 2 * ff + s * part):
                block = jnp.concatenate(
                    [hold[c][:, start : start + part] for c in range(TP)], axis=1
                ).astype(f32)
                if start < ff:
                    gate_ref[:, pl.ds(s * ff_z, ff_z)] = block
                elif start < 2 * ff:
                    up_ref[:, pl.ds(s * ff_z, ff_z)] = block
                else:
                    down_ref[pl.ds(s * d_rows, d_rows), :] = block

    gate, up, down = call(
        kernel,
        [
            shape((d_rows, nz * ff_z), f32),
            shape((d_rows, nz * ff_z), f32),
            shape((nz * d_rows, ff_z), f32),
        ],
        [at, mine, by_x, by_y, by_xy, odd],
        scratch=[pltpu.VMEM((TP, d_rows, 3 * ff), bf16)],
        limit=32,
        cost=7.0,
    )
    return gate, up, down.T


def projection_outputs(at, slots, width):
    d_rows = slots[0].shape[0] - 16

    def kernel(at_ref, *refs):
        parts, (q_ref, k_ref, v_ref, o_ref, one_ref, two_ref, hold) = refs[:TP], refs[TP:]
        tp = at_ref[0]
        total = jnp.zeros((16, 3 * OWN), f32)
        for j in range(TP):
            hold[tp ^ j] = parts[j][...].astype(f32)
            total = total + parts[j][pl.ds(d_rows, 16), :].astype(f32)
        one_ref[...] = total[0:1, :d_rows]
        two_ref[...] = total[1:2, :d_rows]
        heads = [hold[c][:d_rows, :OWN] for c in range(TP)]
        q_ref[...] = jnp.concatenate(heads, axis=1)[:, :width]
        heads = [hold[c][:d_rows, 2 * OWN :] for c in range(TP)]
        o_ref[...] = jnp.concatenate(heads, axis=1)[:, :width]
        kv = [hold[c][:d_rows, OWN : 2 * OWN] for c in range(TP)]
        kv = [kv[0], kv[1] + kv[2], kv[3] + kv[4], kv[5], kv[6]]
        for c in range(KV_HEADS):
            turned = kv[c].T
            k_ref[pl.ds(c * HEAD, HEAD), :] = turned[:HEAD]
            v_ref[pl.ds(c * HEAD, HEAD), :] = turned[HEAD:]

    query, key, value, out, one, two = call(
        kernel,
        [
            shape((d_rows, width), f32),
            shape((KV_HEADS * HEAD, d_rows), f32),
            shape((KV_HEADS * HEAD, d_rows), f32),
            shape((d_rows, width), f32),
            shape((1, d_rows), f32),
            shape((1, d_rows), f32),
        ],
        [at, *slots],
        scratch=[pltpu.VMEM((TP, d_rows + 16, 3 * OWN), f32)],
        limit=12,
        cost=0.01,
    )
    return query, key.T, value.T, out, one, two


def body(
    tokens,
    pair_order,
    gain_attn,
    gain_mlp,
    w_query,
    w_key,
    w_value,
    w_out,
    w_gate,
    w_up,
    w_down,
    cotangent,
):
    local_rows, width = tokens.shape
    half_rows = local_rows // 2
    nz = lax.axis_size("fsdp")
    outer = lax.axis_size("ctx") // TP
    count = lax.axis_size(AXES)
    groups = outer * nz
    me = lax.axis_index(AXES)
    z = lax.axis_index("fsdp")
    tp = lax.axis_index("ctx") % TP
    kv_index = (4 * (tp // 2)) // GROUP + tp % 2
    at = jnp.stack([tp, z, kv_index]).astype(i32)
    send = functools.partial(exchange, count=count)
    group_mask = [(g // nz) * TP * nz + g % nz for g in range(groups)]

    def after(value, *others):
        return lax.optimization_barrier((value, *others))[0]

    def level(*arrays):
        return list(lax.optimization_barrier(arrays))

    def gather_even(block):
        return [block] + [send(block, j * nz) for j in range(2, TP, 2)]

    def gather_odd(even):
        return [piece for e in even for piece in (e, send(e, nz))]

    def scatter_far(pieces):
        return [send(piece, 2 * (j + 1) * nz) for j, piece in enumerate(pieces)]

    def from_z(block):
        return [block] + [send(block, s) for s in range(1, nz)]

    pack_one = slice_attention_weights(at, w_query, w_key, w_value, w_out, gain_attn, gain_mlp)
    token_slots = gather_odd(level(*gather_even(tokens)))
    pack_two = slice_ff_weights(after(at, pack_one), w_gate, w_up, w_down, nz)
    pack_one = from_z(pack_one)

    slot_of = jnp.array([[m | (j * nz) for j in range(TP)] for m in group_mask], dtype=i32)
    low = pair_order[me ^ slot_of]
    base = jnp.stack([low, 2 * count - 1 - low], axis=1) * half_rows
    query_base = base[0].reshape(2 * TP)
    partner = jnp.array([j ^ 1 for j in range(TP)], dtype=i32)
    key_base = jnp.stack([base, base[:, :, partner]]).reshape(2 * groups, 2 * TP)
    places = (query_base[:, None] + jnp.arange(half_rows, dtype=i32)[None, :]).reshape(-1)
    lane = jnp.arange(OWN)
    freqs = base_theta ** (-2.0 * (lane % (HEAD // 2)).astype(f32) / HEAD)
    angles = places.astype(f32)[:, None] * freqs[None, :]
    cosine = jnp.cos(angles)
    sine = jnp.sin(angles) * jnp.where(lane % HEAD < HEAD // 2, -1.0, 1.0)[None, :]
    select = jnp.where((2 * tp + jnp.arange(2)) // GROUP == kv_index, 0, 1).astype(i32)

    mask_x, mask_y = 2 * nz, 4 * nz
    hidden_one, kv, w_qkv, side, gains = project_keys(
        after(at, pack_two, select, key_base, query_base),
        token_slots,
        pack_one,
        cosine,
        sine,
        cotangent,
    )
    own_kv = [kv] + [send(kv, m) for m in group_mask[1:]]
    side_x, side_y = send(side, mask_x), send(side, mask_y)
    inputs, turned_query = project_queries(
        token_slots, after(hidden_one, kv), w_qkv, cosine, sine
    )
    side_x, side_y, inputs, turned_query, *own_kv = level(
        side_x, side_y, inputs, turned_query, *own_kv
    )
    other_kv = level(*[send(slot, nz) for slot in own_kv])
    one, near = send(after(pack_two, *own_kv), 1), send(after(pack_two, *own_kv), 2)
    side_xy = send(side_x, mask_y)
    side_odd, odd_x = send(after(side, *other_kv), nz), send(after(side_x, *other_kv), nz)
    attended, attended_own, log_mass = attention_forward(
        select, key_base, query_base, turned_query, own_kv, other_kv, half_rows
    )
    attended_own, near, one, side_xy, side_odd, odd_x = level(
        attended_own, near, one, side_xy, side_odd, odd_x
    )
    far, side_xy, *even = level(send(near, 1), side_xy, *gather_even(attended_own))
    attended_slots = gather_odd(even)
    packs = [pack_two, one, near, far]
    odd_y = send(after(side_y, side_xy), nz)
    sides = [side, side_odd, side_x, odd_x, side_y, odd_y, side_xy, send(side_xy, nz)]

    resid, grad_keep, grad_pass, gain_sums, w_down_own, *ff_blocks, product = feed_forward(
        at, inputs, attended_slots, sides, packs, gains, nz
    )
    ff_own, ff_one, ff_two, ff_three = ff_blocks
    first, *rest = add_crossed(grad_keep, send(grad_pass, nz), TP // 2)
    attended_low, w_out_all, out_keep, out_pass, ff_three, first, *rest = level(
        *feed_forward_rest(after(at, first), attended_slots, sides, product, w_down_own),
        send(after(ff_three, first), 1),
        first,
        *scatter_far(rest),
    )
    grad_resid, trade_keep, trade_pass = branch_gradient(
        at, [first, *rest], resid, cotangent, w_out_all, gains
    )
    crossed, out_crossed = level(send(trade_pass, nz), send(after(out_pass, first), nz))
    pairs = level(*scatter_far(pair_up(trade_keep, crossed, TP // 2)))
    out_near, out_far = add_crossed(out_keep, out_crossed, 2)
    ff_one = send(after(ff_one, crossed), 1)
    ff_two = send(first_sum(ff_two, ff_three), 2)
    out_far = send(after(out_far, *pairs), mask_y)

    grad_query, kv_keep, kv_pass, branch_columns = attention_backward(
        after(select, out_near),
        key_base,
        query_base,
        turned_query,
        own_kv,
        other_kv,
        [trade_keep, crossed, *pairs],
        attended,
        log_mass,
        half_rows,
    )
    kv_pass, ff_one, ff_two, out_far = level(kv_pass, ff_one, ff_two, out_far)
    kv_crossed = send(kv_pass, nz)
    first, *rest = add_crossed(kv_keep, kv_crossed, groups)
    grad_out = tn(attended_low[:, :width], after(branch_columns, rest[0]))
    ff_total = last_sum(after(ff_own, grad_out), ff_one, ff_two)

    for step in range(outer.bit_length() - 1):
        crossing = send(ff_total, TP * nz << step).astype(f32)
        ff_total = (ff_total.astype(f32) + crossing).astype(bf16)
    out_near, out_far = add_crossed(after(out_near, rest[0]), out_far, 2)
    ff_x, ff_y, *grad_kv = level(
        send(ff_total, mask_x),
        send(ff_total, mask_y),
        *[send(piece, m) for piece, m in zip(rest, group_mask[1:])],
    )

    last_keep, last_pass, last_own, *last_sends = projection_gradient(
        at,
        grad_query,
        [first, *grad_kv],
        inputs,
        hidden_one,
        w_qkv,
        gain_sums,
        cosine,
        sine,
        grad_out,
        nz,
    )
    near, far = add_crossed(last_keep, send(last_pass, nz), 2, out_far)
    ff_xy, far, *arrived = level(
        send(after(ff_x, last_own), mask_y),
        send(far, mask_x),
        *[send(piece, s + 1) for s, piece in enumerate(last_sends)],
    )
    layer_out = layer_output(out_near, far, resid)
    near, far = add_crossed(near, far, 2)
    last_total = last_own
    for piece in arrived:
        last_total = last_total + piece.astype(f32)
    for step in range(outer.bit_length() - 1):
        last_total = last_total + send(last_total.astype(bf16), TP * nz << step).astype(f32)
    last_total = last_total.astype(bf16)
    ff_slots = [ff_total, ff_x, ff_y, ff_xy]
    ff_slots.append(send(jnp.concatenate(ff_slots, axis=0), nz))
    grad_gate, grad_up, grad_down = ff_outputs(at, *ff_slots, w_down.shape[0], nz)
    far = send(far, mask_y)
    grad_gate, *even = level(grad_gate, *gather_even(last_total))
    last_slots = gather_odd(even)
    grad_w_query, grad_w_key, grad_w_value, grad_out, gain_one, gain_two = projection_outputs(
        at, last_slots, width
    )
    grad_tokens = token_gradient([after(near, grad_w_query), far], tokens, grad_resid, gains)
    return (
        layer_out,
        grad_tokens,
        gain_one.reshape(-1),
        gain_two.reshape(-1),
        grad_w_query,
        grad_w_key,
        grad_w_value,
        grad_out,
        grad_gate,
        grad_up,
        grad_down,
    )


def solution(mesh):
    return jax.shard_map(
        body,
        mesh=mesh,
        in_specs=(
            P(("ctx", "fsdp"), None),
            P(),
            P("fsdp"),
            P("fsdp"),
            P("fsdp", None),
            P("fsdp", None),
            P("fsdp", None),
            P("fsdp", None),
            P("fsdp", None),
            P("fsdp", None),
            P("fsdp", None),
            P(("ctx", "fsdp"), None),
        ),
        out_specs=(
            P(("ctx", "fsdp"), None),
            P(("ctx", "fsdp"), None),
            P("fsdp"),
            P("fsdp"),
            P("fsdp", None),
            P("fsdp", None),
            P("fsdp", None),
            P("fsdp", None),
            P("fsdp", None),
            P("fsdp", None),
            P("fsdp", None),
        ),
        check_vma=False,
    )
```

```python
import functools

import jax
import jax.numpy as jnp
from jax import lax
from jax.experimental import pallas as pl
from jax.experimental.pallas import tpu as pltpu
from jax.sharding import PartitionSpec as P

HEADS = 15
KV_HEADS = 5
HEAD = 64
TP = 8
GROUP = HEADS // KV_HEADS
OWN = 2 * HEAD
epsilon = 1e-05
base_theta = 100000.0
far_below = -1e30
f32 = jnp.float32
bf16 = jnp.bfloat16
i32 = jnp.int32
AXES = ("ctx", "fsdp")
MIB = 1024 * 1024
smem = pl.BlockSpec(memory_space=pltpu.SMEM)
vmem = pl.BlockSpec(memory_space=pltpu.VMEM)


def exchange(array, mask, count):
    return lax.ppermute(array, AXES, [(i, i ^ mask) for i in range(count)])


def nn(left, right):
    return lax.dot_general(left, right, (((1,), (0,)), ((), ())), preferred_element_type=f32)


def tn(left, right):
    return lax.dot_general(left, right, (((0,), (0,)), ((), ())), preferred_element_type=f32)


def nt(left, right):
    return lax.dot_general(left, right, (((1,), (1,)), ((), ())), preferred_element_type=f32)


def shape(dims, dtype):
    return jax.ShapeDtypeStruct(dims, dtype)


def call(kernel, outs, inputs, scalars=1, scratch=(), limit=56, cost=1.0, far=(), far_out=()):
    specs = [smem] * scalars + [vmem] * (len(inputs) - scalars)
    for i in far:
        specs[i] = pl.BlockSpec(memory_space=pltpu.HBM)
    out_specs = [vmem for unused in outs]
    for i in far_out:
        out_specs[i] = pl.BlockSpec(memory_space=pltpu.HBM)
    return pl.pallas_call(
        kernel,
        out_shape=tuple(outs),
        in_specs=specs,
        out_specs=tuple(out_specs),
        scratch_shapes=list(scratch),
        compiler_params=pltpu.CompilerParams(vmem_limit_bytes=limit * MIB),
        cost_estimate=pl.CostEstimate(
            flops=int(cost * 1e9), bytes_accessed=int(cost * 1e6), transcendentals=0
        ),
    )(*inputs)


def one_hot(rows, columns, start):
    row = lax.broadcasted_iota(i32, (rows, columns), 0)
    column = lax.broadcasted_iota(i32, (rows, columns), 1)
    return jnp.where(row == column + start, 1.0, 0.0).astype(bf16)


def query_positions(base_ref, at, width, half_rows):
    lane = lax.broadcasted_iota(i32, (1, width), 1)
    place = jnp.zeros((1, width), i32)
    for block in range(width // half_rows):
        start = base_ref[at + block] - block * half_rows
        place = jnp.where(lane >= block * half_rows, start + lane, place)
    return place


def key_positions(base_ref, row, at, count, half_rows, width):
    offset = lax.broadcasted_iota(i32, (half_rows, width), 0)
    return jnp.concatenate([offset + base_ref[row, at + b] for b in range(count)], axis=0)


def swap_halves(matrix):
    lane = lax.broadcasted_iota(i32, matrix.shape, 1)
    ahead = pltpu.roll(matrix, matrix.shape[1] - HEAD // 2, 1)
    behind = pltpu.roll(matrix, HEAD // 2, 1)
    return jnp.where(lane % HEAD < HEAD // 2, ahead, behind)


def norm_scale(matrix):
    return lax.rsqrt(jnp.mean(matrix * matrix, axis=1, keepdims=True) + epsilon)


def slice_attention_weights(at, w_query, w_key, w_value, w_out, gain_one, gain_two):
    d_rows, width = w_query.shape
    lanes = 2 * OWN + OWN
    rest = width - (TP - 1) * OWN

    def kernel(at_ref, q_ref, k_ref, v_ref, o_ref, g1_ref, g2_ref, out_ref, cols, heads, whole, sems):
        tp = at_ref[0]
        kv = at_ref[2]
        wides, narrows = (q_ref, o_ref), (k_ref, v_ref)

        columns = pl.ds(pl.multiple_of(tp * OWN, OWN), OWN)
        rows = pl.ds(pl.multiple_of(kv * HEAD, HEAD), HEAD)

        def wide_copies():
            return [
                pltpu.make_async_copy(ref.at[:, columns], cols.at[i], sems.at[i])
                for i, ref in enumerate(wides)
            ]

        def whole_copies():
            return [
                pltpu.make_async_copy(ref, whole.at[i], sems.at[i]) for i, ref in enumerate(wides)
            ]

        def head_copies():
            return [
                pltpu.make_async_copy(ref.at[rows, :], heads.at[i], sems.at[2 + i])
                for i, ref in enumerate(narrows)
            ]

        @pl.when(tp < TP - 1)
        def most():
            for copy in wide_copies():
                copy.start()

        @pl.when(tp == TP - 1)
        def last():
            for copy in whole_copies():
                copy.start()

        @pl.when(kv < KV_HEADS)
        def real():
            for copy in head_copies():
                copy.start()

        @pl.when(kv >= KV_HEADS)
        def none():
            heads[...] = jnp.zeros_like(heads)

        @pl.when(tp < TP - 1)
        def most_came():
            for copy in wide_copies():
                copy.wait()

        @pl.when(tp == TP - 1)
        def last_came():
            for copy in whole_copies():
                copy.wait()
            for i in range(2):
                cols[i] = jnp.zeros((d_rows, OWN), bf16)
                cols[i, :, pl.ds(0, rest)] = whole[i, :, pl.ds(width - rest, rest)]

        @pl.when(kv < KV_HEADS)
        def real_came():
            for copy in head_copies():
                copy.wait()

        out_ref[pl.ds(0, d_rows), pl.ds(0, OWN)] = cols[0]
        turned = jnp.concatenate([heads[0], heads[1]], axis=0).astype(f32).T
        out_ref[pl.ds(0, d_rows), pl.ds(OWN, OWN)] = turned.astype(bf16)
        out_ref[pl.ds(0, d_rows), pl.ds(2 * OWN, OWN)] = cols[1]
        out_ref[pl.ds(d_rows, 16), :] = jnp.zeros((16, lanes), bf16)
        out_ref[d_rows, pl.ds(0, d_rows)] = g1_ref[...]
        out_ref[d_rows + 1, pl.ds(0, d_rows)] = g2_ref[...]

    return call(
        kernel,
        [shape((d_rows + 16, lanes), bf16)],
        [at, w_query, w_key.T, w_value.T, w_out, gain_one, gain_two],
        scratch=[
            pltpu.VMEM((2, d_rows, OWN), bf16),
            pltpu.VMEM((2, HEAD, d_rows), bf16),
            pltpu.VMEM((2, d_rows, width), bf16),
            pltpu.SemaphoreType.DMA((4,)),
        ],
        limit=60,
        cost=2.0,
        far=(1, 2, 3, 4),
    )[0]


def slice_ff_weights(at, w_gate, w_up, w_down, nz):
    d_rows = w_gate.shape[0]
    ff_z, width = w_down.shape
    part = ff_z // TP
    own = part * nz


    def kernel(at_ref, g_ref, u_ref, d_ref, out_ref):
        pick = one_hot(ff_z, part, at_ref[0] * part)
        for ref, start in ((g_ref, 0), (u_ref, own)):
            pieces = [nn(ref[:, pl.ds(s * ff_z, ff_z)], pick) for s in range(nz)]
            out_ref[:, pl.ds(start, own)] = jnp.concatenate(pieces, axis=1).astype(bf16)
        pieces = [nn(d_ref[pl.ds(s * d_rows, d_rows), :], pick) for s in range(nz)]
        out_ref[:, pl.ds(2 * own, own)] = jnp.concatenate(pieces, axis=1).astype(bf16)

    return call(
        kernel,
        [shape((d_rows, 3 * own), bf16)],
        [at, w_gate, w_up, w_down.T],
        limit=16,
        cost=4.0,
    )[0]


def project_keys(at, tokens, packs, cosine, sine, cotangent):
    local, width = tokens[0].shape
    half_rows = local // 2
    rows = TP * local
    nz = len(packs)
    pack_rows, lanes = packs[0].shape
    d_rows = pack_rows - 16
    per = 4
    tiles = 2 * TP // per

    def kernel(at_ref, *refs):
        toks, refs = refs[:TP], refs[TP:]
        pack, refs = refs[:nz], refs[nz:]
        cos_ref, sin_ref, cot_ref, hid_ref, kv_ref, w_ref, side_ref, gain_ref, hold, kept, sems = refs
        z = at_ref[1]
        for s in range(nz):
            hold[z ^ s] = pack[s][...]
        for s in range(nz):
            w_ref[pl.ds(s * d_rows, d_rows), :] = hold[s, pl.ds(0, d_rows), pl.ds(0, 2 * OWN)]
        gains = [hold[s, pl.ds(d_rows, 16), pl.ds(0, d_rows)].astype(f32) for s in range(nz)]
        gain_ref[...] = jnp.concatenate(gains, axis=1)[:8]
        gain = gain_ref[pl.ds(0, 1), :]
        side_ref[pl.ds(0, local), pl.ds(0, width)] = cot_ref[...]
        turned = [
            hold[s, pl.ds(0, d_rows), pl.ds(2 * OWN, OWN)].astype(f32) for s in range(nz)
        ]
        side_ref[pl.ds(local, OWN), pl.ds(0, width)] = jnp.concatenate(turned, axis=0).T.astype(bf16)
        copies = []
        for tile in range(tiles):
            side, first = (tile * per) // TP, (tile * per) % TP
            at_rows = pl.ds(tile * per * half_rows, per * half_rows)
            block = jnp.concatenate(
                [toks[first + j][pl.ds(side * half_rows, half_rows), :] for j in range(per)], axis=0
            )
            inputs = block.astype(f32)
            hidden = (inputs * norm_scale(inputs) * gain).astype(bf16)
            kept[at_rows, :] = hidden
            copy = pltpu.make_async_copy(kept.at[at_rows, :], hid_ref.at[at_rows, :], sems.at[tile])
            copy.start()
            copies.append(copy)
            pair = nn(hidden, w_ref[:, pl.ds(OWN, OWN)])
            turned = pair * cos_ref[at_rows, :] + swap_halves(pair) * sin_ref[at_rows, :]
            lane = lax.broadcasted_iota(i32, pair.shape, 1)
            kv_ref[at_rows, :] = jnp.where(lane < HEAD, turned, pair).astype(bf16)
        for copy in copies:
            copy.wait()

    return call(
        kernel,
        [
            shape((rows, width), bf16),
            shape((rows, OWN), bf16),
            shape((width, 2 * OWN), bf16),
            shape((local + OWN, TP * OWN), bf16),
            shape((8, width), f32),
        ],
        [at, *tokens, *packs, cosine, sine, cotangent],
        scratch=[
            pltpu.VMEM((nz, pack_rows, lanes), bf16),
            pltpu.VMEM((rows, width), bf16),
            pltpu.SemaphoreType.DMA((tiles,)),
        ],
        limit=30,
        cost=4.0,
        far_out=(0,),
    )


def project_queries(tokens, hidden, w_qkv, cosine, sine):
    local, width = tokens[0].shape
    half_rows = local // 2
    rows = TP * local
    per = 4

    def kernel(*refs):
        toks, refs = refs[:TP], refs[TP:]
        hid_ref, w_ref, cos_ref, sin_ref, x_ref, qt_ref = refs
        for tile in range(2 * TP // per):
            side, first = (tile * per) // TP, (tile * per) % TP
            at_rows = pl.ds(tile * per * half_rows, per * half_rows)
            for j in range(per):
                x_ref[pl.ds((tile * per + j) * half_rows, half_rows), :] = toks[first + j][
                    pl.ds(side * half_rows, half_rows), :
                ]
            query = nn(hid_ref[at_rows, :], w_ref[:, pl.ds(0, OWN)])
            query = query * cos_ref[at_rows, :] + swap_halves(query) * sin_ref[at_rows, :]
            qt_ref[:, at_rows] = (query.astype(bf16).astype(f32) * HEAD**-0.5).T.astype(bf16)

    return call(
        kernel,
        [shape((rows, width), bf16), shape((OWN, rows), bf16)],
        [*tokens, hidden, w_qkv, cosine, sine],
        scalars=0,
        limit=30,
        cost=4.0,
    )


def attention_forward(select, key_base, query_base, turned_query, own_kv, other_kv, half_rows):
    groups = len(own_kv)
    rows = own_kv[0].shape[0]
    half = rows // 2
    blocks = half // half_rows
    wide, deep = 128, 128

    def kernel(sel_ref, key_ref, query_ref, q_ref, *refs):
        own, other = refs[:groups], refs[groups : 2 * groups]
        out_ref, low_ref, lse_ref, kv_ref, kvt_ref, top_ref, mass_ref, place_ref = refs[2 * groups :]
        for head in range(2):
            chosen = sel_ref[head] == 0
            for group in range(groups):

                @pl.when(chosen)
                def take_own():
                    kv_ref[head, group] = own[group][...]
                    kvt_ref[head, group] = own[group][...].T

                @pl.when(jnp.logical_not(chosen))
                def take_other():
                    kv_ref[head, group] = other[group][...]
                    kvt_ref[head, group] = other[group][...].T

        top_ref[...] = jnp.full_like(top_ref, far_below)
        mass_ref[...] = jnp.zeros_like(mass_ref)
        out_ref[...] = jnp.zeros_like(out_ref)

        def one_group(group, unused):
            for head in range(2):
                row = sel_ref[head] * groups + group
                own_rows = pl.ds(head * HEAD, HEAD)
                stat = pl.ds(head, 1)
                place_ref[...] = key_positions(key_ref, row, 0, 2 * blocks, half_rows, 128)
                for k_start in range(0, rows, deep):
                    keys_at = pl.ds(k_start, deep)
                    k_side = k_start // half
                    block = kv_ref[head, group, keys_at, :]
                    values = kvt_ref[head, group, pl.ds(HEAD, HEAD), keys_at]
                    for start in range(k_side * half, rows, wide):
                        lanes = pl.ds(start, wide)
                        turned = q_ref[own_rows, lanes]
                        padded = jnp.concatenate([turned, jnp.zeros_like(turned)], axis=0)
                        scores = nn(block, padded)
                        if start // half == k_side:
                            places = query_positions(
                                query_ref, start // half_rows, wide, half_rows
                            )
                            scores = jnp.where(place_ref[keys_at, :] <= places, scores, far_below)
                        before = top_ref[stat, lanes]
                        top = jnp.maximum(before, jnp.max(scores, axis=0, keepdims=True))
                        weights = jnp.exp(scores - top)
                        fade = jnp.exp(before - top)
                        top_ref[stat, lanes] = top
                        mass_ref[stat, lanes] = mass_ref[stat, lanes] * fade + jnp.sum(
                            weights, axis=0, keepdims=True
                        )
                        out_ref[own_rows, lanes] = out_ref[own_rows, lanes] * fade + nn(
                            values, weights.astype(bf16)
                        )
            return unused

        lax.fori_loop(0, groups, one_group, 0)
        for head in range(2):
            own_rows = pl.ds(head * HEAD, HEAD)
            mass = mass_ref[pl.ds(head, 1), :]
            out_ref[own_rows, :] = out_ref[own_rows, :] / mass
            lse_ref[pl.ds(head, 1), :] = top_ref[pl.ds(head, 1), :] + jnp.log(mass)
        low_ref[...] = out_ref[...].T.astype(bf16)

    return call(
        kernel,
        [shape((OWN, rows), f32), shape((rows, OWN), bf16), shape((2, rows), f32)],
        [select, key_base, query_base, turned_query, *own_kv, *other_kv],
        scalars=3,
        scratch=[
            pltpu.VMEM((2, groups, rows, OWN), bf16),
            pltpu.VMEM((2, groups, OWN, rows), bf16),
            pltpu.VMEM((2, rows), f32),
            pltpu.VMEM((2, rows), f32),
            pltpu.VMEM((rows, 128), i32),
        ],
        limit=36,
        cost=14.0,
    )


def attention_backward(
    select, key_base, query_base, turned_query, own_kv, other_kv, traded, attended, log_mass, half_rows
):
    groups = len(own_kv)
    rows = own_kv[0].shape[0]
    half = rows // 2
    blocks = half // half_rows
    wide, deep = 512, 256

    def kernel(sel_ref, key_ref, query_ref, q_ref, *refs):
        own, other = refs[:groups], refs[groups : 2 * groups]
        refs = refs[2 * groups :]
        local = 2 * half_rows
        parts = [refs[0], refs[1]] + [
            refs[2 + j].at[pl.ds(k * local, local), :] for j in range(TP // 2 - 1) for k in range(2)
        ]
        refs = refs[1 + TP // 2 :]
        att_ref, lse_ref, dq_ref, keep_ref, pass_ref, gb_ref = refs[:6]
        kv_ref, sum_ref, g_ref, rq_ref, rg_ref, delta_ref, pos_ref = refs[6:]
        for group in range(groups):
            kv_ref[0, group] = own[group][...]
            kv_ref[1, group] = other[group][...]
        sum_ref[...] = jnp.zeros_like(sum_ref)
        dq_ref[...] = jnp.zeros_like(dq_ref)
        zeros = jnp.zeros((rows, HEAD), bf16)
        for j in range(0, TP, 2):
            for side in range(2):
                at = pl.ds(side * half + j * half_rows, 2 * half_rows)
                pair = jnp.concatenate(
                    [parts[j + k][pl.ds(side * half_rows, half_rows), :] for k in range(2)], axis=0
                )
                g_ref[:, at] = pair[:, :OWN].T
                gb_ref[at, :] = pair[:, OWN:]
        for head in range(2):
            own_rows = pl.ds(head * HEAD, HEAD)
            rq_ref[head] = jnp.concatenate([q_ref[own_rows, :].T, zeros], axis=1)
            grad = g_ref[own_rows, :]
            rg_ref[head] = jnp.concatenate([zeros, grad.T], axis=1)
            delta_ref[pl.ds(head, 1), :] = jnp.sum(
                grad.astype(f32) * att_ref[own_rows, :], axis=0, keepdims=True
            )

        def one_group(group, unused):
            for head in range(2):
                which = sel_ref[head]
                own_rows = pl.ds(head * HEAD, HEAD)
                stat = pl.ds(head, 1)
                pos_ref[...] = key_positions(
                    key_ref, which * groups + group, 0, 2 * blocks, half_rows, 128
                )
                for k_start in range(0, rows, deep):
                    keys_at = pl.ds(k_start, deep)
                    k_side = k_start // half
                    block = kv_ref[which, group, keys_at, :]
                    turned_keys = block.T[:HEAD]
                    for start in range(k_side * half, rows, wide):
                        lanes = pl.ds(start, wide)
                        turned = q_ref[own_rows, lanes]
                        padded = jnp.concatenate([turned, jnp.zeros_like(turned)], axis=0)
                        scores = nn(block, padded)
                        if start // half == k_side:
                            places = query_positions(
                                query_ref, start // half_rows, wide, half_rows
                            )
                            at = jnp.concatenate([pos_ref[keys_at, :]] * (wide // 128), axis=1)
                            scores = jnp.where(at <= places, scores, far_below)
                        probs = jnp.exp(scores - lse_ref[stat, lanes])
                        grads = g_ref[own_rows, lanes]
                        padded = jnp.concatenate([jnp.zeros_like(grads), grads], axis=0)
                        grad_probs = nn(block, padded)
                        grad_scores = probs * (grad_probs - delta_ref[stat, lanes])
                        probs = probs.astype(bf16)
                        grad_scores = grad_scores.astype(bf16)
                        sum_ref[which, group, keys_at, :] += nn(
                            grad_scores, rq_ref[head, lanes, :]
                        ) + nn(probs, rg_ref[head, lanes, :])
                        dq_ref[own_rows, lanes] += nn(turned_keys, grad_scores)
            return unused

        lax.fori_loop(0, groups, one_group, 0)
        for group in range(groups):
            keep_ref[pl.ds(group * rows, rows), :] = sum_ref[0, group]
            pass_ref[pl.ds(group * rows, rows), :] = sum_ref[1, group].astype(bf16)

    return call(
        kernel,
        [
            shape((OWN, rows), f32),
            shape((groups * rows, OWN), f32),
            shape((groups * rows, OWN), bf16),
            shape((rows, OWN), bf16),
        ],
        [
            select,
            key_base,
            query_base,
            turned_query,
            *own_kv,
            *other_kv,
            *traded,
            attended,
            log_mass,
        ],
        scalars=3,
        scratch=[
            pltpu.VMEM((2, groups, rows, OWN), bf16),
            pltpu.VMEM((2, groups, rows, OWN), f32),
            pltpu.VMEM((OWN, rows), bf16),
            pltpu.VMEM((2, rows, OWN), bf16),
            pltpu.VMEM((2, rows, OWN), bf16),
            pltpu.VMEM((2, rows), f32),
            pltpu.VMEM((rows, 128), i32),
        ],
        limit=28,
        cost=18.0,
    )


def store_blocks(part, tile, per, half_rows, keep_ref, pass_ref, x_first=False):
    side = (tile * per) // TP
    first = lax.rem(tile * per, TP) // 2
    for j in range(per):
        piece = part[j * half_rows : (j + 1) * half_rows]
        place = first // 2 + j if x_first else first + j // 2
        if x_first and j % 2:
            place = first // 2 + j - 1
        row = (2 * place + side) * half_rows
        at = pl.ds(pl.multiple_of(row, half_rows), half_rows)
        target = keep_ref if j % 2 == 0 else pass_ref
        target[at, pl.ds(0, piece.shape[1])] = piece.astype(target.dtype)


def feed_forward(at, inputs, attended, sides, packs, gains, nz):
    rows, width = inputs.shape
    local = rows // TP
    half_rows = local // 2
    half = rows // 2
    d_rows, lanes = packs[0].shape
    ff = lanes // 3
    part_rows = ff // nz
    per = 4
    tile_rows = per * half_rows
    tiles = 2 * TP // per

    def kernel(at_ref, x_ref, *refs):
        att, refs = refs[:TP], refs[TP:]
        extra, refs = refs[:TP], refs[TP:]
        pack, refs = refs[:nz], refs[nz:]
        gain_ref, refs = refs[0], refs[1:]
        resid_out, gk_ref, gp_ref, gain_out, dn_w = refs[:5]
        targets, prod_out, refs = refs[5 : 5 + nz], refs[5 + nz], refs[6 + nz :]
        att_ref, wo_ref, gu_w, cot_ref, hold, acc_gu, acc_dn, blocks, prod_ref, sems = refs
        tp = at_ref[0]
        z = at_ref[1]
        for j in range(TP):
            columns = pl.ds(pl.multiple_of((tp ^ j) * OWN, OWN), OWN)
            wo_ref[columns, :] = extra[j][pl.ds(local, OWN), pl.ds(0, width)]
            for side in range(2):
                for k in range(TP):
                    att_ref[pl.ds(side * half + k * half_rows, half_rows), columns] = att[j][
                        pl.ds(side * half + (k ^ j) * half_rows, half_rows), :
                    ]
                cot_ref[pl.ds(side * half + j * half_rows, half_rows), :] = extra[j][
                    pl.ds(side * half_rows, half_rows), pl.ds(0, width)
                ]
        for s in range(nz):
            hold[z ^ s] = pack[s][...]
        for s in range(nz):
            rows_at = pl.ds(s * d_rows, d_rows)
            gu_w[rows_at, :] = hold[s, :, pl.ds(0, 2 * ff)]
            dn_w[rows_at, :] = jnp.concatenate(
                [
                    hold[b][:, 2 * ff + s * part_rows : 2 * ff + (s + 1) * part_rows]
                    for b in range(nz)
                ],
                axis=1,
            )
        gain = gain_ref[pl.ds(1, 1), :]
        gain_out[...] = jnp.zeros_like(gain_out)
        acc_gu[...] = jnp.zeros_like(acc_gu)
        acc_dn[...] = jnp.zeros_like(acc_dn)

        def copy_of(tile):
            at_rows = pl.ds(pl.multiple_of(tile * tile_rows, tile_rows), tile_rows)
            return pltpu.make_async_copy(
                prod_ref.at[at_rows, :], prod_out.at[at_rows, :], sems.at[tile]
            )

        def one_tile(tile, unused):
            at_rows = pl.ds(pl.multiple_of(tile * tile_rows, tile_rows), tile_rows)
            branch = nt(att_ref[at_rows, :][:, :width], wo_ref[pl.ds(0, width), :])
            resid = x_ref[at_rows, :].astype(f32) + branch
            side = (tile * per) // TP

            @pl.when(lax.rem(tile * per, TP) == 0)
            def keep_own():
                resid_out[pl.ds(pl.multiple_of(side * half_rows, half_rows), half_rows), :] = resid[
                    :half_rows
                ]

            normal = resid * norm_scale(resid)
            hidden = (normal * gain).astype(bf16)
            gate_up = nn(hidden, gu_w[...])
            gate, up = gate_up[:, :ff], gate_up[:, ff:]
            sigmoid = 1.0 / (1.0 + jnp.exp(-gate))
            activated = gate * sigmoid
            product = (activated * up).astype(bf16)
            prod_ref[at_rows, :] = product
            copy_of(tile).start()
            cotangent = cot_ref[at_rows, :]
            grad_product = nn(cotangent, dn_w[...])
            grad_gate = grad_product * up * sigmoid * (1.0 + gate * (1.0 - sigmoid))
            grad_gu = jnp.concatenate([grad_gate, grad_product * activated], axis=1).astype(bf16)
            partial = nt(grad_gu, gu_w[...])
            gain_out[pl.ds(0, 1), :] += jnp.sum(partial * normal, axis=0, keepdims=True)
            store_blocks(partial, tile, per, half_rows, gk_ref, gp_ref)
            acc_gu[...] += tn(hidden, grad_gu)
            acc_dn[...] += tn(cotangent, product)
            return unused

        lax.fori_loop(0, tiles, one_tile, 0)
        for b in range(nz):
            blocks[b] = jnp.concatenate(
                [
                    acc_dn[pl.ds(s * d_rows, d_rows), :][:, b * part_rows : (b + 1) * part_rows]
                    for s in range(nz)
                ],
                axis=1,
            )
        for s in range(nz):
            block = pl.ds(pl.multiple_of((z ^ s) * d_rows, 8), d_rows)
            targets[s][:, pl.ds(0, 2 * ff)] = acc_gu[block, :].astype(targets[s].dtype)
            targets[s][:, pl.ds(2 * ff, ff)] = blocks[z ^ s].astype(targets[s].dtype)
        for tile in range(tiles):
            copy_of(tile).wait()

    return call(
        kernel,
        [
            shape((local, width), f32),
            shape((TP // 2 * local, width), bf16),
            shape((TP // 2 * local, TP * OWN), bf16),
            shape((8, width), f32),
            shape((width, ff), bf16),
        ]
        + [shape((d_rows, lanes), f32 if s % 2 == 0 else bf16) for s in range(nz)]
        + [shape((rows, ff), bf16)],
        [at, inputs, *attended, *sides, *packs, gains],
        scratch=[
            pltpu.VMEM((rows, TP * OWN), bf16),
            pltpu.VMEM((TP * OWN, width), bf16),
            pltpu.VMEM((width, 2 * ff), bf16),
            pltpu.VMEM((rows, width), bf16),
            pltpu.VMEM((nz, d_rows, lanes), bf16),
            pltpu.VMEM((width, 2 * ff), f32),
            pltpu.VMEM((width, ff), f32),
            pltpu.VMEM((nz, d_rows, ff), f32),
            pltpu.VMEM((rows, ff), bf16),
            pltpu.SemaphoreType.DMA((tiles,)),
        ],
        limit=36,
        cost=17.0,
        far_out=(5 + nz,),
    )


def feed_forward_rest(at, attended, sides, product, w_down):
    rows = attended[0].shape[0]
    width, ff = w_down.shape
    local = rows // TP
    half_rows = local // 2
    half = rows // 2
    per = 4
    tile_rows = per * half_rows

    def kernel(at_ref, *refs):
        att, refs = refs[:TP], refs[TP:]
        extra, refs = refs[:TP], refs[TP:]
        prod_ref, dn_w, att_out, wo_out, lk_ref, lp_ref = refs
        tp = at_ref[0]
        for j in range(TP):
            columns = pl.ds(pl.multiple_of((tp ^ j) * OWN, OWN), OWN)
            wo_out[columns, :] = extra[j][pl.ds(local, OWN), pl.ds(0, width)]
            for side in range(2):
                for k in range(TP):
                    att_out[pl.ds(side * half + k * half_rows, half_rows), columns] = att[j][
                        pl.ds(side * half + (k ^ j) * half_rows, half_rows), :
                    ]

        def one_tile(tile, unused):
            at_rows = pl.ds(pl.multiple_of(tile * tile_rows, tile_rows), tile_rows)
            part = nt(prod_ref[at_rows, :], dn_w[...])
            store_blocks(part, tile, per, half_rows, lk_ref, lp_ref)
            return unused

        lax.fori_loop(0, 2 * TP // per, one_tile, 0)

    return call(
        kernel,
        [
            shape((rows, TP * OWN), bf16),
            shape((TP * OWN, width), bf16),
            shape((TP // 2 * local, width), bf16),
            shape((TP // 2 * local, TP * OWN), bf16),
        ],
        [at, *attended, *sides, product, w_down],
        limit=24,
        cost=5.0,
    )


def add_crossed(keep, crossed, count, tail=None):
    local, width = keep.shape[0] // count, keep.shape[1]
    tails = [] if tail is None else [tail]
    more = 0 if tail is None else tail.shape[0]

    def kernel(keep_ref, cross_ref, *refs):
        own_ref, *sends = refs[len(tails) :]
        for j in range(count):
            at = pl.ds(j * local, local)
            target = own_ref if j == 0 else sends[j - 1]
            target[pl.ds(0, local), pl.ds(0, width)] = (
                keep_ref[at, :].astype(f32) + cross_ref[at, pl.ds(0, width)].astype(f32)
            ).astype(target.dtype)
        if tails:
            sends[-1][pl.ds(local, more), pl.ds(0, width)] = refs[0][...]

    return call(
        kernel,
        [shape((local, width), f32)]
        + [shape((local, width), bf16)] * (count - 2)
        + [shape((local + more, TP * OWN if tails else width), bf16)],
        [keep, crossed, *tails],
        scalars=0,
        limit=12,
        cost=1.0,
    )


def branch_gradient(at, sums, resid, cotangent, w_out, gains):
    local, width = resid.shape

    def kernel(at_ref, *refs):
        parts, refs = refs[: len(sums)], refs[len(sums) :]
        resid_ref, cot_ref, wo_ref, gain_ref, grad_ref, keep_ref, pass_ref, ga_ref, gb_ref = refs
        tp = at_ref[0]
        grad_hidden = parts[0][...]
        for part in parts[1:]:
            grad_hidden = grad_hidden + part[...].astype(f32)
        resid = resid_ref[...]
        scale = norm_scale(resid)
        normal = resid * scale
        grad = grad_hidden * gain_ref[pl.ds(1, 1), :]
        grad = scale * (grad - normal * jnp.mean(grad * normal, axis=1, keepdims=True))
        grad = grad + cot_ref[...].astype(f32)
        grad_ref[...] = grad
        low = grad.astype(bf16)
        gb_ref[...] = jnp.zeros_like(gb_ref)
        gb_ref[:, pl.ds(0, width)] = low
        ga_ref[...] = jnp.zeros_like(ga_ref)
        ga_ref[:, pl.ds(0, width)] = nn(low, wo_ref[pl.ds(0, width), :]).astype(bf16)
        for j in range(TP):
            columns = pl.ds(pl.multiple_of((tp ^ j) * OWN, OWN), OWN)
            target = keep_ref if j % 2 == 0 else pass_ref
            rows = pl.ds((j // 2) * local, local)
            target[rows, pl.ds(0, OWN)] = ga_ref[:, columns]
            target[rows, pl.ds(OWN, OWN)] = gb_ref[:, columns]

    blocks = shape((TP // 2 * local, 2 * OWN), bf16)
    return call(
        kernel,
        [shape((local, width), f32), blocks, blocks],
        [at, *sums, resid, cotangent, w_out, gains],
        scratch=[pltpu.VMEM((local, TP * OWN), bf16), pltpu.VMEM((local, TP * OWN), bf16)],
        limit=16,
        cost=3.0,
    )


def pair_up(keep, crossed, count):
    local, width = keep.shape[0] // count, keep.shape[1]

    def kernel(keep_ref, cross_ref, *outs):
        for j in range(1, count):
            at = pl.ds(j * local, local)
            outs[j - 1][pl.ds(0, local), :] = keep_ref[at, :]
            outs[j - 1][pl.ds(local, local), :] = cross_ref[at, :]

    return call(
        kernel,
        [shape((2 * local, width), bf16)] * (count - 1),
        [keep, crossed],
        scalars=0,
        limit=8,
        cost=0.7,
    )


def projection_gradient(
    at, grad_query, grad_kv, inputs, hidden, w_qkv, gain_sums, cosine, sine, grad_out, nz
):
    rows, width = inputs.shape
    local = rows // TP
    half_rows = local // 2
    d_rows = width // nz
    per = 4
    tile_rows = per * half_rows
    pieces = len(grad_kv)

    def kernel(at_ref, dq_ref, *refs):
        kvs, refs = refs[:pieces], refs[pieces:]
        x_ref, hid_ref, w_ref, gain_two_ref, cos_ref, sin_ref, wo_ref = refs[:7]
        keep_ref, pass_ref, own_ref = refs[7:10]
        sends, refs = refs[10 : 10 + nz - 1], refs[10 + nz - 1 :]
        turn_ref, acc_ref, gain_acc, hold = refs
        z = at_ref[1]
        turn_ref[...] = dq_ref[...].T * HEAD**-0.5
        acc_ref[...] = jnp.zeros_like(acc_ref)
        gain_acc[...] = jnp.zeros_like(gain_acc)

        def one_tile(tile, unused):
            at_rows = pl.ds(pl.multiple_of(tile * tile_rows, tile_rows), tile_rows)
            cos, sin = cos_ref[at_rows, :], sin_ref[at_rows, :]
            query = turn_ref[at_rows, :]
            query = query * cos - swap_halves(query) * sin
            pair = kvs[0][at_rows, :].astype(f32)
            for piece in kvs[1:]:
                pair = pair + piece[at_rows, :].astype(f32)
            turned = pair * cos - swap_halves(pair) * sin
            lane = lax.broadcasted_iota(i32, pair.shape, 1)
            pair = jnp.where(lane < HEAD, turned, pair)
            grad = jnp.concatenate([query, pair], axis=1).astype(bf16)
            partial = nt(grad, w_ref[...])
            x = x_ref[at_rows, :].astype(f32)
            gain_acc[pl.ds(0, 1), :] += jnp.sum(partial * (x * norm_scale(x)), axis=0, keepdims=True)
            store_blocks(partial, tile, per, half_rows, keep_ref, pass_ref, True)
            acc_ref[...] += tn(hid_ref[at_rows, :], grad)
            return unused

        lax.fori_loop(0, 2 * TP // per, one_tile, 0)
        hold[...] = jnp.zeros_like(hold)
        for s in range(nz):
            columns = slice(s * d_rows, (s + 1) * d_rows)
            hold[s, pl.ds(0, 1), pl.ds(0, d_rows)] = gain_acc[pl.ds(0, 1), :][:, columns]
            hold[s, pl.ds(1, 1), pl.ds(0, d_rows)] = gain_two_ref[pl.ds(0, 1), :][:, columns]
        for s in range(nz):
            block = z ^ s
            target = own_ref if s == 0 else sends[s - 1]
            rows_at = pl.ds(pl.multiple_of(block * d_rows, 8), d_rows)
            part = pl.ds(0, d_rows)
            target[part, pl.ds(0, 2 * OWN)] = acc_ref[rows_at, :].astype(target.dtype)
            target[part, pl.ds(2 * OWN, OWN)] = wo_ref[rows_at, :].astype(target.dtype)
            target[pl.ds(d_rows, 16), :] = hold[block].astype(target.dtype)

    return call(
        kernel,
        [
            shape((TP // 2 * local, width), bf16),
            shape((TP // 2 * local, TP * OWN), bf16),
            shape((d_rows + 16, 3 * OWN), f32),
        ]
        + [shape((d_rows + 16, 3 * OWN), bf16)] * (nz - 1),
        [at, grad_query, *grad_kv, inputs, hidden, w_qkv, gain_sums, cosine, sine, grad_out],
        scratch=[
            pltpu.VMEM((rows, OWN), f32),
            pltpu.VMEM((width, 2 * OWN), f32),
            pltpu.VMEM((8, width), f32),
            pltpu.VMEM((nz, 16, 3 * OWN), f32),
        ],
        limit=32,
        cost=8.0,
    )


def token_gradient(sums, tokens, grad_resid, gains):
    local, width = tokens.shape

    def kernel(*refs):
        parts, refs = refs[: len(sums)], refs[len(sums) :]
        x_ref, grad_ref, gain_ref, out_ref = refs
        grad_hidden = parts[0][...]
        for part in parts[1:]:
            grad_hidden = grad_hidden + part[...].astype(f32)
        x = x_ref[...].astype(f32)
        scale = norm_scale(x)
        normal = x * scale
        grad = grad_hidden * gain_ref[pl.ds(0, 1), :]
        grad = scale * (grad - normal * jnp.mean(grad * normal, axis=1, keepdims=True))
        out_ref[...] = (grad + grad_ref[...]).T

    return call(
        kernel,
        [shape((width, local), f32)],
        [*sums, tokens, grad_resid, gains],
        scalars=0,
        limit=8,
        cost=1.0,
    )[0].T


def layer_output(near, arrived, resid):
    local, width = resid.shape
    start = arrived.shape[0] - local

    def kernel(near_ref, in_ref, resid_ref, out_ref):
        total = resid_ref[...] + near_ref[...] + in_ref[pl.ds(start, local), pl.ds(0, width)].astype(f32)
        out_ref[...] = total.T.astype(bf16)

    turned = shape(resid.shape[::-1], bf16)
    return call(kernel, [turned], [near, arrived, resid], scalars=0, limit=8, cost=1.0)[0].T


def first_sum(own, arrived):
    def kernel(own_ref, in_ref, out_ref):
        out_ref[...] = (own_ref[...] + in_ref[...].astype(f32)).astype(bf16)

    return call(
        kernel, [shape(own.shape, bf16)], [own, arrived], scalars=0, limit=8, cost=1.0
    )[0]


def last_sum(own, *arrived):
    rows, lanes = own.shape

    def kernel(own_ref, *refs):
        total = own_ref[...]
        for ref in refs[:-1]:
            total = total + ref[...].astype(f32)
        refs[-1][:, pl.ds(0, lanes)] = total.astype(bf16)

    return call(
        kernel, [shape((rows, TP * OWN), bf16)], [own, *arrived], scalars=0, limit=8, cost=1.0
    )[0]


def ff_outputs(at, mine, by_x, by_y, by_xy, odd, ff_z, nz):
    d_rows = mine.shape[0]
    part = ff_z // TP
    ff = part * nz

    def kernel(at_ref, m_ref, x_ref, y_ref, xy_ref, odd_ref, gate_ref, up_ref, down_ref, hold):
        tp = at_ref[0]
        lanes = pl.ds(0, 3 * ff)
        for j, ref in enumerate((m_ref, x_ref, y_ref, xy_ref)):
            hold[tp ^ (2 * j)] = ref[:, lanes]
        for j in range(TP // 2):
            hold[tp ^ (2 * j + 1)] = odd_ref[pl.ds(d_rows * j, d_rows), lanes]
        for s in range(nz):
            for start in (s * part, ff + s * part, 2 * ff + s * part):
                block = jnp.concatenate(
                    [hold[c][:, start : start + part] for c in range(TP)], axis=1
                ).astype(f32)
                if start < ff:
                    gate_ref[:, pl.ds(s * ff_z, ff_z)] = block
                elif start < 2 * ff:
                    up_ref[:, pl.ds(s * ff_z, ff_z)] = block
                else:
                    down_ref[pl.ds(s * d_rows, d_rows), :] = block

    gate, up, down = call(
        kernel,
        [
            shape((d_rows, nz * ff_z), f32),
            shape((d_rows, nz * ff_z), f32),
            shape((nz * d_rows, ff_z), f32),
        ],
        [at, mine, by_x, by_y, by_xy, odd],
        scratch=[pltpu.VMEM((TP, d_rows, 3 * ff), bf16)],
        limit=32,
        cost=7.0,
    )
    return gate, up, down.T


def projection_outputs(at, slots, width):
    d_rows = slots[0].shape[0] - 16

    def kernel(at_ref, *refs):
        parts, (q_ref, k_ref, v_ref, o_ref, one_ref, two_ref, hold) = refs[:TP], refs[TP:]
        tp = at_ref[0]
        total = jnp.zeros((16, 3 * OWN), f32)
        for j in range(TP):
            hold[tp ^ j] = parts[j][...].astype(f32)
            total = total + parts[j][pl.ds(d_rows, 16), :].astype(f32)
        one_ref[...] = total[0:1, :d_rows]
        two_ref[...] = total[1:2, :d_rows]
        heads = [hold[c][:d_rows, :OWN] for c in range(TP)]
        q_ref[...] = jnp.concatenate(heads, axis=1)[:, :width]
        heads = [hold[c][:d_rows, 2 * OWN :] for c in range(TP)]
        o_ref[...] = jnp.concatenate(heads, axis=1)[:, :width]
        kv = [hold[c][:d_rows, OWN : 2 * OWN] for c in range(TP)]
        kv = [kv[0], kv[1] + kv[2], kv[3] + kv[4], kv[5], kv[6]]
        for c in range(KV_HEADS):
            turned = kv[c].T
            k_ref[pl.ds(c * HEAD, HEAD), :] = turned[:HEAD]
            v_ref[pl.ds(c * HEAD, HEAD), :] = turned[HEAD:]

    query, key, value, out, one, two = call(
        kernel,
        [
            shape((d_rows, width), f32),
            shape((KV_HEADS * HEAD, d_rows), f32),
            shape((KV_HEADS * HEAD, d_rows), f32),
            shape((d_rows, width), f32),
            shape((1, d_rows), f32),
            shape((1, d_rows), f32),
        ],
        [at, *slots],
        scratch=[pltpu.VMEM((TP, d_rows + 16, 3 * OWN), f32)],
        limit=12,
        cost=0.01,
    )
    return query, key.T, value.T, out, one, two


def body(
    tokens,
    pair_order,
    gain_attn,
    gain_mlp,
    w_query,
    w_key,
    w_value,
    w_out,
    w_gate,
    w_up,
    w_down,
    cotangent,
):
    local_rows, width = tokens.shape
    half_rows = local_rows // 2
    nz = lax.axis_size("fsdp")
    outer = lax.axis_size("ctx") // TP
    count = lax.axis_size(AXES)
    groups = outer * nz
    me = lax.axis_index(AXES)
    z = lax.axis_index("fsdp")
    tp = lax.axis_index("ctx") % TP
    kv_index = (4 * (tp // 2)) // GROUP + tp % 2
    at = jnp.stack([tp, z, kv_index]).astype(i32)
    send = functools.partial(exchange, count=count)
    group_mask = [(g // nz) * TP * nz + g % nz for g in range(groups)]

    def after(value, *others):
        return lax.optimization_barrier((value, *others))[0]

    def level(*arrays):
        return list(lax.optimization_barrier(arrays))

    def gather_even(block):
        return [block] + [send(block, j * nz) for j in range(2, TP, 2)]

    def gather_odd(even):
        return [piece for e in even for piece in (e, send(e, nz))]

    def scatter_far(pieces):
        return [send(piece, 2 * (j + 1) * nz) for j, piece in enumerate(pieces)]

    def from_z(block):
        return [block] + [send(block, s) for s in range(1, nz)]

    pack_one = slice_attention_weights(at, w_query, w_key, w_value, w_out, gain_attn, gain_mlp)
    token_slots = gather_odd(level(*gather_even(tokens)))
    pack_two = slice_ff_weights(after(at, pack_one), w_gate, w_up, w_down, nz)
    pack_one = from_z(pack_one)

    slot_of = jnp.array([[m | (j * nz) for j in range(TP)] for m in group_mask], dtype=i32)
    low = pair_order[me ^ slot_of]
    base = jnp.stack([low, 2 * count - 1 - low], axis=1) * half_rows
    query_base = base[0].reshape(2 * TP)
    partner = jnp.array([j ^ 1 for j in range(TP)], dtype=i32)
    key_base = jnp.stack([base, base[:, :, partner]]).reshape(2 * groups, 2 * TP)
    places = (query_base[:, None] + jnp.arange(half_rows, dtype=i32)[None, :]).reshape(-1)
    lane = jnp.arange(OWN)
    freqs = base_theta ** (-2.0 * (lane % (HEAD // 2)).astype(f32) / HEAD)
    angles = places.astype(f32)[:, None] * freqs[None, :]
    cosine = jnp.cos(angles)
    sine = jnp.sin(angles) * jnp.where(lane % HEAD < HEAD // 2, -1.0, 1.0)[None, :]
    select = jnp.where((2 * tp + jnp.arange(2)) // GROUP == kv_index, 0, 1).astype(i32)

    mask_x, mask_y = 2 * nz, 4 * nz
    hidden_one, kv, w_qkv, side, gains = project_keys(
        after(at, pack_two, select, key_base, query_base),
        token_slots,
        pack_one,
        cosine,
        sine,
        cotangent,
    )
    own_kv = [kv] + [send(kv, m) for m in group_mask[1:]]
    side_x, side_y = send(side, mask_x), send(side, mask_y)
    inputs, turned_query = project_queries(
        token_slots, after(hidden_one, kv), w_qkv, cosine, sine
    )
    side_x, side_y, inputs, turned_query, *own_kv = level(
        side_x, side_y, inputs, turned_query, *own_kv
    )
    other_kv = level(*[send(slot, nz) for slot in own_kv])
    one, near = send(after(pack_two, *own_kv), 1), send(after(pack_two, *own_kv), 2)
    side_xy = send(side_x, mask_y)
    side_odd, odd_x = send(after(side, *other_kv), nz), send(after(side_x, *other_kv), nz)
    attended, attended_own, log_mass = attention_forward(
        select, key_base, query_base, turned_query, own_kv, other_kv, half_rows
    )
    attended_own, near, one, side_xy, side_odd, odd_x = level(
        attended_own, near, one, side_xy, side_odd, odd_x
    )
    far, side_xy, *even = level(send(near, 1), side_xy, *gather_even(attended_own))
    attended_slots = gather_odd(even)
    packs = [pack_two, one, near, far]
    odd_y = send(after(side_y, side_xy), nz)
    sides = [side, side_odd, side_x, odd_x, side_y, odd_y, side_xy, send(side_xy, nz)]

    resid, grad_keep, grad_pass, gain_sums, w_down_own, *ff_blocks, product = feed_forward(
        at, inputs, attended_slots, sides, packs, gains, nz
    )
    ff_own, ff_one, ff_two, ff_three = ff_blocks
    first, *rest = add_crossed(grad_keep, send(grad_pass, nz), TP // 2)
    attended_low, w_out_all, out_keep, out_pass, ff_three, first, *rest = level(
        *feed_forward_rest(after(at, first), attended_slots, sides, product, w_down_own),
        send(after(ff_three, first), 1),
        first,
        *scatter_far(rest),
    )
    grad_resid, trade_keep, trade_pass = branch_gradient(
        at, [first, *rest], resid, cotangent, w_out_all, gains
    )
    crossed, out_crossed = level(send(trade_pass, nz), send(after(out_pass, first), nz))
    pairs = level(*scatter_far(pair_up(trade_keep, crossed, TP // 2)))
    out_near, out_far = add_crossed(out_keep, out_crossed, 2)
    ff_one = send(after(ff_one, crossed), 1)
    ff_two = send(first_sum(ff_two, ff_three), 2)
    out_far = send(after(out_far, *pairs), mask_y)

    grad_query, kv_keep, kv_pass, branch_columns = attention_backward(
        after(select, out_near),
        key_base,
        query_base,
        turned_query,
        own_kv,
        other_kv,
        [trade_keep, crossed, *pairs],
        attended,
        log_mass,
        half_rows,
    )
    kv_pass, ff_one, ff_two, out_far = level(kv_pass, ff_one, ff_two, out_far)
    kv_crossed = send(kv_pass, nz)
    first, *rest = add_crossed(kv_keep, kv_crossed, groups)
    grad_out = tn(attended_low[:, :width], after(branch_columns, rest[0]))
    ff_total = last_sum(after(ff_own, grad_out), ff_one, ff_two)

    for step in range(outer.bit_length() - 1):
        crossing = send(ff_total, TP * nz << step).astype(f32)
        ff_total = (ff_total.astype(f32) + crossing).astype(bf16)
    out_near, out_far = add_crossed(after(out_near, rest[0]), out_far, 2)
    ff_x, ff_y, *grad_kv = level(
        send(ff_total, mask_x),
        send(ff_total, mask_y),
        *[send(piece, m) for piece, m in zip(rest, group_mask[1:])],
    )

    last_keep, last_pass, last_own, *last_sends = projection_gradient(
        at,
        grad_query,
        [first, *grad_kv],
        inputs,
        hidden_one,
        w_qkv,
        gain_sums,
        cosine,
        sine,
        grad_out,
        nz,
    )
    near, far = add_crossed(last_keep, send(last_pass, nz), 2, out_far)
    ff_xy, far, *arrived = level(
        send(after(ff_x, last_own), mask_y),
        send(far, mask_x),
        *[send(piece, s + 1) for s, piece in enumerate(last_sends)],
    )
    layer_out = layer_output(out_near, far, resid)
    near, far = add_crossed(near, far, 2)
    last_total = last_own
    for piece in arrived:
        last_total = last_total + piece.astype(f32)
    for step in range(outer.bit_length() - 1):
        last_total = last_total + send(last_total.astype(bf16), TP * nz << step).astype(f32)
    last_total = last_total.astype(bf16)
    ff_slots = [ff_total, ff_x, ff_y, ff_xy]
    ff_slots.append(send(jnp.concatenate(ff_slots, axis=0), nz))
    grad_gate, grad_up, grad_down = ff_outputs(at, *ff_slots, w_down.shape[0], nz)
    far = send(far, mask_y)
    grad_gate, *even = level(grad_gate, *gather_even(last_total))
    last_slots = gather_odd(even)
    grad_w_query, grad_w_key, grad_w_value, grad_out, gain_one, gain_two = projection_outputs(
        at, last_slots, width
    )
    grad_tokens = token_gradient([after(near, grad_w_query), far], tokens, grad_resid, gains)
    return (
        layer_out,
        grad_tokens,
        gain_one.reshape(-1),
        gain_two.reshape(-1),
        grad_w_query,
        grad_w_key,
        grad_w_value,
        grad_out,
        grad_gate,
        grad_up,
        grad_down,
    )


def solution(mesh):
    return jax.shard_map(
        body,
        mesh=mesh,
        in_specs=(
            P(("ctx", "fsdp"), None),
            P(),
            P("fsdp"),
            P("fsdp"),
            P("fsdp", None),
            P("fsdp", None),
            P("fsdp", None),
            P("fsdp", None),
            P("fsdp", None),
            P("fsdp", None),
            P("fsdp", None),
            P(("ctx", "fsdp"), None),
        ),
        out_specs=(
            P(("ctx", "fsdp"), None),
            P(("ctx", "fsdp"), None),
            P("fsdp"),
            P("fsdp"),
            P("fsdp", None),
            P("fsdp", None),
            P("fsdp", None),
            P("fsdp", None),
            P("fsdp", None),
            P("fsdp", None),
            P("fsdp", None),
        ),
        check_vma=False,
    )
```

```python
import functools

import jax
import jax.numpy as jnp
from jax import lax
from jax.experimental import pallas as pl
from jax.experimental.pallas import tpu as pltpu
from jax.sharding import PartitionSpec as P

HEADS = 15
KV_HEADS = 5
HEAD = 64
TP = 8
GROUP = HEADS // KV_HEADS
OWN = 2 * HEAD
epsilon = 1e-05
base_theta = 100000.0
far_below = -1e30
f32 = jnp.float32
bf16 = jnp.bfloat16
i32 = jnp.int32
AXES = ("ctx", "fsdp")
MIB = 1024 * 1024
smem = pl.BlockSpec(memory_space=pltpu.SMEM)
vmem = pl.BlockSpec(memory_space=pltpu.VMEM)


def exchange(array, mask, count):
    return lax.ppermute(array, AXES, [(i, i ^ mask) for i in range(count)])


def nn(left, right):
    return lax.dot_general(left, right, (((1,), (0,)), ((), ())), preferred_element_type=f32)


def tn(left, right):
    return lax.dot_general(left, right, (((0,), (0,)), ((), ())), preferred_element_type=f32)


def nt(left, right):
    return lax.dot_general(left, right, (((1,), (1,)), ((), ())), preferred_element_type=f32)


def shape(dims, dtype):
    return jax.ShapeDtypeStruct(dims, dtype)


def call(kernel, outs, inputs, scalars=1, scratch=(), limit=56, cost=1.0, far=(), far_out=()):
    specs = [smem] * scalars + [vmem] * (len(inputs) - scalars)
    for i in far:
        specs[i] = pl.BlockSpec(memory_space=pltpu.HBM)
    out_specs = [vmem for unused in outs]
    for i in far_out:
        out_specs[i] = pl.BlockSpec(memory_space=pltpu.HBM)
    return pl.pallas_call(
        kernel,
        out_shape=tuple(outs),
        in_specs=specs,
        out_specs=tuple(out_specs),
        scratch_shapes=list(scratch),
        compiler_params=pltpu.CompilerParams(vmem_limit_bytes=limit * MIB),
        cost_estimate=pl.CostEstimate(
            flops=int(cost * 1e9), bytes_accessed=int(cost * 1e6), transcendentals=0
        ),
    )(*inputs)


def one_hot(rows, columns, start):
    row = lax.broadcasted_iota(i32, (rows, columns), 0)
    column = lax.broadcasted_iota(i32, (rows, columns), 1)
    return jnp.where(row == column + start, 1.0, 0.0).astype(bf16)


def query_positions(base_ref, at, width, half_rows):
    lane = lax.broadcasted_iota(i32, (1, width), 1)
    place = jnp.zeros((1, width), i32)
    for block in range(width // half_rows):
        start = base_ref[at + block] - block * half_rows
        place = jnp.where(lane >= block * half_rows, start + lane, place)
    return place


def key_positions(base_ref, row, at, count, half_rows, width):
    offset = lax.broadcasted_iota(i32, (half_rows, width), 0)
    return jnp.concatenate([offset + base_ref[row, at + b] for b in range(count)], axis=0)


def swap_halves(matrix):
    lane = lax.broadcasted_iota(i32, matrix.shape, 1)
    ahead = pltpu.roll(matrix, matrix.shape[1] - HEAD // 2, 1)
    behind = pltpu.roll(matrix, HEAD // 2, 1)
    return jnp.where(lane % HEAD < HEAD // 2, ahead, behind)


def norm_scale(matrix):
    return lax.rsqrt(jnp.mean(matrix * matrix, axis=1, keepdims=True) + epsilon)


def slice_attention_weights(at, w_query, w_key, w_value, w_out, gain_one, gain_two):
    d_rows, width = w_query.shape
    lanes = 2 * OWN + OWN
    rest = width - (TP - 1) * OWN

    def kernel(at_ref, q_ref, k_ref, v_ref, o_ref, g1_ref, g2_ref, out_ref, cols, heads, whole, sems):
        tp = at_ref[0]
        kv = at_ref[2]
        wides, narrows = (q_ref, o_ref), (k_ref, v_ref)

        columns = pl.ds(pl.multiple_of(tp * OWN, OWN), OWN)
        rows = pl.ds(pl.multiple_of(kv * HEAD, HEAD), HEAD)

        def wide_copies():
            return [
                pltpu.make_async_copy(ref.at[:, columns], cols.at[i], sems.at[i])
                for i, ref in enumerate(wides)
            ]

        def whole_copies():
            return [
                pltpu.make_async_copy(ref, whole.at[i], sems.at[i]) for i, ref in enumerate(wides)
            ]

        def head_copies():
            return [
                pltpu.make_async_copy(ref.at[rows, :], heads.at[i], sems.at[2 + i])
                for i, ref in enumerate(narrows)
            ]

        @pl.when(tp < TP - 1)
        def most():
            for copy in wide_copies():
                copy.start()

        @pl.when(tp == TP - 1)
        def last():
            for copy in whole_copies():
                copy.start()

        @pl.when(kv < KV_HEADS)
        def real():
            for copy in head_copies():
                copy.start()

        @pl.when(kv >= KV_HEADS)
        def none():
            heads[...] = jnp.zeros_like(heads)

        @pl.when(tp < TP - 1)
        def most_came():
            for copy in wide_copies():
                copy.wait()

        @pl.when(tp == TP - 1)
        def last_came():
            for copy in whole_copies():
                copy.wait()
            for i in range(2):
                cols[i] = jnp.zeros((d_rows, OWN), bf16)
                cols[i, :, pl.ds(0, rest)] = whole[i, :, pl.ds(width - rest, rest)]

        @pl.when(kv < KV_HEADS)
        def real_came():
            for copy in head_copies():
                copy.wait()

        out_ref[pl.ds(0, d_rows), pl.ds(0, OWN)] = cols[0]
        turned = jnp.concatenate([heads[0], heads[1]], axis=0).astype(f32).T
        out_ref[pl.ds(0, d_rows), pl.ds(OWN, OWN)] = turned.astype(bf16)
        out_ref[pl.ds(0, d_rows), pl.ds(2 * OWN, OWN)] = cols[1]
        out_ref[pl.ds(d_rows, 16), :] = jnp.zeros((16, lanes), bf16)
        out_ref[d_rows, pl.ds(0, d_rows)] = g1_ref[...]
        out_ref[d_rows + 1, pl.ds(0, d_rows)] = g2_ref[...]

    return call(
        kernel,
        [shape((d_rows + 16, lanes), bf16)],
        [at, w_query, w_key.T, w_value.T, w_out, gain_one, gain_two],
        scratch=[
            pltpu.VMEM((2, d_rows, OWN), bf16),
            pltpu.VMEM((2, HEAD, d_rows), bf16),
            pltpu.VMEM((2, d_rows, width), bf16),
            pltpu.SemaphoreType.DMA((4,)),
        ],
        limit=60,
        cost=2.0,
        far=(1, 2, 3, 4),
    )[0]


def slice_ff_weights(at, w_gate, w_up, w_down, nz):
    d_rows = w_gate.shape[0]
    ff_z, width = w_down.shape
    part = ff_z // TP
    own = part * nz


    def kernel(at_ref, g_ref, u_ref, d_ref, out_ref):
        pick = one_hot(ff_z, part, at_ref[0] * part)
        for ref, start in ((g_ref, 0), (u_ref, own)):
            pieces = [nn(ref[:, pl.ds(s * ff_z, ff_z)], pick) for s in range(nz)]
            out_ref[:, pl.ds(start, own)] = jnp.concatenate(pieces, axis=1).astype(bf16)
        pieces = [nn(d_ref[pl.ds(s * d_rows, d_rows), :], pick) for s in range(nz)]
        out_ref[:, pl.ds(2 * own, own)] = jnp.concatenate(pieces, axis=1).astype(bf16)

    return call(
        kernel,
        [shape((d_rows, 3 * own), bf16)],
        [at, w_gate, w_up, w_down.T],
        limit=16,
        cost=4.0,
    )[0]


def project_keys(at, tokens, packs, cosine, sine, cotangent):
    local, width = tokens[0].shape
    half_rows = local // 2
    rows = TP * local
    nz = len(packs)
    pack_rows, lanes = packs[0].shape
    d_rows = pack_rows - 16
    per = 4
    tiles = 2 * TP // per

    def kernel(at_ref, *refs):
        toks, refs = refs[:TP], refs[TP:]
        pack, refs = refs[:nz], refs[nz:]
        cos_ref, sin_ref, cot_ref, hid_ref, kv_ref, w_ref, side_ref, gain_ref, hold, kept, sems = refs
        z = at_ref[1]
        for s in range(nz):
            hold[z ^ s] = pack[s][...]
        for s in range(nz):
            w_ref[pl.ds(s * d_rows, d_rows), :] = hold[s, pl.ds(0, d_rows), pl.ds(0, 2 * OWN)]
        gains = [hold[s, pl.ds(d_rows, 16), pl.ds(0, d_rows)].astype(f32) for s in range(nz)]
        gain_ref[...] = jnp.concatenate(gains, axis=1)[:8]
        gain = gain_ref[pl.ds(0, 1), :]
        side_ref[pl.ds(0, local), pl.ds(0, width)] = cot_ref[...]
        turned = [
            hold[s, pl.ds(0, d_rows), pl.ds(2 * OWN, OWN)].astype(f32) for s in range(nz)
        ]
        side_ref[pl.ds(local, OWN), pl.ds(0, width)] = jnp.concatenate(turned, axis=0).T.astype(bf16)
        copies = []
        for tile in range(tiles):
            side, first = (tile * per) // TP, (tile * per) % TP
            at_rows = pl.ds(tile * per * half_rows, per * half_rows)
            block = jnp.concatenate(
                [toks[first + j][pl.ds(side * half_rows, half_rows), :] for j in range(per)], axis=0
            )
            inputs = block.astype(f32)
            hidden = (inputs * norm_scale(inputs) * gain).astype(bf16)
            kept[at_rows, :] = hidden
            copy = pltpu.make_async_copy(kept.at[at_rows, :], hid_ref.at[at_rows, :], sems.at[tile])
            copy.start()
            copies.append(copy)
            pair = nn(hidden, w_ref[:, pl.ds(OWN, OWN)])
            turned = pair * cos_ref[at_rows, :] + swap_halves(pair) * sin_ref[at_rows, :]
            lane = lax.broadcasted_iota(i32, pair.shape, 1)
            kv_ref[at_rows, :] = jnp.where(lane < HEAD, turned, pair).astype(bf16)
        for copy in copies:
            copy.wait()

    return call(
        kernel,
        [
            shape((rows, width), bf16),
            shape((rows, OWN), bf16),
            shape((width, 2 * OWN), bf16),
            shape((local + OWN, TP * OWN), bf16),
            shape((8, width), f32),
        ],
        [at, *tokens, *packs, cosine, sine, cotangent],
        scratch=[
            pltpu.VMEM((nz, pack_rows, lanes), bf16),
            pltpu.VMEM((rows, width), bf16),
            pltpu.SemaphoreType.DMA((tiles,)),
        ],
        limit=30,
        cost=4.0,
        far_out=(0,),
    )


def project_queries(tokens, hidden, w_qkv, cosine, sine):
    local, width = tokens[0].shape
    half_rows = local // 2
    rows = TP * local
    per = 4

    def kernel(*refs):
        toks, refs = refs[:TP], refs[TP:]
        hid_ref, w_ref, cos_ref, sin_ref, x_ref, qt_ref = refs
        for tile in range(2 * TP // per):
            side, first = (tile * per) // TP, (tile * per) % TP
            at_rows = pl.ds(tile * per * half_rows, per * half_rows)
            for j in range(per):
                x_ref[pl.ds((tile * per + j) * half_rows, half_rows), :] = toks[first + j][
                    pl.ds(side * half_rows, half_rows), :
                ]
            query = nn(hid_ref[at_rows, :], w_ref[:, pl.ds(0, OWN)])
            query = query * cos_ref[at_rows, :] + swap_halves(query) * sin_ref[at_rows, :]
            qt_ref[:, at_rows] = (query.astype(bf16).astype(f32) * HEAD**-0.5).T.astype(bf16)

    return call(
        kernel,
        [shape((rows, width), bf16), shape((OWN, rows), bf16)],
        [*tokens, hidden, w_qkv, cosine, sine],
        scalars=0,
        limit=30,
        cost=4.0,
    )


def attention_forward(select, key_base, query_base, turned_query, own_kv, other_kv, half_rows):
    groups = len(own_kv)
    rows = own_kv[0].shape[0]
    half = rows // 2
    blocks = half // half_rows
    wide, deep = 128, 128

    def kernel(sel_ref, key_ref, query_ref, q_ref, *refs):
        own, other = refs[:groups], refs[groups : 2 * groups]
        out_ref, low_ref, lse_ref, kv_ref, kvt_ref, top_ref, mass_ref, place_ref = refs[2 * groups :]
        for head in range(2):
            chosen = sel_ref[head] == 0
            for group in range(groups):

                @pl.when(chosen)
                def take_own():
                    kv_ref[head, group] = own[group][...]
                    kvt_ref[head, group] = own[group][...].T

                @pl.when(jnp.logical_not(chosen))
                def take_other():
                    kv_ref[head, group] = other[group][...]
                    kvt_ref[head, group] = other[group][...].T

        top_ref[...] = jnp.full_like(top_ref, far_below)
        mass_ref[...] = jnp.zeros_like(mass_ref)
        out_ref[...] = jnp.zeros_like(out_ref)

        def one_step(step, unused):
            group, head = step // 2, lax.rem(step, 2)
            row = sel_ref[head] * groups + group
            own_rows = pl.ds(pl.multiple_of(head * HEAD, HEAD), HEAD)
            place_ref[...] = key_positions(key_ref, row, 0, 2 * blocks, half_rows, 128)
            for k_start in range(0, rows, deep):
                keys_at = pl.ds(k_start, deep)
                k_side = k_start // half
                block = kv_ref[head, group, keys_at, :]
                values = kvt_ref[head, group, pl.ds(HEAD, HEAD), keys_at]
                for start in range(k_side * half, rows, wide):
                    lanes = pl.ds(start, wide)
                    turned = q_ref[own_rows, lanes]
                    padded = jnp.concatenate([turned, jnp.zeros_like(turned)], axis=0)
                    scores = nn(block, padded)
                    if start // half == k_side:
                        places = query_positions(
                            query_ref, start // half_rows, wide, half_rows
                        )
                        scores = jnp.where(place_ref[keys_at, :] <= places, scores, far_below)
                    before = top_ref[head, :, lanes]
                    top = jnp.maximum(before, jnp.max(scores, axis=0, keepdims=True))
                    weights = jnp.exp(scores - top)
                    fade = jnp.exp(before - top)
                    top_ref[head, :, lanes] = top
                    mass_ref[head, :, lanes] = mass_ref[head, :, lanes] * fade + jnp.sum(
                        weights, axis=0, keepdims=True
                    )
                    out_ref[own_rows, lanes] = out_ref[own_rows, lanes] * fade + nn(
                        values, weights.astype(bf16)
                    )
            return unused

        lax.fori_loop(0, 2 * groups, one_step, 0)
        for head in range(2):
            own_rows = pl.ds(head * HEAD, HEAD)
            mass = mass_ref[head]
            out_ref[own_rows, :] = out_ref[own_rows, :] / mass
            lse_ref[pl.ds(head, 1), :] = top_ref[head] + jnp.log(mass)
        low_ref[...] = out_ref[...].T.astype(bf16)

    return call(
        kernel,
        [shape((OWN, rows), f32), shape((rows, OWN), bf16), shape((2, rows), f32)],
        [select, key_base, query_base, turned_query, *own_kv, *other_kv],
        scalars=3,
        scratch=[
            pltpu.VMEM((2, groups, rows, OWN), bf16),
            pltpu.VMEM((2, groups, OWN, rows), bf16),
            pltpu.VMEM((2, 1, rows), f32),
            pltpu.VMEM((2, 1, rows), f32),
            pltpu.VMEM((rows, 128), i32),
        ],
        limit=36,
        cost=14.0,
    )


def attention_backward(
    select, key_base, query_base, turned_query, own_kv, other_kv, traded, attended, log_mass, half_rows
):
    groups = len(own_kv)
    rows = own_kv[0].shape[0]
    half = rows // 2
    blocks = half // half_rows
    wide, deep = 512, 256

    def kernel(sel_ref, key_ref, query_ref, q_ref, *refs):
        own, other = refs[:groups], refs[groups : 2 * groups]
        refs = refs[2 * groups :]
        local = 2 * half_rows
        parts = [refs[0], refs[1]] + [
            refs[2 + j].at[pl.ds(k * local, local), :] for j in range(TP // 2 - 1) for k in range(2)
        ]
        refs = refs[1 + TP // 2 :]
        att_ref, lse_ref, dq_ref, keep_ref, pass_ref, gb_ref = refs[:6]
        kv_ref, sum_ref, g_ref, rq_ref, rg_ref, delta_ref, pos_ref = refs[6:]
        for group in range(groups):
            kv_ref[0, group] = own[group][...]
            kv_ref[1, group] = other[group][...]
        sum_ref[...] = jnp.zeros_like(sum_ref)
        dq_ref[...] = jnp.zeros_like(dq_ref)
        zeros = jnp.zeros((rows, HEAD), bf16)
        for j in range(0, TP, 2):
            for side in range(2):
                at = pl.ds(side * half + j * half_rows, 2 * half_rows)
                pair = jnp.concatenate(
                    [parts[j + k][pl.ds(side * half_rows, half_rows), :] for k in range(2)], axis=0
                )
                g_ref[:, at] = pair[:, :OWN].T
                gb_ref[at, :] = pair[:, OWN:]
        for head in range(2):
            own_rows = pl.ds(head * HEAD, HEAD)
            rq_ref[head] = jnp.concatenate([q_ref[own_rows, :].T, zeros], axis=1)
            grad = g_ref[own_rows, :]
            rg_ref[head] = jnp.concatenate([zeros, grad.T], axis=1)
            delta_ref[pl.ds(head, 1), :] = jnp.sum(
                grad.astype(f32) * att_ref[own_rows, :], axis=0, keepdims=True
            )

        def one_group(group, unused):
            for head in range(2):
                which = sel_ref[head]
                own_rows = pl.ds(head * HEAD, HEAD)
                stat = pl.ds(head, 1)
                pos_ref[...] = key_positions(
                    key_ref, which * groups + group, 0, 2 * blocks, half_rows, 128
                )
                for k_start in range(0, rows, deep):
                    keys_at = pl.ds(k_start, deep)
                    k_side = k_start // half
                    block = kv_ref[which, group, keys_at, :]
                    turned_keys = block.T[:HEAD]
                    for start in range(k_side * half, rows, wide):
                        lanes = pl.ds(start, wide)
                        turned = q_ref[own_rows, lanes]
                        padded = jnp.concatenate([turned, jnp.zeros_like(turned)], axis=0)
                        scores = nn(block, padded)
                        if start // half == k_side:
                            places = query_positions(
                                query_ref, start // half_rows, wide, half_rows
                            )
                            at = jnp.concatenate([pos_ref[keys_at, :]] * (wide // 128), axis=1)
                            scores = jnp.where(at <= places, scores, far_below)
                        probs = jnp.exp(scores - lse_ref[stat, lanes])
                        grads = g_ref[own_rows, lanes]
                        padded = jnp.concatenate([jnp.zeros_like(grads), grads], axis=0)
                        grad_probs = nn(block, padded)
                        grad_scores = probs * (grad_probs - delta_ref[stat, lanes])
                        probs = probs.astype(bf16)
                        grad_scores = grad_scores.astype(bf16)
                        sum_ref[which, group, keys_at, :] += nn(
                            grad_scores, rq_ref[head, lanes, :]
                        ) + nn(probs, rg_ref[head, lanes, :])
                        dq_ref[own_rows, lanes] += nn(turned_keys, grad_scores)
            return unused

        lax.fori_loop(0, groups, one_group, 0)
        for group in range(groups):
            keep_ref[pl.ds(group * rows, rows), :] = sum_ref[0, group]
            pass_ref[pl.ds(group * rows, rows), :] = sum_ref[1, group].astype(bf16)

    return call(
        kernel,
        [
            shape((OWN, rows), f32),
            shape((groups * rows, OWN), f32),
            shape((groups * rows, OWN), bf16),
            shape((rows, OWN), bf16),
        ],
        [
            select,
            key_base,
            query_base,
            turned_query,
            *own_kv,
            *other_kv,
            *traded,
            attended,
            log_mass,
        ],
        scalars=3,
        scratch=[
            pltpu.VMEM((2, groups, rows, OWN), bf16),
            pltpu.VMEM((2, groups, rows, OWN), f32),
            pltpu.VMEM((OWN, rows), bf16),
            pltpu.VMEM((2, rows, OWN), bf16),
            pltpu.VMEM((2, rows, OWN), bf16),
            pltpu.VMEM((2, rows), f32),
            pltpu.VMEM((rows, 128), i32),
        ],
        limit=28,
        cost=18.0,
    )


def store_blocks(part, tile, per, half_rows, keep_ref, pass_ref, x_first=False):
    side = (tile * per) // TP
    first = lax.rem(tile * per, TP) // 2
    for j in range(per):
        piece = part[j * half_rows : (j + 1) * half_rows]
        place = first // 2 + j if x_first else first + j // 2
        if x_first and j % 2:
            place = first // 2 + j - 1
        row = (2 * place + side) * half_rows
        at = pl.ds(pl.multiple_of(row, half_rows), half_rows)
        target = keep_ref if j % 2 == 0 else pass_ref
        target[at, pl.ds(0, piece.shape[1])] = piece.astype(target.dtype)


def feed_forward(at, inputs, attended, sides, packs, gains, nz):
    rows, width = inputs.shape
    local = rows // TP
    half_rows = local // 2
    half = rows // 2
    d_rows, lanes = packs[0].shape
    ff = lanes // 3
    part_rows = ff // nz
    per = 4
    tile_rows = per * half_rows
    tiles = 2 * TP // per

    def kernel(at_ref, x_ref, *refs):
        att, refs = refs[:TP], refs[TP:]
        extra, refs = refs[:TP], refs[TP:]
        pack, refs = refs[:nz], refs[nz:]
        gain_ref, refs = refs[0], refs[1:]
        resid_out, gk_ref, gp_ref, gain_out, dn_w = refs[:5]
        targets, prod_out, refs = refs[5 : 5 + nz], refs[5 + nz], refs[6 + nz :]
        att_ref, wo_ref, gu_w, cot_ref, hold, acc_gu, acc_dn, blocks, prod_ref, sems = refs
        tp = at_ref[0]
        z = at_ref[1]
        for j in range(TP):
            columns = pl.ds(pl.multiple_of((tp ^ j) * OWN, OWN), OWN)
            wo_ref[columns, :] = extra[j][pl.ds(local, OWN), pl.ds(0, width)]
            for side in range(2):
                for k in range(TP):
                    att_ref[pl.ds(side * half + k * half_rows, half_rows), columns] = att[j][
                        pl.ds(side * half + (k ^ j) * half_rows, half_rows), :
                    ]
                cot_ref[pl.ds(side * half + j * half_rows, half_rows), :] = extra[j][
                    pl.ds(side * half_rows, half_rows), pl.ds(0, width)
                ]
        for s in range(nz):
            hold[z ^ s] = pack[s][...]
        for s in range(nz):
            rows_at = pl.ds(s * d_rows, d_rows)
            gu_w[rows_at, :] = hold[s, :, pl.ds(0, 2 * ff)]
            dn_w[rows_at, :] = jnp.concatenate(
                [
                    hold[b][:, 2 * ff + s * part_rows : 2 * ff + (s + 1) * part_rows]
                    for b in range(nz)
                ],
                axis=1,
            )
        gain = gain_ref[pl.ds(1, 1), :]
        gain_out[...] = jnp.zeros_like(gain_out)
        acc_gu[...] = jnp.zeros_like(acc_gu)
        acc_dn[...] = jnp.zeros_like(acc_dn)

        def copy_of(tile):
            at_rows = pl.ds(pl.multiple_of(tile * tile_rows, tile_rows), tile_rows)
            return pltpu.make_async_copy(
                prod_ref.at[at_rows, :], prod_out.at[at_rows, :], sems.at[tile]
            )

        def one_tile(tile, unused):
            at_rows = pl.ds(pl.multiple_of(tile * tile_rows, tile_rows), tile_rows)
            branch = nt(att_ref[at_rows, :][:, :width], wo_ref[pl.ds(0, width), :])
            resid = x_ref[at_rows, :].astype(f32) + branch
            side = (tile * per) // TP

            @pl.when(lax.rem(tile * per, TP) == 0)
            def keep_own():
                resid_out[pl.ds(pl.multiple_of(side * half_rows, half_rows), half_rows), :] = resid[
                    :half_rows
                ]

            normal = resid * norm_scale(resid)
            hidden = (normal * gain).astype(bf16)
            gate_up = nn(hidden, gu_w[...])
            gate, up = gate_up[:, :ff], gate_up[:, ff:]
            sigmoid = 1.0 / (1.0 + jnp.exp(-gate))
            activated = gate * sigmoid
            product = (activated * up).astype(bf16)
            prod_ref[at_rows, :] = product
            copy_of(tile).start()
            cotangent = cot_ref[at_rows, :]
            grad_product = nn(cotangent, dn_w[...])
            grad_gate = grad_product * up * sigmoid * (1.0 + gate * (1.0 - sigmoid))
            grad_gu = jnp.concatenate([grad_gate, grad_product * activated], axis=1).astype(bf16)
            partial = nt(grad_gu, gu_w[...])
            gain_out[pl.ds(0, 1), :] += jnp.sum(partial * normal, axis=0, keepdims=True)
            store_blocks(partial, tile, per, half_rows, gk_ref, gp_ref)
            acc_gu[...] += tn(hidden, grad_gu)
            acc_dn[...] += tn(cotangent, product)
            return unused

        lax.fori_loop(0, tiles, one_tile, 0)
        for b in range(nz):
            blocks[b] = jnp.concatenate(
                [
                    acc_dn[pl.ds(s * d_rows, d_rows), :][:, b * part_rows : (b + 1) * part_rows]
                    for s in range(nz)
                ],
                axis=1,
            )
        for s in range(nz):
            block = pl.ds(pl.multiple_of((z ^ s) * d_rows, 8), d_rows)
            targets[s][:, pl.ds(0, 2 * ff)] = acc_gu[block, :].astype(targets[s].dtype)
            targets[s][:, pl.ds(2 * ff, ff)] = blocks[z ^ s].astype(targets[s].dtype)
        for tile in range(tiles):
            copy_of(tile).wait()

    return call(
        kernel,
        [
            shape((local, width), f32),
            shape((TP // 2 * local, width), bf16),
            shape((TP // 2 * local, TP * OWN), bf16),
            shape((8, width), f32),
            shape((width, ff), bf16),
        ]
        + [shape((d_rows, lanes), f32 if s % 2 == 0 else bf16) for s in range(nz)]
        + [shape((rows, ff), bf16)],
        [at, inputs, *attended, *sides, *packs, gains],
        scratch=[
            pltpu.VMEM((rows, TP * OWN), bf16),
            pltpu.VMEM((TP * OWN, width), bf16),
            pltpu.VMEM((width, 2 * ff), bf16),
            pltpu.VMEM((rows, width), bf16),
            pltpu.VMEM((nz, d_rows, lanes), bf16),
            pltpu.VMEM((width, 2 * ff), f32),
            pltpu.VMEM((width, ff), f32),
            pltpu.VMEM((nz, d_rows, ff), f32),
            pltpu.VMEM((rows, ff), bf16),
            pltpu.SemaphoreType.DMA((tiles,)),
        ],
        limit=36,
        cost=17.0,
        far_out=(5 + nz,),
    )


def feed_forward_rest(at, attended, sides, product, w_down):
    rows = attended[0].shape[0]
    width, ff = w_down.shape
    local = rows // TP
    half_rows = local // 2
    half = rows // 2
    per = 4
    tile_rows = per * half_rows

    def kernel(at_ref, *refs):
        att, refs = refs[:TP], refs[TP:]
        extra, refs = refs[:TP], refs[TP:]
        prod_ref, dn_w, att_out, wo_out, lk_ref, lp_ref = refs
        tp = at_ref[0]
        for j in range(TP):
            columns = pl.ds(pl.multiple_of((tp ^ j) * OWN, OWN), OWN)
            wo_out[columns, :] = extra[j][pl.ds(local, OWN), pl.ds(0, width)]
            for side in range(2):
                for k in range(TP):
                    att_out[pl.ds(side * half + k * half_rows, half_rows), columns] = att[j][
                        pl.ds(side * half + (k ^ j) * half_rows, half_rows), :
                    ]

        def one_tile(tile, unused):
            at_rows = pl.ds(pl.multiple_of(tile * tile_rows, tile_rows), tile_rows)
            part = nt(prod_ref[at_rows, :], dn_w[...])
            store_blocks(part, tile, per, half_rows, lk_ref, lp_ref)
            return unused

        lax.fori_loop(0, 2 * TP // per, one_tile, 0)

    return call(
        kernel,
        [
            shape((rows, TP * OWN), bf16),
            shape((TP * OWN, width), bf16),
            shape((TP // 2 * local, width), bf16),
            shape((TP // 2 * local, TP * OWN), bf16),
        ],
        [at, *attended, *sides, product, w_down],
        limit=24,
        cost=5.0,
    )


def add_crossed(keep, crossed, count, tail=None):
    local, width = keep.shape[0] // count, keep.shape[1]
    tails = [] if tail is None else [tail]
    more = 0 if tail is None else tail.shape[0]

    def kernel(keep_ref, cross_ref, *refs):
        own_ref, *sends = refs[len(tails) :]
        for j in range(count):
            at = pl.ds(j * local, local)
            target = own_ref if j == 0 else sends[j - 1]
            target[pl.ds(0, local), pl.ds(0, width)] = (
                keep_ref[at, :].astype(f32) + cross_ref[at, pl.ds(0, width)].astype(f32)
            ).astype(target.dtype)
        if tails:
            sends[-1][pl.ds(local, more), pl.ds(0, width)] = refs[0][...]

    return call(
        kernel,
        [shape((local, width), f32)]
        + [shape((local, width), bf16)] * (count - 2)
        + [shape((local + more, TP * OWN if tails else width), bf16)],
        [keep, crossed, *tails],
        scalars=0,
        limit=12,
        cost=1.0,
    )


def branch_gradient(at, sums, resid, cotangent, w_out, gains):
    local, width = resid.shape

    def kernel(at_ref, *refs):
        parts, refs = refs[: len(sums)], refs[len(sums) :]
        resid_ref, cot_ref, wo_ref, gain_ref, grad_ref, keep_ref, pass_ref, ga_ref, gb_ref = refs
        tp = at_ref[0]
        grad_hidden = parts[0][...]
        for part in parts[1:]:
            grad_hidden = grad_hidden + part[...].astype(f32)
        resid = resid_ref[...]
        scale = norm_scale(resid)
        normal = resid * scale
        grad = grad_hidden * gain_ref[pl.ds(1, 1), :]
        grad = scale * (grad - normal * jnp.mean(grad * normal, axis=1, keepdims=True))
        grad = grad + cot_ref[...].astype(f32)
        grad_ref[...] = grad
        low = grad.astype(bf16)
        gb_ref[...] = jnp.zeros_like(gb_ref)
        gb_ref[:, pl.ds(0, width)] = low
        ga_ref[...] = jnp.zeros_like(ga_ref)
        ga_ref[:, pl.ds(0, width)] = nn(low, wo_ref[pl.ds(0, width), :]).astype(bf16)
        for j in range(TP):
            columns = pl.ds(pl.multiple_of((tp ^ j) * OWN, OWN), OWN)
            target = keep_ref if j % 2 == 0 else pass_ref
            rows = pl.ds((j // 2) * local, local)
            target[rows, pl.ds(0, OWN)] = ga_ref[:, columns]
            target[rows, pl.ds(OWN, OWN)] = gb_ref[:, columns]

    blocks = shape((TP // 2 * local, 2 * OWN), bf16)
    return call(
        kernel,
        [shape((local, width), f32), blocks, blocks],
        [at, *sums, resid, cotangent, w_out, gains],
        scratch=[pltpu.VMEM((local, TP * OWN), bf16), pltpu.VMEM((local, TP * OWN), bf16)],
        limit=16,
        cost=3.0,
    )


def pair_up(keep, crossed, count):
    local, width = keep.shape[0] // count, keep.shape[1]

    def kernel(keep_ref, cross_ref, *outs):
        for j in range(1, count):
            at = pl.ds(j * local, local)
            outs[j - 1][pl.ds(0, local), :] = keep_ref[at, :]
            outs[j - 1][pl.ds(local, local), :] = cross_ref[at, :]

    return call(
        kernel,
        [shape((2 * local, width), bf16)] * (count - 1),
        [keep, crossed],
        scalars=0,
        limit=8,
        cost=0.7,
    )


def projection_gradient(
    at, grad_query, grad_kv, inputs, hidden, w_qkv, gain_sums, cosine, sine, grad_out, nz
):
    rows, width = inputs.shape
    local = rows // TP
    half_rows = local // 2
    d_rows = width // nz
    per = 4
    tile_rows = per * half_rows
    pieces = len(grad_kv)

    def kernel(at_ref, dq_ref, *refs):
        kvs, refs = refs[:pieces], refs[pieces:]
        x_ref, hid_ref, w_ref, gain_two_ref, cos_ref, sin_ref, wo_ref = refs[:7]
        keep_ref, pass_ref, own_ref = refs[7:10]
        sends, refs = refs[10 : 10 + nz - 1], refs[10 + nz - 1 :]
        turn_ref, acc_ref, gain_acc, hold = refs
        z = at_ref[1]
        turn_ref[...] = dq_ref[...].T * HEAD**-0.5
        acc_ref[...] = jnp.zeros_like(acc_ref)
        gain_acc[...] = jnp.zeros_like(gain_acc)

        def one_tile(tile, unused):
            at_rows = pl.ds(pl.multiple_of(tile * tile_rows, tile_rows), tile_rows)
            cos, sin = cos_ref[at_rows, :], sin_ref[at_rows, :]
            query = turn_ref[at_rows, :]
            query = query * cos - swap_halves(query) * sin
            pair = kvs[0][at_rows, :].astype(f32)
            for piece in kvs[1:]:
                pair = pair + piece[at_rows, :].astype(f32)
            turned = pair * cos - swap_halves(pair) * sin
            lane = lax.broadcasted_iota(i32, pair.shape, 1)
            pair = jnp.where(lane < HEAD, turned, pair)
            grad = jnp.concatenate([query, pair], axis=1).astype(bf16)
            partial = nt(grad, w_ref[...])
            x = x_ref[at_rows, :].astype(f32)
            gain_acc[pl.ds(0, 1), :] += jnp.sum(partial * (x * norm_scale(x)), axis=0, keepdims=True)
            store_blocks(partial, tile, per, half_rows, keep_ref, pass_ref, True)
            acc_ref[...] += tn(hid_ref[at_rows, :], grad)
            return unused

        lax.fori_loop(0, 2 * TP // per, one_tile, 0)
        hold[...] = jnp.zeros_like(hold)
        for s in range(nz):
            columns = slice(s * d_rows, (s + 1) * d_rows)
            hold[s, pl.ds(0, 1), pl.ds(0, d_rows)] = gain_acc[pl.ds(0, 1), :][:, columns]
            hold[s, pl.ds(1, 1), pl.ds(0, d_rows)] = gain_two_ref[pl.ds(0, 1), :][:, columns]
        for s in range(nz):
            block = z ^ s
            target = own_ref if s == 0 else sends[s - 1]
            rows_at = pl.ds(pl.multiple_of(block * d_rows, 8), d_rows)
            part = pl.ds(0, d_rows)
            target[part, pl.ds(0, 2 * OWN)] = acc_ref[rows_at, :].astype(target.dtype)
            target[part, pl.ds(2 * OWN, OWN)] = wo_ref[rows_at, :].astype(target.dtype)
            target[pl.ds(d_rows, 16), :] = hold[block].astype(target.dtype)

    return call(
        kernel,
        [
            shape((TP // 2 * local, width), bf16),
            shape((TP // 2 * local, TP * OWN), bf16),
            shape((d_rows + 16, 3 * OWN), f32),
        ]
        + [shape((d_rows + 16, 3 * OWN), bf16)] * (nz - 1),
        [at, grad_query, *grad_kv, inputs, hidden, w_qkv, gain_sums, cosine, sine, grad_out],
        scratch=[
            pltpu.VMEM((rows, OWN), f32),
            pltpu.VMEM((width, 2 * OWN), f32),
            pltpu.VMEM((8, width), f32),
            pltpu.VMEM((nz, 16, 3 * OWN), f32),
        ],
        limit=32,
        cost=8.0,
    )


def token_gradient(sums, tokens, grad_resid, gains):
    local, width = tokens.shape

    def kernel(*refs):
        parts, refs = refs[: len(sums)], refs[len(sums) :]
        x_ref, grad_ref, gain_ref, out_ref = refs
        grad_hidden = parts[0][...]
        for part in parts[1:]:
            grad_hidden = grad_hidden + part[...].astype(f32)
        x = x_ref[...].astype(f32)
        scale = norm_scale(x)
        normal = x * scale
        grad = grad_hidden * gain_ref[pl.ds(0, 1), :]
        grad = scale * (grad - normal * jnp.mean(grad * normal, axis=1, keepdims=True))
        out_ref[...] = (grad + grad_ref[...]).T

    return call(
        kernel,
        [shape((width, local), f32)],
        [*sums, tokens, grad_resid, gains],
        scalars=0,
        limit=8,
        cost=1.0,
    )[0].T


def layer_output(near, arrived, resid):
    local, width = resid.shape
    start = arrived.shape[0] - local

    def kernel(near_ref, in_ref, resid_ref, out_ref):
        total = resid_ref[...] + near_ref[...] + in_ref[pl.ds(start, local), pl.ds(0, width)].astype(f32)
        out_ref[...] = total.T.astype(bf16)

    turned = shape(resid.shape[::-1], bf16)
    return call(kernel, [turned], [near, arrived, resid], scalars=0, limit=8, cost=1.0)[0].T


def first_sum(own, arrived):
    def kernel(own_ref, in_ref, out_ref):
        out_ref[...] = (own_ref[...] + in_ref[...].astype(f32)).astype(bf16)

    return call(
        kernel, [shape(own.shape, bf16)], [own, arrived], scalars=0, limit=8, cost=1.0
    )[0]


def last_sum(own, *arrived):
    rows, lanes = own.shape

    def kernel(own_ref, *refs):
        total = own_ref[...]
        for ref in refs[:-1]:
            total = total + ref[...].astype(f32)
        refs[-1][:, pl.ds(0, lanes)] = total.astype(bf16)

    return call(
        kernel, [shape((rows, TP * OWN), bf16)], [own, *arrived], scalars=0, limit=8, cost=1.0
    )[0]


def ff_outputs(at, mine, by_x, by_y, by_xy, odd, ff_z, nz):
    d_rows = mine.shape[0]
    part = ff_z // TP
    ff = part * nz

    def kernel(at_ref, m_ref, x_ref, y_ref, xy_ref, odd_ref, gate_ref, up_ref, down_ref, hold):
        tp = at_ref[0]
        lanes = pl.ds(0, 3 * ff)
        for j, ref in enumerate((m_ref, x_ref, y_ref, xy_ref)):
            hold[tp ^ (2 * j)] = ref[:, lanes]
        for j in range(TP // 2):
            hold[tp ^ (2 * j + 1)] = odd_ref[pl.ds(d_rows * j, d_rows), lanes]
        for s in range(nz):
            for start in (s * part, ff + s * part, 2 * ff + s * part):
                block = jnp.concatenate(
                    [hold[c][:, start : start + part] for c in range(TP)], axis=1
                ).astype(f32)
                if start < ff:
                    gate_ref[:, pl.ds(s * ff_z, ff_z)] = block
                elif start < 2 * ff:
                    up_ref[:, pl.ds(s * ff_z, ff_z)] = block
                else:
                    down_ref[pl.ds(s * d_rows, d_rows), :] = block

    gate, up, down = call(
        kernel,
        [
            shape((d_rows, nz * ff_z), f32),
            shape((d_rows, nz * ff_z), f32),
            shape((nz * d_rows, ff_z), f32),
        ],
        [at, mine, by_x, by_y, by_xy, odd],
        scratch=[pltpu.VMEM((TP, d_rows, 3 * ff), bf16)],
        limit=32,
        cost=7.0,
    )
    return gate, up, down.T


def projection_outputs(at, slots, width):
    d_rows = slots[0].shape[0] - 16

    def kernel(at_ref, *refs):
        parts, (q_ref, k_ref, v_ref, o_ref, one_ref, two_ref, hold) = refs[:TP], refs[TP:]
        tp = at_ref[0]
        total = jnp.zeros((16, 3 * OWN), f32)
        for j in range(TP):
            hold[tp ^ j] = parts[j][...].astype(f32)
            total = total + parts[j][pl.ds(d_rows, 16), :].astype(f32)
        one_ref[...] = total[0:1, :d_rows]
        two_ref[...] = total[1:2, :d_rows]
        heads = [hold[c][:d_rows, :OWN] for c in range(TP)]
        q_ref[...] = jnp.concatenate(heads, axis=1)[:, :width]
        heads = [hold[c][:d_rows, 2 * OWN :] for c in range(TP)]
        o_ref[...] = jnp.concatenate(heads, axis=1)[:, :width]
        kv = [hold[c][:d_rows, OWN : 2 * OWN] for c in range(TP)]
        kv = [kv[0], kv[1] + kv[2], kv[3] + kv[4], kv[5], kv[6]]
        for c in range(KV_HEADS):
            turned = kv[c].T
            k_ref[pl.ds(c * HEAD, HEAD), :] = turned[:HEAD]
            v_ref[pl.ds(c * HEAD, HEAD), :] = turned[HEAD:]

    query, key, value, out, one, two = call(
        kernel,
        [
            shape((d_rows, width), f32),
            shape((KV_HEADS * HEAD, d_rows), f32),
            shape((KV_HEADS * HEAD, d_rows), f32),
            shape((d_rows, width), f32),
            shape((1, d_rows), f32),
            shape((1, d_rows), f32),
        ],
        [at, *slots],
        scratch=[pltpu.VMEM((TP, d_rows + 16, 3 * OWN), f32)],
        limit=12,
        cost=0.01,
    )
    return query, key.T, value.T, out, one, two


def body(
    tokens,
    pair_order,
    gain_attn,
    gain_mlp,
    w_query,
    w_key,
    w_value,
    w_out,
    w_gate,
    w_up,
    w_down,
    cotangent,
):
    local_rows, width = tokens.shape
    half_rows = local_rows // 2
    nz = lax.axis_size("fsdp")
    outer = lax.axis_size("ctx") // TP
    count = lax.axis_size(AXES)
    groups = outer * nz
    me = lax.axis_index(AXES)
    z = lax.axis_index("fsdp")
    tp = lax.axis_index("ctx") % TP
    kv_index = (4 * (tp // 2)) // GROUP + tp % 2
    at = jnp.stack([tp, z, kv_index]).astype(i32)
    send = functools.partial(exchange, count=count)
    group_mask = [(g // nz) * TP * nz + g % nz for g in range(groups)]

    def after(value, *others):
        return lax.optimization_barrier((value, *others))[0]

    def level(*arrays):
        return list(lax.optimization_barrier(arrays))

    def gather_even(block):
        return [block] + [send(block, j * nz) for j in range(2, TP, 2)]

    def gather_odd(even):
        return [piece for e in even for piece in (e, send(e, nz))]

    def scatter_far(pieces):
        return [send(piece, 2 * (j + 1) * nz) for j, piece in enumerate(pieces)]

    def from_z(block):
        return [block] + [send(block, s) for s in range(1, nz)]

    pack_one = slice_attention_weights(at, w_query, w_key, w_value, w_out, gain_attn, gain_mlp)
    token_slots = gather_odd(level(*gather_even(tokens)))
    pack_two = slice_ff_weights(after(at, pack_one), w_gate, w_up, w_down, nz)
    pack_one = from_z(pack_one)

    slot_of = jnp.array([[m | (j * nz) for j in range(TP)] for m in group_mask], dtype=i32)
    low = pair_order[me ^ slot_of]
    base = jnp.stack([low, 2 * count - 1 - low], axis=1) * half_rows
    query_base = base[0].reshape(2 * TP)
    partner = jnp.array([j ^ 1 for j in range(TP)], dtype=i32)
    key_base = jnp.stack([base, base[:, :, partner]]).reshape(2 * groups, 2 * TP)
    places = (query_base[:, None] + jnp.arange(half_rows, dtype=i32)[None, :]).reshape(-1)
    lane = jnp.arange(OWN)
    freqs = base_theta ** (-2.0 * (lane % (HEAD // 2)).astype(f32) / HEAD)
    angles = places.astype(f32)[:, None] * freqs[None, :]
    cosine = jnp.cos(angles)
    sine = jnp.sin(angles) * jnp.where(lane % HEAD < HEAD // 2, -1.0, 1.0)[None, :]
    select = jnp.where((2 * tp + jnp.arange(2)) // GROUP == kv_index, 0, 1).astype(i32)

    mask_x, mask_y = 2 * nz, 4 * nz
    hidden_one, kv, w_qkv, side, gains = project_keys(
        after(at, pack_two, select, key_base, query_base),
        token_slots,
        pack_one,
        cosine,
        sine,
        cotangent,
    )
    own_kv = [kv] + [send(kv, m) for m in group_mask[1:]]
    side_x, side_y = send(side, mask_x), send(side, mask_y)
    inputs, turned_query = project_queries(
        token_slots, after(hidden_one, kv), w_qkv, cosine, sine
    )
    side_x, side_y, inputs, turned_query, *own_kv = level(
        side_x, side_y, inputs, turned_query, *own_kv
    )
    other_kv = level(*[send(slot, nz) for slot in own_kv])
    one, near = send(after(pack_two, *own_kv), 1), send(after(pack_two, *own_kv), 2)
    side_xy = send(side_x, mask_y)
    side_odd, odd_x = send(after(side, *other_kv), nz), send(after(side_x, *other_kv), nz)
    attended, attended_own, log_mass = attention_forward(
        select, key_base, query_base, turned_query, own_kv, other_kv, half_rows
    )
    attended_own, near, one, side_xy, side_odd, odd_x = level(
        attended_own, near, one, side_xy, side_odd, odd_x
    )
    far, side_xy, *even = level(send(near, 1), side_xy, *gather_even(attended_own))
    attended_slots = gather_odd(even)
    packs = [pack_two, one, near, far]
    odd_y = send(after(side_y, side_xy), nz)
    sides = [side, side_odd, side_x, odd_x, side_y, odd_y, side_xy, send(side_xy, nz)]

    resid, grad_keep, grad_pass, gain_sums, w_down_own, *ff_blocks, product = feed_forward(
        at, inputs, attended_slots, sides, packs, gains, nz
    )
    ff_own, ff_one, ff_two, ff_three = ff_blocks
    first, *rest = add_crossed(grad_keep, send(grad_pass, nz), TP // 2)
    attended_low, w_out_all, out_keep, out_pass, ff_three, first, *rest = level(
        *feed_forward_rest(after(at, first), attended_slots, sides, product, w_down_own),
        send(after(ff_three, first), 1),
        first,
        *scatter_far(rest),
    )
    grad_resid, trade_keep, trade_pass = branch_gradient(
        at, [first, *rest], resid, cotangent, w_out_all, gains
    )
    crossed, out_crossed = level(send(trade_pass, nz), send(after(out_pass, first), nz))
    pairs = level(*scatter_far(pair_up(trade_keep, crossed, TP // 2)))
    out_near, out_far = add_crossed(out_keep, out_crossed, 2)
    ff_one = send(after(ff_one, crossed), 1)
    ff_two = send(first_sum(ff_two, ff_three), 2)
    out_far = send(after(out_far, *pairs), mask_y)

    grad_query, kv_keep, kv_pass, branch_columns = attention_backward(
        after(select, out_near),
        key_base,
        query_base,
        turned_query,
        own_kv,
        other_kv,
        [trade_keep, crossed, *pairs],
        attended,
        log_mass,
        half_rows,
    )
    kv_pass, ff_one, ff_two, out_far = level(kv_pass, ff_one, ff_two, out_far)
    kv_crossed = send(kv_pass, nz)
    first, *rest = add_crossed(kv_keep, kv_crossed, groups)
    grad_out = tn(attended_low[:, :width], after(branch_columns, rest[0]))
    ff_total = last_sum(after(ff_own, grad_out), ff_one, ff_two)

    for step in range(outer.bit_length() - 1):
        crossing = send(ff_total, TP * nz << step).astype(f32)
        ff_total = (ff_total.astype(f32) + crossing).astype(bf16)
    out_near, out_far = add_crossed(after(out_near, rest[0]), out_far, 2)
    ff_x, ff_y, *grad_kv = level(
        send(ff_total, mask_x),
        send(ff_total, mask_y),
        *[send(piece, m) for piece, m in zip(rest, group_mask[1:])],
    )

    last_keep, last_pass, last_own, *last_sends = projection_gradient(
        at,
        grad_query,
        [first, *grad_kv],
        inputs,
        hidden_one,
        w_qkv,
        gain_sums,
        cosine,
        sine,
        grad_out,
        nz,
    )
    near, far = add_crossed(last_keep, send(last_pass, nz), 2, out_far)
    ff_xy, far, *arrived = level(
        send(after(ff_x, last_own), mask_y),
        send(far, mask_x),
        *[send(piece, s + 1) for s, piece in enumerate(last_sends)],
    )
    layer_out = layer_output(out_near, far, resid)
    near, far = add_crossed(near, far, 2)
    last_total = last_own
    for piece in arrived:
        last_total = last_total + piece.astype(f32)
    for step in range(outer.bit_length() - 1):
        last_total = last_total + send(last_total.astype(bf16), TP * nz << step).astype(f32)
    last_total = last_total.astype(bf16)
    ff_slots = [ff_total, ff_x, ff_y, ff_xy]
    ff_slots.append(send(jnp.concatenate(ff_slots, axis=0), nz))
    grad_gate, grad_up, grad_down = ff_outputs(at, *ff_slots, w_down.shape[0], nz)
    far = send(far, mask_y)
    grad_gate, *even = level(grad_gate, *gather_even(last_total))
    last_slots = gather_odd(even)
    grad_w_query, grad_w_key, grad_w_value, grad_out, gain_one, gain_two = projection_outputs(
        at, last_slots, width
    )
    grad_tokens = token_gradient([after(near, grad_w_query), far], tokens, grad_resid, gains)
    return (
        layer_out,
        grad_tokens,
        gain_one.reshape(-1),
        gain_two.reshape(-1),
        grad_w_query,
        grad_w_key,
        grad_w_value,
        grad_out,
        grad_gate,
        grad_up,
        grad_down,
    )


def solution(mesh):
    return jax.shard_map(
        body,
        mesh=mesh,
        in_specs=(
            P(("ctx", "fsdp"), None),
            P(),
            P("fsdp"),
            P("fsdp"),
            P("fsdp", None),
            P("fsdp", None),
            P("fsdp", None),
            P("fsdp", None),
            P("fsdp", None),
            P("fsdp", None),
            P("fsdp", None),
            P(("ctx", "fsdp"), None),
        ),
        out_specs=(
            P(("ctx", "fsdp"), None),
            P(("ctx", "fsdp"), None),
            P("fsdp"),
            P("fsdp"),
            P("fsdp", None),
            P("fsdp", None),
            P("fsdp", None),
            P("fsdp", None),
            P("fsdp", None),
            P("fsdp", None),
            P("fsdp", None),
        ),
        check_vma=False,
    )
```

```python
import functools

import jax
import jax.numpy as jnp
from jax import lax
from jax.experimental import pallas as pl
from jax.experimental.pallas import tpu as pltpu
from jax.sharding import PartitionSpec as P

HEADS = 15
KV_HEADS = 5
HEAD = 64
TP = 8
GROUP = HEADS // KV_HEADS
OWN = 2 * HEAD
epsilon = 1e-05
base_theta = 100000.0
far_below = -1e30
f32 = jnp.float32
bf16 = jnp.bfloat16
i32 = jnp.int32
AXES = ("ctx", "fsdp")
MIB = 1024 * 1024
smem = pl.BlockSpec(memory_space=pltpu.SMEM)
vmem = pl.BlockSpec(memory_space=pltpu.VMEM)


def exchange(array, mask, count):
    return lax.ppermute(array, AXES, [(i, i ^ mask) for i in range(count)])


def nn(left, right):
    return lax.dot_general(left, right, (((1,), (0,)), ((), ())), preferred_element_type=f32)


def tn(left, right):
    return lax.dot_general(left, right, (((0,), (0,)), ((), ())), preferred_element_type=f32)


def nt(left, right):
    return lax.dot_general(left, right, (((1,), (1,)), ((), ())), preferred_element_type=f32)


def shape(dims, dtype):
    return jax.ShapeDtypeStruct(dims, dtype)


def call(kernel, outs, inputs, scalars=1, scratch=(), limit=56, cost=1.0, far=(), far_out=()):
    specs = [smem] * scalars + [vmem] * (len(inputs) - scalars)
    for i in far:
        specs[i] = pl.BlockSpec(memory_space=pltpu.HBM)
    out_specs = [vmem for unused in outs]
    for i in far_out:
        out_specs[i] = pl.BlockSpec(memory_space=pltpu.HBM)
    return pl.pallas_call(
        kernel,
        out_shape=tuple(outs),
        in_specs=specs,
        out_specs=tuple(out_specs),
        scratch_shapes=list(scratch),
        compiler_params=pltpu.CompilerParams(vmem_limit_bytes=limit * MIB),
        cost_estimate=pl.CostEstimate(
            flops=int(cost * 1e9), bytes_accessed=int(cost * 1e6), transcendentals=0
        ),
    )(*inputs)


def one_hot(rows, columns, start):
    row = lax.broadcasted_iota(i32, (rows, columns), 0)
    column = lax.broadcasted_iota(i32, (rows, columns), 1)
    return jnp.where(row == column + start, 1.0, 0.0).astype(bf16)


def query_positions(base_ref, at, width, half_rows):
    lane = lax.broadcasted_iota(i32, (1, width), 1)
    place = jnp.zeros((1, width), i32)
    for block in range(width // half_rows):
        start = base_ref[at + block] - block * half_rows
        place = jnp.where(lane >= block * half_rows, start + lane, place)
    return place


def key_positions(base_ref, row, at, count, half_rows, width):
    offset = lax.broadcasted_iota(i32, (half_rows, width), 0)
    return jnp.concatenate([offset + base_ref[row, at + b] for b in range(count)], axis=0)


def swap_halves(matrix):
    lane = lax.broadcasted_iota(i32, matrix.shape, 1)
    ahead = pltpu.roll(matrix, matrix.shape[1] - HEAD // 2, 1)
    behind = pltpu.roll(matrix, HEAD // 2, 1)
    return jnp.where(lane % HEAD < HEAD // 2, ahead, behind)


def norm_scale(matrix):
    return lax.rsqrt(jnp.mean(matrix * matrix, axis=1, keepdims=True) + epsilon)


def slice_attention_weights(at, w_query, w_key, w_value, w_out, gain_one, gain_two):
    d_rows, width = w_query.shape
    lanes = 2 * OWN + OWN
    rest = width - (TP - 1) * OWN

    def kernel(at_ref, q_ref, k_ref, v_ref, o_ref, g1_ref, g2_ref, out_ref, cols, heads, whole, sems):
        tp = at_ref[0]
        kv = at_ref[2]
        wides, narrows = (q_ref, o_ref), (k_ref, v_ref)

        columns = pl.ds(pl.multiple_of(tp * OWN, OWN), OWN)
        rows = pl.ds(pl.multiple_of(kv * HEAD, HEAD), HEAD)

        def wide_copies():
            return [
                pltpu.make_async_copy(ref.at[:, columns], cols.at[i], sems.at[i])
                for i, ref in enumerate(wides)
            ]

        def whole_copies():
            return [
                pltpu.make_async_copy(ref, whole.at[i], sems.at[i]) for i, ref in enumerate(wides)
            ]

        def head_copies():
            return [
                pltpu.make_async_copy(ref.at[rows, :], heads.at[i], sems.at[2 + i])
                for i, ref in enumerate(narrows)
            ]

        @pl.when(tp < TP - 1)
        def most():
            for copy in wide_copies():
                copy.start()

        @pl.when(tp == TP - 1)
        def last():
            for copy in whole_copies():
                copy.start()

        @pl.when(kv < KV_HEADS)
        def real():
            for copy in head_copies():
                copy.start()

        @pl.when(kv >= KV_HEADS)
        def none():
            heads[...] = jnp.zeros_like(heads)

        @pl.when(tp < TP - 1)
        def most_came():
            for copy in wide_copies():
                copy.wait()

        @pl.when(tp == TP - 1)
        def last_came():
            for copy in whole_copies():
                copy.wait()
            for i in range(2):
                cols[i] = jnp.zeros((d_rows, OWN), bf16)
                cols[i, :, pl.ds(0, rest)] = whole[i, :, pl.ds(width - rest, rest)]

        @pl.when(kv < KV_HEADS)
        def real_came():
            for copy in head_copies():
                copy.wait()

        out_ref[pl.ds(0, d_rows), pl.ds(0, OWN)] = cols[0]
        turned = jnp.concatenate([heads[0], heads[1]], axis=0).astype(f32).T
        out_ref[pl.ds(0, d_rows), pl.ds(OWN, OWN)] = turned.astype(bf16)
        out_ref[pl.ds(0, d_rows), pl.ds(2 * OWN, OWN)] = cols[1]
        out_ref[pl.ds(d_rows, 16), :] = jnp.zeros((16, lanes), bf16)
        out_ref[d_rows, pl.ds(0, d_rows)] = g1_ref[...]
        out_ref[d_rows + 1, pl.ds(0, d_rows)] = g2_ref[...]

    return call(
        kernel,
        [shape((d_rows + 16, lanes), bf16)],
        [at, w_query, w_key.T, w_value.T, w_out, gain_one, gain_two],
        scratch=[
            pltpu.VMEM((2, d_rows, OWN), bf16),
            pltpu.VMEM((2, HEAD, d_rows), bf16),
            pltpu.VMEM((2, d_rows, width), bf16),
            pltpu.SemaphoreType.DMA((4,)),
        ],
        limit=60,
        cost=2.0,
        far=(1, 2, 3, 4),
    )[0]


def slice_ff_weights(at, w_gate, w_up, w_down, nz):
    d_rows = w_gate.shape[0]
    ff_z, width = w_down.shape
    part = ff_z // TP
    own = part * nz


    def kernel(at_ref, g_ref, u_ref, d_ref, out_ref):
        pick = one_hot(ff_z, part, at_ref[0] * part)
        for ref, start in ((g_ref, 0), (u_ref, own)):
            pieces = [nn(ref[:, pl.ds(s * ff_z, ff_z)], pick) for s in range(nz)]
            out_ref[:, pl.ds(start, own)] = jnp.concatenate(pieces, axis=1).astype(bf16)
        pieces = [nn(d_ref[pl.ds(s * d_rows, d_rows), :], pick) for s in range(nz)]
        out_ref[:, pl.ds(2 * own, own)] = jnp.concatenate(pieces, axis=1).astype(bf16)

    return call(
        kernel,
        [shape((d_rows, 3 * own), bf16)],
        [at, w_gate, w_up, w_down.T],
        limit=16,
        cost=4.0,
    )[0]


def project_keys(at, tokens, packs, cosine, sine, cotangent):
    local, width = tokens[0].shape
    half_rows = local // 2
    rows = TP * local
    nz = len(packs)
    pack_rows, lanes = packs[0].shape
    d_rows = pack_rows - 16
    per = 4
    tiles = 2 * TP // per

    def kernel(at_ref, *refs):
        toks, refs = refs[:TP], refs[TP:]
        pack, refs = refs[:nz], refs[nz:]
        cos_ref, sin_ref, cot_ref, hid_ref, kv_ref, w_ref, side_ref, gain_ref, hold, kept, sems = refs
        z = at_ref[1]
        for s in range(nz):
            hold[z ^ s] = pack[s][...]
        for s in range(nz):
            w_ref[pl.ds(s * d_rows, d_rows), :] = hold[s, pl.ds(0, d_rows), pl.ds(0, 2 * OWN)]
        gains = [hold[s, pl.ds(d_rows, 16), pl.ds(0, d_rows)].astype(f32) for s in range(nz)]
        gain_ref[...] = jnp.concatenate(gains, axis=1)[:8]
        gain = gain_ref[pl.ds(0, 1), :]
        side_ref[pl.ds(0, local), pl.ds(0, width)] = cot_ref[...]
        turned = [
            hold[s, pl.ds(0, d_rows), pl.ds(2 * OWN, OWN)].astype(f32) for s in range(nz)
        ]
        side_ref[pl.ds(local, OWN), pl.ds(0, width)] = jnp.concatenate(turned, axis=0).T.astype(bf16)
        copies = []
        for tile in range(tiles):
            side, first = (tile * per) // TP, (tile * per) % TP
            at_rows = pl.ds(tile * per * half_rows, per * half_rows)
            block = jnp.concatenate(
                [toks[first + j][pl.ds(side * half_rows, half_rows), :] for j in range(per)], axis=0
            )
            inputs = block.astype(f32)
            hidden = (inputs * norm_scale(inputs) * gain).astype(bf16)
            kept[at_rows, :] = hidden
            copy = pltpu.make_async_copy(kept.at[at_rows, :], hid_ref.at[at_rows, :], sems.at[tile])
            copy.start()
            copies.append(copy)
            pair = nn(hidden, w_ref[:, pl.ds(OWN, OWN)])
            turned = pair * cos_ref[at_rows, :] + swap_halves(pair) * sin_ref[at_rows, :]
            lane = lax.broadcasted_iota(i32, pair.shape, 1)
            kv_ref[at_rows, :] = jnp.where(lane < HEAD, turned, pair).astype(bf16)
        for copy in copies:
            copy.wait()

    return call(
        kernel,
        [
            shape((rows, width), bf16),
            shape((rows, OWN), bf16),
            shape((width, 2 * OWN), bf16),
            shape((local + OWN, TP * OWN), bf16),
            shape((8, width), f32),
        ],
        [at, *tokens, *packs, cosine, sine, cotangent],
        scratch=[
            pltpu.VMEM((nz, pack_rows, lanes), bf16),
            pltpu.VMEM((rows, width), bf16),
            pltpu.SemaphoreType.DMA((tiles,)),
        ],
        limit=30,
        cost=4.0,
        far_out=(0,),
    )


def project_queries(tokens, hidden, w_qkv, cosine, sine):
    local, width = tokens[0].shape
    half_rows = local // 2
    rows = TP * local
    per = 4

    def kernel(*refs):
        toks, refs = refs[:TP], refs[TP:]
        hid_ref, w_ref, cos_ref, sin_ref, x_ref, qt_ref = refs
        for tile in range(2 * TP // per):
            side, first = (tile * per) // TP, (tile * per) % TP
            at_rows = pl.ds(tile * per * half_rows, per * half_rows)
            for j in range(per):
                x_ref[pl.ds((tile * per + j) * half_rows, half_rows), :] = toks[first + j][
                    pl.ds(side * half_rows, half_rows), :
                ]
            query = nn(hid_ref[at_rows, :], w_ref[:, pl.ds(0, OWN)])
            query = query * cos_ref[at_rows, :] + swap_halves(query) * sin_ref[at_rows, :]
            qt_ref[:, at_rows] = (query.astype(bf16).astype(f32) * HEAD**-0.5).T.astype(bf16)

    return call(
        kernel,
        [shape((rows, width), bf16), shape((OWN, rows), bf16)],
        [*tokens, hidden, w_qkv, cosine, sine],
        scalars=0,
        limit=30,
        cost=4.0,
    )


def attention_forward(select, key_base, query_base, turned_query, own_kv, other_kv, half_rows):
    groups = len(own_kv)
    rows = own_kv[0].shape[0]
    half = rows // 2
    blocks = half // half_rows
    wide, deep = 128, 128

    def kernel(sel_ref, key_ref, query_ref, q_ref, *refs):
        own, other = refs[:groups], refs[groups : 2 * groups]
        out_ref, low_ref, lse_ref, kv_ref, kvt_ref, top_ref, mass_ref, place_ref = refs[2 * groups :]
        for head in range(2):
            chosen = sel_ref[head] == 0
            for group in range(groups):

                @pl.when(chosen)
                def take_own():
                    kv_ref[head, group] = own[group][...]
                    kvt_ref[head, group] = own[group][...].T

                @pl.when(jnp.logical_not(chosen))
                def take_other():
                    kv_ref[head, group] = other[group][...]
                    kvt_ref[head, group] = other[group][...].T

        top_ref[...] = jnp.full_like(top_ref, far_below)
        mass_ref[...] = jnp.zeros_like(mass_ref)
        out_ref[...] = jnp.zeros_like(out_ref)

        def one_step(step, unused):
            group, head = step // 2, lax.rem(step, 2)
            row = sel_ref[head] * groups + group
            own_rows = pl.ds(pl.multiple_of(head * HEAD, HEAD), HEAD)
            place_ref[...] = key_positions(key_ref, row, 0, 2 * blocks, half_rows, 128)
            for k_start in range(0, rows, deep):
                keys_at = pl.ds(k_start, deep)
                k_side = k_start // half
                block = kv_ref[head, group, keys_at, :]
                values = kvt_ref[head, group, pl.ds(HEAD, HEAD), keys_at]
                for start in range(k_side * half, rows, wide):
                    lanes = pl.ds(start, wide)
                    turned = q_ref[own_rows, lanes]
                    padded = jnp.concatenate([turned, jnp.zeros_like(turned)], axis=0)
                    scores = nn(block, padded)
                    if start // half == k_side:
                        places = query_positions(
                            query_ref, start // half_rows, wide, half_rows
                        )
                        scores = jnp.where(place_ref[keys_at, :] <= places, scores, far_below)
                    before = top_ref[head, :, lanes]
                    top = jnp.maximum(before, jnp.max(scores, axis=0, keepdims=True))
                    weights = jnp.exp(scores - top)
                    fade = jnp.exp(before - top)
                    top_ref[head, :, lanes] = top
                    mass_ref[head, :, lanes] = mass_ref[head, :, lanes] * fade + jnp.sum(
                        weights, axis=0, keepdims=True
                    )
                    out_ref[own_rows, lanes] = out_ref[own_rows, lanes] * fade + nn(
                        values, weights.astype(bf16)
                    )
            return unused

        lax.fori_loop(0, 2 * groups, one_step, 0)
        for head in range(2):
            own_rows = pl.ds(head * HEAD, HEAD)
            mass = mass_ref[head]
            out_ref[own_rows, :] = out_ref[own_rows, :] / mass
            lse_ref[pl.ds(head, 1), :] = top_ref[head] + jnp.log(mass)
        low_ref[...] = out_ref[...].T.astype(bf16)

    return call(
        kernel,
        [shape((OWN, rows), f32), shape((rows, OWN), bf16), shape((2, rows), f32)],
        [select, key_base, query_base, turned_query, *own_kv, *other_kv],
        scalars=3,
        scratch=[
            pltpu.VMEM((2, groups, rows, OWN), bf16),
            pltpu.VMEM((2, groups, OWN, rows), bf16),
            pltpu.VMEM((2, 1, rows), f32),
            pltpu.VMEM((2, 1, rows), f32),
            pltpu.VMEM((rows, 128), i32),
        ],
        limit=36,
        cost=14.0,
    )


def attention_backward(
    select, key_base, query_base, turned_query, own_kv, other_kv, traded, attended, log_mass, half_rows
):
    groups = len(own_kv)
    rows = own_kv[0].shape[0]
    half = rows // 2
    blocks = half // half_rows
    wide, deep = 512, 256

    def kernel(sel_ref, key_ref, query_ref, q_ref, *refs):
        own, other = refs[:groups], refs[groups : 2 * groups]
        refs = refs[2 * groups :]
        local = 2 * half_rows
        parts = [refs[0], refs[1]] + [
            refs[2 + j].at[pl.ds(k * local, local), :] for j in range(TP // 2 - 1) for k in range(2)
        ]
        refs = refs[1 + TP // 2 :]
        att_ref, lse_ref, dq_ref, keep_ref, pass_ref, gb_ref = refs[:6]
        kv_ref, sum_ref, g_ref, rq_ref, rg_ref, delta_ref, pos_ref = refs[6:]
        for group in range(groups):
            kv_ref[0, group] = own[group][...]
            kv_ref[1, group] = other[group][...]
        sum_ref[...] = jnp.zeros_like(sum_ref)
        dq_ref[...] = jnp.zeros_like(dq_ref)
        zeros = jnp.zeros((rows, HEAD), bf16)
        for j in range(0, TP, 2):
            for side in range(2):
                at = pl.ds(side * half + j * half_rows, 2 * half_rows)
                pair = jnp.concatenate(
                    [parts[j + k][pl.ds(side * half_rows, half_rows), :] for k in range(2)], axis=0
                )
                g_ref[:, at] = pair[:, :OWN].T
                gb_ref[at, :] = pair[:, OWN:]
        for head in range(2):
            own_rows = pl.ds(head * HEAD, HEAD)
            rq_ref[head] = jnp.concatenate([q_ref[own_rows, :].T, zeros], axis=1)
            grad = g_ref[own_rows, :]
            rg_ref[head] = jnp.concatenate([zeros, grad.T], axis=1)
            delta_ref[pl.ds(head, 1), :] = jnp.sum(
                grad.astype(f32) * att_ref[own_rows, :], axis=0, keepdims=True
            )

        def one_group(group, unused):
            for head in range(2):
                which = sel_ref[head]
                own_rows = pl.ds(head * HEAD, HEAD)
                stat = pl.ds(head, 1)
                pos_ref[...] = key_positions(
                    key_ref, which * groups + group, 0, 2 * blocks, half_rows, 128
                )
                for k_start in range(0, rows, deep):
                    keys_at = pl.ds(k_start, deep)
                    k_side = k_start // half
                    block = kv_ref[which, group, keys_at, :]
                    turned_keys = block.T[:HEAD]
                    for start in range(k_side * half, rows, wide):
                        lanes = pl.ds(start, wide)
                        turned = q_ref[own_rows, lanes]
                        padded = jnp.concatenate([turned, jnp.zeros_like(turned)], axis=0)
                        scores = nn(block, padded)
                        if start // half == k_side:
                            places = query_positions(
                                query_ref, start // half_rows, wide, half_rows
                            )
                            at = jnp.concatenate([pos_ref[keys_at, :]] * (wide // 128), axis=1)
                            scores = jnp.where(at <= places, scores, far_below)
                        probs = jnp.exp(scores - lse_ref[stat, lanes])
                        grads = g_ref[own_rows, lanes]
                        padded = jnp.concatenate([jnp.zeros_like(grads), grads], axis=0)
                        grad_probs = nn(block, padded)
                        grad_scores = probs * (grad_probs - delta_ref[stat, lanes])
                        probs = probs.astype(bf16)
                        grad_scores = grad_scores.astype(bf16)
                        sum_ref[which, group, keys_at, :] += nn(
                            grad_scores, rq_ref[head, lanes, :]
                        ) + nn(probs, rg_ref[head, lanes, :])
                        dq_ref[own_rows, lanes] += nn(turned_keys, grad_scores)
            return unused

        lax.fori_loop(0, groups, one_group, 0)
        for group in range(groups):
            keep_ref[pl.ds(group * rows, rows), :] = sum_ref[0, group]
            pass_ref[pl.ds(group * rows, rows), :] = sum_ref[1, group].astype(bf16)

    return call(
        kernel,
        [
            shape((OWN, rows), f32),
            shape((groups * rows, OWN), f32),
            shape((groups * rows, OWN), bf16),
            shape((rows, OWN), bf16),
        ],
        [
            select,
            key_base,
            query_base,
            turned_query,
            *own_kv,
            *other_kv,
            *traded,
            attended,
            log_mass,
        ],
        scalars=3,
        scratch=[
            pltpu.VMEM((2, groups, rows, OWN), bf16),
            pltpu.VMEM((2, groups, rows, OWN), f32),
            pltpu.VMEM((OWN, rows), bf16),
            pltpu.VMEM((2, rows, OWN), bf16),
            pltpu.VMEM((2, rows, OWN), bf16),
            pltpu.VMEM((2, rows), f32),
            pltpu.VMEM((rows, 128), i32),
        ],
        limit=28,
        cost=18.0,
    )


def store_blocks(part, tile, per, half_rows, keep_ref, pass_ref, x_first=False):
    side = (tile * per) // TP
    first = lax.rem(tile * per, TP) // 2
    for j in range(per):
        piece = part[j * half_rows : (j + 1) * half_rows]
        place = first // 2 + j if x_first else first + j // 2
        if x_first and j % 2:
            place = first // 2 + j - 1
        row = (2 * place + side) * half_rows
        at = pl.ds(pl.multiple_of(row, half_rows), half_rows)
        target = keep_ref if j % 2 == 0 else pass_ref
        target[at, pl.ds(0, piece.shape[1])] = piece.astype(target.dtype)


def feed_forward(at, inputs, attended, sides, packs, gains, nz):
    rows, width = inputs.shape
    local = rows // TP
    half_rows = local // 2
    half = rows // 2
    d_rows, lanes = packs[0].shape
    ff = lanes // 3
    part_rows = ff // nz
    per = 4
    tile_rows = per * half_rows
    tiles = 2 * TP // per

    def kernel(at_ref, x_ref, *refs):
        att, refs = refs[:TP], refs[TP:]
        extra, refs = refs[:TP], refs[TP:]
        pack, refs = refs[:nz], refs[nz:]
        gain_ref, refs = refs[0], refs[1:]
        resid_out, gk_ref, gp_ref, gain_out, dn_w = refs[:5]
        targets, prod_out, refs = refs[5 : 5 + nz], refs[5 + nz], refs[6 + nz :]
        att_ref, wo_ref, gu_w, cot_ref, hold, acc_gu, acc_dn, blocks, prod_ref, sems = refs
        tp = at_ref[0]
        z = at_ref[1]
        for j in range(TP):
            columns = pl.ds(pl.multiple_of((tp ^ j) * OWN, OWN), OWN)
            wo_ref[columns, :] = extra[j][pl.ds(local, OWN), pl.ds(0, width)]
            for side in range(2):
                for k in range(TP):
                    att_ref[pl.ds(side * half + k * half_rows, half_rows), columns] = att[j][
                        pl.ds(side * half + (k ^ j) * half_rows, half_rows), :
                    ]
                cot_ref[pl.ds(side * half + j * half_rows, half_rows), :] = extra[j][
                    pl.ds(side * half_rows, half_rows), pl.ds(0, width)
                ]
        for s in range(nz):
            hold[z ^ s] = pack[s][...]
        for s in range(nz):
            rows_at = pl.ds(s * d_rows, d_rows)
            gu_w[rows_at, :] = hold[s, :, pl.ds(0, 2 * ff)]
            dn_w[rows_at, :] = jnp.concatenate(
                [
                    hold[b][:, 2 * ff + s * part_rows : 2 * ff + (s + 1) * part_rows]
                    for b in range(nz)
                ],
                axis=1,
            )
        gain = gain_ref[pl.ds(1, 1), :]
        gain_out[...] = jnp.zeros_like(gain_out)
        acc_gu[...] = jnp.zeros_like(acc_gu)
        acc_dn[...] = jnp.zeros_like(acc_dn)

        def copy_of(tile):
            at_rows = pl.ds(pl.multiple_of(tile * tile_rows, tile_rows), tile_rows)
            return pltpu.make_async_copy(
                prod_ref.at[at_rows, :], prod_out.at[at_rows, :], sems.at[tile]
            )

        def one_tile(tile, unused):
            at_rows = pl.ds(pl.multiple_of(tile * tile_rows, tile_rows), tile_rows)
            branch = nt(att_ref[at_rows, :][:, :width], wo_ref[pl.ds(0, width), :])
            resid = x_ref[at_rows, :].astype(f32) + branch
            side = (tile * per) // TP

            @pl.when(lax.rem(tile * per, TP) == 0)
            def keep_own():
                resid_out[pl.ds(pl.multiple_of(side * half_rows, half_rows), half_rows), :] = resid[
                    :half_rows
                ]

            normal = resid * norm_scale(resid)
            hidden = (normal * gain).astype(bf16)
            gate_up = nn(hidden, gu_w[...])
            gate, up = gate_up[:, :ff], gate_up[:, ff:]
            sigmoid = 1.0 / (1.0 + jnp.exp(-gate))
            activated = gate * sigmoid
            product = (activated * up).astype(bf16)
            prod_ref[at_rows, :] = product
            copy_of(tile).start()
            cotangent = cot_ref[at_rows, :]
            grad_product = nn(cotangent, dn_w[...])
            grad_gate = grad_product * up * sigmoid * (1.0 + gate * (1.0 - sigmoid))
            grad_gu = jnp.concatenate([grad_gate, grad_product * activated], axis=1).astype(bf16)
            partial = nt(grad_gu, gu_w[...])
            gain_out[pl.ds(0, 1), :] += jnp.sum(partial * normal, axis=0, keepdims=True)
            store_blocks(partial, tile, per, half_rows, gk_ref, gp_ref)
            acc_gu[...] += tn(hidden, grad_gu)
            acc_dn[...] += tn(cotangent, product)
            return unused

        lax.fori_loop(0, tiles, one_tile, 0)
        for b in range(nz):
            blocks[b] = jnp.concatenate(
                [
                    acc_dn[pl.ds(s * d_rows, d_rows), :][:, b * part_rows : (b + 1) * part_rows]
                    for s in range(nz)
                ],
                axis=1,
            )
        for s in range(nz):
            block = pl.ds(pl.multiple_of((z ^ s) * d_rows, 8), d_rows)
            targets[s][:, pl.ds(0, 2 * ff)] = acc_gu[block, :].astype(targets[s].dtype)
            targets[s][:, pl.ds(2 * ff, ff)] = blocks[z ^ s].astype(targets[s].dtype)
        for tile in range(tiles):
            copy_of(tile).wait()

    return call(
        kernel,
        [
            shape((local, width), f32),
            shape((TP // 2 * local, width), bf16),
            shape((TP // 2 * local, TP * OWN), bf16),
            shape((8, width), f32),
            shape((width, ff), bf16),
        ]
        + [shape((d_rows, lanes), f32 if s % 2 == 0 else bf16) for s in range(nz)]
        + [shape((rows, ff), bf16)],
        [at, inputs, *attended, *sides, *packs, gains],
        scratch=[
            pltpu.VMEM((rows, TP * OWN), bf16),
            pltpu.VMEM((TP * OWN, width), bf16),
            pltpu.VMEM((width, 2 * ff), bf16),
            pltpu.VMEM((rows, width), bf16),
            pltpu.VMEM((nz, d_rows, lanes), bf16),
            pltpu.VMEM((width, 2 * ff), f32),
            pltpu.VMEM((width, ff), f32),
            pltpu.VMEM((nz, d_rows, ff), f32),
            pltpu.VMEM((rows, ff), bf16),
            pltpu.SemaphoreType.DMA((tiles,)),
        ],
        limit=36,
        cost=17.0,
        far_out=(5 + nz,),
    )


def feed_forward_rest(at, attended, sides, product, w_down):
    rows = attended[0].shape[0]
    width, ff = w_down.shape
    local = rows // TP
    half_rows = local // 2
    half = rows // 2
    per = 4
    tile_rows = per * half_rows

    def kernel(at_ref, *refs):
        att, refs = refs[:TP], refs[TP:]
        extra, refs = refs[:TP], refs[TP:]
        prod_ref, dn_w, att_out, wo_out, lk_ref, lp_ref = refs
        tp = at_ref[0]
        for j in range(TP):
            columns = pl.ds(pl.multiple_of((tp ^ j) * OWN, OWN), OWN)
            wo_out[columns, :] = extra[j][pl.ds(local, OWN), pl.ds(0, width)]
            for side in range(2):
                for k in range(TP):
                    att_out[pl.ds(side * half + k * half_rows, half_rows), columns] = att[j][
                        pl.ds(side * half + (k ^ j) * half_rows, half_rows), :
                    ]

        def one_tile(tile, unused):
            at_rows = pl.ds(pl.multiple_of(tile * tile_rows, tile_rows), tile_rows)
            part = nt(prod_ref[at_rows, :], dn_w[...])
            store_blocks(part, tile, per, half_rows, lk_ref, lp_ref)
            return unused

        lax.fori_loop(0, 2 * TP // per, one_tile, 0)

    return call(
        kernel,
        [
            shape((rows, TP * OWN), bf16),
            shape((TP * OWN, width), bf16),
            shape((TP // 2 * local, width), bf16),
            shape((TP // 2 * local, TP * OWN), bf16),
        ],
        [at, *attended, *sides, product, w_down],
        limit=24,
        cost=5.0,
    )


def add_crossed(keep, crossed, count, tail=None):
    local, width = keep.shape[0] // count, keep.shape[1]
    tails = [] if tail is None else [tail]
    more = 0 if tail is None else tail.shape[0]

    def kernel(keep_ref, cross_ref, *refs):
        own_ref, *sends = refs[len(tails) :]
        for j in range(count):
            at = pl.ds(j * local, local)
            target = own_ref if j == 0 else sends[j - 1]
            target[pl.ds(0, local), pl.ds(0, width)] = (
                keep_ref[at, :].astype(f32) + cross_ref[at, pl.ds(0, width)].astype(f32)
            ).astype(target.dtype)
        if tails:
            sends[-1][pl.ds(local, more), pl.ds(0, width)] = refs[0][...]

    return call(
        kernel,
        [shape((local, width), f32)]
        + [shape((local, width), bf16)] * (count - 2)
        + [shape((local + more, TP * OWN if tails else width), bf16)],
        [keep, crossed, *tails],
        scalars=0,
        limit=12,
        cost=1.0,
    )


def branch_gradient(at, sums, resid, cotangent, w_out, gains):
    local, width = resid.shape

    def kernel(at_ref, *refs):
        parts, refs = refs[: len(sums)], refs[len(sums) :]
        resid_ref, cot_ref, wo_ref, gain_ref, grad_ref, keep_ref, pass_ref, ga_ref, gb_ref = refs
        tp = at_ref[0]
        grad_hidden = parts[0][...]
        for part in parts[1:]:
            grad_hidden = grad_hidden + part[...].astype(f32)
        resid = resid_ref[...]
        scale = norm_scale(resid)
        normal = resid * scale
        grad = grad_hidden * gain_ref[pl.ds(1, 1), :]
        grad = scale * (grad - normal * jnp.mean(grad * normal, axis=1, keepdims=True))
        grad = grad + cot_ref[...].astype(f32)
        grad_ref[...] = grad
        low = grad.astype(bf16)
        gb_ref[...] = jnp.zeros_like(gb_ref)
        gb_ref[:, pl.ds(0, width)] = low
        ga_ref[...] = jnp.zeros_like(ga_ref)
        ga_ref[:, pl.ds(0, width)] = nn(low, wo_ref[pl.ds(0, width), :]).astype(bf16)
        for j in range(TP):
            columns = pl.ds(pl.multiple_of((tp ^ j) * OWN, OWN), OWN)
            target = keep_ref if j % 2 == 0 else pass_ref
            rows = pl.ds((j // 2) * local, local)
            target[rows, pl.ds(0, OWN)] = ga_ref[:, columns]
            target[rows, pl.ds(OWN, OWN)] = gb_ref[:, columns]

    blocks = shape((TP // 2 * local, 2 * OWN), bf16)
    return call(
        kernel,
        [shape((local, width), f32), blocks, blocks],
        [at, *sums, resid, cotangent, w_out, gains],
        scratch=[pltpu.VMEM((local, TP * OWN), bf16), pltpu.VMEM((local, TP * OWN), bf16)],
        limit=16,
        cost=3.0,
    )


def pair_up(keep, crossed, count):
    local, width = keep.shape[0] // count, keep.shape[1]

    def kernel(keep_ref, cross_ref, *outs):
        for j in range(1, count):
            at = pl.ds(j * local, local)
            outs[j - 1][pl.ds(0, local), :] = keep_ref[at, :]
            outs[j - 1][pl.ds(local, local), :] = cross_ref[at, :]

    return call(
        kernel,
        [shape((2 * local, width), bf16)] * (count - 1),
        [keep, crossed],
        scalars=0,
        limit=8,
        cost=0.7,
    )


def projection_gradient(
    at, grad_query, grad_kv, inputs, hidden, w_qkv, gain_sums, cosine, sine, grad_out, nz
):
    rows, width = inputs.shape
    local = rows // TP
    half_rows = local // 2
    d_rows = width // nz
    per = 4
    tile_rows = per * half_rows
    pieces = len(grad_kv)

    def kernel(at_ref, dq_ref, *refs):
        kvs, refs = refs[:pieces], refs[pieces:]
        x_ref, hid_ref, w_ref, gain_two_ref, cos_ref, sin_ref, wo_ref = refs[:7]
        keep_ref, pass_ref, own_ref = refs[7:10]
        sends, refs = refs[10 : 10 + nz - 1], refs[10 + nz - 1 :]
        turn_ref, acc_ref, gain_acc, hold = refs
        z = at_ref[1]
        turn_ref[...] = dq_ref[...].T * HEAD**-0.5
        acc_ref[...] = jnp.zeros_like(acc_ref)
        gain_acc[...] = jnp.zeros_like(gain_acc)

        def one_tile(tile, unused):
            at_rows = pl.ds(pl.multiple_of(tile * tile_rows, tile_rows), tile_rows)
            cos, sin = cos_ref[at_rows, :], sin_ref[at_rows, :]
            query = turn_ref[at_rows, :]
            query = query * cos - swap_halves(query) * sin
            pair = kvs[0][at_rows, :].astype(f32)
            for piece in kvs[1:]:
                pair = pair + piece[at_rows, :].astype(f32)
            turned = pair * cos - swap_halves(pair) * sin
            lane = lax.broadcasted_iota(i32, pair.shape, 1)
            pair = jnp.where(lane < HEAD, turned, pair)
            grad = jnp.concatenate([query, pair], axis=1).astype(bf16)
            partial = nt(grad, w_ref[...])
            x = x_ref[at_rows, :].astype(f32)
            gain_acc[pl.ds(0, 1), :] += jnp.sum(partial * (x * norm_scale(x)), axis=0, keepdims=True)
            store_blocks(partial, tile, per, half_rows, keep_ref, pass_ref, True)
            acc_ref[...] += tn(hid_ref[at_rows, :], grad)
            return unused

        lax.fori_loop(0, 2 * TP // per, one_tile, 0)
        hold[...] = jnp.zeros_like(hold)
        for s in range(nz):
            columns = slice(s * d_rows, (s + 1) * d_rows)
            hold[s, pl.ds(0, 1), pl.ds(0, d_rows)] = gain_acc[pl.ds(0, 1), :][:, columns]
            hold[s, pl.ds(1, 1), pl.ds(0, d_rows)] = gain_two_ref[pl.ds(0, 1), :][:, columns]
        for s in range(nz):
            block = z ^ s
            target = own_ref if s == 0 else sends[s - 1]
            rows_at = pl.ds(pl.multiple_of(block * d_rows, 8), d_rows)
            part = pl.ds(0, d_rows)
            target[part, pl.ds(0, 2 * OWN)] = acc_ref[rows_at, :].astype(target.dtype)
            target[part, pl.ds(2 * OWN, OWN)] = wo_ref[rows_at, :].astype(target.dtype)
            target[pl.ds(d_rows, 16), :] = hold[block].astype(target.dtype)

    return call(
        kernel,
        [
            shape((TP // 2 * local, width), bf16),
            shape((TP // 2 * local, TP * OWN), bf16),
            shape((d_rows + 16, 3 * OWN), f32),
        ]
        + [shape((d_rows + 16, 3 * OWN), bf16)] * (nz - 1),
        [at, grad_query, *grad_kv, inputs, hidden, w_qkv, gain_sums, cosine, sine, grad_out],
        scratch=[
            pltpu.VMEM((rows, OWN), f32),
            pltpu.VMEM((width, 2 * OWN), f32),
            pltpu.VMEM((8, width), f32),
            pltpu.VMEM((nz, 16, 3 * OWN), f32),
        ],
        limit=32,
        cost=8.0,
    )


def token_gradient(sums, tokens, grad_resid, gains):
    local, width = tokens.shape

    def kernel(*refs):
        parts, refs = refs[: len(sums)], refs[len(sums) :]
        x_ref, grad_ref, gain_ref, out_ref = refs
        grad_hidden = parts[0][...]
        for part in parts[1:]:
            grad_hidden = grad_hidden + part[...].astype(f32)
        x = x_ref[...].astype(f32)
        scale = norm_scale(x)
        normal = x * scale
        grad = grad_hidden * gain_ref[pl.ds(0, 1), :]
        grad = scale * (grad - normal * jnp.mean(grad * normal, axis=1, keepdims=True))
        out_ref[...] = (grad + grad_ref[...]).T

    return call(
        kernel,
        [shape((width, local), f32)],
        [*sums, tokens, grad_resid, gains],
        scalars=0,
        limit=8,
        cost=1.0,
    )[0].T


def layer_output(near, arrived, resid):
    local, width = resid.shape
    start = arrived.shape[0] - local

    def kernel(near_ref, in_ref, resid_ref, out_ref):
        total = resid_ref[...] + near_ref[...] + in_ref[pl.ds(start, local), pl.ds(0, width)].astype(f32)
        out_ref[...] = total.T.astype(bf16)

    turned = shape(resid.shape[::-1], bf16)
    return call(kernel, [turned], [near, arrived, resid], scalars=0, limit=8, cost=1.0)[0].T


def first_sum(own, arrived):
    def kernel(own_ref, in_ref, out_ref):
        out_ref[...] = (own_ref[...] + in_ref[...].astype(f32)).astype(bf16)

    return call(
        kernel, [shape(own.shape, bf16)], [own, arrived], scalars=0, limit=8, cost=1.0
    )[0]


def last_sum(own, *arrived):
    rows, lanes = own.shape

    def kernel(own_ref, *refs):
        total = own_ref[...]
        for ref in refs[:-1]:
            total = total + ref[...].astype(f32)
        refs[-1][:, pl.ds(0, lanes)] = total.astype(bf16)

    return call(
        kernel, [shape((rows, TP * OWN), bf16)], [own, *arrived], scalars=0, limit=8, cost=1.0
    )[0]


def ff_outputs(at, mine, by_x, by_y, by_xy, odd, ff_z, nz):
    d_rows = mine.shape[0]
    part = ff_z // TP
    ff = part * nz

    def kernel(at_ref, m_ref, x_ref, y_ref, xy_ref, odd_ref, gate_ref, up_ref, down_ref, hold):
        tp = at_ref[0]
        lanes = pl.ds(0, 3 * ff)
        for j, ref in enumerate((m_ref, x_ref, y_ref, xy_ref)):
            hold[tp ^ (2 * j)] = ref[:, lanes]
        for j in range(TP // 2):
            hold[tp ^ (2 * j + 1)] = odd_ref[pl.ds(d_rows * j, d_rows), lanes]
        for s in range(nz):
            for start in (s * part, ff + s * part, 2 * ff + s * part):
                block = jnp.concatenate(
                    [hold[c][:, start : start + part] for c in range(TP)], axis=1
                ).astype(f32)
                if start < ff:
                    gate_ref[:, pl.ds(s * ff_z, ff_z)] = block
                elif start < 2 * ff:
                    up_ref[:, pl.ds(s * ff_z, ff_z)] = block
                else:
                    down_ref[pl.ds(s * d_rows, d_rows), :] = block

    gate, up, down = call(
        kernel,
        [
            shape((d_rows, nz * ff_z), f32),
            shape((d_rows, nz * ff_z), f32),
            shape((nz * d_rows, ff_z), f32),
        ],
        [at, mine, by_x, by_y, by_xy, odd],
        scratch=[pltpu.VMEM((TP, d_rows, 3 * ff), bf16)],
        limit=32,
        cost=7.0,
    )
    return gate, up, down.T


def projection_outputs(at, slots, width):
    d_rows = slots[0].shape[0] - 16

    def kernel(at_ref, *refs):
        parts, (q_ref, k_ref, v_ref, o_ref, one_ref, two_ref, hold) = refs[:TP], refs[TP:]
        tp = at_ref[0]
        total = jnp.zeros((16, 3 * OWN), f32)
        for j in range(TP):
            hold[tp ^ j] = parts[j][...]
            total = total + parts[j][pl.ds(d_rows, 16), :].astype(f32)
        one_ref[...] = total[0:1, :d_rows]
        two_ref[...] = total[1:2, :d_rows]
        heads = [hold[c][:d_rows, :OWN] for c in range(TP)]
        q_ref[...] = jnp.concatenate(heads, axis=1)[:, :width].astype(f32)
        heads = [hold[c][:d_rows, 2 * OWN :] for c in range(TP)]
        o_ref[...] = jnp.concatenate(heads, axis=1)[:, :width].astype(f32)
        kv = [hold[c][:d_rows, OWN : 2 * OWN].astype(f32) for c in range(TP)]
        kv = [kv[0], kv[1] + kv[2], kv[3] + kv[4], kv[5], kv[6]]
        for c in range(KV_HEADS):
            turned = kv[c].T
            k_ref[pl.ds(c * HEAD, HEAD), :] = turned[:HEAD]
            v_ref[pl.ds(c * HEAD, HEAD), :] = turned[HEAD:]

    query, key, value, out, one, two = call(
        kernel,
        [
            shape((d_rows, width), f32),
            shape((KV_HEADS * HEAD, d_rows), f32),
            shape((KV_HEADS * HEAD, d_rows), f32),
            shape((d_rows, width), f32),
            shape((1, d_rows), f32),
            shape((1, d_rows), f32),
        ],
        [at, *slots],
        scratch=[pltpu.VMEM((TP, d_rows + 16, 3 * OWN), bf16)],
        limit=12,
        cost=0.01,
    )
    return query, key.T, value.T, out, one, two


def body(
    tokens,
    pair_order,
    gain_attn,
    gain_mlp,
    w_query,
    w_key,
    w_value,
    w_out,
    w_gate,
    w_up,
    w_down,
    cotangent,
):
    local_rows, width = tokens.shape
    half_rows = local_rows // 2
    nz = lax.axis_size("fsdp")
    outer = lax.axis_size("ctx") // TP
    count = lax.axis_size(AXES)
    groups = outer * nz
    me = lax.axis_index(AXES)
    z = lax.axis_index("fsdp")
    tp = lax.axis_index("ctx") % TP
    kv_index = (4 * (tp // 2)) // GROUP + tp % 2
    at = jnp.stack([tp, z, kv_index]).astype(i32)
    send = functools.partial(exchange, count=count)
    group_mask = [(g // nz) * TP * nz + g % nz for g in range(groups)]

    def after(value, *others):
        return lax.optimization_barrier((value, *others))[0]

    def level(*arrays):
        return list(lax.optimization_barrier(arrays))

    def gather_even(block):
        return [block] + [send(block, j * nz) for j in range(2, TP, 2)]

    def gather_odd(even):
        return [piece for e in even for piece in (e, send(e, nz))]

    def scatter_far(pieces):
        return [send(piece, 2 * (j + 1) * nz) for j, piece in enumerate(pieces)]

    def from_z(block):
        return [block] + [send(block, s) for s in range(1, nz)]

    pack_one = slice_attention_weights(at, w_query, w_key, w_value, w_out, gain_attn, gain_mlp)
    token_slots = gather_odd(level(*gather_even(tokens)))
    pack_two = slice_ff_weights(after(at, pack_one), w_gate, w_up, w_down, nz)
    pack_one = from_z(pack_one)

    slot_of = jnp.array([[m | (j * nz) for j in range(TP)] for m in group_mask], dtype=i32)
    low = pair_order[me ^ slot_of]
    base = jnp.stack([low, 2 * count - 1 - low], axis=1) * half_rows
    query_base = base[0].reshape(2 * TP)
    partner = jnp.array([j ^ 1 for j in range(TP)], dtype=i32)
    key_base = jnp.stack([base, base[:, :, partner]]).reshape(2 * groups, 2 * TP)
    places = (query_base[:, None] + jnp.arange(half_rows, dtype=i32)[None, :]).reshape(-1)
    lane = jnp.arange(OWN)
    freqs = base_theta ** (-2.0 * (lane % (HEAD // 2)).astype(f32) / HEAD)
    angles = places.astype(f32)[:, None] * freqs[None, :]
    cosine = jnp.cos(angles)
    sine = jnp.sin(angles) * jnp.where(lane % HEAD < HEAD // 2, -1.0, 1.0)[None, :]
    select = jnp.where((2 * tp + jnp.arange(2)) // GROUP == kv_index, 0, 1).astype(i32)

    mask_x, mask_y = 2 * nz, 4 * nz
    hidden_one, kv, w_qkv, side, gains = project_keys(
        after(at, pack_two, select, key_base, query_base),
        token_slots,
        pack_one,
        cosine,
        sine,
        cotangent,
    )
    own_kv = [kv] + [send(kv, m) for m in group_mask[1:]]
    side_x, side_y = send(side, mask_x), send(side, mask_y)
    inputs, turned_query = project_queries(
        token_slots, after(hidden_one, kv), w_qkv, cosine, sine
    )
    side_x, side_y, inputs, turned_query, *own_kv = level(
        side_x, side_y, inputs, turned_query, *own_kv
    )
    other_kv = level(*[send(slot, nz) for slot in own_kv])
    near = send(after(pack_two, *own_kv), 2)
    one = send(after(pack_two, *other_kv), 1)
    side_xy = send(side_x, mask_y)
    side_odd, odd_x = send(after(side, *other_kv), nz), send(after(side_x, *other_kv), nz)
    attended, attended_own, log_mass = attention_forward(
        select, key_base, query_base, turned_query, own_kv, other_kv, half_rows
    )
    attended_own, near, one, side_xy, side_odd, odd_x = level(
        attended_own, near, one, side_xy, side_odd, odd_x
    )
    far, side_xy, *even = level(send(near, 1), side_xy, *gather_even(attended_own))
    attended_slots = gather_odd(even)
    packs = [pack_two, one, near, far]
    odd_y = send(after(side_y, side_xy), nz)
    sides = [side, side_odd, side_x, odd_x, side_y, odd_y, side_xy, send(side_xy, nz)]

    resid, grad_keep, grad_pass, gain_sums, w_down_own, *ff_blocks, product = feed_forward(
        at, inputs, attended_slots, sides, packs, gains, nz
    )
    ff_own, ff_one, ff_two, ff_three = ff_blocks
    first, *rest = add_crossed(grad_keep, send(grad_pass, nz), TP // 2)
    attended_low, w_out_all, out_keep, out_pass, ff_three, first, *rest = level(
        *feed_forward_rest(after(at, first), attended_slots, sides, product, w_down_own),
        send(after(ff_three, first), 1),
        first,
        *scatter_far(rest),
    )
    grad_resid, trade_keep, trade_pass = branch_gradient(
        at, [first, *rest], resid, cotangent, w_out_all, gains
    )
    crossed, out_crossed = level(send(trade_pass, nz), send(after(out_pass, first), nz))
    pairs = level(*scatter_far(pair_up(trade_keep, crossed, TP // 2)))
    out_near, out_far = add_crossed(out_keep, out_crossed, 2)
    ff_one = send(after(ff_one, crossed), 1)
    ff_two = send(first_sum(ff_two, ff_three), 2)
    out_far = send(after(out_far, *pairs), mask_y)

    grad_query, kv_keep, kv_pass, branch_columns = attention_backward(
        after(select, out_near),
        key_base,
        query_base,
        turned_query,
        own_kv,
        other_kv,
        [trade_keep, crossed, *pairs],
        attended,
        log_mass,
        half_rows,
    )
    kv_pass, ff_one, ff_two, out_far = level(kv_pass, ff_one, ff_two, out_far)
    kv_crossed = send(kv_pass, nz)
    first, *rest = add_crossed(kv_keep, kv_crossed, groups)
    grad_out = tn(attended_low[:, :width], after(branch_columns, rest[0]))
    ff_total = last_sum(after(ff_own, grad_out), ff_one, ff_two)

    for step in range(outer.bit_length() - 1):
        crossing = send(ff_total, TP * nz << step).astype(f32)
        ff_total = (ff_total.astype(f32) + crossing).astype(bf16)
    out_near, out_far = add_crossed(after(out_near, rest[0]), out_far, 2)
    ff_x, ff_y, *grad_kv = level(
        send(ff_total, mask_x),
        send(ff_total, mask_y),
        *[send(piece, m) for piece, m in zip(rest, group_mask[1:])],
    )

    last_keep, last_pass, last_own, *last_sends = projection_gradient(
        at,
        grad_query,
        [first, *grad_kv],
        inputs,
        hidden_one,
        w_qkv,
        gain_sums,
        cosine,
        sine,
        grad_out,
        nz,
    )
    near, far = add_crossed(last_keep, send(last_pass, nz), 2, out_far)
    ff_xy, far, *arrived = level(
        send(after(ff_x, last_own), mask_y),
        send(far, mask_x),
        *[send(piece, s + 1) for s, piece in enumerate(last_sends)],
    )
    layer_out = layer_output(out_near, far, resid)
    near, far = add_crossed(near, far, 2)
    last_total = last_own
    for piece in arrived:
        last_total = last_total + piece.astype(f32)
    for step in range(outer.bit_length() - 1):
        last_total = last_total + send(last_total.astype(bf16), TP * nz << step).astype(f32)
    last_total = last_total.astype(bf16)
    ff_slots = [ff_total, ff_x, ff_y, ff_xy]
    ff_slots.append(send(jnp.concatenate(ff_slots, axis=0), nz))
    grad_gate, grad_up, grad_down = ff_outputs(at, *ff_slots, w_down.shape[0], nz)
    far = send(far, mask_y)
    grad_gate, *even = level(grad_gate, *gather_even(last_total))
    last_slots = gather_odd(even)
    grad_w_query, grad_w_key, grad_w_value, grad_out, gain_one, gain_two = projection_outputs(
        at, last_slots, width
    )
    grad_tokens = token_gradient([after(near, grad_w_query), far], tokens, grad_resid, gains)
    return (
        layer_out,
        grad_tokens,
        gain_one.reshape(-1),
        gain_two.reshape(-1),
        grad_w_query,
        grad_w_key,
        grad_w_value,
        grad_out,
        grad_gate,
        grad_up,
        grad_down,
    )


def solution(mesh):
    return jax.shard_map(
        body,
        mesh=mesh,
        in_specs=(
            P(("ctx", "fsdp"), None),
            P(),
            P("fsdp"),
            P("fsdp"),
            P("fsdp", None),
            P("fsdp", None),
            P("fsdp", None),
            P("fsdp", None),
            P("fsdp", None),
            P("fsdp", None),
            P("fsdp", None),
            P(("ctx", "fsdp"), None),
        ),
        out_specs=(
            P(("ctx", "fsdp"), None),
            P(("ctx", "fsdp"), None),
            P("fsdp"),
            P("fsdp"),
            P("fsdp", None),
            P("fsdp", None),
            P("fsdp", None),
            P("fsdp", None),
            P("fsdp", None),
            P("fsdp", None),
            P("fsdp", None),
        ),
        check_vma=False,
    )
```
